32 devices in a mesh: dp: 4 (over z), context: 2 (over x), expert: 4 (over y, core).
Axes of the slice: x: 2, y: 2, z: 4, core: 2. Of those that a mesh axis runs over, the one named last changes fastest.
Arguments:
- hidden_in: bfloat16 [16, 1024, 768], P(('dp', 'expert'), 'context'), may hold values from -6 to 6
- prev_logits: float32 [16, 1024, 12], P(('dp', 'expert'), 'context'), may hold values from -6 to 6
- segment_ids: int32 [16, 1024], P(('dp', 'expert'), 'context'), may hold values from 0 to 6, as said below
- routes: int32 [16, 1024, 2], P(('dp', 'expert'), 'context'), may hold values from 0 to 11, as said below
- adapter_ids: int32 [16], replicated, may hold values from 0 to 7
- attn_gain: bfloat16 [768], replicated, may hold values from 0.5 to 1.5
- w_qkv: bfloat16 [768, 2304], replicated, may hold values from -0.21875 to 0.21875
- w_out: bfloat16 [768, 768], replicated, may hold values from -2 to 2
- attn_down: bfloat16 [8, 4, 768, 16], replicated, may hold values from -0.21875 to 0.21875
- attn_up: bfloat16 [8, 4, 16, 768], replicated, may hold values from -0.75 to 0.75
- ffn_gain: bfloat16 [768], replicated, may hold values from 0.5 to 1.5
- router_weight: bfloat16 [768, 12], replicated, may hold values from -0.109375 to 0.109375
- gate_mix: float32 [12, 12], replicated, may hold values from -0.875 to 0.875
- const_mix: bfloat16 [2, 768, 2], replicated, may hold values from -0.21875 to 0.21875
- const_vec: bfloat16 [2, 768], replicated, may hold values from -6 to 6
- w_gate_up: bfloat16 [8, 768, 4096], P('expert'), may hold values from -0.21875 to 0.21875
- w_down: bfloat16 [8, 2048, 768], P('expert'), may hold values from -0.125 to 0.125
- exp_in_down: bfloat16 [8, 8, 768, 32], P(None, 'expert'), may hold values from -0.21875 to 0.21875
- exp_in_up: bfloat16 [8, 8, 2, 16, 2048], P(None, 'expert'), may hold values from -0.75 to 0.75
- exp_out_down: bfloat16 [8, 8, 2048, 16], P(None, 'expert'), may hold values from -0.125 to 0.125
- exp_out_up: bfloat16 [8, 8, 16, 768], P(None, 'expert'), may hold values from -0.75 to 0.75
- cotangent: bfloat16 [16, 1024, 768], P(('dp', 'expert'), 'context'), may hold values from -6 to 6
Outputs:
- hidden_out: bfloat16 [16, 1024, 768], P(('dp', 'expert'), 'context')
- grad_in: float32 [16, 1024, 768], P(('dp', 'expert'), 'context')
- grad_prev: float32 [16, 1024, 12], P(('dp', 'expert'), 'context')
- grad_attn_down: float32 [8, 4, 768, 16], replicated
- grad_attn_up: float32 [8, 4, 16, 768], replicated
- grad_exp_in_down: float32 [8, 8, 768, 32], P(None, 'expert')
- grad_exp_in_up: float32 [8, 8, 2, 16, 2048], P(None, 'expert')
- grad_exp_out_down: float32 [8, 8, 2048, 16], P(None, 'expert')
- grad_exp_out_up: float32 [8, 8, 16, 768], P(None, 'expert')
The draws below stay inside these ranges and needn't reach their ends.
Inputs may be any that keep to these rules, and one draw needn't show every extreme that they name: `segment_ids`: segment ids never fall along a sequence; all changes of segment lie in a sequence's first 512 and last 512 positions. `routes`: each token names two different kinds: 0 to 7 are FFN experts, 8 the zero expert, 9 the copy expert, 10 and 11 the constant experts. Among the 512 tokens of one device the counts of the 12 kinds are, in some order, 8, 8, 7, 6, 6, 5, 5, 4, 4, 4, 4, 3 times 512 // 32, so no kind is named more than 512 // 4 times; among the devices that share their dp and context indices, one FFN expert is named exactly 512 // 4 times on each.
All inputs are finite; a program needn't handle non-finite values.
Results may differ from the reference program's by a relative error of at most 0.017.
The reference program's roundings to bfloat16 on the way count: a program that leaves them out, or rounds other values in their place, can miss the bound.
Values may be sent and summed in bfloat16 or wider, within the bound.
A program may use at most 256 MiB of HBM per device.

```python
import math
import jax
import jax.numpy as jnp
from jax import lax

D = 768
HEADS = 12
FF = 2048
EXPERTS = 8
ROUTE_KINDS = 12
RANK = 16
ADAPTERS = 8
TOK_DEV = 512
SEQS = 16
SEQ_LEN = 1024
N_EXPERT = 4


def draw_segment_ids(key, part):
    key = jax.random.fold_in(key, 11)
    first_key, last_key = jax.random.split(key)
    early_bounds = jax.random.randint(first_key, (SEQS, 3), 1, TOK_DEV)
    late_bounds = jax.random.randint(last_key, (SEQS, 3), SEQ_LEN - TOK_DEV + 1, SEQ_LEN)
    bounds = jnp.concatenate([early_bounds, late_bounds], 1)
    places = jnp.arange(SEQ_LEN, dtype=jnp.int32)
    return jnp.sum((places[None, :, None] >= bounds[:, None, :]).astype(jnp.int32), 2)


def draw_routes(key, part):
    key = jax.random.fold_in(key, 23)
    unit_rows = TOK_DEV // 32
    loads = jnp.array([8, 8, 7, 6, 6, 5, 5, 4, 4, 4, 4, 3], jnp.int32) * unit_rows
    load_ends = jnp.cumsum(loads)
    places = jnp.arange(2 * TOK_DEV, dtype=jnp.int32)
    run_index = jnp.sum((places[:, None] >= load_ends[None, :]).astype(jnp.int32), 1)

    def one_block(member_key, full_kind):
        perm_key, token_key = jax.random.split(member_key)
        kind_order = jax.random.permutation(perm_key, ROUTE_KINDS)
        sort_key = jnp.where(kind_order == full_kind, -1, jnp.arange(ROUTE_KINDS, dtype=jnp.int32))
        kind_order = kind_order[jnp.argsort(sort_key)]
        labels = kind_order[run_index]
        token_pairs = jnp.stack([labels[:TOK_DEV], labels[TOK_DEV:]], 1)
        token_order = jax.random.permutation(token_key, TOK_DEV)
        return jnp.zeros((TOK_DEV, 2), jnp.int32).at[token_order].set(token_pairs)

    def one_group(group_key):
        full_key, member_key = jax.random.split(group_key)
        full_kind = jax.random.randint(full_key, (), 0, EXPERTS)
        return jax.vmap(lambda member: one_block(member, full_kind))(jax.random.split(member_key, N_EXPERT))
    group_count = SEQS // N_EXPERT * (SEQ_LEN // TOK_DEV)
    drawn = jax.vmap(one_group)(jax.random.split(key, group_count))
    drawn = drawn.reshape(SEQS // N_EXPERT, SEQ_LEN // TOK_DEV, N_EXPERT, TOK_DEV, 2)
    return jnp.transpose(drawn, (0, 2, 1, 3, 4)).reshape(SEQS, SEQ_LEN, 2)


def with_ends(entries, own_key, least, top_value):
    longest = entries.shape.index(max(entries.shape))
    spots = []
    for shift in (0, 1):
        where = [jax.random.randint(jax.random.fold_in(own_key, axis), (), 0, length) for axis, length in enumerate(entries.shape)]
        where[longest] = (where[longest] + shift) % entries.shape[longest]
        spots.append(tuple(where))
    return entries.at[spots[0]].set(least).at[spots[1]].set(top_value)


def level_of(rng, extent, pieces, least, largest):
    loudness, own = 1.0, jax.random.fold_in(rng, 6)
    for axis_at, blocks in pieces:
        steps = jnp.exp(jax.random.uniform(jax.random.fold_in(own, axis_at), (blocks,), jnp.float32, least / len(pieces), largest / len(pieces)))
        loudness = loudness * jnp.repeat(steps, extent[axis_at] // blocks).reshape([-1 if axis == axis_at else 1 for axis in range(len(extent))])
    return loudness


def normal_values(key, extent, width, limit, cuts=(), held_as=jnp.bfloat16):
    values = width * jax.random.normal(key, extent, jnp.float32)
    if cuts:
        values = values * level_of(key, extent, cuts, -0.22, 0.18)
    return jnp.clip(values, -limit, limit).astype(held_as)


def setup_inputs(seed: int = 0) -> dict:
    arg_keys = jax.random.split(jax.random.key(seed), 23)
    hidden_in = normal_values(arg_keys[0], (SEQS, SEQ_LEN, D), 1.0, 6.0, ((0, 16), (1, 2)))
    prev_logits = normal_values(arg_keys[1], (SEQS, SEQ_LEN, ROUTE_KINDS), 1.0, 6.0, ((0, 16), (1, 2)), jnp.float32)
    segment_ids = draw_segment_ids(jax.random.fold_in(arg_keys[22], 71), 0)
    routes = draw_routes(jax.random.fold_in(arg_keys[22], 71), 0)
    adapter_ids = with_ends(jax.random.randint(arg_keys[4], (SEQS,), 0, ADAPTERS), jax.random.fold_in(arg_keys[4], 1), 0, ADAPTERS - 1).astype(jnp.int32)
    attn_gain = jnp.clip(1.0 + 0.1 * jax.random.normal(arg_keys[5], (D,), jnp.float32), 0.5, 1.5).astype(jnp.bfloat16)
    w_qkv = normal_values(arg_keys[6], (D, 3 * D), D ** -0.5, 0.21875)
    w_out = normal_values(arg_keys[7], (D, D), 8 ** -0.5, 2.0)
    attn_down = normal_values(arg_keys[8], (ADAPTERS, 4, D, RANK), D ** -0.5, 0.21875)
    attn_up = normal_values(arg_keys[9], (ADAPTERS, 4, RANK, D), (4 * RANK) ** -0.5, 0.75)
    ffn_gain = jnp.clip(1.0 + 0.1 * jax.random.normal(arg_keys[10], (D,), jnp.float32), 0.5, 1.5).astype(jnp.bfloat16)
    router_weight = normal_values(arg_keys[11], (D, ROUTE_KINDS), (4 * D) ** -0.5, 0.109375)
    gate_mix = normal_values(arg_keys[12], (ROUTE_KINDS, ROUTE_KINDS), (4 * ROUTE_KINDS) ** -0.5, 0.875, (), jnp.float32)
    const_mix = normal_values(arg_keys[13], (2, D, 2), D ** -0.5, 0.21875)
    const_vec = normal_values(arg_keys[14], (2, D), 1.0, 6.0)
    w_gate_up = normal_values(arg_keys[15], (EXPERTS, D, 2 * FF), D ** -0.5, 0.21875, ((0, 4),))
    w_down = normal_values(arg_keys[16], (EXPERTS, FF, D), FF ** -0.5, 0.125, ((0, 4),))
    exp_in_down = normal_values(arg_keys[17], (ADAPTERS, EXPERTS, D, 2 * RANK), D ** -0.5, 0.21875, ((1, 4),))
    exp_in_up = normal_values(arg_keys[18], (ADAPTERS, EXPERTS, 2, RANK, FF), (4 * RANK) ** -0.5, 0.75, ((1, 4),))
    exp_out_down = normal_values(arg_keys[19], (ADAPTERS, EXPERTS, FF, RANK), FF ** -0.5, 0.125, ((1, 4),))
    exp_out_up = normal_values(arg_keys[20], (ADAPTERS, EXPERTS, RANK, D), (4 * RANK) ** -0.5, 0.75, ((1, 4),))
    cotangent = normal_values(arg_keys[21], (SEQS, SEQ_LEN, D), 1.0, 6.0, ((0, 16), (1, 2)))
    return {"hidden_in": hidden_in, "prev_logits": prev_logits, "segment_ids": segment_ids, "routes": routes, "adapter_ids": adapter_ids, "attn_gain": attn_gain, "w_qkv": w_qkv, "w_out": w_out, "attn_down": attn_down, "attn_up": attn_up, "ffn_gain": ffn_gain, "router_weight": router_weight, "gate_mix": gate_mix, "const_mix": const_mix, "const_vec": const_vec, "w_gate_up": w_gate_up, "w_down": w_down, "exp_in_down": exp_in_down, "exp_in_up": exp_in_up, "exp_out_down": exp_out_down, "exp_out_up": exp_out_up, "cotangent": cotangent}


@jax.custom_vjp
def low(v):
    return lax.optimization_barrier(v.astype(jnp.bfloat16)).astype(jnp.float32)

@jax.custom_vjp
def low_back(v):
    return v

def low_keep(v):
    return (low(v), None)

def low_pass(kept, grad):
    return (grad,)

def back_keep(v):
    return (v, None)

def back_low(kept, grad):
    return (low(grad),)
low.defvjp(low_keep, low_pass)
low_back.defvjp(back_keep, back_low)
HIGH = lax.Precision.HIGHEST
EPSILON = 1e-06
ADAPT_SCALE = 2.0
NEG = -1e+30

def rotate(vectors, positions, direction):
    half_dim = vectors.shape[-1] // 2
    frequency = jnp.exp(jnp.arange(half_dim).astype(jnp.float32) * (-2.0 * math.log(10000.0) / vectors.shape[-1]))
    angles = positions[:, None] * frequency[None, :]
    cosine = jnp.cos(angles)[:, None, :]
    sine_part = direction * jnp.sin(angles)[:, None, :]
    first_half = vectors[..., :half_dim]
    second_half = vectors[..., half_dim:]
    return jnp.concatenate([first_half * cosine - second_half * sine_part, first_half * sine_part + second_half * cosine], -1)

def matmul(left, right):
    return jnp.dot(left, right, precision=HIGH)

def rms_norm(vectors, gain_vec):
    return vectors * lax.rsqrt(lax.optimization_barrier(jnp.mean(vectors * vectors, -1, keepdims=True)) + EPSILON) * gain_vec

def adapted(inputs, base_weight, down_factor, up_factor):
    rank_part = low(low_back(matmul(inputs, down_factor)))
    return matmul(inputs, base_weight) + ADAPT_SCALE * matmul(rank_part, up_factor)

def attend(queries, key_rows, value_rows, query_pos, query_seg, key_pos, key_seg):
    scores = low_back(jnp.einsum('qhd,khd->hqk', queries, key_rows, precision=HIGH) * queries.shape[-1] ** (-0.5))
    allowed = (query_seg[:, None] == key_seg[None, :]) & (key_pos[None, :] <= query_pos[:, None])
    weights = low(jax.nn.softmax(jnp.where(allowed[None], scores, NEG), axis=-1))
    return jnp.einsum('hqk,khd->qhd', weights, value_rows, precision=HIGH)

def expert_rows(rows_in, gate_up_weight, down_weight, in_down, in_up, out_down, out_up):
    ffn_width = down_weight.shape[0]
    rank_dim = in_up.shape[1]
    joined_rows = matmul(rows_in, gate_up_weight)
    rank_in = low(low_back(matmul(rows_in, in_down)))
    gate_pre = low_back(joined_rows[:, :ffn_width] + ADAPT_SCALE * matmul(rank_in[:, :rank_dim], in_up[0]))
    up_pre = low_back(joined_rows[:, ffn_width:] + ADAPT_SCALE * matmul(rank_in[:, rank_dim:], in_up[1]))
    activated = low(low_back(jax.nn.silu(gate_pre) * up_pre))
    return low(low_back(adapted(activated, down_weight, out_down, out_up)))

def sequence_layer(resid_in, prev_row, seg_ids, route_pairs, adapter_id, adapters, frozen):
    down_attn, up_attn, down_in, up_in, down_out, up_out = adapters
    attn_gain, w_qkv, w_out, ffn_gain, router_weight, gate_mix, const_mix, const_vec, w_gate_up, w_down = frozen
    seq_len, model_dim = resid_in.shape
    head_dim = model_dim // HEADS
    positions = jnp.arange(seq_len, dtype=jnp.int32)
    rope_pos = positions.astype(jnp.float32)
    down_sel = lax.dynamic_index_in_dim(down_attn, adapter_id, 0, keepdims=False)
    up_sel = lax.dynamic_index_in_dim(up_attn, adapter_id, 0, keepdims=False)
    normed_low = low(rms_norm(resid_in, attn_gain))
    projected = [low_back(adapted(normed_low, w_qkv[:, branch_index * model_dim:(branch_index + 1) * model_dim], down_sel[branch_index], up_sel[branch_index])) for branch_index in range(3)]
    shape_heads = (seq_len, HEADS, head_dim)
    queries = low(rotate(projected[0].reshape(shape_heads), rope_pos, 1.0))
    key_rows = low(rotate(projected[1].reshape(shape_heads), rope_pos, 1.0))
    value_rows = low(projected[2].reshape(shape_heads))
    block_rows = min(512, seq_len)
    block_count = seq_len // block_rows

    def one_block(packed):
        return attend(packed[0], key_rows, value_rows, packed[1], packed[2], positions, seg_ids)
    attn_out = lax.map(jax.checkpoint(one_block), (queries.reshape((block_count, block_rows) + shape_heads[1:]), positions.reshape(block_count, block_rows), seg_ids.reshape(block_count, block_rows)))
    attn_flat = low(low_back(attn_out.reshape(seq_len, model_dim)))
    mid_resid = resid_in + low_back(adapted(attn_flat, w_out, down_sel[3], up_sel[3]))
    normed_two = rms_norm(mid_resid, ffn_gain)
    rows_low = low(normed_two)
    logits = matmul(rows_low, router_weight) + matmul(prev_row, gate_mix)
    probs_all = jax.nn.softmax(logits, -1)
    kind_count = prev_row.shape[-1]
    ffn_count = w_gate_up.shape[0]
    kind_match = (route_pairs[:, :, None] == jnp.arange(kind_count, dtype=jnp.int32)[None, None, :]).astype(jnp.float32)
    gate_values = lax.optimization_barrier(jnp.sum(kind_match * probs_all[:, None, :], -1))
    mix_weight = lax.optimization_barrier(jnp.sum(gate_values[:, :, None] * kind_match, 1))
    in_down_sel = lax.dynamic_index_in_dim(down_in, adapter_id, 0, keepdims=False)
    in_up_sel = lax.dynamic_index_in_dim(up_in, adapter_id, 0, keepdims=False)
    out_down_sel = lax.dynamic_index_in_dim(down_out, adapter_id, 0, keepdims=False)
    out_up_sel = lax.dynamic_index_in_dim(up_out, adapter_id, 0, keepdims=False)

    def one_expert(packed):
        return expert_rows(rows_low, packed[0], packed[1], packed[2], packed[3], packed[4], packed[5])
    ffn_out = lax.map(jax.checkpoint(one_expert), (w_gate_up, w_down, in_down_sel, in_up_sel, out_down_sel, out_up_sel))
    mix_const = jax.nn.softmax(jnp.einsum('ld,idc->lic', rows_low, const_mix, precision=HIGH), -1)
    mixture = jnp.einsum('le,eld->ld', mix_weight[:, :ffn_count], ffn_out, precision=HIGH)
    mixture = mixture + mix_weight[:, ffn_count + 1:ffn_count + 2] * normed_two
    for branch_index in range(2):
        const_term = mix_const[:, branch_index, 0:1] * normed_two + mix_const[:, branch_index, 1:2] * const_vec[branch_index]
        mixture = mixture + mix_weight[:, ffn_count + 2 + branch_index:ffn_count + 3 + branch_index] * const_term
    return mid_resid + mixture

def reference(hidden_in, prev_logits, segment_ids, routes, adapter_ids, attn_gain, w_qkv, w_out, attn_down, attn_up, ffn_gain, router_weight, gate_mix, const_mix, const_vec, w_gate_up, w_down, exp_in_down, exp_in_up, exp_out_down, exp_out_up, cotangent):

    def to_float(array_in):
        return array_in.astype(jnp.float32)
    frozen = tuple((to_float(item) for item in (attn_gain, w_qkv, w_out, ffn_gain, router_weight, gate_mix, const_mix, const_vec, w_gate_up, w_down)))

    def forward(resid_all, prev_all, down_attn, up_attn, down_in, up_in, down_out, up_out):
        adapters = (down_attn, up_attn, down_in, up_in, down_out, up_out)

        def one_sequence(carried, packed):
            out_seq = jax.checkpoint(sequence_layer)(packed[0], packed[1], packed[2], packed[3], packed[4], adapters, frozen)
            return (carried, out_seq)
        unused, outputs = lax.scan(one_sequence, jnp.int32(0), (resid_all, prev_all, segment_ids, routes, adapter_ids))
        return outputs
    layer_out, pullback = jax.vjp(forward, to_float(hidden_in), to_float(prev_logits), to_float(attn_down), to_float(attn_up), to_float(exp_in_down), to_float(exp_in_up), to_float(exp_out_down), to_float(exp_out_up))
    gradients = pullback(to_float(cotangent))
    return (layer_out.astype(jnp.bfloat16), gradients[0], gradients[1], gradients[2], gradients[3], gradients[4], gradients[5], gradients[6], gradients[7])
```

```python
import functools
import math

import jax
import jax.numpy as jnp
from jax import lax
from jax.experimental import pallas as pl
from jax.experimental.pallas import tpu as pltpu
from jax.sharding import PartitionSpec as P

MESH = pl.DeviceIdType.MESH
VLIMIT = 60 * 1024 * 1024
BF = jnp.bfloat16
F32 = jnp.float32

HEADS = 12


EPSILON = 1e-06
ADAPT_SCALE = 2.0
NEG = -1e30
HIGH = lax.Precision.HIGHEST


def rotate(vectors, positions, direction):
    half_dim = vectors.shape[-1] // 2
    frequency = jnp.exp(
        jnp.arange(half_dim).astype(jnp.float32) * (-2.0 * math.log(10000.0) / vectors.shape[-1])
    )
    angles = positions[:, None] * frequency[None, :]
    cosine = jnp.cos(angles)[:, None, :]
    sine_part = direction * jnp.sin(angles)[:, None, :]
    first_half = vectors[..., :half_dim]
    second_half = vectors[..., half_dim:]
    return jnp.concatenate(
        [
            first_half * cosine - second_half * sine_part,
            first_half * sine_part + second_half * cosine,
        ],
        -1,
    )


def bdot(form, left, right):
    return jnp.einsum(form, left, right, preferred_element_type=jnp.float32)


def fdot(form, left, right):
    return jnp.einsum(form, left, right, precision=HIGH, preferred_element_type=jnp.float32)


def masked_scores(queries, key_rows, query_pos, query_seg, key_pos, key_seg):
    raw_scores = bdot("qhd,khd->hqk", queries, key_rows) * queries.shape[-1] ** (-0.5)
    allowed = (query_seg[:, None] == key_seg[None, :]) & (key_pos[None, :] <= query_pos[:, None])
    return jnp.where(allowed[None], raw_scores, NEG)


def block_grads(
    queries,
    d_out,
    log_total,
    row_delta,
    query_pos,
    query_seg,
    key_rows,
    value_rows,
    key_pos,
    key_seg,
):
    probs_block = jnp.exp(
        masked_scores(queries, key_rows, query_pos, query_seg, key_pos, key_seg)
        - log_total[:, :, None]
    )
    rounded = probs_block.astype(jnp.bfloat16)
    d_probs = bdot("qhd,khd->hqk", d_out, value_rows)
    d_scores = (probs_block * (d_probs - row_delta[:, :, None])).astype(jnp.bfloat16)
    score_scale = queries.shape[-1] ** (-0.5)
    d_query = bdot("hqk,khd->qhd", d_scores, key_rows) * score_scale
    d_key = bdot("hqk,qhd->khd", d_scores, queries) * score_scale
    d_value = bdot("hqk,qhd->khd", rounded, d_out)
    return (d_query, d_key, d_value)


def expert_hidden(arrived, tables, w_gate_up, ffn_width):
    rank_dim = tables[1].shape[3]
    joined_rows = bdot("jecd,edf->jecf", arrived, w_gate_up)
    rank_in = bdot("jecd,jedr->jecr", arrived, tables[0]).astype(jnp.bfloat16)
    gate_pre = joined_rows[..., :ffn_width] + ADAPT_SCALE * bdot(
        "jecr,jerf->jecf", rank_in[..., :rank_dim], tables[1][:, :, 0]
    )
    up_pre = joined_rows[..., ffn_width:] + ADAPT_SCALE * bdot(
        "jecr,jerf->jecf", rank_in[..., rank_dim:], tables[1][:, :, 1]
    )
    return (gate_pre, up_pre, rank_in)


def expert_forward(arrived, tables, w_gate_up, w_down):
    gate_pre, up_pre, rank_in = expert_hidden(arrived, tables, w_gate_up, w_down.shape[1])
    activated = (jax.nn.silu(gate_pre) * up_pre).astype(jnp.bfloat16)
    rank_mid = bdot("jecf,jefr->jecr", activated, tables[2]).astype(jnp.bfloat16)
    result = bdot("jecf,efd->jecd", activated, w_down) + ADAPT_SCALE * bdot(
        "jecr,jerd->jecd", rank_mid, tables[3]
    )
    return result.astype(jnp.bfloat16)


def expert_backward(arrived, d_result, tables, w_gate_up, w_down):
    gate_pre, up_pre, rank_in = expert_hidden(arrived, tables, w_gate_up, w_down.shape[1])
    rank_dim = tables[1].shape[3]
    sigmoid_gate = jax.nn.sigmoid(gate_pre)
    silu_gate = gate_pre * sigmoid_gate
    activated = (silu_gate * up_pre).astype(jnp.bfloat16)
    rank_mid = bdot("jecf,jefr->jecr", activated, tables[2]).astype(jnp.bfloat16)
    d_rank_mid = (ADAPT_SCALE * bdot("jecd,jerd->jecr", d_result, tables[3])).astype(jnp.bfloat16)
    grad_out_up = ADAPT_SCALE * bdot("jecr,jecd->jerd", rank_mid, d_result)
    grad_out_down = bdot("jecf,jecr->jerf", activated, d_rank_mid)
    d_act = (
        (bdot("jecd,efd->jecf", d_result, w_down) + bdot("jecr,jefr->jecf", d_rank_mid, tables[2]))
        .astype(jnp.bfloat16)
        .astype(jnp.float32)
    )
    d_gate = (d_act * up_pre * sigmoid_gate * (1.0 + gate_pre * (1.0 - sigmoid_gate))).astype(
        jnp.bfloat16
    )
    d_up = (d_act * silu_gate).astype(jnp.bfloat16)
    d_rank_in = (
        ADAPT_SCALE
        * jnp.concatenate(
            [
                bdot("jecf,jerf->jecr", d_gate, tables[1][:, :, 0]),
                bdot("jecf,jerf->jecr", d_up, tables[1][:, :, 1]),
            ],
            -1,
        )
    ).astype(jnp.bfloat16)
    grad_in_up = ADAPT_SCALE * jnp.stack(
        [
            bdot("jecr,jecf->jerf", rank_in[..., :rank_dim], d_gate),
            bdot("jecr,jecf->jerf", rank_in[..., rank_dim:], d_up),
        ],
        2,
    )
    grad_in_down = bdot("jecd,jecr->jerd", arrived, d_rank_in)
    d_arrived = bdot("jecf,edf->jecd", jnp.concatenate([d_gate, d_up], -1), w_gate_up) + bdot(
        "jecr,jedr->jecd", d_rank_in, tables[0]
    )
    return (d_arrived, (grad_in_down, grad_in_up, grad_out_down, grad_out_up))


def to_tiles(table):
    lead, (rows, cols) = table.shape[:-2], table.shape[-2:]
    cut = table.reshape(lead + (rows // 16, 16, cols // 128, 128))
    cut = jnp.swapaxes(cut, -3, -2)
    return cut.reshape(lead + (rows * cols // 2048, 16, 128))


def reduce_kernel(
    sizes, ids_ref, grads_ref, attn_ref, table_ref, attn_table_ref,
    held, arrived_x, part_z, arrived_z,
    load_sem, ready_send, ready_recv, x_send, x_recv, z_send, z_recv, az_send, az_recv,
    ax_send, ax_recv, e_send, e_recv,
):
    ctx_n, dp_n, exp_n, adapters, tiles, attn_tiles, x_tiles, z_tiles = sizes
    own_attn = attn_tiles // exp_n
    ctx, dp, exp = lax.axis_index("context"), lax.axis_index("dp"), lax.axis_index("expert")
    barrier = pltpu.get_barrier_semaphore()
    for axis, size, index in (("context", ctx_n, ctx), ("dp", dp_n, dp), ("expert", exp_n, exp)):
        for step in range(1, size):
            pl.semaphore_signal(
                barrier, inc=1, device_id={axis: lax.rem(index + step, size)}, device_id_type=MESH
            )
    load = pltpu.make_async_copy(grads_ref, held.at[:, pl.ds(0, tiles)], load_sem)
    load.start()
    keep = pltpu.make_async_copy(
        attn_ref.at[pl.ds(exp * own_attn, own_attn)],
        held.at[exp, pl.ds(tiles, own_attn)],
        ready_send.at[exp_n - 1],
    )
    keep.start()
    pl.semaphore_wait(barrier, ctx_n + dp_n + exp_n - 3)

    def copy(src, dst, send, recv, axis, target):
        return pltpu.make_async_remote_copy(
            src_ref=src, dst_ref=dst, send_sem=send, recv_sem=recv,
            device_id={axis: target}, device_id_type=MESH,
        )

    waits = []
    first = []
    for step in range(1, exp_n):
        peer = lax.rem(exp + step, exp_n)
        send = copy(
            attn_ref.at[pl.ds(peer * own_attn, own_attn)],
            held.at[exp, pl.ds(tiles, own_attn)],
            ready_send.at[step - 1], ready_recv.at[step - 1], "expert", peer,
        )
        send.start()
        first.append(send)
    load.wait()
    keep.wait()
    for send in first:
        send.wait()
    for k in range(1, dp_n + 1):
        part = lax.rem(dp + k, dp_n)
        for step in range(1, ctx_n):
            peer = lax.rem(ctx + step, ctx_n)
            send = copy(
                held.at[:, pl.ds(peer * x_tiles + part * z_tiles, z_tiles)],
                arrived_x.at[step - 1, k - 1],
                x_send.at[step - 1, k - 1], x_recv.at[step - 1, k - 1], "context", peer,
            )
            send.start()
            waits.append(send)
    z_sends = []
    for k in range(1, dp_n + 1):
        part = lax.rem(dp + k, dp_n)
        for step in range(1, ctx_n):
            waits[(k - 1) * (ctx_n - 1) + step - 1].wait_recv()
        base = ctx * x_tiles + part * z_tiles

        def add(tile, carry, k=k, base=base):
            total = held[:, pl.ds(base + tile, 1)].astype(F32)
            for step in range(1, ctx_n):
                total = total + arrived_x[step - 1, k - 1, :, pl.ds(tile, 1)].astype(F32)
            part_z[k - 1, :, pl.ds(tile, 1)] = total.astype(BF)
            return carry

        lax.fori_loop(0, z_tiles, add, 0)
        if k < dp_n:
            send = copy(
                part_z.at[k - 1], arrived_z.at[k - 1], z_send.at[k - 1], z_recv.at[k - 1], "dp", part
            )
            send.start()
            z_sends.append(send)
    for send in z_sends:
        send.wait_recv()

    weights = []
    for k in range(dp_n):
        origin = lax.rem(dp - k + dp_n, dp_n)
        for source in range(exp_n):
            name = ids_ref[origin * exp_n + source]
            weights.append([jnp.where(name == a, 1.0, 0.0).astype(F32) for a in range(adapters)])

    def combine(tile, carry):
        totals = [jnp.zeros((16, 128), F32)] * adapters
        for k in range(dp_n):
            for source in range(exp_n):
                ref = part_z.at[dp_n - 1] if k == 0 else arrived_z.at[k - 1]
                value = ref[source, tile].astype(F32)
                marks = weights[k * exp_n + source]
                totals = [total + mark * value for total, mark in zip(totals, marks)]
        for a in range(adapters):
            table_ref[ctx, dp, a, tile] = totals[a].astype(BF)
        return carry

    lax.fori_loop(0, z_tiles, combine, 0)
    az_sends, ax_sends = [], []
    for k in range(1, dp_n):
        send = copy(
            table_ref.at[ctx, dp], table_ref.at[ctx, dp], az_send.at[k - 1], az_recv.at[k - 1],
            "dp", lax.rem(dp + k, dp_n),
        )
        send.start()
        az_sends.append(send)
    for k in range(dp_n):
        if k > 0:
            az_sends[k - 1].wait_recv()
        origin = lax.rem(dp - k + dp_n, dp_n)
        for step in range(1, ctx_n):
            send = copy(
                table_ref.at[ctx, origin], table_ref.at[ctx, origin],
                ax_send.at[step - 1, k], ax_recv.at[step - 1, k],
                "context", lax.rem(ctx + step, ctx_n),
            )
            send.start()
            ax_sends.append(send)
    for send in ax_sends:
        send.wait_recv()
    for index in range(own_attn):
        tile = tiles + index
        where = (tile // x_tiles, (tile % x_tiles) // z_tiles, tile % x_tiles % z_tiles)
        for a in range(adapters):
            attn_table_ref[exp, index, a] = table_ref[where[0], where[1], a, where[2]]
    last = []
    for step in range(1, exp_n):
        send = copy(
            attn_table_ref.at[exp], attn_table_ref.at[exp], e_send.at[step - 1], e_recv.at[step - 1],
            "expert", lax.rem(exp + step, exp_n),
        )
        send.start()
        last.append(send)
    for send in last:
        send.wait()
    for send in waits + z_sends + az_sends + ax_sends:
        send.wait_send()


def unpack_kernel(sizes, table_ref, attn_ref, down_ref, up_ref, in_down_ref, in_up_ref, out_down_ref, out_up_ref):
    x_tiles, z_tiles, own_attn = sizes

    def tile_at(tile):
        local = tile % x_tiles
        return table_ref[tile // x_tiles, local // z_tiles, 0, local % z_tiles].astype(F32)

    tile = 0
    for expert in range(in_up_ref.shape[1]):
        for out_ref in (in_down_ref, in_up_ref, out_down_ref, out_up_ref):
            rows, cols = out_ref.shape[2:]
            for row in range(rows // 16):
                for col in range(cols // 128):
                    out_ref[0, expert, row * 16 : row * 16 + 16, col * 128 : col * 128 + 128] = tile_at(tile)
                    tile += 1
    tile = 0
    for out_ref in (down_ref, up_ref):
        rows, cols = out_ref.shape[1:]
        for row in range(rows // 16):
            for col in range(cols // 128):
                out_ref[0, row * 16 : row * 16 + 16, col * 128 : col * 128 + 128] = attn_ref[
                    tile // own_attn, tile % own_attn, 0
                ].astype(F32)
                tile += 1


def reduce_adapters(adapter_ids, expert_grads, attn_down, attn_up, adapters):
    ctx_n, dp_n, exp_n = (lax.axis_size(axis) for axis in ("context", "dp", "expert"))
    experts = expert_grads[0].shape[1]
    packed = jnp.concatenate(
        [to_tiles(g)[:, e] for e in range(experts) for g in expert_grads], 1
    ).astype(BF)
    attn = jnp.concatenate([to_tiles(attn_down), to_tiles(attn_up)], 0).astype(BF)
    tiles, attn_tiles = packed.shape[1], attn.shape[0]
    own_attn = attn_tiles // exp_n
    z_tiles = pl.cdiv(tiles + own_attn, ctx_n * dp_n)
    x_tiles = z_tiles * dp_n
    sizes = (ctx_n, dp_n, exp_n, adapters, tiles, attn_tiles, x_tiles, z_tiles)
    dma = pltpu.SemaphoreType.DMA
    many = max(ctx_n - 1, 1)
    table, attn_table = pl.pallas_call(
        functools.partial(reduce_kernel, sizes),
        out_shape=(
            jax.ShapeDtypeStruct((ctx_n, dp_n, adapters, z_tiles, 16, 128), BF),
            jax.ShapeDtypeStruct((exp_n, own_attn, adapters, 16, 128), BF),
        ),
        in_specs=[
            pl.BlockSpec(memory_space=pltpu.SMEM),
            pl.BlockSpec(memory_space=pl.ANY),
            pl.BlockSpec(memory_space=pltpu.VMEM),
        ],
        out_specs=(pl.BlockSpec(memory_space=pltpu.VMEM), pl.BlockSpec(memory_space=pltpu.VMEM)),
        scratch_shapes=[
            pltpu.VMEM((exp_n, ctx_n * x_tiles, 16, 128), BF),
            pltpu.VMEM((many, dp_n, exp_n, z_tiles, 16, 128), BF),
            pltpu.VMEM((dp_n, exp_n, z_tiles, 16, 128), BF),
            pltpu.VMEM((max(dp_n - 1, 1), exp_n, z_tiles, 16, 128), BF),
            dma, dma((exp_n,)), dma((exp_n,)), dma((many, dp_n)), dma((many, dp_n)),
            dma((dp_n,)), dma((dp_n,)), dma((dp_n,)), dma((dp_n,)),
            dma((many, dp_n)), dma((many, dp_n)), dma((exp_n,)), dma((exp_n,)),
        ],
        compiler_params=pltpu.CompilerParams(
            collective_id=1, has_side_effects=True, vmem_limit_bytes=VLIMIT
        ),
        name="reduce_adapters",
    )(adapter_ids, packed, attn)
    shapes = [
        (adapters,) + attn_down.shape,
        (adapters,) + attn_up.shape,
    ] + [(adapters,) + g.shape[1:] for g in expert_grads]
    return pl.pallas_call(
        functools.partial(unpack_kernel, (x_tiles, z_tiles, own_attn)),
        grid=(adapters,),
        out_shape=tuple(jax.ShapeDtypeStruct(shape, F32) for shape in shapes),
        in_specs=[
            pl.BlockSpec((ctx_n, dp_n, 1, z_tiles, 16, 128), lambda a: (0, 0, a, 0, 0, 0)),
            pl.BlockSpec((exp_n, own_attn, 1, 16, 128), lambda a: (0, 0, a, 0, 0)),
        ],
        out_specs=tuple(
            pl.BlockSpec((1,) + shape[1:], lambda a, n=len(shape): (a,) + (0,) * (n - 1))
            for shape in shapes
        ),
        compiler_params=pltpu.CompilerParams(vmem_limit_bytes=VLIMIT),
        name="unpack_adapters",
    )(table, attn_table)


def local(
    hidden_in,
    prev_logits,
    segment_ids,
    routes,
    adapter_ids,
    attn_gain,
    w_qkv,
    w_out,
    attn_down,
    attn_up,
    ffn_gain,
    router_weight,
    gate_mix,
    const_mix,
    const_vec,
    w_gate_up,
    w_down,
    exp_in_down,
    exp_in_up,
    exp_out_down,
    exp_out_up,
    cotangent,
):
    tok_count = hidden_in.shape[1]
    model_dim = hidden_in.shape[2]
    kind_count = prev_logits.shape[2]
    local_experts = w_gate_up.shape[0]
    adapter_count = attn_down.shape[0]
    key_block = min(512, tok_count)
    ctx_size = lax.axis_size("context")
    ctx_index = lax.axis_index("context")
    exp_size = lax.axis_size("expert")
    exp_index = lax.axis_index("expert")
    dp_index = lax.axis_index("dp")
    ffn_count = local_experts * exp_size
    capacity = tok_count // 4
    seq_total = tok_count * ctx_size
    my_adapter = lax.dynamic_index_in_dim(
        adapter_ids, dp_index * exp_size + exp_index, 0, keepdims=False
    )
    tok_pos = ctx_index * tok_count + jnp.arange(tok_count, dtype=jnp.int32)
    rope_pos = tok_pos.astype(jnp.float32)
    seg_local = segment_ids[0]
    head_shape = (tok_count, HEADS, model_dim // HEADS)
    resid_in = hidden_in[0].astype(jnp.float32)
    gain_one = attn_gain.astype(jnp.float32)
    inv_one = lax.rsqrt(jnp.mean(resid_in * resid_in, -1, keepdims=True) + EPSILON)
    normed_low = (resid_in * inv_one * gain_one).astype(jnp.bfloat16)
    down_sel = lax.dynamic_index_in_dim(attn_down, my_adapter, 0, keepdims=False)
    up_sel = lax.dynamic_index_in_dim(attn_up, my_adapter, 0, keepdims=False)
    rank_qkv = bdot("td,pdr->ptr", normed_low, down_sel[:3]).astype(jnp.bfloat16)
    proj_qkv = bdot("td,de->te", normed_low, w_qkv).reshape(
        tok_count, 3, model_dim
    ) + ADAPT_SCALE * bdot("ptr,prd->tpd", rank_qkv, up_sel[:3])
    queries = rotate(proj_qkv[:, 0].reshape(head_shape), rope_pos, 1.0).astype(jnp.bfloat16)
    key_rows = rotate(proj_qkv[:, 1].reshape(head_shape), rope_pos, 1.0).astype(jnp.bfloat16)
    value_rows = proj_qkv[:, 2].reshape(head_shape).astype(jnp.bfloat16)
    all_keys, all_values, all_segs = (
        lax.all_gather(key_rows, "context", axis=0, tiled=True),
        lax.all_gather(value_rows, "context", axis=0, tiled=True),
        lax.all_gather(seg_local, "context", axis=0, tiled=True),
    )
    block_total = seq_total // key_block

    def key_slice(block_index):
        offset = block_index * key_block
        return (
            lax.dynamic_slice_in_dim(all_keys, offset, key_block, 0),
            lax.dynamic_slice_in_dim(all_values, offset, key_block, 0),
            lax.dynamic_slice_in_dim(all_segs, offset, key_block, 0),
            offset + jnp.arange(key_block, dtype=jnp.int32),
        )

    def max_step(block_index, totals):
        run_max, run_sum = totals
        blk_keys, blk_values, blk_segs, blk_pos = key_slice(block_index)
        scores = masked_scores(queries, blk_keys, tok_pos, seg_local, blk_pos, blk_segs)
        new_max = jnp.maximum(run_max, jnp.max(scores, -1))
        new_sum = run_sum * jnp.exp(run_max - new_max) + jnp.sum(
            jnp.exp(scores - new_max[:, :, None]), -1
        )
        return (new_max, new_sum)

    start_max = jnp.full((HEADS, tok_count), NEG, jnp.float32)
    run_max, run_sum = lax.fori_loop(
        0, block_total, max_step, (start_max, jnp.zeros((HEADS, tok_count), jnp.float32))
    )
    log_total = run_max + jnp.log(run_sum)

    def value_step(block_index, totals):
        high_acc, low_acc = totals
        blk_keys, blk_values, blk_segs, blk_pos = key_slice(block_index)
        probs_block = jnp.exp(
            masked_scores(queries, blk_keys, tok_pos, seg_local, blk_pos, blk_segs)
            - log_total[:, :, None]
        )
        rounded = probs_block.astype(jnp.bfloat16)
        residue = (probs_block - rounded.astype(jnp.float32)).astype(jnp.bfloat16)
        return (
            high_acc + bdot("hqk,khd->qhd", rounded, blk_values),
            low_acc + bdot("hqk,khd->qhd", residue, blk_values),
        )

    zero_heads = jnp.zeros(head_shape, jnp.float32)
    attn_high, attn_low = lax.fori_loop(0, block_total, value_step, (zero_heads, zero_heads))
    attn_exact = attn_high + attn_low
    attn_flat = attn_high.reshape(tok_count, model_dim).astype(jnp.bfloat16)
    rank_out = bdot("td,dr->tr", attn_flat, down_sel[3]).astype(jnp.bfloat16)
    mid_resid = (
        resid_in
        + bdot("td,de->te", attn_flat, w_out)
        + ADAPT_SCALE * bdot("tr,rd->td", rank_out, up_sel[3])
    )
    gain_two = ffn_gain.astype(jnp.float32)
    inv_two = lax.rsqrt(jnp.mean(mid_resid * mid_resid, -1, keepdims=True) + EPSILON)
    normed_two = mid_resid * inv_two * gain_two
    rows_low = normed_two.astype(jnp.bfloat16)
    logits = bdot("td,de->te", rows_low, router_weight) + fdot(
        "te,ef->tf", prev_logits[0], gate_mix
    )
    probs_all = jax.nn.softmax(logits, -1)
    route_tok = routes[0]
    kind_match = (
        route_tok[:, :, None] == jnp.arange(kind_count, dtype=jnp.int32)[None, None, :]
    ).astype(jnp.float32)
    gate_values = jnp.sum(kind_match * probs_all[:, None, :], -1)
    mix_const = jax.nn.softmax(bdot("td,idc->tic", rows_low, const_mix), -1)
    const_full = const_vec.astype(jnp.float32)
    const_terms = (
        mix_const[:, :, 0:1] * normed_two[:, None, :]
        + mix_const[:, :, 1:2] * const_full[None, :, :]
    )
    flat_route = route_tok.reshape(-1)
    is_ffn = flat_route < ffn_count
    ffn_match = (flat_route[:, None] == jnp.arange(ffn_count, dtype=jnp.int32)[None, :]).astype(
        jnp.int32
    )
    slot_rank = jnp.sum((jnp.cumsum(ffn_match, 0) - 1) * ffn_match, 1)
    slot_index = jnp.where(is_ffn, flat_route * capacity + slot_rank, ffn_count * capacity)
    safe_index = jnp.minimum(slot_index, ffn_count * capacity - 1)
    buffer_shape = (exp_size, local_experts, capacity, model_dim)
    outgoing = (
        jnp.zeros((ffn_count * capacity, model_dim), jnp.bfloat16)
        .at[slot_index]
        .set(jnp.repeat(rows_low, 2, 0), mode="drop")
        .reshape(buffer_shape)
    )
    source_ids = lax.dynamic_slice_in_dim(adapter_ids, dp_index * exp_size, exp_size, 0)
    source_match = source_ids[:, None] == jnp.arange(adapter_count, dtype=jnp.int32)[None, :]
    pick_table = source_match.astype(jnp.bfloat16)
    tables = tuple(
        (
            bdot("ja,a...->j...", pick_table, table_in).astype(jnp.bfloat16)
            for table_in in (exp_in_down, exp_in_up, exp_out_down, exp_out_up)
        )
    )
    arrived = lax.all_to_all(outgoing, "expert", split_axis=0, concat_axis=0, tiled=True)
    result = expert_forward(arrived, tables, w_gate_up, w_down)
    returned = lax.all_to_all(result, "expert", split_axis=0, concat_axis=0, tiled=True)
    ffn_rows = jnp.where(
        is_ffn[:, None], returned.reshape(ffn_count * capacity, model_dim)[safe_index], 0.0
    ).reshape(tok_count, 2, model_dim)
    branch_terms = ffn_rows.astype(jnp.float32) + jnp.where(
        (route_tok == ffn_count + 1)[:, :, None], normed_two[:, None, :], 0.0
    )
    for const_index in range(2):
        branch_terms = branch_terms + jnp.where(
            (route_tok == ffn_count + 2 + const_index)[:, :, None],
            const_terms[:, const_index][:, None, :],
            0.0,
        )
    layer_out = mid_resid + jnp.sum(gate_values[:, :, None] * branch_terms, 1)
    d_out = cotangent[0].astype(jnp.float32)
    d_gates = jnp.sum(d_out[:, None, :] * branch_terms, -1)
    d_kinds = jnp.sum(kind_match * d_gates[:, :, None], 1)
    d_logits = probs_all * (d_kinds - jnp.sum(probs_all * d_kinds, -1, keepdims=True))
    grad_prev = fdot("tf,ef->te", d_logits, gate_mix)
    d_normed = fdot("te,de->td", d_logits, router_weight.astype(jnp.float32))
    copy_weight = jnp.sum(gate_values * (route_tok == ffn_count + 1).astype(jnp.float32), 1)
    d_normed = d_normed + copy_weight[:, None] * d_out
    for const_index in range(2):
        const_weight = jnp.sum(
            gate_values * (route_tok == ffn_count + 2 + const_index).astype(jnp.float32), 1
        )
        d_term = const_weight[:, None] * d_out
        mix_pair = mix_const[:, const_index]
        d_normed = d_normed + mix_pair[:, 0:1] * d_term
        d_mix = jnp.stack(
            [
                jnp.sum(d_term * normed_two, -1),
                jnp.sum(d_term * const_full[const_index][None, :], -1),
            ],
            -1,
        )
        d_inner = mix_pair * (d_mix - jnp.sum(mix_pair * d_mix, -1, keepdims=True))
        d_normed = d_normed + fdot("tc,dc->td", d_inner, const_mix[const_index].astype(jnp.float32))
    d_pairs = (
        (gate_values[:, :, None] * d_out[:, None, :])
        .astype(jnp.bfloat16)
        .reshape(2 * tok_count, model_dim)
    )
    d_outgoing = (
        jnp.zeros((ffn_count * capacity, model_dim), jnp.bfloat16)
        .at[slot_index]
        .set(d_pairs, mode="drop")
        .reshape(buffer_shape)
    )
    d_arrived = lax.all_to_all(d_outgoing, "expert", split_axis=0, concat_axis=0, tiled=True)
    d_kept, owner_grads = expert_backward(arrived, d_arrived, tables, w_gate_up, w_down)
    d_back = lax.all_to_all(
        d_kept.astype(jnp.bfloat16), "expert", split_axis=0, concat_axis=0, tiled=True
    ).astype(d_kept.dtype)
    d_back_rows = jnp.where(
        is_ffn[:, None], d_back.reshape(ffn_count * capacity, model_dim)[safe_index], 0.0
    ).reshape(tok_count, 2, model_dim)
    d_normed = d_normed + jnp.sum(d_back_rows, 1)
    scaled_two = d_normed * gain_two
    d_mid = (
        d_out
        + inv_two * scaled_two
        - mid_resid
        * (inv_two * inv_two * inv_two)
        * jnp.mean(scaled_two * mid_resid, -1, keepdims=True)
    )
    d_branch = d_mid.astype(jnp.bfloat16)
    d_rank_out = (ADAPT_SCALE * bdot("td,rd->tr", d_branch, up_sel[3])).astype(jnp.bfloat16)
    grad_up_out = ADAPT_SCALE * bdot("tr,td->rd", rank_out, d_branch)
    grad_down_out = bdot("td,tr->rd", attn_flat, d_rank_out)
    d_attn = (
        (bdot("te,de->td", d_branch, w_out) + bdot("tr,dr->td", d_rank_out, down_sel[3]))
        .astype(jnp.bfloat16)
        .reshape(head_shape)
    )
    row_delta = jnp.transpose(jnp.sum(d_attn.astype(jnp.float32) * attn_exact, -1))

    def grad_step(block_index, totals):
        d_query_acc, d_key_all, d_value_all = totals
        blk_keys, blk_values, blk_segs, blk_pos = key_slice(block_index)
        d_query_part, d_key_part, d_value_part = block_grads(
            queries,
            d_attn,
            log_total,
            row_delta,
            tok_pos,
            seg_local,
            blk_keys,
            blk_values,
            blk_pos,
            blk_segs,
        )
        offset = block_index * key_block
        return (
            d_query_acc + d_query_part,
            lax.dynamic_update_slice_in_dim(d_key_all, d_key_part, offset, 0),
            lax.dynamic_update_slice_in_dim(d_value_all, d_value_part, offset, 0),
        )

    zero_all = jnp.zeros((seq_total,) + head_shape[1:], jnp.float32)
    d_queries, d_key_all, d_value_all = lax.fori_loop(
        0, block_total, grad_step, (zero_heads, zero_all, zero_all)
    )
    d_keys, d_values = (
        lax.psum_scatter(
            d_key_all.astype(jnp.bfloat16), "context", scatter_dimension=0, tiled=True
        ).astype(jnp.float32),
        lax.psum_scatter(
            d_value_all.astype(jnp.bfloat16), "context", scatter_dimension=0, tiled=True
        ).astype(jnp.float32),
    )
    d_query_flat = rotate(d_queries, rope_pos, -1.0).reshape(tok_count, model_dim)
    d_key_flat = rotate(d_keys, rope_pos, -1.0).reshape(tok_count, model_dim)
    d_proj = jnp.stack(
        [d_query_flat, d_key_flat, d_values.reshape(tok_count, model_dim)], 1
    ).astype(jnp.bfloat16)
    d_rank_qkv = (ADAPT_SCALE * bdot("tpd,prd->ptr", d_proj, up_sel[:3])).astype(jnp.bfloat16)
    grad_up_qkv = ADAPT_SCALE * bdot("ptr,tpd->prd", rank_qkv, d_proj)
    grad_down_qkv = bdot("td,ptr->prd", normed_low, d_rank_qkv)
    d_normed_one = bdot("te,de->td", d_proj.reshape(tok_count, 3 * model_dim), w_qkv) + bdot(
        "ptr,pdr->td", d_rank_qkv, down_sel[:3]
    )
    scaled_one = d_normed_one * gain_one
    grad_in = (
        d_mid
        + inv_one * scaled_one
        - resid_in
        * (inv_one * inv_one * inv_one)
        * jnp.mean(scaled_one * resid_in, -1, keepdims=True)
    )
    grad_down_all = jnp.concatenate([grad_down_qkv, grad_down_out[None]], 0)
    grad_up_all = jnp.concatenate([grad_up_qkv, grad_up_out[None]], 0)
    in_down, in_up, out_down, out_up = owner_grads
    sources, experts, _, rank_dim, ffn_width = in_up.shape
    sums = reduce_adapters(
        adapter_ids,
        (in_down, in_up.reshape(sources, experts, 2 * rank_dim, ffn_width), out_down, out_up),
        grad_down_all.reshape(4 * rank_dim, model_dim),
        grad_up_all.reshape(4 * rank_dim, model_dim),
        adapter_count,
    )
    grad_attn_down = jnp.swapaxes(sums[0].reshape(adapter_count, 4, rank_dim, model_dim), 2, 3)
    grad_attn_up = sums[1].reshape(adapter_count, 4, rank_dim, model_dim)
    grad_in_down = jnp.swapaxes(sums[2], 2, 3)
    grad_in_up = sums[3].reshape(adapter_count, experts, 2, rank_dim, ffn_width)
    grad_out_down = jnp.swapaxes(sums[4], 2, 3)
    grad_out_up = sums[5]
    return (
        layer_out.astype(jnp.bfloat16)[None],
        grad_in[None],
        grad_prev[None],
        grad_attn_down,
        grad_attn_up,
        grad_in_down,
        grad_in_up,
        grad_out_down,
        grad_out_up,
    )


def solution(mesh):
    return jax.shard_map(
        local,
        mesh=mesh,
        in_specs=(
            P(("dp", "expert"), "context", None),
            P(("dp", "expert"), "context", None),
            P(("dp", "expert"), "context"),
            P(("dp", "expert"), "context", None),
            P(),
            P(),
            P(),
            P(),
            P(),
            P(),
            P(),
            P(),
            P(),
            P(),
            P(),
            P("expert", None, None),
            P("expert", None, None),
            P(None, "expert", None, None),
            P(None, "expert", None, None, None),
            P(None, "expert", None, None),
            P(None, "expert", None, None),
            P(("dp", "expert"), "context", None),
        ),
        out_specs=(
            P(("dp", "expert"), "context", None),
            P(("dp", "expert"), "context", None),
            P(("dp", "expert"), "context", None),
            P(),
            P(),
            P(None, "expert", None, None),
            P(None, "expert", None, None, None),
            P(None, "expert", None, None),
            P(None, "expert", None, None),
        ),
        check_vma=False,
    )
```

```python
import functools
import math

import jax
import jax.numpy as jnp
import numpy as np
from jax import lax
from jax.experimental import pallas as pl
from jax.experimental.pallas import tpu as pltpu
from jax.sharding import PartitionSpec as P

MESH = pl.DeviceIdType.MESH
VLIMIT = 60 * 1024 * 1024
BF = jnp.bfloat16
F32 = jnp.float32

HEADS = 12


EPSILON = 1e-06
ADAPT_SCALE = 2.0
NEG = -1e30
HIGH = lax.Precision.HIGHEST


def bdot(form, left, right):
    return jnp.einsum(form, left, right, preferred_element_type=jnp.float32)


def fdot(form, left, right):
    return jnp.einsum(form, left, right, precision=HIGH, preferred_element_type=jnp.float32)


def expert_hidden(arrived, tables, w_gate_up, ffn_width):
    rank_dim = tables[1].shape[3]
    joined_rows = bdot("jecd,edf->jecf", arrived, w_gate_up)
    rank_in = bdot("jecd,jedr->jecr", arrived, tables[0]).astype(jnp.bfloat16)
    gate_pre = joined_rows[..., :ffn_width] + ADAPT_SCALE * bdot(
        "jecr,jerf->jecf", rank_in[..., :rank_dim], tables[1][:, :, 0]
    )
    up_pre = joined_rows[..., ffn_width:] + ADAPT_SCALE * bdot(
        "jecr,jerf->jecf", rank_in[..., rank_dim:], tables[1][:, :, 1]
    )
    return (gate_pre, up_pre, rank_in)


def expert_forward(arrived, tables, w_gate_up, w_down):
    gate_pre, up_pre, rank_in = expert_hidden(arrived, tables, w_gate_up, w_down.shape[1])
    activated = (jax.nn.silu(gate_pre) * up_pre).astype(jnp.bfloat16)
    rank_mid = bdot("jecf,jefr->jecr", activated, tables[2]).astype(jnp.bfloat16)
    result = bdot("jecf,efd->jecd", activated, w_down) + ADAPT_SCALE * bdot(
        "jecr,jerd->jecd", rank_mid, tables[3]
    )
    return result.astype(jnp.bfloat16)


def expert_backward(arrived, d_result, tables, w_gate_up, w_down):
    gate_pre, up_pre, rank_in = expert_hidden(arrived, tables, w_gate_up, w_down.shape[1])
    rank_dim = tables[1].shape[3]
    sigmoid_gate = jax.nn.sigmoid(gate_pre)
    silu_gate = gate_pre * sigmoid_gate
    activated = (silu_gate * up_pre).astype(jnp.bfloat16)
    rank_mid = bdot("jecf,jefr->jecr", activated, tables[2]).astype(jnp.bfloat16)
    d_rank_mid = (ADAPT_SCALE * bdot("jecd,jerd->jecr", d_result, tables[3])).astype(jnp.bfloat16)
    grad_out_up = ADAPT_SCALE * bdot("jecr,jecd->jerd", rank_mid, d_result)
    grad_out_down = bdot("jecf,jecr->jerf", activated, d_rank_mid)
    d_act = (
        (bdot("jecd,efd->jecf", d_result, w_down) + bdot("jecr,jefr->jecf", d_rank_mid, tables[2]))
        .astype(jnp.bfloat16)
        .astype(jnp.float32)
    )
    d_gate = (d_act * up_pre * sigmoid_gate * (1.0 + gate_pre * (1.0 - sigmoid_gate))).astype(
        jnp.bfloat16
    )
    d_up = (d_act * silu_gate).astype(jnp.bfloat16)
    d_rank_in = (
        ADAPT_SCALE
        * jnp.concatenate(
            [
                bdot("jecf,jerf->jecr", d_gate, tables[1][:, :, 0]),
                bdot("jecf,jerf->jecr", d_up, tables[1][:, :, 1]),
            ],
            -1,
        )
    ).astype(jnp.bfloat16)
    grad_in_up = ADAPT_SCALE * jnp.stack(
        [
            bdot("jecr,jecf->jerf", rank_in[..., :rank_dim], d_gate),
            bdot("jecr,jecf->jerf", rank_in[..., rank_dim:], d_up),
        ],
        2,
    )
    grad_in_down = bdot("jecd,jecr->jerd", arrived, d_rank_in)
    d_arrived = bdot("jecf,edf->jecd", jnp.concatenate([d_gate, d_up], -1), w_gate_up) + bdot(
        "jecr,jedr->jecd", d_rank_in, tables[0]
    )
    return (d_arrived, (grad_in_down, grad_in_up, grad_out_down, grad_out_up))


def nt(left, right):
    return lax.dot_general(left, right, (((1,), (1,)), ((), ())), preferred_element_type=F32)


def tn(left, right):
    return lax.dot_general(left, right, (((0,), (0,)), ((), ())), preferred_element_type=F32)


def nn(left, right):
    return jnp.dot(left, right, preferred_element_type=F32)


def rope_tables(positions, width):
    half = width // 2
    frequency = np.exp(np.arange(half) * (-2.0 * math.log(10000.0) / width))
    angles = np.arange(positions)[:, None] * frequency[None, :]
    cosine, sine = np.cos(angles), np.sin(angles)
    return (
        np.concatenate([cosine] * 4, 1).astype(np.float32),
        np.concatenate([-sine, sine] * 2, 1).astype(np.float32),
    )


def turn(block, cosine, sine, width):
    half = width // 2
    lane = lax.broadcasted_iota(jnp.int32, block.shape, 1)
    other = jnp.where(
        lane % width < half, pltpu.roll(block, 128 - half, 1), pltpu.roll(block, half, 1)
    )
    return block * cosine + other * sine


def greet(axes):
    barrier = pltpu.get_barrier_semaphore()
    count = 0
    for axis, size in axes:
        index = lax.axis_index(axis)
        for step in range(1, size):
            pl.semaphore_signal(
                barrier, inc=1, device_id={axis: lax.rem(index + step, size)}, device_id_type=MESH
            )
        count += size - 1
    return lambda: pl.semaphore_wait(barrier, count)


def remote(src, dst, send, recv, axis, target):
    return pltpu.make_async_remote_copy(
        src_ref=src, dst_ref=dst, send_sem=send, recv_sem=recv,
        device_id={axis: target}, device_id_type=MESH,
    )


def blocks_of(ctx_n, ctx, count):
    return [lax.rem(ctx + 1 + j, ctx_n) for j in range(count)]


def fill_bias(bias_ref, seg_all, ctx_n, ctx, tok, count):
    own = jnp.broadcast_to(seg_all[ctx, 0:1, :].astype(F32), (128, tok))
    query_seg = jnp.transpose(own)[:, 0:1]
    query_pos = ctx * tok + lax.broadcasted_iota(jnp.int32, (tok, tok), 0)
    for j, block in enumerate([ctx] + blocks_of(ctx_n, ctx, count)):
        key_seg = seg_all[block, 0:1, :].astype(F32)
        key_pos = block * tok + lax.broadcasted_iota(jnp.int32, (tok, tok), 1)
        allowed = (query_seg == key_seg) & (key_pos <= query_pos)
        bias_ref[j] = jnp.where(allowed, 0.0, NEG).astype(bias_ref.dtype)


def attention_kernel(
    sizes, ids_ref, x_ref, seg_ref, mixed_ref, gain_one_ref, w_qkv_ref, w_out_ref, down_ref, up_ref,
    gain_two_ref, router_ref, cos_ref, sin_ref,
    q_ref, k_ref, v_ref, normed_ref, rank_ref, total_ref, flat_ref, rank_out_ref, mid_ref, rows_ref,
    logits_ref, seg_all,
    x_all, bias_ref, send_sem, recv_sem, seg_send, seg_recv,
):
    ctx_n, exp_n, rank = sizes
    ctx = lax.axis_index("context")
    sequence = lax.axis_index("dp") * exp_n + lax.axis_index("expert")
    tok, model = x_ref.shape
    pairs, head_dim = model // 128, 64
    entered = greet([("context", ctx_n)])
    seg_all[ctx] = jnp.broadcast_to(seg_ref[...], (8, tok))
    if ctx_n > 1:
        entered()
        copies = []
        for step in range(1, ctx_n):
            peer = lax.rem(ctx + step, ctx_n)
            copies.append(
                (
                    peer,
                    step,
                    remote(x_ref, x_all.at[ctx], send_sem.at[step - 1], recv_sem.at[step - 1], "context", peer),
                    remote(seg_all.at[ctx], seg_all.at[ctx], seg_send.at[step - 1], seg_recv.at[step - 1], "context", peer),
                )
            )

        def to_later(peer):
            return ctx < peer if ctx_n == 2 else ctx < ctx_n

        def from_earlier(step):
            return lax.rem(ctx - step + ctx_n, ctx_n) < ctx if ctx_n == 2 else ctx < ctx_n

        for peer, step, rows_copy, seg_copy in copies:
            @pl.when(to_later(peer))
            def _(rows_copy=rows_copy, seg_copy=seg_copy):
                seg_copy.start()
                rows_copy.start()

    adapter = ids_ref[sequence]
    down = down_ref[adapter]
    up = up_ref[adapter]
    gain_one = gain_one_ref[...].astype(F32)
    column = lax.broadcasted_iota(jnp.int32, (tok, down.shape[0]), 1) // rank

    def project(values, block, first):
        wide = values.astype(F32)
        inv = lax.rsqrt(jnp.mean(wide * wide, -1, keepdims=True) + EPSILON)
        normed_ref[block] = (wide * inv * gain_one).astype(BF)
        normed = normed_ref[block]
        ranks = nt(normed, down).astype(BF)
        rank_ref[block] = ranks
        start = pl.multiple_of(block * tok, tok)
        for p in range(first, 3):
            part = jnp.where(column == p, ADAPT_SCALE * ranks.astype(F32), 0.0).astype(BF)

            def chunk(i, carry, p=p, part=part):
                wide_cols = pl.ds(pl.multiple_of(p * model + i * 256, 256), 256)
                cols = pl.ds(pl.multiple_of(i * 256, 256), 256)
                proj = nn(normed_ref[block], w_qkv_ref[:, wide_cols]) + nn(
                    part, up_cols[:, cols]
                )
                for half in range(2):
                    piece = proj[:, half * 128 : half * 128 + 128]
                    if p < 2:
                        piece = turn(
                            piece, cos_ref[pl.ds(start, tok)], sin_ref[pl.ds(start, tok)], head_dim
                        )
                    if p == 0:
                        q_ref[2 * i + half] = (piece * head_dim ** (-0.5)).astype(BF)
                    else:
                        (k_ref if p == 1 else v_ref)[block, 2 * i + half] = piece.astype(BF)
                return carry

            up_cols = up_ref.at[adapter]
            lax.fori_loop(0, model // 256, chunk, 0)

    project(x_ref[...], ctx, 0)
    lane = lax.broadcasted_iota(jnp.int32, (1, 128), 1)
    marks = [(lane < 64), (lane >= 64)]
    half_rows = tok // 2

    def attend(count):
        fill_bias(bias_ref, seg_all, ctx_n, ctx, tok, count)
        others = blocks_of(ctx_n, ctx, count)

        def pair(i, carry):
            for half in range(2):
                rows = slice(half * half_rows, (half + 1) * half_rows)
                own_width = (half + 1) * half_rows
                q = q_ref[i, rows]
                result = jnp.zeros((half_rows, 128), F32)
                stats = total_ref[rows]
                for head in range(2):
                    mark = marks[head]
                    q_head = jnp.where(mark, q, 0)
                    scores = [
                        nt(q_head, k_ref[ctx, i, 0:own_width]) + bias_ref[0, rows, 0:own_width]
                    ]
                    for j, block in enumerate(others):
                        scores.append(nt(q_head, k_ref[block, i]) + bias_ref[j + 1, rows])
                    top = functools.reduce(
                        jnp.maximum, [jnp.max(s, -1, keepdims=True) for s in scores]
                    )
                    exps = [jnp.exp(s - top) for s in scores]
                    total = functools.reduce(jnp.add, [jnp.sum(e, -1, keepdims=True) for e in exps])
                    stats = jnp.where(lane == 2 * i + head, top + jnp.log(total), stats)
                    inv = 1.0 / total
                    for e, block in zip(exps, [ctx] + others):
                        v = k_v(block, i, e.shape[1])
                        result = result + nn((e * inv).astype(BF), jnp.where(mark, v, 0))
                total_ref[rows] = stats
                flat_ref[rows, pl.ds(pl.multiple_of(i * 128, 128), 128)] = result.astype(BF)
            return carry

        def k_v(block, i, width):
            return v_ref[block, i, 0:width]

        lax.fori_loop(0, pairs, pair, 0)

    total_ref[...] = jnp.zeros_like(total_ref)
    if ctx_n == 1:
        attend(0)
    else:
        for peer, step, rows_copy, seg_copy in copies:
            @pl.when(from_earlier(step))
            def _(step=step, rows_copy=rows_copy, seg_copy=seg_copy):
                rows_copy.wait_recv()
                seg_copy.wait_recv()
                block = lax.rem(ctx - step + ctx_n, ctx_n)
                project(x_all[block], block, 1)

        @pl.when(ctx == 0)
        def _():
            if ctx_n == 2:
                attend(0)
            else:
                attend(ctx_n - 1)

        @pl.when(ctx > 0)
        def _():
            attend(ctx_n - 1)

        for peer, step, rows_copy, seg_copy in copies:
            @pl.when(to_later(peer))
            def _(rows_copy=rows_copy, seg_copy=seg_copy):
                seg_copy.wait_send()
                rows_copy.wait_send()

    rank_out = nt(flat_ref[...], down).astype(BF)
    rank_out_ref[...] = rank_out
    part = jnp.where(column == 3, ADAPT_SCALE * rank_out.astype(F32), 0.0).astype(BF)

    def out_chunk(i, carry):
        cols = pl.ds(pl.multiple_of(i * 256, 256), 256)
        mid_ref[:, cols] = (
            x_ref[:, cols].astype(F32)
            + nn(flat_ref[...], w_out_ref[:, cols])
            + nn(part, up_ref[adapter, :, cols])
        )
        return carry

    lax.fori_loop(0, model // 256, out_chunk, 0)
    gain_two = gain_two_ref[...].astype(F32)
    step_rows = 128

    def norm_rows(i, carry):
        rows = pl.ds(pl.multiple_of(i * step_rows, step_rows), step_rows)
        mid = mid_ref[rows]
        inv = lax.rsqrt(jnp.mean(mid * mid, -1, keepdims=True) + EPSILON)
        rows_ref[rows] = (mid * inv * gain_two).astype(BF)
        return carry

    lax.fori_loop(0, tok // step_rows, norm_rows, 0)
    logits_ref[...] = nt(rows_ref[...], router_ref[...]) + mixed_ref[...]


def attention_forward(hidden, segments, mixed, ids, gain_one, w_qkv, w_out, down, up, gain_two, router):
    ctx_n, exp_n = lax.axis_size("context"), lax.axis_size("expert")
    tok, model = hidden.shape
    pairs = model // 128
    wide = down.shape[1]
    cos_table, sin_table = rope_tables(ctx_n * tok, 64)
    vmem = pl.BlockSpec(memory_space=pltpu.VMEM)
    dma = pltpu.SemaphoreType.DMA
    many = max(ctx_n - 1, 1)
    shape = jax.ShapeDtypeStruct
    return pl.pallas_call(
        functools.partial(attention_kernel, (ctx_n, exp_n, wide // 4)),
        out_shape=(
            shape((pairs, tok, 128), BF),
            shape((ctx_n, pairs, tok, 128), BF),
            shape((ctx_n, pairs, tok, 128), BF),
            shape((ctx_n, tok, model), BF),
            shape((ctx_n, tok, wide), BF),
            shape((tok, 128), F32),
            shape((tok, model), BF),
            shape((tok, wide), BF),
            shape((tok, model), F32),
            shape((tok, model), BF),
            shape((tok, 128), F32),
            shape((ctx_n, 8, tok), jnp.int32),
        ),
        in_specs=[pl.BlockSpec(memory_space=pltpu.SMEM)] + [vmem] * 12,
        out_specs=(vmem,) * 12,
        scratch_shapes=[
            pltpu.VMEM((ctx_n, tok, model), BF),
            pltpu.VMEM((ctx_n, tok, tok), F32),
            dma((many,)), dma((many,)), dma((many,)), dma((many,)),
        ],
        compiler_params=pltpu.CompilerParams(
            collective_id=2, has_side_effects=True, vmem_limit_bytes=VLIMIT
        ),
        name="attention_forward",
    )(
        ids, hidden, segments, mixed, gain_one.reshape(1, model), w_qkv, w_out, down, up,
        gain_two.reshape(1, model), router, jnp.asarray(cos_table), jnp.asarray(sin_table),
    )


def put_tiles(tiles_ref, first, value):
    for col in range(value.shape[1] // 128):
        tiles_ref[first + col] = value[:, col * 128 : col * 128 + 128].astype(tiles_ref.dtype)


def backward_kernel(
    sizes, ids_ref, d_mid_ref, q_ref, k_ref, v_ref, normed_ref, rank_ref, total_ref, flat_ref,
    rank_out_ref, x_ref, seg_all, gain_one_ref, w_qkv_ref, w_out_ref, down_ref, up_ref, cos_ref,
    sin_ref,
    grad_ref, tiles_ref, *scratch,
):
    ctx_n, exp_n, rank = sizes
    (
        recv_buf, do_ref, bias_ref, dk_acc, dv_acc, dq_all, dkv_all, send_buf, grad_up, grad_down,
        normed_buf, send_sem, recv_sem, load_sem,
    ) = scratch
    ctx = lax.axis_index("context")
    sequence = lax.axis_index("dp") * exp_n + lax.axis_index("expert")
    tok, model = x_ref.shape
    pairs, head_dim = model // 128, 64
    entered = greet([("context", ctx_n)])
    order = [ctx] + blocks_of(ctx_n, ctx, ctx_n - 1)

    def fetch(j):
        return pltpu.make_async_copy(
            normed_ref.at[order[j]], normed_buf.at[min(j, 1)], load_sem.at[min(j, 1)]
        )

    fetch(0).start()
    if ctx_n > 1:
        fetch(1).start()
    adapter = ids_ref[sequence]
    down = down_ref[adapter]
    up = up_ref[adapter]
    wide = down.shape[0]
    column = lax.broadcasted_iota(jnp.int32, (tok, wide), 1) // rank
    d_branch = d_mid_ref[...].astype(BF)
    d_rank_out = jnp.where(column == 3, ADAPT_SCALE * nt(d_branch, up), 0.0).astype(BF)
    twice_out = jnp.where(column == 3, ADAPT_SCALE * rank_out_ref[...].astype(F32), 0.0).astype(BF)
    grad_up[...] = tn(twice_out, d_branch)
    grad_down[...] = tn(d_rank_out, flat_ref[...])

    def attn_chunk(i, carry):
        rows = pl.ds(pl.multiple_of(i * 256, 256), 256)
        d_attn = nt(d_branch, w_out_ref[rows, :]) + nn(d_rank_out, down_ref[adapter, :, rows])
        do_ref[2 * i] = d_attn[:, :128].astype(BF)
        do_ref[2 * i + 1] = d_attn[:, 128:].astype(BF)
        return carry

    lax.fori_loop(0, model // 256, attn_chunk, 0)
    lane = lax.broadcasted_iota(jnp.int32, (1, 128), 1)
    marks = [(lane < 64), (lane >= 64)]
    half_rows = tok // 2

    def attend(count):
        fill_bias(bias_ref, seg_all, ctx_n, ctx, tok, count)
        others = blocks_of(ctx_n, ctx, count)

        def pair(i, carry):
            cols = pl.ds(pl.multiple_of(i * 128, 128), 128)
            for half in (1, 0):
                rows = slice(half * half_rows, (half + 1) * half_rows)
                own_width = (half + 1) * half_rows
                q = q_ref[i, rows]
                d_out = do_ref[i, rows]
                stats = total_ref[rows]
                d_query = jnp.zeros((half_rows, 128), F32)
                for head in range(2):
                    mark = marks[head]
                    q_head = jnp.where(mark, q, 0)
                    do_head = jnp.where(mark, d_out, 0)
                    total = jnp.sum(
                        jnp.where(lane == 2 * i + head, stats, 0.0), -1, keepdims=True
                    )
                    parts = []
                    delta = jnp.zeros((half_rows, 1), F32)
                    for j, block in enumerate([ctx] + others):
                        width = own_width if j == 0 else tok
                        probs = jnp.exp(
                            nt(q_head, k_ref[block, i, 0:width])
                            + bias_ref[j, rows, 0:width]
                            - total
                        )
                        d_probs = nt(do_head, v_ref[block, i, 0:width])
                        delta = delta + jnp.sum(probs * d_probs, -1, keepdims=True)
                        parts.append((probs, d_probs))
                    for j, block in enumerate([ctx] + others):
                        width = own_width if j == 0 else tok
                        probs, d_probs = parts[j]
                        d_scores = (probs * (d_probs - delta)).astype(BF)
                        k_head = jnp.where(mark, k_ref[block, i, 0:width], 0)
                        d_query = d_query + nn(d_scores, k_head)
                        d_key = tn(q_head, d_scores)
                        d_value = tn(do_head, probs.astype(BF))
                        if half == 1 and head == 0:
                            dk_acc[j, :, 0:width] = d_key
                            dv_acc[j, :, 0:width] = d_value
                        else:
                            dk_acc[j, :, 0:width] += d_key
                            dv_acc[j, :, 0:width] += d_value
                start = pl.multiple_of(ctx * tok + half * half_rows, half_rows)
                d_query = d_query * head_dim ** (-0.5)
                dq_all[rows, cols] = turn(
                    d_query, cos_ref[pl.ds(start, half_rows)], -sin_ref[pl.ds(start, half_rows)], head_dim
                ).astype(BF)
            for j, block in enumerate([ctx] + others):
                start = pl.multiple_of(block * tok, tok)
                d_key = turn(
                    jnp.transpose(dk_acc[j]), cos_ref[pl.ds(start, tok)], -sin_ref[pl.ds(start, tok)], head_dim
                )
                dkv_all[j, 0, :, cols] = d_key.astype(BF)
                dkv_all[j, 1, :, cols] = jnp.transpose(dv_acc[j]).astype(BF)
            return carry

        lax.fori_loop(0, pairs, pair, 0)

    def fold(j, block, first, write):
        normed = normed_buf[min(j, 1)]
        ranks = rank_ref[block].astype(F32)
        d_ranks = jnp.zeros((tok, wide), F32)
        for p in range(first, 3):
            d_proj = dq_all[...] if p == 0 else dkv_all[j, p - 1]
            twice = jnp.where(column == p, ADAPT_SCALE * ranks, 0.0).astype(BF)
            grad_up[...] += tn(twice, d_proj)
            d_ranks = d_ranks + jnp.where(column == p, ADAPT_SCALE * nt(d_proj, up), 0.0)
        d_ranks = d_ranks.astype(BF)
        grad_down[...] += tn(d_ranks, normed)

        def chunk(i, carry):
            rows = pl.ds(pl.multiple_of(i * 256, 256), 256)
            value = nn(d_ranks, down_ref[adapter, :, rows])
            for p in range(first, 3):
                d_proj = dq_all[...] if p == 0 else dkv_all[j, p - 1]
                value = value + nt(d_proj, w_qkv_ref[rows, p * model : (p + 1) * model])
            write(rows, value)
            return carry

        lax.fori_loop(0, model // 256, chunk, 0)

    def write_own(cols, value):
        grad_ref[:, cols] = value

    copies = []
    for step in range(1, ctx_n):
        peer = lax.rem(ctx + step, ctx_n)
        copies.append(
            remote(send_buf, recv_buf.at[step - 1], send_sem.at[step - 1], recv_sem.at[step - 1], "context", peer)
        )

    if ctx_n == 1:
        attend(0)
    elif ctx_n == 2:
        entered()

        @pl.when(ctx == 0)
        def _():
            attend(0)
    else:
        entered()

    def spread():
        attend(ctx_n - 1)
        for j, block in enumerate(blocks_of(ctx_n, ctx, ctx_n - 1)):
            def write(cols, value):
                send_buf[:, cols] = value.astype(BF)

            fetch(j + 1).wait()
            if j > 0:
                copies[j - 1].wait_send()
            fold(j + 1, block, 1, write)
            copies[j].start()
            if j + 2 < ctx_n:
                fetch(j + 2).start()

    if ctx_n == 2:
        pl.when(ctx == 1)(spread)
        pl.when(ctx == 0)(fetch(1).wait)
    elif ctx_n > 2:
        spread()
    fetch(0).wait()
    fold(0, ctx, 0, write_own)
    if ctx_n == 2:
        @pl.when(ctx == 0)
        def _():
            copies[0].wait_recv()

        @pl.when(ctx == 1)
        def _():
            recv_buf[...] = jnp.zeros_like(recv_buf)
    elif ctx_n > 2:
        copies[-1].wait_send()
        for step, item in enumerate(copies):
            item.wait_recv()
            load = pltpu.make_async_copy(recv_buf.at[step], send_buf, load_sem.at[0])
            load.start()
            load.wait()
            grad_ref[...] += send_buf[...].astype(F32)
    gain_one = gain_one_ref[...].astype(F32)

    def finish(i, carry):
        rows = pl.ds(pl.multiple_of(i * 128, 128), 128)
        value = grad_ref[rows]
        if ctx_n == 2:
            value = value + recv_buf[0, rows].astype(F32)
        x = x_ref[rows].astype(F32)
        inv = lax.rsqrt(jnp.mean(x * x, -1, keepdims=True) + EPSILON)
        scaled = value * gain_one
        grad_ref[rows] = (
            d_mid_ref[rows]
            + inv * scaled
            - x * (inv * inv * inv) * jnp.mean(scaled * x, -1, keepdims=True)
        )
        return carry

    lax.fori_loop(0, tok // 128, finish, 0)
    per = model // 128
    for p in range(4):
        put_tiles(tiles_ref, p * per, grad_down[p * rank : (p + 1) * rank])
        put_tiles(tiles_ref, (4 + p) * per, grad_up[p * rank : (p + 1) * rank])
    if ctx_n == 2:
        @pl.when(ctx == 1)
        def _():
            copies[0].wait_send()


def attention_backward(d_mid, saved, hidden, ids, gain_one, w_qkv, w_out, down, up):
    ctx_n, exp_n = lax.axis_size("context"), lax.axis_size("expert")
    tok, model = hidden.shape
    pairs = model // 128
    wide = down.shape[1]
    cos_table, sin_table = rope_tables(ctx_n * tok, 64)
    vmem = pl.BlockSpec(memory_space=pltpu.VMEM)
    dma = pltpu.SemaphoreType.DMA
    many = max(ctx_n - 1, 1)
    shape = jax.ShapeDtypeStruct
    q, k, v, normed, ranks, totals, flat, rank_out, seg_all = saved
    in_specs = [vmem] * 18
    in_specs[4] = pl.BlockSpec(memory_space=pl.ANY)
    spill = ctx_n > 2
    landing = ((many, tok, model), BF)
    results = pl.pallas_call(
        functools.partial(backward_kernel, (ctx_n, exp_n, wide // 4)),
        out_shape=(shape((tok, model), F32), shape((8 * pairs, 16, 128), BF))
        + ((shape(*landing),) if spill else ()),
        in_specs=[pl.BlockSpec(memory_space=pltpu.SMEM)] + in_specs,
        out_specs=(vmem,) * 2 + ((pl.BlockSpec(memory_space=pl.ANY),) if spill else ()),
        scratch_shapes=([] if spill else [pltpu.VMEM(*landing)])
        + [
            pltpu.VMEM((pairs, tok, 128), BF),
            pltpu.VMEM((ctx_n, tok, tok), BF if spill else F32),
            pltpu.VMEM((ctx_n, 128, tok), F32),
            pltpu.VMEM((ctx_n, 128, tok), F32),
            pltpu.VMEM((tok, model), BF),
            pltpu.VMEM((ctx_n, 2, tok, model), BF),
            pltpu.VMEM((tok, model), BF),
            pltpu.VMEM((wide, model), F32),
            pltpu.VMEM((wide, model), F32),
            pltpu.VMEM((min(ctx_n, 2), tok, model), BF),
            dma((many,)), dma((many,)), dma((2,)),
        ],
        compiler_params=pltpu.CompilerParams(
            collective_id=3, has_side_effects=True, vmem_limit_bytes=VLIMIT + 5 * 2**19
        ),
        name="attention_backward",
    )(
        ids, d_mid, q, k, v, normed, ranks, totals, flat, rank_out, hidden, seg_all,
        gain_one.reshape(1, model), w_qkv, w_out, down, up, jnp.asarray(cos_table),
        jnp.asarray(sin_table),
    )
    return results[:2]


def to_tiles(table):
    lead, (rows, cols) = table.shape[:-2], table.shape[-2:]
    cut = table.reshape(lead + (rows // 16, 16, cols // 128, 128))
    cut = jnp.swapaxes(cut, -3, -2)
    return cut.reshape(lead + (rows * cols // 2048, 16, 128))


def reduce_kernel(
    sizes, ids_ref, grads_ref, attn_ref, table_ref, attn_table_ref,
    held, arrived_x, part_z, arrived_z,
    load_sem, ready_send, ready_recv, x_send, x_recv, z_send, z_recv, az_send, az_recv,
    ax_send, ax_recv, e_send, e_recv,
):
    ctx_n, dp_n, exp_n, adapters, tiles, attn_tiles, x_tiles, z_tiles = sizes
    own_attn = attn_tiles // exp_n
    ctx, dp, exp = lax.axis_index("context"), lax.axis_index("dp"), lax.axis_index("expert")
    barrier = pltpu.get_barrier_semaphore()
    for axis, size, index in (("context", ctx_n, ctx), ("dp", dp_n, dp), ("expert", exp_n, exp)):
        for step in range(1, size):
            pl.semaphore_signal(
                barrier, inc=1, device_id={axis: lax.rem(index + step, size)}, device_id_type=MESH
            )
    load = pltpu.make_async_copy(grads_ref, held.at[:, pl.ds(0, tiles)], load_sem)
    load.start()
    keep = pltpu.make_async_copy(
        attn_ref.at[pl.ds(exp * own_attn, own_attn)],
        held.at[exp, pl.ds(tiles, own_attn)],
        ready_send.at[exp_n - 1],
    )
    keep.start()
    pl.semaphore_wait(barrier, ctx_n + dp_n + exp_n - 3)

    def copy(src, dst, send, recv, axis, target):
        return pltpu.make_async_remote_copy(
            src_ref=src, dst_ref=dst, send_sem=send, recv_sem=recv,
            device_id={axis: target}, device_id_type=MESH,
        )

    waits = []
    first = []
    for step in range(1, exp_n):
        peer = lax.rem(exp + step, exp_n)
        send = copy(
            attn_ref.at[pl.ds(peer * own_attn, own_attn)],
            held.at[exp, pl.ds(tiles, own_attn)],
            ready_send.at[step - 1], ready_recv.at[step - 1], "expert", peer,
        )
        send.start()
        first.append(send)
    load.wait()
    keep.wait()
    for send in first:
        send.wait()
    for k in range(1, dp_n + 1):
        part = lax.rem(dp + k, dp_n)
        for step in range(1, ctx_n):
            peer = lax.rem(ctx + step, ctx_n)
            send = copy(
                held.at[:, pl.ds(peer * x_tiles + part * z_tiles, z_tiles)],
                arrived_x.at[step - 1, k - 1],
                x_send.at[step - 1, k - 1], x_recv.at[step - 1, k - 1], "context", peer,
            )
            send.start()
            waits.append(send)
    z_sends = []
    for k in range(1, dp_n + 1):
        part = lax.rem(dp + k, dp_n)
        for step in range(1, ctx_n):
            waits[(k - 1) * (ctx_n - 1) + step - 1].wait_recv()
        base = ctx * x_tiles + part * z_tiles

        def add(tile, carry, k=k, base=base):
            total = held[:, pl.ds(base + tile, 1)].astype(F32)
            for step in range(1, ctx_n):
                total = total + arrived_x[step - 1, k - 1, :, pl.ds(tile, 1)].astype(F32)
            part_z[k - 1, :, pl.ds(tile, 1)] = total.astype(BF)
            return carry

        lax.fori_loop(0, z_tiles, add, 0)
        if k < dp_n:
            send = copy(
                part_z.at[k - 1], arrived_z.at[k - 1], z_send.at[k - 1], z_recv.at[k - 1], "dp", part
            )
            send.start()
            z_sends.append(send)
    for send in z_sends:
        send.wait_recv()

    weights = []
    for k in range(dp_n):
        origin = lax.rem(dp - k + dp_n, dp_n)
        for source in range(exp_n):
            name = ids_ref[origin * exp_n + source]
            weights.append([jnp.where(name == a, 1.0, 0.0).astype(F32) for a in range(adapters)])

    def combine(tile, carry):
        totals = [jnp.zeros((16, 128), F32)] * adapters
        for k in range(dp_n):
            for source in range(exp_n):
                ref = part_z.at[dp_n - 1] if k == 0 else arrived_z.at[k - 1]
                value = ref[source, tile].astype(F32)
                marks = weights[k * exp_n + source]
                totals = [total + mark * value for total, mark in zip(totals, marks)]
        for a in range(adapters):
            table_ref[ctx, dp, a, tile] = totals[a].astype(BF)
        return carry

    lax.fori_loop(0, z_tiles, combine, 0)
    az_sends, ax_sends = [], []
    for k in range(1, dp_n):
        send = copy(
            table_ref.at[ctx, dp], table_ref.at[ctx, dp], az_send.at[k - 1], az_recv.at[k - 1],
            "dp", lax.rem(dp + k, dp_n),
        )
        send.start()
        az_sends.append(send)
    for k in range(dp_n):
        if k > 0:
            az_sends[k - 1].wait_recv()
        origin = lax.rem(dp - k + dp_n, dp_n)
        for step in range(1, ctx_n):
            send = copy(
                table_ref.at[ctx, origin], table_ref.at[ctx, origin],
                ax_send.at[step - 1, k], ax_recv.at[step - 1, k],
                "context", lax.rem(ctx + step, ctx_n),
            )
            send.start()
            ax_sends.append(send)
    for send in ax_sends:
        send.wait_recv()
    for index in range(own_attn):
        tile = tiles + index
        where = (tile // x_tiles, (tile % x_tiles) // z_tiles, tile % x_tiles % z_tiles)
        for a in range(adapters):
            attn_table_ref[exp, index, a] = table_ref[where[0], where[1], a, where[2]]
    last = []
    for step in range(1, exp_n):
        send = copy(
            attn_table_ref.at[exp], attn_table_ref.at[exp], e_send.at[step - 1], e_recv.at[step - 1],
            "expert", lax.rem(exp + step, exp_n),
        )
        send.start()
        last.append(send)
    for send in last:
        send.wait()
    for send in waits + z_sends + az_sends + ax_sends:
        send.wait_send()


def unpack_kernel(sizes, table_ref, attn_ref, down_ref, up_ref, in_down_ref, in_up_ref, out_down_ref, out_up_ref):
    x_tiles, z_tiles, own_attn = sizes

    def tile_at(tile):
        local = tile % x_tiles
        return table_ref[tile // x_tiles, local // z_tiles, 0, local % z_tiles].astype(F32)

    tile = 0
    for expert in range(in_up_ref.shape[1]):
        for out_ref in (in_down_ref, in_up_ref, out_down_ref, out_up_ref):
            rows, cols = out_ref.shape[2:]
            for row in range(rows // 16):
                for col in range(cols // 128):
                    out_ref[0, expert, row * 16 : row * 16 + 16, col * 128 : col * 128 + 128] = tile_at(tile)
                    tile += 1
    tile = 0
    for out_ref in (down_ref, up_ref):
        rows, cols = out_ref.shape[1:]
        for row in range(rows // 16):
            for col in range(cols // 128):
                out_ref[0, row * 16 : row * 16 + 16, col * 128 : col * 128 + 128] = attn_ref[
                    tile // own_attn, tile % own_attn, 0
                ].astype(F32)
                tile += 1


def reduce_adapters(adapter_ids, expert_grads, attn, attn_shape, adapters):
    ctx_n, dp_n, exp_n = (lax.axis_size(axis) for axis in ("context", "dp", "expert"))
    experts = expert_grads[0].shape[1]
    packed = jnp.concatenate(
        [to_tiles(g)[:, e] for e in range(experts) for g in expert_grads], 1
    ).astype(BF)
    tiles, attn_tiles = packed.shape[1], attn.shape[0]
    own_attn = attn_tiles // exp_n
    z_tiles = pl.cdiv(tiles + own_attn, ctx_n * dp_n)
    x_tiles = z_tiles * dp_n
    sizes = (ctx_n, dp_n, exp_n, adapters, tiles, attn_tiles, x_tiles, z_tiles)
    dma = pltpu.SemaphoreType.DMA
    many = max(ctx_n - 1, 1)
    table, attn_table = pl.pallas_call(
        functools.partial(reduce_kernel, sizes),
        out_shape=(
            jax.ShapeDtypeStruct((ctx_n, dp_n, adapters, z_tiles, 16, 128), BF),
            jax.ShapeDtypeStruct((exp_n, own_attn, adapters, 16, 128), BF),
        ),
        in_specs=[
            pl.BlockSpec(memory_space=pltpu.SMEM),
            pl.BlockSpec(memory_space=pl.ANY),
            pl.BlockSpec(memory_space=pltpu.VMEM),
        ],
        out_specs=(pl.BlockSpec(memory_space=pltpu.VMEM), pl.BlockSpec(memory_space=pltpu.VMEM)),
        scratch_shapes=[
            pltpu.VMEM((exp_n, ctx_n * x_tiles, 16, 128), BF),
            pltpu.VMEM((many, dp_n, exp_n, z_tiles, 16, 128), BF),
            pltpu.VMEM((dp_n, exp_n, z_tiles, 16, 128), BF),
            pltpu.VMEM((max(dp_n - 1, 1), exp_n, z_tiles, 16, 128), BF),
            dma, dma((exp_n,)), dma((exp_n,)), dma((many, dp_n)), dma((many, dp_n)),
            dma((dp_n,)), dma((dp_n,)), dma((dp_n,)), dma((dp_n,)),
            dma((many, dp_n)), dma((many, dp_n)), dma((exp_n,)), dma((exp_n,)),
        ],
        compiler_params=pltpu.CompilerParams(
            collective_id=1, has_side_effects=True, vmem_limit_bytes=VLIMIT
        ),
        name="reduce_adapters",
    )(adapter_ids, packed, attn)
    shapes = [
        (adapters,) + attn_shape,
        (adapters,) + attn_shape,
    ] + [(adapters,) + g.shape[1:] for g in expert_grads]
    return pl.pallas_call(
        functools.partial(unpack_kernel, (x_tiles, z_tiles, own_attn)),
        grid=(adapters,),
        out_shape=tuple(jax.ShapeDtypeStruct(shape, F32) for shape in shapes),
        in_specs=[
            pl.BlockSpec((ctx_n, dp_n, 1, z_tiles, 16, 128), lambda a: (0, 0, a, 0, 0, 0)),
            pl.BlockSpec((exp_n, own_attn, 1, 16, 128), lambda a: (0, 0, a, 0, 0)),
        ],
        out_specs=tuple(
            pl.BlockSpec((1,) + shape[1:], lambda a, n=len(shape): (a,) + (0,) * (n - 1))
            for shape in shapes
        ),
        compiler_params=pltpu.CompilerParams(vmem_limit_bytes=VLIMIT),
        name="unpack_adapters",
    )(table, attn_table)


def local(
    hidden_in,
    prev_logits,
    segment_ids,
    routes,
    adapter_ids,
    attn_gain,
    w_qkv,
    w_out,
    attn_down,
    attn_up,
    ffn_gain,
    router_weight,
    gate_mix,
    const_mix,
    const_vec,
    w_gate_up,
    w_down,
    exp_in_down,
    exp_in_up,
    exp_out_down,
    exp_out_up,
    cotangent,
):
    tok_count = hidden_in.shape[1]
    model_dim = hidden_in.shape[2]
    kind_count = prev_logits.shape[2]
    local_experts = w_gate_up.shape[0]
    adapter_count = attn_down.shape[0]
    key_block = min(512, tok_count)
    ctx_size = lax.axis_size("context")
    ctx_index = lax.axis_index("context")
    exp_size = lax.axis_size("expert")
    exp_index = lax.axis_index("expert")
    dp_index = lax.axis_index("dp")
    ffn_count = local_experts * exp_size
    capacity = tok_count // 4
    seq_total = tok_count * ctx_size
    my_adapter = lax.dynamic_index_in_dim(
        adapter_ids, dp_index * exp_size + exp_index, 0, keepdims=False
    )
    tok_pos = ctx_index * tok_count + jnp.arange(tok_count, dtype=jnp.int32)
    rope_pos = tok_pos.astype(jnp.float32)
    seg_local = segment_ids[0]
    head_shape = (tok_count, HEADS, model_dim // HEADS)
    rank_dim = attn_up.shape[2]
    down_all = jnp.swapaxes(attn_down, 2, 3).reshape(adapter_count, 4 * rank_dim, model_dim)
    up_all = attn_up.reshape(adapter_count, 4 * rank_dim, model_dim)
    router_rows = jnp.concatenate(
        [router_weight.T, const_mix.transpose(0, 2, 1).reshape(4, model_dim)], 0
    )
    router_rows = jnp.pad(router_rows, ((0, 128 - router_rows.shape[0]), (0, 0)))
    mixed = jnp.pad(fdot("te,ef->tf", prev_logits[0], gate_mix), ((0, 0), (0, 128 - kind_count)))
    (
        q_pairs, k_pairs, v_pairs, normed_all, rank_all, log_cols, attn_flat, rank_out_all, mid_resid,
        rows_low, logits_all, seg_all,
    ) = attention_forward(
        hidden_in[0], segment_ids, mixed, adapter_ids, attn_gain, w_qkv, w_out, down_all, up_all,
        ffn_gain, router_rows,
    )
    gain_two = ffn_gain.astype(jnp.float32)
    inv_two = lax.rsqrt(jnp.mean(mid_resid * mid_resid, -1, keepdims=True) + EPSILON)
    normed_two = mid_resid * inv_two * gain_two
    logits = logits_all[:, :kind_count]
    probs_all = jax.nn.softmax(logits, -1)
    route_tok = routes[0]
    kind_match = (
        route_tok[:, :, None] == jnp.arange(kind_count, dtype=jnp.int32)[None, None, :]
    ).astype(jnp.float32)
    gate_values = jnp.sum(kind_match * probs_all[:, None, :], -1)
    mix_const = jax.nn.softmax(logits_all[:, kind_count : kind_count + 4].reshape(tok_count, 2, 2), -1)
    const_full = const_vec.astype(jnp.float32)
    const_terms = (
        mix_const[:, :, 0:1] * normed_two[:, None, :]
        + mix_const[:, :, 1:2] * const_full[None, :, :]
    )
    flat_route = route_tok.reshape(-1)
    is_ffn = flat_route < ffn_count
    ffn_match = (flat_route[:, None] == jnp.arange(ffn_count, dtype=jnp.int32)[None, :]).astype(
        jnp.int32
    )
    slot_rank = jnp.sum((jnp.cumsum(ffn_match, 0) - 1) * ffn_match, 1)
    slot_index = jnp.where(is_ffn, flat_route * capacity + slot_rank, ffn_count * capacity)
    safe_index = jnp.minimum(slot_index, ffn_count * capacity - 1)
    buffer_shape = (exp_size, local_experts, capacity, model_dim)
    outgoing = (
        jnp.zeros((ffn_count * capacity, model_dim), jnp.bfloat16)
        .at[slot_index]
        .set(jnp.repeat(rows_low, 2, 0), mode="drop")
        .reshape(buffer_shape)
    )
    source_ids = lax.dynamic_slice_in_dim(adapter_ids, dp_index * exp_size, exp_size, 0)
    source_match = source_ids[:, None] == jnp.arange(adapter_count, dtype=jnp.int32)[None, :]
    pick_table = source_match.astype(jnp.bfloat16)
    tables = tuple(
        (
            bdot("ja,a...->j...", pick_table, table_in).astype(jnp.bfloat16)
            for table_in in (exp_in_down, exp_in_up, exp_out_down, exp_out_up)
        )
    )
    arrived = lax.all_to_all(outgoing, "expert", split_axis=0, concat_axis=0, tiled=True)
    result = expert_forward(arrived, tables, w_gate_up, w_down)
    returned = lax.all_to_all(result, "expert", split_axis=0, concat_axis=0, tiled=True)
    ffn_rows = jnp.where(
        is_ffn[:, None], returned.reshape(ffn_count * capacity, model_dim)[safe_index], 0.0
    ).reshape(tok_count, 2, model_dim)
    branch_terms = ffn_rows.astype(jnp.float32) + jnp.where(
        (route_tok == ffn_count + 1)[:, :, None], normed_two[:, None, :], 0.0
    )
    for const_index in range(2):
        branch_terms = branch_terms + jnp.where(
            (route_tok == ffn_count + 2 + const_index)[:, :, None],
            const_terms[:, const_index][:, None, :],
            0.0,
        )
    layer_out = mid_resid + jnp.sum(gate_values[:, :, None] * branch_terms, 1)
    d_out = cotangent[0].astype(jnp.float32)
    d_gates = jnp.sum(d_out[:, None, :] * branch_terms, -1)
    d_kinds = jnp.sum(kind_match * d_gates[:, :, None], 1)
    d_logits = probs_all * (d_kinds - jnp.sum(probs_all * d_kinds, -1, keepdims=True))
    grad_prev = fdot("tf,ef->te", d_logits, gate_mix)
    d_normed = fdot("te,de->td", d_logits, router_weight.astype(jnp.float32))
    copy_weight = jnp.sum(gate_values * (route_tok == ffn_count + 1).astype(jnp.float32), 1)
    d_normed = d_normed + copy_weight[:, None] * d_out
    for const_index in range(2):
        const_weight = jnp.sum(
            gate_values * (route_tok == ffn_count + 2 + const_index).astype(jnp.float32), 1
        )
        d_term = const_weight[:, None] * d_out
        mix_pair = mix_const[:, const_index]
        d_normed = d_normed + mix_pair[:, 0:1] * d_term
        d_mix = jnp.stack(
            [
                jnp.sum(d_term * normed_two, -1),
                jnp.sum(d_term * const_full[const_index][None, :], -1),
            ],
            -1,
        )
        d_inner = mix_pair * (d_mix - jnp.sum(mix_pair * d_mix, -1, keepdims=True))
        d_normed = d_normed + fdot("tc,dc->td", d_inner, const_mix[const_index].astype(jnp.float32))
    d_pairs = (
        (gate_values[:, :, None] * d_out[:, None, :])
        .astype(jnp.bfloat16)
        .reshape(2 * tok_count, model_dim)
    )
    d_outgoing = (
        jnp.zeros((ffn_count * capacity, model_dim), jnp.bfloat16)
        .at[slot_index]
        .set(d_pairs, mode="drop")
        .reshape(buffer_shape)
    )
    d_arrived = lax.all_to_all(d_outgoing, "expert", split_axis=0, concat_axis=0, tiled=True)
    d_kept, owner_grads = expert_backward(arrived, d_arrived, tables, w_gate_up, w_down)
    d_back = lax.all_to_all(
        d_kept.astype(jnp.bfloat16), "expert", split_axis=0, concat_axis=0, tiled=True
    ).astype(d_kept.dtype)
    d_back_rows = jnp.where(
        is_ffn[:, None], d_back.reshape(ffn_count * capacity, model_dim)[safe_index], 0.0
    ).reshape(tok_count, 2, model_dim)
    d_normed = d_normed + jnp.sum(d_back_rows, 1)
    scaled_two = d_normed * gain_two
    d_mid = (
        d_out
        + inv_two * scaled_two
        - mid_resid
        * (inv_two * inv_two * inv_two)
        * jnp.mean(scaled_two * mid_resid, -1, keepdims=True)
    )
    grad_in, attn_tiles = attention_backward(
        d_mid,
        (q_pairs, k_pairs, v_pairs, normed_all, rank_all, log_cols, attn_flat, rank_out_all, seg_all),
        hidden_in[0], adapter_ids, attn_gain, w_qkv, w_out, down_all, up_all,
    )
    in_down, in_up, out_down, out_up = owner_grads
    sources, experts, _, rank_dim, ffn_width = in_up.shape
    sums = reduce_adapters(
        adapter_ids,
        (in_down, in_up.reshape(sources, experts, 2 * rank_dim, ffn_width), out_down, out_up),
        attn_tiles,
        (4 * rank_dim, model_dim),
        adapter_count,
    )
    grad_attn_down = jnp.swapaxes(sums[0].reshape(adapter_count, 4, rank_dim, model_dim), 2, 3)
    grad_attn_up = sums[1].reshape(adapter_count, 4, rank_dim, model_dim)
    grad_in_down = jnp.swapaxes(sums[2], 2, 3)
    grad_in_up = sums[3].reshape(adapter_count, experts, 2, rank_dim, ffn_width)
    grad_out_down = jnp.swapaxes(sums[4], 2, 3)
    grad_out_up = sums[5]
    return (
        layer_out.astype(jnp.bfloat16)[None],
        grad_in[None],
        grad_prev[None],
        grad_attn_down,
        grad_attn_up,
        grad_in_down,
        grad_in_up,
        grad_out_down,
        grad_out_up,
    )


def solution(mesh):
    return jax.shard_map(
        local,
        mesh=mesh,
        in_specs=(
            P(("dp", "expert"), "context", None),
            P(("dp", "expert"), "context", None),
            P(("dp", "expert"), "context"),
            P(("dp", "expert"), "context", None),
            P(),
            P(),
            P(),
            P(),
            P(),
            P(),
            P(),
            P(),
            P(),
            P(),
            P(),
            P("expert", None, None),
            P("expert", None, None),
            P(None, "expert", None, None),
            P(None, "expert", None, None, None),
            P(None, "expert", None, None),
            P(None, "expert", None, None),
            P(("dp", "expert"), "context", None),
        ),
        out_specs=(
            P(("dp", "expert"), "context", None),
            P(("dp", "expert"), "context", None),
            P(("dp", "expert"), "context", None),
            P(),
            P(),
            P(None, "expert", None, None),
            P(None, "expert", None, None, None),
            P(None, "expert", None, None),
            P(None, "expert", None, None),
        ),
        check_vma=False,
    )
```

```python
import functools
import math

import jax
import jax.numpy as jnp
import numpy as np
from jax import lax
from jax.experimental import pallas as pl
from jax.experimental.pallas import tpu as pltpu
from jax.sharding import PartitionSpec as P

MESH = pl.DeviceIdType.MESH
VLIMIT = 60 * 1024 * 1024
BF = jnp.bfloat16
F32 = jnp.float32

HEADS = 12


EPSILON = 1e-06
ADAPT_SCALE = 2.0
NEG = -1e30
HIGH = lax.Precision.HIGHEST


def fdot(form, left, right):
    return jnp.einsum(form, left, right, precision=HIGH, preferred_element_type=jnp.float32)


def nt(left, right):
    return lax.dot_general(left, right, (((1,), (1,)), ((), ())), preferred_element_type=F32)


def tn(left, right):
    return lax.dot_general(left, right, (((0,), (0,)), ((), ())), preferred_element_type=F32)


def nn(left, right):
    return jnp.dot(left, right, preferred_element_type=F32)


def rope_tables(positions, width):
    half = width // 2
    frequency = np.exp(np.arange(half) * (-2.0 * math.log(10000.0) / width))
    angles = np.arange(positions)[:, None] * frequency[None, :]
    cosine, sine = np.cos(angles), np.sin(angles)
    return (
        np.concatenate([cosine] * 4, 1).astype(np.float32),
        np.concatenate([-sine, sine] * 2, 1).astype(np.float32),
    )


def turn(block, cosine, sine, width):
    half = width // 2
    lane = lax.broadcasted_iota(jnp.int32, block.shape, 1)
    other = jnp.where(
        lane % width < half, pltpu.roll(block, 128 - half, 1), pltpu.roll(block, half, 1)
    )
    return block * cosine + other * sine


def greet(axes):
    barrier = pltpu.get_barrier_semaphore()
    count = 0
    for axis, size in axes:
        index = lax.axis_index(axis)
        for step in range(1, size):
            pl.semaphore_signal(
                barrier, inc=1, device_id={axis: lax.rem(index + step, size)}, device_id_type=MESH
            )
        count += size - 1
    return lambda: pl.semaphore_wait(barrier, count)


def remote(src, dst, send, recv, axis, target):
    return pltpu.make_async_remote_copy(
        src_ref=src, dst_ref=dst, send_sem=send, recv_sem=recv,
        device_id={axis: target}, device_id_type=MESH,
    )


def blocks_of(ctx_n, ctx, count):
    return [lax.rem(ctx + 1 + j, ctx_n) for j in range(count)]


def fill_bias(bias_ref, seg_all, ctx_n, ctx, tok, count):
    own = jnp.broadcast_to(seg_all[ctx, 0:1, :].astype(F32), (128, tok))
    query_seg = jnp.transpose(own)[:, 0:1]
    query_pos = ctx * tok + lax.broadcasted_iota(jnp.int32, (tok, tok), 0)
    for j, block in enumerate([ctx] + blocks_of(ctx_n, ctx, count)):
        key_seg = seg_all[block, 0:1, :].astype(F32)
        key_pos = block * tok + lax.broadcasted_iota(jnp.int32, (tok, tok), 1)
        allowed = (query_seg == key_seg) & (key_pos <= query_pos)
        bias_ref[j] = jnp.where(allowed, 0.0, NEG).astype(bias_ref.dtype)


def attention_kernel(
    sizes, ids_ref, x_ref, seg_ref, mixed_ref, gain_one_ref, w_qkv_ref, w_out_ref, down_ref, up_ref,
    gain_two_ref, router_ref, cos_ref, sin_ref, dy_ref, routes_ref,
    q_ref, k_ref, v_ref, normed_ref, rank_ref, total_ref, flat_ref, rank_out_ref, mid_ref, rows_ref,
    logits_ref, seg_all, arrived_dy, slots_ref,
    x_all, bias_ref, sent_dy, send_sem, recv_sem, seg_send, seg_recv, dy_send, dy_recv,
):
    ctx_n, exp_n, rank = sizes
    ctx = lax.axis_index("context")
    sequence = lax.axis_index("dp") * exp_n + lax.axis_index("expert")
    tok, model = x_ref.shape
    pairs, head_dim = model // 128, 64
    entered = greet([("context", ctx_n), ("expert", exp_n)])
    seg_all[ctx] = jnp.broadcast_to(seg_ref[...], (8, tok))
    me = lax.axis_index("expert")
    experts, capacity = arrived_dy.shape[1], arrived_dy.shape[3]
    others = partners(exp_n, me)
    entered()
    dy_copies = []
    if ctx_n > 1:
        copies = []
        for step in range(1, ctx_n):
            peer = lax.rem(ctx + step, ctx_n)
            copies.append(
                (
                    peer,
                    step,
                    remote(x_ref, x_all.at[ctx], send_sem.at[step - 1], recv_sem.at[step - 1], "context", peer),
                    remote(seg_all.at[ctx], seg_all.at[ctx], seg_send.at[step - 1], seg_recv.at[step - 1], "context", peer),
                )
            )

        def to_later(peer):
            return ctx < peer if ctx_n == 2 else ctx < ctx_n

        def from_earlier(step):
            return lax.rem(ctx - step + ctx_n, ctx_n) < ctx if ctx_n == 2 else ctx < ctx_n

        for peer, step, rows_copy, seg_copy in copies:
            @pl.when(to_later(peer))
            def _(rows_copy=rows_copy, seg_copy=seg_copy):
                seg_copy.start()
                rows_copy.start()

    kind_rows = jnp.concatenate([routes_ref[...], jnp.full((6, tok), -1, jnp.int32)], 0)
    sub = lax.broadcasted_iota(jnp.int32, (16, tok), 0)
    uses = jnp.where((sub == kind_rows[0:1]) | (sub == kind_rows[1:2]), 1.0, 0.0).astype(BF)
    earlier = jnp.where(
        lax.broadcasted_iota(jnp.int32, (tok, tok), 0) < lax.broadcasted_iota(jnp.int32, (tok, tok), 1), 1.0, 0.0
    ).astype(BF)
    places = nn(uses, earlier) + (sub * capacity).astype(F32)
    slot_rows = []
    for j in range(2):
        kind = kind_rows[j : j + 1]
        place = jnp.sum(jnp.where(sub == kind, places, 0.0), 0, keepdims=True)
        slot_rows.append(jnp.where(kind < exp_n * experts, place, -1.0))
    row8 = lax.broadcasted_iota(jnp.int32, (8, tok), 0)
    slots_ref[...] = jnp.where(
        row8 < 2, kind_rows.astype(F32), jnp.where(row8 == 2, slot_rows[0], jnp.where(row8 == 3, slot_rows[1], 0.0))
    )
    slot_ints = [row.astype(jnp.int32) for row in slot_rows]

    def pick_dy(owner):
        hots = [hot_rows(row, owner * experts * capacity, experts * capacity) for row in slot_ints]
        hot = jnp.where(hots[0] | hots[1], 1.0, 0.0).astype(BF)
        return nn(hot, dy_ref[...]).astype(BF)

    for i, peer in enumerate(others):
        picked = pick_dy(peer)
        for e in range(experts):
            sent_dy[i, e] = picked[e * capacity : (e + 1) * capacity]
        copy = remote(
            sent_dy.at[i], arrived_dy.at[me // 2, :, lax.rem(me, 2)], dy_send.at[i], dy_recv.at[me], "expert", peer
        )
        copy.start()
        dy_copies.append(copy)
    picked = pick_dy(me)
    for e in range(experts):
        arrived_dy[me // 2, e, lax.rem(me, 2)] = picked[e * capacity : (e + 1) * capacity]
    adapter = ids_ref[sequence]
    down = down_ref[adapter]
    up = up_ref[adapter]
    gain_one = gain_one_ref[...].astype(F32)
    column = lax.broadcasted_iota(jnp.int32, (tok, down.shape[0]), 1) // rank

    def project(values, block, first):
        wide = values.astype(F32)
        inv = lax.rsqrt(jnp.mean(wide * wide, -1, keepdims=True) + EPSILON)
        normed_ref[block] = (wide * inv * gain_one).astype(BF)
        normed = normed_ref[block]
        ranks = nt(normed, down).astype(BF)
        rank_ref[block] = ranks
        start = pl.multiple_of(block * tok, tok)
        for p in range(first, 3):
            part = jnp.where(column == p, ADAPT_SCALE * ranks.astype(F32), 0.0).astype(BF)

            def chunk(i, carry, p=p, part=part):
                wide_cols = pl.ds(pl.multiple_of(p * model + i * 256, 256), 256)
                cols = pl.ds(pl.multiple_of(i * 256, 256), 256)
                proj = nn(normed_ref[block], w_qkv_ref[:, wide_cols]) + nn(
                    part, up_cols[:, cols]
                )
                for half in range(2):
                    piece = proj[:, half * 128 : half * 128 + 128]
                    if p < 2:
                        piece = turn(
                            piece, cos_ref[pl.ds(start, tok)], sin_ref[pl.ds(start, tok)], head_dim
                        )
                    if p == 0:
                        q_ref[2 * i + half] = (piece * head_dim ** (-0.5)).astype(BF)
                    else:
                        (k_ref if p == 1 else v_ref)[block, 2 * i + half] = piece.astype(BF)
                return carry

            up_cols = up_ref.at[adapter]
            lax.fori_loop(0, model // 256, chunk, 0)

    project(x_ref[...], ctx, 0)
    lane = lax.broadcasted_iota(jnp.int32, (1, 128), 1)
    marks = [(lane < 64), (lane >= 64)]
    half_rows = tok // 2

    def attend(count):
        fill_bias(bias_ref, seg_all, ctx_n, ctx, tok, count)
        others = blocks_of(ctx_n, ctx, count)

        def pair(i, carry):
            for half in range(2):
                rows = slice(half * half_rows, (half + 1) * half_rows)
                own_width = (half + 1) * half_rows
                q = q_ref[i, rows]
                result = jnp.zeros((half_rows, 128), F32)
                stats = total_ref[rows]
                for head in range(2):
                    mark = marks[head]
                    q_head = jnp.where(mark, q, 0)
                    scores = [
                        nt(q_head, k_ref[ctx, i, 0:own_width]) + bias_ref[0, rows, 0:own_width]
                    ]
                    for j, block in enumerate(others):
                        scores.append(nt(q_head, k_ref[block, i]) + bias_ref[j + 1, rows])
                    top = functools.reduce(
                        jnp.maximum, [jnp.max(s, -1, keepdims=True) for s in scores]
                    )
                    exps = [jnp.exp(s - top) for s in scores]
                    total = functools.reduce(jnp.add, [jnp.sum(e, -1, keepdims=True) for e in exps])
                    stats = jnp.where(lane == 2 * i + head, top + jnp.log(total), stats)
                    inv = 1.0 / total
                    for e, block in zip(exps, [ctx] + others):
                        v = k_v(block, i, e.shape[1])
                        result = result + nn((e * inv).astype(BF), jnp.where(mark, v, 0))
                total_ref[rows] = stats
                flat_ref[rows, pl.ds(pl.multiple_of(i * 128, 128), 128)] = result.astype(BF)
            return carry

        def k_v(block, i, width):
            return v_ref[block, i, 0:width]

        lax.fori_loop(0, pairs, pair, 0)

    total_ref[...] = jnp.zeros_like(total_ref)
    if ctx_n == 1:
        attend(0)
    else:
        for peer, step, rows_copy, seg_copy in copies:
            @pl.when(from_earlier(step))
            def _(step=step, rows_copy=rows_copy, seg_copy=seg_copy):
                rows_copy.wait_recv()
                seg_copy.wait_recv()
                block = lax.rem(ctx - step + ctx_n, ctx_n)
                project(x_all[block], block, 1)

        @pl.when(ctx == 0)
        def _():
            if ctx_n == 2:
                attend(0)
            else:
                attend(ctx_n - 1)

        @pl.when(ctx > 0)
        def _():
            attend(ctx_n - 1)

        for peer, step, rows_copy, seg_copy in copies:
            @pl.when(to_later(peer))
            def _(rows_copy=rows_copy, seg_copy=seg_copy):
                seg_copy.wait_send()
                rows_copy.wait_send()

    rank_out = nt(flat_ref[...], down).astype(BF)
    rank_out_ref[...] = rank_out
    part = jnp.where(column == 3, ADAPT_SCALE * rank_out.astype(F32), 0.0).astype(BF)

    def out_chunk(i, carry):
        cols = pl.ds(pl.multiple_of(i * 256, 256), 256)
        mid_ref[:, cols] = (
            x_ref[:, cols].astype(F32)
            + nn(flat_ref[...], w_out_ref[:, cols])
            + nn(part, up_ref[adapter, :, cols])
        )
        return carry

    lax.fori_loop(0, model // 256, out_chunk, 0)
    gain_two = gain_two_ref[...].astype(F32)
    step_rows = 128

    def norm_rows(i, carry):
        rows = pl.ds(pl.multiple_of(i * step_rows, step_rows), step_rows)
        mid = mid_ref[rows]
        inv = lax.rsqrt(jnp.mean(mid * mid, -1, keepdims=True) + EPSILON)
        rows_ref[rows] = (mid * inv * gain_two).astype(BF)
        return carry

    lax.fori_loop(0, tok // step_rows, norm_rows, 0)
    logits_ref[...] = nt(rows_ref[...], router_ref[...]) + mixed_ref[...]
    for copy in dy_copies:
        copy.wait_send()
    for peer in others:
        remote(
            sent_dy.at[0], arrived_dy.at[peer // 2, :, lax.rem(peer, 2)], dy_send.at[0], dy_recv.at[peer], "expert", peer
        ).wait_recv()


def attention_forward(hidden, segments, mixed, ids, gain_one, w_qkv, w_out, down, up, gain_two, router, dy, routes, experts):
    ctx_n, exp_n = lax.axis_size("context"), lax.axis_size("expert")
    tok, model = hidden.shape
    pairs = model // 128
    wide = down.shape[1]
    cos_table, sin_table = rope_tables(ctx_n * tok, 64)
    vmem = pl.BlockSpec(memory_space=pltpu.VMEM)
    dma = pltpu.SemaphoreType.DMA
    many = max(ctx_n - 1, 1)
    shape = jax.ShapeDtypeStruct
    return pl.pallas_call(
        functools.partial(attention_kernel, (ctx_n, exp_n, wide // 4)),
        out_shape=(
            shape((pairs, tok, 128), BF),
            shape((ctx_n, pairs, tok, 128), BF),
            shape((ctx_n, pairs, tok, 128), BF),
            shape((ctx_n, tok, model), BF),
            shape((ctx_n, tok, wide), BF),
            shape((tok, 128), F32),
            shape((tok, model), BF),
            shape((tok, wide), BF),
            shape((tok, model), F32),
            shape((tok, model), BF),
            shape((tok, 128), F32),
            shape((ctx_n, 8, tok), jnp.int32),
            shape((exp_n // 2, experts, 2, tok // 4, model), BF),
            shape((8, tok), F32),
        ),
        in_specs=[pl.BlockSpec(memory_space=pltpu.SMEM)] + [vmem] * 14,
        out_specs=(vmem,) * 14,
        scratch_shapes=[
            pltpu.VMEM((ctx_n, tok, model), BF),
            pltpu.VMEM((ctx_n, tok, tok), BF if ctx_n > 2 else F32),
            pltpu.VMEM((exp_n - 1, experts, tok // 4, model), BF),
            dma((many,)), dma((many,)), dma((many,)), dma((many,)), dma((exp_n - 1,)), dma((exp_n,)),
        ],
        compiler_params=pltpu.CompilerParams(
            collective_id=2, has_side_effects=True, vmem_limit_bytes=VLIMIT
        ),
        name="attention_forward",
    )(
        ids, hidden, segments, mixed, gain_one.reshape(1, model), w_qkv, w_out, down, up,
        gain_two.reshape(1, model), router, jnp.asarray(cos_table), jnp.asarray(sin_table), dy, routes,
    )


def put_tiles(tiles_ref, first, value):
    for col in range(value.shape[1] // 128):
        tiles_ref[first + col] = value[:, col * 128 : col * 128 + 128].astype(tiles_ref.dtype)


def backward_kernel(
    sizes, ids_ref, d_mid_ref, q_ref, k_ref, v_ref, normed_ref, rank_ref, total_ref, flat_ref,
    rank_out_ref, x_ref, seg_all, gain_one_ref, w_qkv_ref, w_out_ref, down_ref, up_ref, cos_ref,
    sin_ref,
    grad_ref, tiles_ref, *scratch,
):
    ctx_n, exp_n, rank = sizes
    (
        recv_buf, do_ref, bias_ref, dk_acc, dv_acc, dq_all, dkv_all, send_buf, grad_up, grad_down,
        normed_buf, send_sem, recv_sem, load_sem,
    ) = scratch
    ctx = lax.axis_index("context")
    sequence = lax.axis_index("dp") * exp_n + lax.axis_index("expert")
    tok, model = x_ref.shape
    pairs, head_dim = model // 128, 64
    entered = greet([("context", ctx_n)])
    order = [ctx] + blocks_of(ctx_n, ctx, ctx_n - 1)

    def fetch(j):
        return pltpu.make_async_copy(
            normed_ref.at[order[j]], normed_buf.at[min(j, 1)], load_sem.at[min(j, 1)]
        )

    fetch(0).start()
    if ctx_n > 1:
        fetch(1).start()
    adapter = ids_ref[sequence]
    down = down_ref[adapter]
    up = up_ref[adapter]
    wide = down.shape[0]
    column = lax.broadcasted_iota(jnp.int32, (tok, wide), 1) // rank
    d_branch = d_mid_ref[...].astype(BF)
    d_rank_out = jnp.where(column == 3, ADAPT_SCALE * nt(d_branch, up), 0.0).astype(BF)
    twice_out = jnp.where(column == 3, ADAPT_SCALE * rank_out_ref[...].astype(F32), 0.0).astype(BF)
    grad_up[...] = tn(twice_out, d_branch)
    grad_down[...] = tn(d_rank_out, flat_ref[...])

    def attn_chunk(i, carry):
        rows = pl.ds(pl.multiple_of(i * 256, 256), 256)
        d_attn = nt(d_branch, w_out_ref[rows, :]) + nn(d_rank_out, down_ref[adapter, :, rows])
        do_ref[2 * i] = d_attn[:, :128].astype(BF)
        do_ref[2 * i + 1] = d_attn[:, 128:].astype(BF)
        return carry

    lax.fori_loop(0, model // 256, attn_chunk, 0)
    lane = lax.broadcasted_iota(jnp.int32, (1, 128), 1)
    marks = [(lane < 64), (lane >= 64)]
    half_rows = tok // 2

    def attend(count):
        fill_bias(bias_ref, seg_all, ctx_n, ctx, tok, count)
        others = blocks_of(ctx_n, ctx, count)

        def pair(i, carry):
            cols = pl.ds(pl.multiple_of(i * 128, 128), 128)
            for half in (1, 0):
                rows = slice(half * half_rows, (half + 1) * half_rows)
                own_width = (half + 1) * half_rows
                q = q_ref[i, rows]
                d_out = do_ref[i, rows]
                stats = total_ref[rows]
                d_query = jnp.zeros((half_rows, 128), F32)
                for head in range(2):
                    mark = marks[head]
                    q_head = jnp.where(mark, q, 0)
                    do_head = jnp.where(mark, d_out, 0)
                    total = jnp.sum(
                        jnp.where(lane == 2 * i + head, stats, 0.0), -1, keepdims=True
                    )
                    parts = []
                    delta = jnp.zeros((half_rows, 1), F32)
                    for j, block in enumerate([ctx] + others):
                        width = own_width if j == 0 else tok
                        probs = jnp.exp(
                            nt(q_head, k_ref[block, i, 0:width])
                            + bias_ref[j, rows, 0:width]
                            - total
                        )
                        d_probs = nt(do_head, v_ref[block, i, 0:width])
                        delta = delta + jnp.sum(probs * d_probs, -1, keepdims=True)
                        parts.append((probs, d_probs))
                    for j, block in enumerate([ctx] + others):
                        width = own_width if j == 0 else tok
                        probs, d_probs = parts[j]
                        d_scores = (probs * (d_probs - delta)).astype(BF)
                        k_head = jnp.where(mark, k_ref[block, i, 0:width], 0)
                        d_query = d_query + nn(d_scores, k_head)
                        d_key = tn(q_head, d_scores)
                        d_value = tn(do_head, probs.astype(BF))
                        if half == 1 and head == 0:
                            dk_acc[j, :, 0:width] = d_key
                            dv_acc[j, :, 0:width] = d_value
                        else:
                            dk_acc[j, :, 0:width] += d_key
                            dv_acc[j, :, 0:width] += d_value
                start = pl.multiple_of(ctx * tok + half * half_rows, half_rows)
                d_query = d_query * head_dim ** (-0.5)
                dq_all[rows, cols] = turn(
                    d_query, cos_ref[pl.ds(start, half_rows)], -sin_ref[pl.ds(start, half_rows)], head_dim
                ).astype(BF)
            for j, block in enumerate([ctx] + others):
                start = pl.multiple_of(block * tok, tok)
                d_key = turn(
                    jnp.transpose(dk_acc[j]), cos_ref[pl.ds(start, tok)], -sin_ref[pl.ds(start, tok)], head_dim
                )
                dkv_all[j, 0, :, cols] = d_key.astype(BF)
                dkv_all[j, 1, :, cols] = jnp.transpose(dv_acc[j]).astype(BF)
            return carry

        lax.fori_loop(0, pairs, pair, 0)

    def fold(j, block, first, write):
        normed = normed_buf[min(j, 1)]
        ranks = rank_ref[block].astype(F32)
        d_ranks = jnp.zeros((tok, wide), F32)
        for p in range(first, 3):
            d_proj = dq_all[...] if p == 0 else dkv_all[j, p - 1]
            twice = jnp.where(column == p, ADAPT_SCALE * ranks, 0.0).astype(BF)
            grad_up[...] += tn(twice, d_proj)
            d_ranks = d_ranks + jnp.where(column == p, ADAPT_SCALE * nt(d_proj, up), 0.0)
        d_ranks = d_ranks.astype(BF)
        grad_down[...] += tn(d_ranks, normed)

        def chunk(i, carry):
            rows = pl.ds(pl.multiple_of(i * 256, 256), 256)
            value = nn(d_ranks, down_ref[adapter, :, rows])
            for p in range(first, 3):
                d_proj = dq_all[...] if p == 0 else dkv_all[j, p - 1]
                value = value + nt(d_proj, w_qkv_ref[rows, p * model : (p + 1) * model])
            write(rows, value)
            return carry

        lax.fori_loop(0, model // 256, chunk, 0)

    def write_own(cols, value):
        grad_ref[:, cols] = value

    copies = []
    for step in range(1, ctx_n):
        peer = lax.rem(ctx + step, ctx_n)
        copies.append(
            remote(send_buf, recv_buf.at[step - 1], send_sem.at[step - 1], recv_sem.at[step - 1], "context", peer)
        )

    if ctx_n == 1:
        attend(0)
    elif ctx_n == 2:
        entered()

        @pl.when(ctx == 0)
        def _():
            attend(0)
    else:
        entered()

    def spread():
        attend(ctx_n - 1)
        for j, block in enumerate(blocks_of(ctx_n, ctx, ctx_n - 1)):
            def write(cols, value):
                send_buf[:, cols] = value.astype(BF)

            fetch(j + 1).wait()
            if j > 0:
                copies[j - 1].wait_send()
            fold(j + 1, block, 1, write)
            copies[j].start()
            if j + 2 < ctx_n:
                fetch(j + 2).start()

    if ctx_n == 2:
        pl.when(ctx == 1)(spread)
        pl.when(ctx == 0)(fetch(1).wait)
    elif ctx_n > 2:
        spread()
    fetch(0).wait()
    fold(0, ctx, 0, write_own)
    if ctx_n == 2:
        @pl.when(ctx == 0)
        def _():
            copies[0].wait_recv()

        @pl.when(ctx == 1)
        def _():
            recv_buf[...] = jnp.zeros_like(recv_buf)
    elif ctx_n > 2:
        copies[-1].wait_send()
        for step, item in enumerate(copies):
            item.wait_recv()
            load = pltpu.make_async_copy(recv_buf.at[step], send_buf, load_sem.at[0])
            load.start()
            load.wait()
            grad_ref[...] += send_buf[...].astype(F32)
    gain_one = gain_one_ref[...].astype(F32)

    def finish(i, carry):
        rows = pl.ds(pl.multiple_of(i * 128, 128), 128)
        value = grad_ref[rows]
        if ctx_n == 2:
            value = value + recv_buf[0, rows].astype(F32)
        x = x_ref[rows].astype(F32)
        inv = lax.rsqrt(jnp.mean(x * x, -1, keepdims=True) + EPSILON)
        scaled = value * gain_one
        grad_ref[rows] = (
            d_mid_ref[rows]
            + inv * scaled
            - x * (inv * inv * inv) * jnp.mean(scaled * x, -1, keepdims=True)
        )
        return carry

    lax.fori_loop(0, tok // 128, finish, 0)
    per = model // 128
    for p in range(4):
        put_tiles(tiles_ref, p * per, grad_down[p * rank : (p + 1) * rank])
        put_tiles(tiles_ref, (4 + p) * per, grad_up[p * rank : (p + 1) * rank])
    if ctx_n == 2:
        @pl.when(ctx == 1)
        def _():
            copies[0].wait_send()


def attention_backward(d_mid, saved, hidden, ids, gain_one, w_qkv, w_out, down, up):
    ctx_n, exp_n = lax.axis_size("context"), lax.axis_size("expert")
    tok, model = hidden.shape
    pairs = model // 128
    wide = down.shape[1]
    cos_table, sin_table = rope_tables(ctx_n * tok, 64)
    vmem = pl.BlockSpec(memory_space=pltpu.VMEM)
    dma = pltpu.SemaphoreType.DMA
    many = max(ctx_n - 1, 1)
    shape = jax.ShapeDtypeStruct
    q, k, v, normed, ranks, totals, flat, rank_out, seg_all = saved
    in_specs = [vmem] * 18
    in_specs[4] = pl.BlockSpec(memory_space=pl.ANY)
    spill = ctx_n > 2
    landing = ((many, tok, model), BF)
    results = pl.pallas_call(
        functools.partial(backward_kernel, (ctx_n, exp_n, wide // 4)),
        out_shape=(shape((tok, model), F32), shape((8 * pairs, 16, 128), BF))
        + ((shape(*landing),) if spill else ()),
        in_specs=[pl.BlockSpec(memory_space=pltpu.SMEM)] + in_specs,
        out_specs=(vmem,) * 2 + ((pl.BlockSpec(memory_space=pl.ANY),) if spill else ()),
        scratch_shapes=([] if spill else [pltpu.VMEM(*landing)])
        + [
            pltpu.VMEM((pairs, tok, 128), BF),
            pltpu.VMEM((ctx_n, tok, tok), BF if spill else F32),
            pltpu.VMEM((ctx_n, 128, tok), F32),
            pltpu.VMEM((ctx_n, 128, tok), F32),
            pltpu.VMEM((tok, model), BF),
            pltpu.VMEM((ctx_n, 2, tok, model), BF),
            pltpu.VMEM((tok, model), BF),
            pltpu.VMEM((wide, model), F32),
            pltpu.VMEM((wide, model), F32),
            pltpu.VMEM((min(ctx_n, 2), tok, model), BF),
            dma((many,)), dma((many,)), dma((2,)),
        ],
        compiler_params=pltpu.CompilerParams(
            collective_id=3, has_side_effects=True, vmem_limit_bytes=VLIMIT + 5 * 2**19
        ),
        name="attention_backward",
    )(
        ids, d_mid, q, k, v, normed, ranks, totals, flat, rank_out, hidden, seg_all,
        gain_one.reshape(1, model), w_qkv, w_out, down, up, jnp.asarray(cos_table),
        jnp.asarray(sin_table),
    )
    return results[:2]


def partners(exp_n, me):
    core = lax.rem(me, 2)
    twin = me + 1 - 2 * core
    far = []
    for step in range(2, exp_n, 2):
        far += [lax.rem(me + step, exp_n), lax.rem(twin + step, exp_n)]
    return far + [twin]


def hot_rows(slot_rows, first, count):
    target = first + lax.broadcasted_iota(jnp.int32, (count, slot_rows.shape[1]), 0)
    return target == slot_rows


def moe_kernel(
    sizes, ids_ref, rows_ref, mid_ref, logits_ref, slots_ref, dy_ref, arrived_dy, gain_ref, router_ref,
    vec_ref, gate_up_hbm, down_hbm, in_down_ref, in_up_ref, out_down_ref, out_up_ref,
    hidden_ref, d_mid_ref, d_logits_ref, tiles_ref,
    gate_up_ref, w_down_ref, sent_rows, sent_gates, arrived_rows, arrived_gates, act_ref, d_pre_ref,
    done_out, done_rows, back_out, back_rows, cols_ref, gates_ref,
    weight_sem, row_send, row_recv, gate_send, gate_recv, out_send, out_recv, in_send, in_recv,
):
    exp_n, kinds, rank = sizes
    me = lax.axis_index("expert")
    my_chip, my_core = me // 2, lax.rem(me, 2)
    first_seq = lax.axis_index("dp") * exp_n
    tok, model = rows_ref.shape
    experts, width = w_down_ref.shape[:2]
    capacity = arrived_rows.shape[3]
    per_owner = experts * capacity
    both = 2 * capacity
    entered = greet([("expert", exp_n)])
    loads = []
    for e in range(experts):
        for hbm, ref, k in ((gate_up_hbm, gate_up_ref, 0), (down_hbm, w_down_ref, 1)):
            load = pltpu.make_async_copy(hbm.at[e], ref.at[e], weight_sem.at[e, k])
            load.start()
            loads.append(load)

    lane = lax.broadcasted_iota(jnp.int32, (tok, 128), 1)
    logits = logits_ref[...]
    masked = jnp.where(lane < kinds, logits, NEG)
    exps = jnp.exp(masked - jnp.max(masked, -1, keepdims=True))
    probs = exps / jnp.sum(exps, -1, keepdims=True)
    slot_cols = jnp.transpose(
        jnp.concatenate([slots_ref[...], jnp.zeros((120, tok), F32)], 0)
    )
    cols_ref[...] = slot_cols
    gates = [
        jnp.sum(jnp.where(lane == slot_cols[:, k : k + 1].astype(jnp.int32), probs, 0.0), -1, keepdims=True)
        for k in range(2)
    ]
    gates_ref[...] = jnp.where(lane == 0, gates[0], jnp.where(lane == 1, gates[1], 0.0))
    gate_rows = jnp.transpose(gates_ref[...])
    parts = []
    sub = lax.broadcasted_iota(jnp.int32, (16, tok), 0)
    for k in range(2):
        whole = jnp.broadcast_to(gate_rows[k : k + 1], (16, tok))
        high = whole.astype(BF).astype(F32)
        middle = (whole - high).astype(BF).astype(F32)
        lowest = whole - high - middle
        parts.append(
            jnp.where(sub == 0, high, jnp.where(sub == 1, middle, jnp.where(sub == 2, lowest, 0.0))).astype(BF)
        )
    slot_rows = [slots_ref[2 + k : 3 + k].astype(jnp.int32) for k in range(2)]

    def pick(owner, rows_to, gates_to):
        hots = [hot_rows(slot_rows[k], owner * per_owner, per_owner) for k in range(2)]
        hot = jnp.where(hots[0] | hots[1], 1.0, 0.0).astype(BF)
        rows_to(nn(hot, rows_ref[...]).astype(BF))
        gates_to(
            sum(nt(parts[k], jnp.where(hots[k], 1.0, 0.0).astype(BF)) for k in range(2)).astype(BF)
        )

    entered()
    sends = []
    others = partners(exp_n, me)
    for i, peer in enumerate(others):
        def rows_to(value, i=i):
            for e in range(experts):
                sent_rows[i, e] = value[e * capacity : (e + 1) * capacity]

        def gates_to(value, i=i):
            for e in range(experts):
                sent_gates[i, e] = value[:, e * capacity : (e + 1) * capacity]

        pick(peer, rows_to, gates_to)
        for src, dst, send, recv in (
            (sent_gates, arrived_gates, gate_send, gate_recv),
            (sent_rows, arrived_rows, row_send, row_recv),
        ):
            copy = remote(
                src.at[i], dst.at[my_chip, :, my_core], send.at[i], recv.at[me], "expert", peer
            )
            copy.start()
            sends.append(copy)

    def own_rows(value):
        for e in range(experts):
            arrived_rows[my_chip, e, my_core] = value[e * capacity : (e + 1) * capacity]

    def own_gates(value):
        for e in range(experts):
            arrived_gates[my_chip, e, my_core] = value[:, e * capacity : (e + 1) * capacity]

    pick(me, own_rows, own_gates)

    def arrive(source):
        for ref, src, send, recv in (
            (arrived_gates, sent_gates, gate_send, gate_recv),
            (arrived_rows, sent_rows, row_send, row_recv),
        ):
            remote(
                src.at[0], ref.at[source // 2, :, lax.rem(source, 2)], send.at[0], recv.at[source],
                "expert", source,
            ).wait_recv()

    row64 = lax.broadcasted_iota(jnp.int32, (both, 4 * rank), 0) // capacity
    col64 = lax.broadcasted_iota(jnp.int32, (both, 4 * rank), 1)
    mine64 = row64 == col64 // (2 * rank)
    is_gate = col64 % (2 * rank) < rank
    mine32 = lax.broadcasted_iota(jnp.int32, (both, 2 * rank), 0) // capacity == (
        lax.broadcasted_iota(jnp.int32, (both, 2 * rank), 1) // rank
    )
    step_cols = 512
    per_step = step_cols // 128
    across, deep = model // 128, width // 128
    first_up = 2 * across
    first_out = first_up + 2 * deep
    first_last = first_out + deep
    per_expert = first_last + across

    def work(chip, e):
        names = [ids_ref[first_seq + 2 * chip + core] for core in range(2)]

        def stack(ref, cols=slice(None)):
            return jnp.concatenate([ref[name, e, :, cols] for name in names], 0)

        rows = arrived_rows[chip, e].reshape(both, model)
        in_down = stack(in_down_ref)
        out_up = stack(out_up_ref)
        gate = []
        for core in range(2):
            piece = arrived_gates[chip, e, core].astype(F32)
            total = piece[0:1] + piece[1:2] + piece[2:3]
            gate.append(jnp.transpose(jnp.broadcast_to(total, (128, capacity)))[:, 0:1])
        gate = jnp.concatenate(gate, 0)
        d_out = (gate * arrived_dy[chip, e].reshape(both, model).astype(F32)).astype(BF)
        ranks = jnp.where(mine64, nt(rows, in_down), 0.0).astype(BF)
        twice = ADAPT_SCALE * ranks.astype(F32)
        twice_gate = jnp.where(is_gate, twice, 0.0).astype(BF)
        twice_up = jnp.where(is_gate, 0.0, twice).astype(BF)
        d_mid_rank = jnp.where(mine32, ADAPT_SCALE * nt(d_out, out_up), 0.0).astype(BF)

        def chunk(i, carry):
            rank_mid, d_rank = carry
            start = pl.multiple_of(i * step_cols, step_cols)
            cols = pl.ds(start, step_cols)
            up_cols = pl.ds(pl.multiple_of(width + i * step_cols, step_cols), step_cols)
            in_up = stack(in_up_ref, cols)
            out_down = stack(out_down_ref, cols)
            gate_pre = nn(rows, gate_up_ref[e, :, cols]) + nn(twice_gate, in_up)
            up_pre = nn(rows, gate_up_ref[e, :, up_cols]) + nn(twice_up, in_up)
            d_act = (nt(d_out, w_down_ref[e, cols, :]) + nn(d_mid_rank, out_down)).astype(BF).astype(F32)
            sigma = 1.0 / (1.0 + jnp.exp(-gate_pre))
            silu = gate_pre * sigma
            act = (silu * up_pre).astype(BF)
            d_gate = (d_act * up_pre * sigma * (1.0 + gate_pre * (1.0 - sigma))).astype(BF)
            d_up = (d_act * silu).astype(BF)
            act_ref[:, cols] = act
            d_pre_ref[:, cols] = d_gate
            d_pre_ref[:, up_cols] = d_up
            rank_mid = rank_mid + nt(act, out_down)
            d_rank = d_rank + jnp.where(is_gate, nt(d_gate, in_up), nt(d_up, in_up))
            grad_up = (tn(twice_gate, d_gate) + tn(twice_up, d_up)).astype(BF)
            grad_out = tn(d_mid_rank, act).astype(BF)
            for core in range(2):
                for t in range(per_step):
                    here = slice(t * 128, t * 128 + 128)
                    tile = i * per_step + t
                    for which in range(2):
                        first = (2 * core + which) * rank
                        tiles_ref[2 * chip + core, e * per_expert + first_up + which * deep + tile] = (
                            grad_up[first : first + rank, here]
                        )
                    tiles_ref[2 * chip + core, e * per_expert + first_out + tile] = (
                        grad_out[core * rank : (core + 1) * rank, here]
                    )
            return rank_mid, d_rank

        rank_mid, d_rank = lax.fori_loop(
            0, width // step_cols, chunk,
            (jnp.zeros((both, 2 * rank), F32), jnp.zeros((both, 4 * rank), F32)),
        )
        twice_mid = jnp.where(
            mine32, ADAPT_SCALE * rank_mid.astype(BF).astype(F32), 0.0
        ).astype(BF)

        def out_chunk(i, carry):
            cols = pl.ds(pl.multiple_of(i * 256, 256), 256)
            value = nn(act_ref[...], w_down_ref[e, :, cols]) + nn(twice_mid, stack(out_up_ref, cols))
            for core in range(2):
                done_out[chip, e, core, :, cols] = value[core * capacity : (core + 1) * capacity].astype(BF)
            return carry

        lax.fori_loop(0, model // 256, out_chunk, 0)
        give_back(chip, e, done_out, back_out, out_send, out_recv)
        d_rank_in = jnp.where(mine64, ADAPT_SCALE * d_rank, 0.0).astype(BF)

        def in_chunk(i, carry):
            cols = pl.ds(pl.multiple_of(i * 256, 256), 256)
            value = nt(d_pre_ref[...], gate_up_ref[e, cols, :]) + nn(d_rank_in, stack(in_down_ref, cols))
            for core in range(2):
                done_rows[chip, e, core, :, cols] = value[core * capacity : (core + 1) * capacity].astype(BF)
            return carry

        lax.fori_loop(0, model // 256, in_chunk, 0)
        give_back(chip, e, done_rows, back_rows, in_send, in_recv)
        grad_last = tn(twice_mid, d_out).astype(BF)
        grad_first = tn(d_rank_in, rows).astype(BF)
        for core in range(2):
            for t in range(across):
                here = slice(t * 128, t * 128 + 128)
                for which in range(2):
                    first = (2 * core + which) * rank
                    tiles_ref[2 * chip + core, e * per_expert + which * across + t] = (
                        grad_first[first : first + rank, here]
                    )
                tiles_ref[2 * chip + core, e * per_expert + first_last + t] = (
                    grad_last[core * rank : (core + 1) * rank, here]
                )

    def give_back(chip, e, done, back, send, recv):
        for core in range(2):
            target = 2 * chip + core
            copy = remote(
                done.at[chip, e, core], back.at[me * experts + e], send.at[target, e], recv.at[me, e],
                "expert", target,
            )

            @pl.when(target == me)
            def _(core=core):
                back[me * experts + e] = done[chip, e, core]

            @pl.when(target != me)
            def _(copy=copy):
                copy.start()

    for load in loads[:2]:
        load.wait()
    arrive(others[-1])
    work(my_chip, 0)
    far_chips = [lax.rem(my_chip + step, exp_n // 2) for step in range(1, exp_n // 2)]
    for load in loads[2:]:
        load.wait()
    for i, chip in enumerate(far_chips):
        arrive(others[2 * i])
        arrive(others[2 * i + 1])
        for e in range(experts):
            work(chip, e)
    for e in range(1, experts):
        work(my_chip, e)

    def collect(done, back, send, recv):
        for owner in others:
            for e in range(experts):
                remote(
                    done.at[0, e, 0], back.at[owner * experts + e], send.at[owner, e], recv.at[owner, e],
                    "expert", owner,
                ).wait_recv()

    slots_total = exp_n * per_owner
    block = 256

    def hot_cols(rows):
        target = lax.broadcasted_iota(jnp.int32, (block, slots_total), 1)
        return [target == cols_ref[rows, 2 + k : 3 + k].astype(jnp.int32) for k in range(2)]

    gain = gain_ref[...].astype(F32)
    lanes = lax.broadcasted_iota(jnp.int32, (block, 128), 1)
    ffn_kinds = exp_n * experts

    def outward(i, carry):
        rows = pl.ds(pl.multiple_of(i * block, block), block)
        hots = hot_cols(rows)
        table = back_out[...].reshape(slots_total, model)
        mid = mid_ref[rows]
        dy = dy_ref[rows].astype(F32)
        normed = mid * lax.rsqrt(jnp.mean(mid * mid, -1, keepdims=True) + EPSILON) * gain
        logits = logits_ref[rows]
        masked = jnp.where(lanes < kinds, logits, NEG)
        exps = jnp.exp(masked - jnp.max(masked, -1, keepdims=True))
        probs = exps / jnp.sum(exps, -1, keepdims=True)
        pairs = []
        for c in range(2):
            one, two = logits[:, kinds + 2 * c : kinds + 2 * c + 1], logits[:, kinds + 2 * c + 1 : kinds + 2 * c + 2]
            pairs.append((1.0 / (1.0 + jnp.exp(two - one)), 1.0 / (1.0 + jnp.exp(one - two))))
        total = mid
        d_kinds = jnp.zeros((block, 128), F32)
        dy_scale = jnp.zeros((block, 1), F32)
        weights = [jnp.zeros((block, 1), F32)] * 2
        for k in range(2):
            kind = cols_ref[rows, k : k + 1].astype(jnp.int32)
            gate = gates_ref[rows, k : k + 1]
            scale = jnp.where(kind == ffn_kinds + 1, 1.0, 0.0)
            term = nn(jnp.where(hots[k], 1.0, 0.0).astype(BF), table)
            for c in range(2):
                here = jnp.where(kind == ffn_kinds + 2 + c, 1.0, 0.0)
                scale = scale + here * pairs[c][0]
                term = term + (here * pairs[c][1]) * vec_ref[c : c + 1].astype(F32)
                weights[c] = weights[c] + here * gate
            term = term + scale * normed
            dy_scale = dy_scale + gate * scale
            total = total + gate * term
            d_gate = jnp.sum(dy * term, -1, keepdims=True)
            d_kinds = d_kinds + jnp.where(lanes == kind, d_gate, 0.0)
        hidden_ref[rows] = total.astype(BF)
        d_logits = probs * (d_kinds - jnp.sum(probs * d_kinds, -1, keepdims=True))
        along = jnp.sum(dy * normed, -1, keepdims=True)
        for c in range(2):
            d_one = weights[c] * along
            d_two = weights[c] * jnp.sum(dy * vec_ref[c : c + 1].astype(F32), -1, keepdims=True)
            mean = pairs[c][0] * d_one + pairs[c][1] * d_two
            d_logits = jnp.where(lanes == kinds + 2 * c, pairs[c][0] * (d_one - mean), d_logits)
            d_logits = jnp.where(lanes == kinds + 2 * c + 1, pairs[c][1] * (d_two - mean), d_logits)
        d_logits_ref[rows] = d_logits
        high = d_logits.astype(BF)
        rest = d_logits - high.astype(F32)
        middle = rest.astype(BF)
        lowest = (rest - middle.astype(F32)).astype(BF)
        router = router_ref[...]
        d_mid_ref[rows] = dy_scale * dy + (nn(high, router) + nn(middle, router) + nn(lowest, router))
        return carry

    def inward(i, carry):
        rows = pl.ds(pl.multiple_of(i * block, block), block)
        hots = hot_cols(rows)
        table = back_rows[...].reshape(slots_total, model)
        hot = jnp.where(hots[0] | hots[1], 1.0, 0.0).astype(BF)
        scaled = (d_mid_ref[rows] + nn(hot, table)) * gain
        mid = mid_ref[rows]
        inv = lax.rsqrt(jnp.mean(mid * mid, -1, keepdims=True) + EPSILON)
        d_mid_ref[rows] = (
            dy_ref[rows].astype(F32)
            + inv * scaled
            - mid * (inv * inv * inv) * jnp.mean(scaled * mid, -1, keepdims=True)
        )
        return carry

    collect(done_out, back_out, out_send, out_recv)
    lax.fori_loop(0, tok // block, outward, 0)
    collect(done_rows, back_rows, in_send, in_recv)
    lax.fori_loop(0, tok // block, inward, 0)
    for copy in sends:
        copy.wait_send()
    for target in others:
        for e in range(experts):
            for done, back, send, recv in (
                (done_out, back_out, out_send, out_recv),
                (done_rows, back_rows, in_send, in_recv),
            ):
                remote(
                    done.at[0, e, 0], back.at[0], send.at[target, e], recv.at[target, e],
                    "expert", target,
                ).wait_send()


def expert_layer(rows, mid, logits, slots, dy, arrived_dy, ids, gain, router, vec, w_gate_up, w_down, tables, kinds):
    exp_n = lax.axis_size("expert")
    tok, model = rows.shape
    experts, width = w_down.shape[:2]
    capacity = tok // 4
    rank = tables[3].shape[2]
    tiles = experts * (3 * model // 128 + 3 * width // 128)
    chips = exp_n // 2
    vmem = pl.BlockSpec(memory_space=pltpu.VMEM)
    hbm = pl.BlockSpec(memory_space=pl.ANY)
    dma = pltpu.SemaphoreType.DMA
    shape = jax.ShapeDtypeStruct
    block = (experts, capacity, model)
    return pl.pallas_call(
        functools.partial(moe_kernel, (exp_n, kinds, rank)),
        out_shape=(
            shape((tok, model), BF),
            shape((tok, model), F32),
            shape((tok, 128), F32),
            shape((exp_n, tiles, 16, 128), BF),
        ),
        in_specs=[pl.BlockSpec(memory_space=pltpu.SMEM)] + [vmem] * 9 + [hbm] * 2 + [vmem] * 4,
        out_specs=(vmem,) * 4,
        scratch_shapes=[
            pltpu.VMEM((experts, model, 2 * width), BF),
            pltpu.VMEM((experts, width, model), BF),
            pltpu.VMEM((exp_n - 1,) + block, BF),
            pltpu.VMEM((exp_n - 1, experts, 16, capacity), BF),
            pltpu.VMEM((chips, experts, 2, capacity, model), BF),
            pltpu.VMEM((chips, experts, 2, 16, capacity), BF),
            pltpu.VMEM((2 * capacity, width), BF),
            pltpu.VMEM((2 * capacity, 2 * width), BF),
            pltpu.VMEM((chips, experts, 2, capacity, model), BF),
            pltpu.VMEM((chips, experts, 2, capacity, model), BF),
            pltpu.VMEM((exp_n * experts, capacity, model), BF),
            pltpu.VMEM((exp_n * experts, capacity, model), BF),
            pltpu.VMEM((tok, 128), F32),
            pltpu.VMEM((tok, 128), F32),
            dma((experts, 2)), dma((exp_n - 1,)), dma((exp_n,)), dma((exp_n - 1,)), dma((exp_n,)),
            dma((exp_n, experts)), dma((exp_n, experts)), dma((exp_n, experts)), dma((exp_n, experts)),
        ],
        compiler_params=pltpu.CompilerParams(
            collective_id=4, has_side_effects=True, vmem_limit_bytes=VLIMIT
        ),
        name="expert_layer",
    )(
        ids, rows, mid, logits, slots, dy, arrived_dy, gain.reshape(1, model), router, vec, w_gate_up,
        w_down, *tables,
    )


def reduce_kernel(
    sizes, ids_ref, grads_ref, attn_ref, table_ref, attn_table_ref,
    held, arrived_x, part_z, arrived_z,
    load_sem, ready_send, ready_recv, x_send, x_recv, z_send, z_recv, az_send, az_recv,
    ax_send, ax_recv, e_send, e_recv,
):
    ctx_n, dp_n, exp_n, adapters, tiles, attn_tiles, x_tiles, z_tiles = sizes
    own_attn = attn_tiles // exp_n
    ctx, dp, exp = lax.axis_index("context"), lax.axis_index("dp"), lax.axis_index("expert")
    barrier = pltpu.get_barrier_semaphore()
    for axis, size, index in (("context", ctx_n, ctx), ("dp", dp_n, dp), ("expert", exp_n, exp)):
        for step in range(1, size):
            pl.semaphore_signal(
                barrier, inc=1, device_id={axis: lax.rem(index + step, size)}, device_id_type=MESH
            )
    load = pltpu.make_async_copy(grads_ref, held.at[:, pl.ds(0, tiles)], load_sem)
    load.start()
    keep = pltpu.make_async_copy(
        attn_ref.at[pl.ds(exp * own_attn, own_attn)],
        held.at[exp, pl.ds(tiles, own_attn)],
        ready_send.at[exp_n - 1],
    )
    keep.start()
    pl.semaphore_wait(barrier, ctx_n + dp_n + exp_n - 3)

    def copy(src, dst, send, recv, axis, target):
        return pltpu.make_async_remote_copy(
            src_ref=src, dst_ref=dst, send_sem=send, recv_sem=recv,
            device_id={axis: target}, device_id_type=MESH,
        )

    waits = []
    first = []
    for step in range(1, exp_n):
        peer = lax.rem(exp + step, exp_n)
        send = copy(
            attn_ref.at[pl.ds(peer * own_attn, own_attn)],
            held.at[exp, pl.ds(tiles, own_attn)],
            ready_send.at[step - 1], ready_recv.at[step - 1], "expert", peer,
        )
        send.start()
        first.append(send)
    load.wait()
    keep.wait()
    for send in first:
        send.wait()
    for k in range(1, dp_n + 1):
        part = lax.rem(dp + k, dp_n)
        for step in range(1, ctx_n):
            peer = lax.rem(ctx + step, ctx_n)
            send = copy(
                held.at[:, pl.ds(peer * x_tiles + part * z_tiles, z_tiles)],
                arrived_x.at[step - 1, k - 1],
                x_send.at[step - 1, k - 1], x_recv.at[step - 1, k - 1], "context", peer,
            )
            send.start()
            waits.append(send)
    z_sends = []
    for k in range(1, dp_n + 1):
        part = lax.rem(dp + k, dp_n)
        for step in range(1, ctx_n):
            waits[(k - 1) * (ctx_n - 1) + step - 1].wait_recv()
        base = ctx * x_tiles + part * z_tiles

        def add(tile, carry, k=k, base=base):
            total = held[:, pl.ds(base + tile, 1)].astype(F32)
            for step in range(1, ctx_n):
                total = total + arrived_x[step - 1, k - 1, :, pl.ds(tile, 1)].astype(F32)
            part_z[k - 1, :, pl.ds(tile, 1)] = total.astype(BF)
            return carry

        lax.fori_loop(0, z_tiles, add, 0)
        if k < dp_n:
            send = copy(
                part_z.at[k - 1], arrived_z.at[k - 1], z_send.at[k - 1], z_recv.at[k - 1], "dp", part
            )
            send.start()
            z_sends.append(send)
    for send in z_sends:
        send.wait_recv()

    weights = []
    for k in range(dp_n):
        origin = lax.rem(dp - k + dp_n, dp_n)
        for source in range(exp_n):
            name = ids_ref[origin * exp_n + source]
            weights.append([jnp.where(name == a, 1.0, 0.0).astype(F32) for a in range(adapters)])

    def combine(tile, carry):
        totals = [jnp.zeros((16, 128), F32)] * adapters
        for k in range(dp_n):
            for source in range(exp_n):
                ref = part_z.at[dp_n - 1] if k == 0 else arrived_z.at[k - 1]
                value = ref[source, tile].astype(F32)
                marks = weights[k * exp_n + source]
                totals = [total + mark * value for total, mark in zip(totals, marks)]
        for a in range(adapters):
            table_ref[ctx, dp, a, tile] = totals[a].astype(BF)
        return carry

    lax.fori_loop(0, z_tiles, combine, 0)
    az_sends, ax_sends = [], []
    for k in range(1, dp_n):
        send = copy(
            table_ref.at[ctx, dp], table_ref.at[ctx, dp], az_send.at[k - 1], az_recv.at[k - 1],
            "dp", lax.rem(dp + k, dp_n),
        )
        send.start()
        az_sends.append(send)
    for k in range(dp_n):
        if k > 0:
            az_sends[k - 1].wait_recv()
        origin = lax.rem(dp - k + dp_n, dp_n)
        for step in range(1, ctx_n):
            send = copy(
                table_ref.at[ctx, origin], table_ref.at[ctx, origin],
                ax_send.at[step - 1, k], ax_recv.at[step - 1, k],
                "context", lax.rem(ctx + step, ctx_n),
            )
            send.start()
            ax_sends.append(send)
    for send in ax_sends:
        send.wait_recv()
    for index in range(own_attn):
        tile = tiles + index
        where = (tile // x_tiles, (tile % x_tiles) // z_tiles, tile % x_tiles % z_tiles)
        for a in range(adapters):
            attn_table_ref[exp, index, a] = table_ref[where[0], where[1], a, where[2]]
    last = []
    for step in range(1, exp_n):
        send = copy(
            attn_table_ref.at[exp], attn_table_ref.at[exp], e_send.at[step - 1], e_recv.at[step - 1],
            "expert", lax.rem(exp + step, exp_n),
        )
        send.start()
        last.append(send)
    for send in last:
        send.wait()
    for send in waits + z_sends + az_sends + ax_sends:
        send.wait_send()


def unpack_kernel(sizes, table_ref, attn_ref, down_ref, up_ref, in_down_ref, in_up_ref, out_down_ref, out_up_ref):
    x_tiles, z_tiles, own_attn = sizes

    def tile_at(tile):
        local = tile % x_tiles
        return table_ref[tile // x_tiles, local // z_tiles, 0, local % z_tiles].astype(F32)

    tile = 0
    for expert in range(in_up_ref.shape[1]):
        for out_ref in (in_down_ref, in_up_ref, out_down_ref, out_up_ref):
            rows, cols = out_ref.shape[2:]
            for row in range(rows // 16):
                for col in range(cols // 128):
                    out_ref[0, expert, row * 16 : row * 16 + 16, col * 128 : col * 128 + 128] = tile_at(tile)
                    tile += 1
    tile = 0
    for out_ref in (down_ref, up_ref):
        rows, cols = out_ref.shape[1:]
        for row in range(rows // 16):
            for col in range(cols // 128):
                out_ref[0, row * 16 : row * 16 + 16, col * 128 : col * 128 + 128] = attn_ref[
                    tile // own_attn, tile % own_attn, 0
                ].astype(F32)
                tile += 1


def reduce_adapters(adapter_ids, packed, table_shapes, attn, attn_shape, adapters):
    ctx_n, dp_n, exp_n = (lax.axis_size(axis) for axis in ("context", "dp", "expert"))
    tiles, attn_tiles = packed.shape[1], attn.shape[0]
    own_attn = attn_tiles // exp_n
    z_tiles = pl.cdiv(tiles + own_attn, ctx_n * dp_n)
    x_tiles = z_tiles * dp_n
    sizes = (ctx_n, dp_n, exp_n, adapters, tiles, attn_tiles, x_tiles, z_tiles)
    dma = pltpu.SemaphoreType.DMA
    many = max(ctx_n - 1, 1)
    table, attn_table = pl.pallas_call(
        functools.partial(reduce_kernel, sizes),
        out_shape=(
            jax.ShapeDtypeStruct((ctx_n, dp_n, adapters, z_tiles, 16, 128), BF),
            jax.ShapeDtypeStruct((exp_n, own_attn, adapters, 16, 128), BF),
        ),
        in_specs=[
            pl.BlockSpec(memory_space=pltpu.SMEM),
            pl.BlockSpec(memory_space=pl.ANY),
            pl.BlockSpec(memory_space=pltpu.VMEM),
        ],
        out_specs=(pl.BlockSpec(memory_space=pltpu.VMEM), pl.BlockSpec(memory_space=pltpu.VMEM)),
        scratch_shapes=[
            pltpu.VMEM((exp_n, ctx_n * x_tiles, 16, 128), BF),
            pltpu.VMEM((many, dp_n, exp_n, z_tiles, 16, 128), BF),
            pltpu.VMEM((dp_n, exp_n, z_tiles, 16, 128), BF),
            pltpu.VMEM((max(dp_n - 1, 1), exp_n, z_tiles, 16, 128), BF),
            dma, dma((exp_n,)), dma((exp_n,)), dma((many, dp_n)), dma((many, dp_n)),
            dma((dp_n,)), dma((dp_n,)), dma((dp_n,)), dma((dp_n,)),
            dma((many, dp_n)), dma((many, dp_n)), dma((exp_n,)), dma((exp_n,)),
        ],
        compiler_params=pltpu.CompilerParams(
            collective_id=1, has_side_effects=True, vmem_limit_bytes=VLIMIT
        ),
        name="reduce_adapters",
    )(adapter_ids, packed, attn)
    shapes = [
        (adapters,) + attn_shape,
        (adapters,) + attn_shape,
    ] + [(adapters,) + shape for shape in table_shapes]
    return pl.pallas_call(
        functools.partial(unpack_kernel, (x_tiles, z_tiles, own_attn)),
        grid=(adapters,),
        out_shape=tuple(jax.ShapeDtypeStruct(shape, F32) for shape in shapes),
        in_specs=[
            pl.BlockSpec((ctx_n, dp_n, 1, z_tiles, 16, 128), lambda a: (0, 0, a, 0, 0, 0)),
            pl.BlockSpec((exp_n, own_attn, 1, 16, 128), lambda a: (0, 0, a, 0, 0)),
        ],
        out_specs=tuple(
            pl.BlockSpec((1,) + shape[1:], lambda a, n=len(shape): (a,) + (0,) * (n - 1))
            for shape in shapes
        ),
        compiler_params=pltpu.CompilerParams(vmem_limit_bytes=VLIMIT),
        name="unpack_adapters",
    )(table, attn_table)


def local(
    hidden_in,
    prev_logits,
    segment_ids,
    routes,
    adapter_ids,
    attn_gain,
    w_qkv,
    w_out,
    attn_down,
    attn_up,
    ffn_gain,
    router_weight,
    gate_mix,
    const_mix,
    const_vec,
    w_gate_up,
    w_down,
    exp_in_down,
    exp_in_up,
    exp_out_down,
    exp_out_up,
    cotangent,
):
    model_dim = hidden_in.shape[2]
    kind_count = prev_logits.shape[2]
    local_experts, ffn_width = w_down.shape[:2]
    adapter_count = attn_down.shape[0]
    rank_dim = attn_up.shape[2]
    down_all = jnp.swapaxes(attn_down, 2, 3).reshape(adapter_count, 4 * rank_dim, model_dim)
    up_all = attn_up.reshape(adapter_count, 4 * rank_dim, model_dim)
    router_rows = jnp.concatenate(
        [router_weight.T, const_mix.transpose(0, 2, 1).reshape(4, model_dim)], 0
    )
    router_rows = jnp.pad(router_rows, ((0, 128 - router_rows.shape[0]), (0, 0)))
    mixed = jnp.pad(fdot("te,ef->tf", prev_logits[0], gate_mix), ((0, 0), (0, 128 - kind_count)))
    (
        q_pairs, k_pairs, v_pairs, normed_all, rank_all, log_cols, attn_flat, rank_out_all, mid_resid,
        rows_low, logits_all, seg_all, arrived_dy, slots,
    ) = attention_forward(
        hidden_in[0], segment_ids, mixed, adapter_ids, attn_gain, w_qkv, w_out, down_all, up_all,
        ffn_gain, router_rows, cotangent[0], routes[0].T, local_experts,
    )
    tables = (
        jnp.swapaxes(exp_in_down, 2, 3),
        exp_in_up.reshape(exp_in_up.shape[:2] + (2 * rank_dim, ffn_width)),
        jnp.swapaxes(exp_out_down, 2, 3),
        exp_out_up,
    )
    hidden_out, d_mid, d_logits, expert_tiles = expert_layer(
        rows_low, mid_resid, logits_all, slots, cotangent[0], arrived_dy, adapter_ids, ffn_gain,
        router_rows, const_vec, w_gate_up, w_down, tables, kind_count,
    )
    grad_prev = fdot("tf,ef->te", d_logits[:, :kind_count], gate_mix)
    grad_in, attn_tiles = attention_backward(
        d_mid,
        (q_pairs, k_pairs, v_pairs, normed_all, rank_all, log_cols, attn_flat, rank_out_all, seg_all),
        hidden_in[0], adapter_ids, attn_gain, w_qkv, w_out, down_all, up_all,
    )
    sums = reduce_adapters(
        adapter_ids,
        expert_tiles,
        [table.shape[1:] for table in tables],
        attn_tiles,
        (4 * rank_dim, model_dim),
        adapter_count,
    )
    grad_attn_down = jnp.swapaxes(sums[0].reshape(adapter_count, 4, rank_dim, model_dim), 2, 3)
    grad_attn_up = sums[1].reshape(adapter_count, 4, rank_dim, model_dim)
    grad_in_down = jnp.swapaxes(sums[2], 2, 3)
    grad_in_up = sums[3].reshape(exp_in_up.shape)
    grad_out_down = jnp.swapaxes(sums[4], 2, 3)
    grad_out_up = sums[5]
    return (
        hidden_out[None],
        grad_in[None],
        grad_prev[None],
        grad_attn_down,
        grad_attn_up,
        grad_in_down,
        grad_in_up,
        grad_out_down,
        grad_out_up,
    )


def solution(mesh):
    return jax.shard_map(
        local,
        mesh=mesh,
        in_specs=(
            P(("dp", "expert"), "context", None),
            P(("dp", "expert"), "context", None),
            P(("dp", "expert"), "context"),
            P(("dp", "expert"), "context", None),
            P(),
            P(),
            P(),
            P(),
            P(),
            P(),
            P(),
            P(),
            P(),
            P(),
            P(),
            P("expert", None, None),
            P("expert", None, None),
            P(None, "expert", None, None),
            P(None, "expert", None, None, None),
            P(None, "expert", None, None),
            P(None, "expert", None, None),
            P(("dp", "expert"), "context", None),
        ),
        out_specs=(
            P(("dp", "expert"), "context", None),
            P(("dp", "expert"), "context", None),
            P(("dp", "expert"), "context", None),
            P(),
            P(),
            P(None, "expert", None, None),
            P(None, "expert", None, None, None),
            P(None, "expert", None, None),
            P(None, "expert", None, None),
        ),
        check_vma=False,
    )
```

```python
import functools
import math

import jax
import jax.numpy as jnp
import numpy as np
from jax import lax
from jax.experimental import pallas as pl
from jax.experimental.pallas import tpu as pltpu
from jax.sharding import PartitionSpec as P

MESH = pl.DeviceIdType.MESH
VLIMIT = 60 * 1024 * 1024
BF = jnp.bfloat16
F32 = jnp.float32

HEADS = 12


EPSILON = 1e-06
ADAPT_SCALE = 2.0
NEG = -1e30
HIGH = lax.Precision.HIGHEST


def fdot(form, left, right):
    return jnp.einsum(form, left, right, precision=HIGH, preferred_element_type=jnp.float32)


def nt(left, right):
    return lax.dot_general(left, right, (((1,), (1,)), ((), ())), preferred_element_type=F32)


def tn(left, right):
    return lax.dot_general(left, right, (((0,), (0,)), ((), ())), preferred_element_type=F32)


def nn(left, right):
    return jnp.dot(left, right, preferred_element_type=F32)


def rope_tables(positions, width):
    half = width // 2
    frequency = np.exp(np.arange(half) * (-2.0 * math.log(10000.0) / width))
    angles = np.arange(positions)[:, None] * frequency[None, :]
    cosine, sine = np.cos(angles), np.sin(angles)
    return (
        np.concatenate([cosine] * 4, 1).astype(np.float32),
        np.concatenate([-sine, sine] * 2, 1).astype(np.float32),
    )


def turn(block, cosine, sine, width):
    half = width // 2
    lane = lax.broadcasted_iota(jnp.int32, block.shape, 1)
    other = jnp.where(
        lane % width < half, pltpu.roll(block, 128 - half, 1), pltpu.roll(block, half, 1)
    )
    return block * cosine + other * sine


def greet(axes):
    barrier = pltpu.get_barrier_semaphore()
    count = 0
    for axis, size in axes:
        index = lax.axis_index(axis)
        for step in range(1, size):
            pl.semaphore_signal(
                barrier, inc=1, device_id={axis: lax.rem(index + step, size)}, device_id_type=MESH
            )
        count += size - 1
    return lambda: pl.semaphore_wait(barrier, count)


def remote(src, dst, send, recv, axis, target):
    return pltpu.make_async_remote_copy(
        src_ref=src, dst_ref=dst, send_sem=send, recv_sem=recv,
        device_id={axis: target}, device_id_type=MESH,
    )


def blocks_of(ctx_n, ctx, count):
    return [lax.rem(ctx + 1 + j, ctx_n) for j in range(count)]


def fill_bias(bias_ref, seg_all, ctx_n, ctx, tok, count):
    own = jnp.broadcast_to(seg_all[ctx, 0:1, :].astype(F32), (128, tok))
    query_seg = jnp.transpose(own)[:, 0:1]
    query_pos = ctx * tok + lax.broadcasted_iota(jnp.int32, (tok, tok), 0)
    for j, block in enumerate([ctx] + blocks_of(ctx_n, ctx, count)):
        key_seg = seg_all[block, 0:1, :].astype(F32)
        key_pos = block * tok + lax.broadcasted_iota(jnp.int32, (tok, tok), 1)
        allowed = (query_seg == key_seg) & (key_pos <= query_pos)
        bias_ref[j] = jnp.where(allowed, 0.0, NEG).astype(bias_ref.dtype)


def attention_kernel(
    sizes, ids_ref, x_ref, seg_ref, mixed_ref, gain_one_ref, w_qkv_ref, w_out_ref, down_ref, up_ref,
    gain_two_ref, router_ref, cos_ref, sin_ref, dy_ref, routes_ref,
    q_ref, k_ref, v_ref, normed_ref, rank_ref, total_ref, flat_ref, rank_out_ref, mid_ref, rows_ref,
    logits_ref, seg_all, arrived_dy, slots_ref,
    x_all, bias_ref, sent_dy, send_sem, recv_sem, seg_send, seg_recv, dy_send, dy_recv,
):
    ctx_n, exp_n, rank = sizes
    ctx = lax.axis_index("context")
    sequence = lax.axis_index("dp") * exp_n + lax.axis_index("expert")
    tok, model = x_ref.shape
    pairs, head_dim = model // 128, 64
    entered = greet([("context", ctx_n), ("expert", exp_n)])
    seg_all[ctx] = jnp.broadcast_to(seg_ref[...], (8, tok))
    me = lax.axis_index("expert")
    experts, capacity = arrived_dy.shape[1], arrived_dy.shape[3]
    others = partners(exp_n, me)
    entered()
    dy_copies = []
    if ctx_n > 1:
        copies = []
        for step in range(1, ctx_n):
            peer = lax.rem(ctx + step, ctx_n)
            copies.append(
                (
                    peer,
                    step,
                    remote(x_ref, x_all.at[ctx], send_sem.at[step - 1], recv_sem.at[step - 1], "context", peer),
                    remote(seg_all.at[ctx], seg_all.at[ctx], seg_send.at[step - 1], seg_recv.at[step - 1], "context", peer),
                )
            )

        def to_later(peer):
            return ctx < peer if ctx_n == 2 else ctx < ctx_n

        def from_earlier(step):
            return lax.rem(ctx - step + ctx_n, ctx_n) < ctx if ctx_n == 2 else ctx < ctx_n

        for peer, step, rows_copy, seg_copy in copies:
            @pl.when(to_later(peer))
            def _(rows_copy=rows_copy, seg_copy=seg_copy):
                seg_copy.start()
                rows_copy.start()

    kind_rows = jnp.concatenate([routes_ref[...], jnp.full((6, tok), -1, jnp.int32)], 0)
    sub = lax.broadcasted_iota(jnp.int32, (16, tok), 0)
    uses = jnp.where((sub == kind_rows[0:1]) | (sub == kind_rows[1:2]), 1.0, 0.0).astype(BF)
    earlier = jnp.where(
        lax.broadcasted_iota(jnp.int32, (tok, tok), 0) < lax.broadcasted_iota(jnp.int32, (tok, tok), 1), 1.0, 0.0
    ).astype(BF)
    places = nn(uses, earlier) + (sub * capacity).astype(F32)
    slot_rows = []
    for j in range(2):
        kind = kind_rows[j : j + 1]
        place = jnp.sum(jnp.where(sub == kind, places, 0.0), 0, keepdims=True)
        slot_rows.append(jnp.where(kind < exp_n * experts, place, -1.0))
    row8 = lax.broadcasted_iota(jnp.int32, (8, tok), 0)
    slots_ref[...] = jnp.where(
        row8 < 2, kind_rows.astype(F32), jnp.where(row8 == 2, slot_rows[0], jnp.where(row8 == 3, slot_rows[1], 0.0))
    )
    slot_ints = [row.astype(jnp.int32) for row in slot_rows]

    def pick_dy(owner):
        hots = [hot_rows(row, owner * experts * capacity, experts * capacity) for row in slot_ints]
        hot = jnp.where(hots[0] | hots[1], 1.0, 0.0).astype(BF)
        return nn(hot, dy_ref[...]).astype(BF)

    for i, peer in enumerate(others):
        picked = pick_dy(peer)
        for e in range(experts):
            sent_dy[i, e] = picked[e * capacity : (e + 1) * capacity]
        copy = remote(
            sent_dy.at[i], arrived_dy.at[me // 2, :, lax.rem(me, 2)], dy_send.at[i], dy_recv.at[me], "expert", peer
        )
        copy.start()
        dy_copies.append(copy)
    picked = pick_dy(me)
    for e in range(experts):
        arrived_dy[me // 2, e, lax.rem(me, 2)] = picked[e * capacity : (e + 1) * capacity]
    adapter = ids_ref[sequence]
    down = down_ref[adapter]
    up = up_ref[adapter]
    gain_one = gain_one_ref[...].astype(F32)
    column = lax.broadcasted_iota(jnp.int32, (tok, down.shape[0]), 1) // rank

    def project(values, block, first):
        wide = values.astype(F32)
        inv = lax.rsqrt(jnp.mean(wide * wide, -1, keepdims=True) + EPSILON)
        normed_ref[block] = (wide * inv * gain_one).astype(BF)
        normed = normed_ref[block]
        ranks = nt(normed, down).astype(BF)
        rank_ref[block] = ranks
        start = pl.multiple_of(block * tok, tok)
        for p in range(first, 3):
            part = jnp.where(column == p, ADAPT_SCALE * ranks.astype(F32), 0.0).astype(BF)

            def chunk(i, carry, p=p, part=part):
                wide_cols = pl.ds(pl.multiple_of(p * model + i * 256, 256), 256)
                cols = pl.ds(pl.multiple_of(i * 256, 256), 256)
                proj = nn(normed_ref[block], w_qkv_ref[:, wide_cols]) + nn(
                    part, up_cols[:, cols]
                )
                for half in range(2):
                    piece = proj[:, half * 128 : half * 128 + 128]
                    if p < 2:
                        piece = turn(
                            piece, cos_ref[pl.ds(start, tok)], sin_ref[pl.ds(start, tok)], head_dim
                        )
                    if p == 0:
                        q_ref[2 * i + half] = (piece * head_dim ** (-0.5)).astype(BF)
                    else:
                        (k_ref if p == 1 else v_ref)[block, 2 * i + half] = piece.astype(BF)
                return carry

            up_cols = up_ref.at[adapter]
            lax.fori_loop(0, model // 256, chunk, 0)

    project(x_ref[...], ctx, 0)
    lane = lax.broadcasted_iota(jnp.int32, (1, 128), 1)
    marks = [(lane < 64), (lane >= 64)]
    half_rows = tok // 2

    def attend(count):
        fill_bias(bias_ref, seg_all, ctx_n, ctx, tok, count)
        others = blocks_of(ctx_n, ctx, count)

        def pair(i, carry):
            for half in range(2):
                rows = slice(half * half_rows, (half + 1) * half_rows)
                own_width = (half + 1) * half_rows
                q = q_ref[i, rows]
                result = jnp.zeros((half_rows, 128), F32)
                stats = total_ref[rows]
                for head in range(2):
                    mark = marks[head]
                    q_head = jnp.where(mark, q, 0)
                    scores = [
                        nt(q_head, k_ref[ctx, i, 0:own_width]) + bias_ref[0, rows, 0:own_width]
                    ]
                    for j, block in enumerate(others):
                        scores.append(nt(q_head, k_ref[block, i]) + bias_ref[j + 1, rows])
                    top = functools.reduce(
                        jnp.maximum, [jnp.max(s, -1, keepdims=True) for s in scores]
                    )
                    exps = [jnp.exp(s - top) for s in scores]
                    total = functools.reduce(jnp.add, [jnp.sum(e, -1, keepdims=True) for e in exps])
                    stats = jnp.where(lane == 2 * i + head, top + jnp.log(total), stats)
                    inv = 1.0 / total
                    for e, block in zip(exps, [ctx] + others):
                        v = k_v(block, i, e.shape[1])
                        result = result + nn((e * inv).astype(BF), jnp.where(mark, v, 0))
                total_ref[rows] = stats
                flat_ref[rows, pl.ds(pl.multiple_of(i * 128, 128), 128)] = result.astype(BF)
            return carry

        def k_v(block, i, width):
            return v_ref[block, i, 0:width]

        lax.fori_loop(0, pairs, pair, 0)

    total_ref[...] = jnp.zeros_like(total_ref)
    if ctx_n == 1:
        attend(0)
    else:
        for peer, step, rows_copy, seg_copy in copies:
            @pl.when(from_earlier(step))
            def _(step=step, rows_copy=rows_copy, seg_copy=seg_copy):
                rows_copy.wait_recv()
                seg_copy.wait_recv()
                block = lax.rem(ctx - step + ctx_n, ctx_n)
                project(x_all[block], block, 1)

        @pl.when(ctx == 0)
        def _():
            if ctx_n == 2:
                attend(0)
            else:
                attend(ctx_n - 1)

        @pl.when(ctx > 0)
        def _():
            attend(ctx_n - 1)

        for peer, step, rows_copy, seg_copy in copies:
            @pl.when(to_later(peer))
            def _(rows_copy=rows_copy, seg_copy=seg_copy):
                seg_copy.wait_send()
                rows_copy.wait_send()

    rank_out = nt(flat_ref[...], down).astype(BF)
    rank_out_ref[...] = rank_out
    part = jnp.where(column == 3, ADAPT_SCALE * rank_out.astype(F32), 0.0).astype(BF)

    def out_chunk(i, carry):
        cols = pl.ds(pl.multiple_of(i * 256, 256), 256)
        mid_ref[:, cols] = (
            x_ref[:, cols].astype(F32)
            + nn(flat_ref[...], w_out_ref[:, cols])
            + nn(part, up_ref[adapter, :, cols])
        )
        return carry

    lax.fori_loop(0, model // 256, out_chunk, 0)
    gain_two = gain_two_ref[...].astype(F32)
    step_rows = 128

    def norm_rows(i, carry):
        rows = pl.ds(pl.multiple_of(i * step_rows, step_rows), step_rows)
        mid = mid_ref[rows]
        inv = lax.rsqrt(jnp.mean(mid * mid, -1, keepdims=True) + EPSILON)
        rows_ref[rows] = (mid * inv * gain_two).astype(BF)
        return carry

    lax.fori_loop(0, tok // step_rows, norm_rows, 0)
    logits_ref[...] = nt(rows_ref[...], router_ref[...]) + mixed_ref[...]
    for copy in dy_copies:
        copy.wait_send()
    for peer in others:
        remote(
            sent_dy.at[0], arrived_dy.at[peer // 2, :, lax.rem(peer, 2)], dy_send.at[0], dy_recv.at[peer], "expert", peer
        ).wait_recv()


def attention_forward(hidden, segments, mixed, ids, gain_one, w_qkv, w_out, down, up, gain_two, router, dy, routes, experts):
    ctx_n, exp_n = lax.axis_size("context"), lax.axis_size("expert")
    tok, model = hidden.shape
    pairs = model // 128
    wide = down.shape[1]
    cos_table, sin_table = rope_tables(ctx_n * tok, 64)
    vmem = pl.BlockSpec(memory_space=pltpu.VMEM)
    dma = pltpu.SemaphoreType.DMA
    many = max(ctx_n - 1, 1)
    shape = jax.ShapeDtypeStruct
    return pl.pallas_call(
        functools.partial(attention_kernel, (ctx_n, exp_n, wide // 4)),
        out_shape=(
            shape((pairs, tok, 128), BF),
            shape((ctx_n, pairs, tok, 128), BF),
            shape((ctx_n, pairs, tok, 128), BF),
            shape((ctx_n, tok, model), BF),
            shape((ctx_n, tok, wide), BF),
            shape((tok, 128), F32),
            shape((tok, model), BF),
            shape((tok, wide), BF),
            shape((tok, model), F32),
            shape((tok, model), BF),
            shape((tok, 128), F32),
            shape((ctx_n, 8, tok), jnp.int32),
            shape((exp_n // 2, experts, 2, tok // 4, model), BF),
            shape((8, tok), F32),
        ),
        in_specs=[pl.BlockSpec(memory_space=pltpu.SMEM)] + [vmem] * 14,
        out_specs=(vmem,) * 14,
        scratch_shapes=[
            pltpu.VMEM((ctx_n, tok, model), BF),
            pltpu.VMEM((ctx_n, tok, tok), BF if ctx_n > 2 else F32),
            pltpu.VMEM((exp_n - 1, experts, tok // 4, model), BF),
            dma((many,)), dma((many,)), dma((many,)), dma((many,)), dma((exp_n - 1,)), dma((exp_n,)),
        ],
        compiler_params=pltpu.CompilerParams(
            collective_id=2, has_side_effects=True, vmem_limit_bytes=VLIMIT
        ),
        name="attention_forward",
    )(
        ids, hidden, segments, mixed, gain_one.reshape(1, model), w_qkv, w_out, down, up,
        gain_two.reshape(1, model), router, jnp.asarray(cos_table), jnp.asarray(sin_table), dy, routes,
    )


def put_tiles(tiles_ref, first, value):
    for col in range(value.shape[1] // 128):
        tiles_ref[first + col] = value[:, col * 128 : col * 128 + 128].astype(tiles_ref.dtype)


def backward_kernel(
    sizes, ids_ref, d_mid_ref, q_ref, k_ref, v_ref, normed_ref, rank_ref, total_ref, flat_ref,
    rank_out_ref, x_ref, seg_all, gain_one_ref, w_qkv_ref, w_out_ref, down_ref, up_ref, cos_ref,
    sin_ref, *rest,
):
    ctx_n, exp_n, rank, fused = sizes
    if fused:
        sums_ref, grad_ref, table_ref, attn_table, tiles_ref = rest[:5]
        scratch, more = rest[5:-24], rest[-24:]
        sums = Sums(fused, ids_ref, sums_ref, tiles_ref, table_ref, attn_table, more)
    else:
        grad_ref, tiles_ref = rest[:2]
        scratch = rest[2:]
    (
        recv_buf, do_ref, bias_ref, dk_acc, dv_acc, dq_all, dkv_all, send_buf, grad_up, grad_down,
        normed_buf, send_sem, recv_sem, load_sem,
    ) = scratch
    ctx = lax.axis_index("context")
    sequence = lax.axis_index("dp") * exp_n + lax.axis_index("expert")
    tok, model = x_ref.shape
    pairs, head_dim = model // 128, 64
    entered = greet([(axis, lax.axis_size(axis)) for axis in (ALL_AXES if fused else ("context",))])
    if fused:
        entered()
        sums.start()
    order = [ctx] + blocks_of(ctx_n, ctx, ctx_n - 1)

    def fetch(j):
        return pltpu.make_async_copy(
            normed_ref.at[order[j]], normed_buf.at[min(j, 1)], load_sem.at[min(j, 1)]
        )

    fetch(0).start()
    if ctx_n > 1:
        fetch(1).start()
    adapter = ids_ref[sequence]
    down = down_ref[adapter]
    up = up_ref[adapter]
    wide = down.shape[0]
    column = lax.broadcasted_iota(jnp.int32, (tok, wide), 1) // rank
    d_branch = d_mid_ref[...].astype(BF)
    d_rank_out = jnp.where(column == 3, ADAPT_SCALE * nt(d_branch, up), 0.0).astype(BF)
    twice_out = jnp.where(column == 3, ADAPT_SCALE * rank_out_ref[...].astype(F32), 0.0).astype(BF)
    grad_up[...] = tn(twice_out, d_branch)
    grad_down[...] = tn(d_rank_out, flat_ref[...])

    def attn_chunk(i, carry):
        rows = pl.ds(pl.multiple_of(i * 256, 256), 256)
        d_attn = nt(d_branch, w_out_ref[rows, :]) + nn(d_rank_out, down_ref[adapter, :, rows])
        do_ref[2 * i] = d_attn[:, :128].astype(BF)
        do_ref[2 * i + 1] = d_attn[:, 128:].astype(BF)
        return carry

    lax.fori_loop(0, model // 256, attn_chunk, 0)
    lane = lax.broadcasted_iota(jnp.int32, (1, 128), 1)
    marks = [(lane < 64), (lane >= 64)]
    half_rows = tok // 2

    def attend(count):
        fill_bias(bias_ref, seg_all, ctx_n, ctx, tok, count)
        others = blocks_of(ctx_n, ctx, count)

        def pair(i, carry):
            cols = pl.ds(pl.multiple_of(i * 128, 128), 128)
            for half in (1, 0):
                rows = slice(half * half_rows, (half + 1) * half_rows)
                own_width = (half + 1) * half_rows
                q = q_ref[i, rows]
                d_out = do_ref[i, rows]
                stats = total_ref[rows]
                d_query = jnp.zeros((half_rows, 128), F32)
                for head in range(2):
                    mark = marks[head]
                    q_head = jnp.where(mark, q, 0)
                    do_head = jnp.where(mark, d_out, 0)
                    total = jnp.sum(
                        jnp.where(lane == 2 * i + head, stats, 0.0), -1, keepdims=True
                    )
                    parts = []
                    delta = jnp.zeros((half_rows, 1), F32)
                    for j, block in enumerate([ctx] + others):
                        width = own_width if j == 0 else tok
                        probs = jnp.exp(
                            nt(q_head, k_ref[block, i, 0:width])
                            + bias_ref[j, rows, 0:width]
                            - total
                        )
                        d_probs = nt(do_head, v_ref[block, i, 0:width])
                        delta = delta + jnp.sum(probs * d_probs, -1, keepdims=True)
                        parts.append((probs, d_probs))
                    for j, block in enumerate([ctx] + others):
                        width = own_width if j == 0 else tok
                        probs, d_probs = parts[j]
                        d_scores = (probs * (d_probs - delta)).astype(BF)
                        k_head = jnp.where(mark, k_ref[block, i, 0:width], 0)
                        d_query = d_query + nn(d_scores, k_head)
                        d_key = tn(q_head, d_scores)
                        d_value = tn(do_head, probs.astype(BF))
                        if half == 1 and head == 0:
                            dk_acc[j, :, 0:width] = d_key
                            dv_acc[j, :, 0:width] = d_value
                        else:
                            dk_acc[j, :, 0:width] += d_key
                            dv_acc[j, :, 0:width] += d_value
                start = pl.multiple_of(ctx * tok + half * half_rows, half_rows)
                d_query = d_query * head_dim ** (-0.5)
                dq_all[rows, cols] = turn(
                    d_query, cos_ref[pl.ds(start, half_rows)], -sin_ref[pl.ds(start, half_rows)], head_dim
                ).astype(BF)
            for j, block in enumerate([ctx] + others):
                start = pl.multiple_of(block * tok, tok)
                d_key = turn(
                    jnp.transpose(dk_acc[j]), cos_ref[pl.ds(start, tok)], -sin_ref[pl.ds(start, tok)], head_dim
                )
                dkv_all[j, 0, :, cols] = d_key.astype(BF)
                dkv_all[j, 1, :, cols] = jnp.transpose(dv_acc[j]).astype(BF)
            return carry

        lax.fori_loop(0, pairs, pair, 0)

    def fold(j, block, first, write):
        normed = normed_buf[min(j, 1)]
        ranks = rank_ref[block].astype(F32)
        d_ranks = jnp.zeros((tok, wide), F32)
        for p in range(first, 3):
            d_proj = dq_all[...] if p == 0 else dkv_all[j, p - 1]
            twice = jnp.where(column == p, ADAPT_SCALE * ranks, 0.0).astype(BF)
            grad_up[...] += tn(twice, d_proj)
            d_ranks = d_ranks + jnp.where(column == p, ADAPT_SCALE * nt(d_proj, up), 0.0)
        d_ranks = d_ranks.astype(BF)
        grad_down[...] += tn(d_ranks, normed)

        def chunk(i, carry):
            rows = pl.ds(pl.multiple_of(i * 256, 256), 256)
            value = nn(d_ranks, down_ref[adapter, :, rows])
            for p in range(first, 3):
                d_proj = dq_all[...] if p == 0 else dkv_all[j, p - 1]
                value = value + nt(d_proj, w_qkv_ref[rows, p * model : (p + 1) * model])
            write(rows, value)
            return carry

        lax.fori_loop(0, model // 256, chunk, 0)

    def write_own(cols, value):
        grad_ref[:, cols] = value

    copies = []
    for step in range(1, ctx_n):
        peer = lax.rem(ctx + step, ctx_n)
        copies.append(
            remote(send_buf, recv_buf.at[step - 1], send_sem.at[step - 1], recv_sem.at[step - 1], "context", peer)
        )

    if ctx_n == 1:
        attend(0)
    elif ctx_n == 2:
        pl.when(ctx == 0)(lambda: attend(0))
    if not fused:
        entered()

    def spread():
        attend(ctx_n - 1)
        for j, block in enumerate(blocks_of(ctx_n, ctx, ctx_n - 1)):
            def write(cols, value):
                send_buf[:, cols] = value.astype(BF)

            fetch(j + 1).wait()
            if j > 0:
                copies[j - 1].wait_send()
            fold(j + 1, block, 1, write)
            copies[j].start()
            if j + 2 < ctx_n:
                fetch(j + 2).start()

    if ctx_n == 2:
        pl.when(ctx == 1)(spread)
        pl.when(ctx == 0)(fetch(1).wait)
    elif ctx_n > 2:
        spread()
    if fused:
        sums.combine()
    fetch(0).wait()
    fold(0, ctx, 0, write_own)
    per = model // 128
    for p in range(4):
        put_tiles(tiles_ref, p * per, grad_down[p * rank : (p + 1) * rank])
        put_tiles(tiles_ref, (4 + p) * per, grad_up[p * rank : (p + 1) * rank])

    def settle():
        take_shares()
        lax.fori_loop(0, tok // 128, finish, 0)

    def take_shares():
        if ctx_n == 2:
            pl.when(ctx == 0)(copies[0].wait_recv)

            @pl.when(ctx == 1)
            def _():
                recv_buf[...] = jnp.zeros_like(recv_buf)

        elif ctx_n > 2:
            copies[-1].wait_send()
            for step, item in enumerate(copies):
                item.wait_recv()
                load = pltpu.make_async_copy(recv_buf.at[step], send_buf, load_sem.at[0])
                load.start()
                load.wait()
                grad_ref[...] += send_buf[...].astype(F32)

    gain_one = gain_one_ref[...].astype(F32)

    def finish(i, carry):
        rows = pl.ds(pl.multiple_of(i * 128, 128), 128)
        value = grad_ref[rows]
        if ctx_n == 2:
            value = value + recv_buf[0, rows].astype(F32)
        x = x_ref[rows].astype(F32)
        inv = lax.rsqrt(jnp.mean(x * x, -1, keepdims=True) + EPSILON)
        scaled = value * gain_one
        grad_ref[rows] = (
            d_mid_ref[rows]
            + inv * scaled
            - x * (inv * inv * inv) * jnp.mean(scaled * x, -1, keepdims=True)
        )
        return carry

    if fused:
        sums.tail([settle] + [functools.partial(sums.forward, k) for k in range(1, fused[1])])
        sums.finish()
    else:
        settle()
    if ctx_n == 2:
        pl.when(ctx == 1)(copies[0].wait_send)


def attention_backward(d_mid, saved, hidden, ids, gain_one, w_qkv, w_out, down, up, expert_sums, experts, width):
    ctx_n, exp_n = lax.axis_size("context"), lax.axis_size("expert")
    tok, model = hidden.shape
    pairs = model // 128
    wide = down.shape[1]
    cos_table, sin_table = rope_tables(ctx_n * tok, 64)
    vmem = pl.BlockSpec(memory_space=pltpu.VMEM)
    dma = pltpu.SemaphoreType.DMA
    many = max(ctx_n - 1, 1)
    shape = jax.ShapeDtypeStruct
    q, k, v, normed, ranks, totals, flat, rank_out, seg_all = saved
    in_specs = [vmem] * 18
    in_specs[4] = pl.BlockSpec(memory_space=pl.ANY)
    spill = ctx_n > 2
    landing = ((many, tok, model), BF)
    attn_tiles, adapters = 8 * pairs, down.shape[0]
    sums_outs, sums_scratch = sums_shapes(experts, model, width, attn_tiles, adapters)
    fused = None
    if not spill:
        fused = tuple(lax.axis_size(axis) for axis in ALL_AXES) + (adapters, attn_tiles)
    tiles_shape = ((attn_tiles, 16, 128), BF)
    results = pl.pallas_call(
        functools.partial(backward_kernel, (ctx_n, exp_n, wide // 4, fused)),
        out_shape=(shape((tok, model), F32),)
        + ((shape(*tiles_shape), shape(*landing)) if spill else sums_outs),
        in_specs=[pl.BlockSpec(memory_space=pltpu.SMEM)] + in_specs + ([] if spill else [vmem]),
        out_specs=(vmem, vmem, pl.BlockSpec(memory_space=pl.ANY) if spill else vmem),
        scratch_shapes=([] if spill else [pltpu.VMEM(*tiles_shape), pltpu.VMEM(*landing)])
        + [
            pltpu.VMEM((pairs, tok, 128), BF),
            pltpu.VMEM((ctx_n, tok, tok), BF if spill else F32),
            pltpu.VMEM((ctx_n, 128, tok), F32),
            pltpu.VMEM((ctx_n, 128, tok), F32),
            pltpu.VMEM((tok, model), BF),
            pltpu.VMEM((ctx_n, 2, tok, model), BF),
            pltpu.VMEM((tok, model), BF),
            pltpu.VMEM((wide, model), F32),
            pltpu.VMEM((wide, model), F32),
            pltpu.VMEM((min(ctx_n, 2), tok, model), BF),
            dma((many,)), dma((many,)), dma((2,)),
        ] + ([] if spill else sums_scratch),
        compiler_params=pltpu.CompilerParams(
            collective_id=3, has_side_effects=True, vmem_limit_bytes=VLIMIT + 5 * 2**19
        ),
        name="attention_backward",
    )(
        ids, d_mid, q, k, v, normed, ranks, totals, flat, rank_out, hidden, seg_all,
        gain_one.reshape(1, model), w_qkv, w_out, down, up, jnp.asarray(cos_table),
        jnp.asarray(sin_table), *([] if spill else [expert_sums]),
    )
    if spill:
        return (results[0],) + tuple(add_up(ids, expert_sums, results[1], experts, width, adapters))
    return results


def partners(exp_n, me):
    core = lax.rem(me, 2)
    twin = me + 1 - 2 * core
    far = []
    for step in range(2, exp_n, 2):
        far += [lax.rem(me + step, exp_n), lax.rem(twin + step, exp_n)]
    return far + [twin]


def hot_rows(slot_rows, first, count):
    target = first + lax.broadcasted_iota(jnp.int32, (count, slot_rows.shape[1]), 0)
    return target == slot_rows


def moe_kernel(
    sizes, ids_ref, rows_ref, mid_ref, logits_ref, slots_ref, dy_ref, arrived_dy, gain_ref, router_ref,
    vec_ref, gate_up_hbm, down_hbm, in_down_ref, in_up_ref, out_down_ref, out_up_ref,
    hidden_ref, d_mid_ref, d_logits_ref, sums_ref,
    tiles_ref, arrived_x, gate_up_ref, w_down_ref, sent_rows, sent_gates, arrived_rows, arrived_gates, act_ref, d_pre_ref,
    done_out, done_rows, back_out, back_rows, cols_ref, gates_ref,
    weight_sem, row_send, row_recv, gate_send, gate_recv, out_send, out_recv, in_send, in_recv,
    x_send, x_recv,
):
    ctx_n, exp_n, kinds, rank, share = sizes
    ctx = lax.axis_index("context")
    me = lax.axis_index("expert")
    my_chip, my_core = me // 2, lax.rem(me, 2)
    first_seq = lax.axis_index("dp") * exp_n
    tok, model = rows_ref.shape
    experts, width = w_down_ref.shape[:2]
    capacity = arrived_rows.shape[3]
    per_owner = experts * capacity
    both = 2 * capacity
    entered = greet([("expert", exp_n), ("context", ctx_n)])
    loads = []
    for e in range(experts):
        for hbm, ref, k in ((gate_up_hbm, gate_up_ref, 0), (down_hbm, w_down_ref, 1)):
            load = pltpu.make_async_copy(hbm.at[e], ref.at[e], weight_sem.at[e, k])
            load.start()
            loads.append(load)

    lane = lax.broadcasted_iota(jnp.int32, (tok, 128), 1)
    logits = logits_ref[...]
    masked = jnp.where(lane < kinds, logits, NEG)
    exps = jnp.exp(masked - jnp.max(masked, -1, keepdims=True))
    probs = exps / jnp.sum(exps, -1, keepdims=True)
    slot_cols = jnp.transpose(
        jnp.concatenate([slots_ref[...], jnp.zeros((120, tok), F32)], 0)
    )
    cols_ref[...] = slot_cols
    gates = [
        jnp.sum(jnp.where(lane == slot_cols[:, k : k + 1].astype(jnp.int32), probs, 0.0), -1, keepdims=True)
        for k in range(2)
    ]
    gates_ref[...] = jnp.where(lane == 0, gates[0], jnp.where(lane == 1, gates[1], 0.0))
    gate_rows = jnp.transpose(gates_ref[...])
    parts = []
    sub = lax.broadcasted_iota(jnp.int32, (16, tok), 0)
    for k in range(2):
        whole = jnp.broadcast_to(gate_rows[k : k + 1], (16, tok))
        high = whole.astype(BF).astype(F32)
        middle = (whole - high).astype(BF).astype(F32)
        lowest = whole - high - middle
        parts.append(
            jnp.where(sub == 0, high, jnp.where(sub == 1, middle, jnp.where(sub == 2, lowest, 0.0))).astype(BF)
        )
    slot_rows = [slots_ref[2 + k : 3 + k].astype(jnp.int32) for k in range(2)]

    def pick(owner, rows_to, gates_to):
        hots = [hot_rows(slot_rows[k], owner * per_owner, per_owner) for k in range(2)]
        hot = jnp.where(hots[0] | hots[1], 1.0, 0.0).astype(BF)
        rows_to(nn(hot, rows_ref[...]).astype(BF))
        gates_to(
            sum(nt(parts[k], jnp.where(hots[k], 1.0, 0.0).astype(BF)) for k in range(2)).astype(BF)
        )

    entered()
    sends = []
    others = partners(exp_n, me)
    for i, peer in enumerate(others):
        def rows_to(value, i=i):
            for e in range(experts):
                sent_rows[i, e] = value[e * capacity : (e + 1) * capacity]

        def gates_to(value, i=i):
            for e in range(experts):
                sent_gates[i, e] = value[:, e * capacity : (e + 1) * capacity]

        pick(peer, rows_to, gates_to)
        for src, dst, send, recv in (
            (sent_gates, arrived_gates, gate_send, gate_recv),
            (sent_rows, arrived_rows, row_send, row_recv),
        ):
            copy = remote(
                src.at[i], dst.at[my_chip, :, my_core], send.at[i], recv.at[me], "expert", peer
            )
            copy.start()
            sends.append(copy)

    def own_rows(value):
        for e in range(experts):
            arrived_rows[my_chip, e, my_core] = value[e * capacity : (e + 1) * capacity]

    def own_gates(value):
        for e in range(experts):
            arrived_gates[my_chip, e, my_core] = value[:, e * capacity : (e + 1) * capacity]

    pick(me, own_rows, own_gates)

    def arrive(source):
        for ref, src, send, recv in (
            (arrived_gates, sent_gates, gate_send, gate_recv),
            (arrived_rows, sent_rows, row_send, row_recv),
        ):
            remote(
                src.at[0], ref.at[source // 2, :, lax.rem(source, 2)], send.at[0], recv.at[source],
                "expert", source,
            ).wait_recv()

    row64 = lax.broadcasted_iota(jnp.int32, (both, 4 * rank), 0) // capacity
    col64 = lax.broadcasted_iota(jnp.int32, (both, 4 * rank), 1)
    mine64 = row64 == col64 // (2 * rank)
    is_gate = col64 % (2 * rank) < rank
    mine32 = lax.broadcasted_iota(jnp.int32, (both, 2 * rank), 0) // capacity == (
        lax.broadcasted_iota(jnp.int32, (both, 2 * rank), 1) // rank
    )
    step_cols = 512
    per_step = step_cols // 128
    across, deep = model // 128, width // 128
    first_up = 2 * across
    first_out = first_up + 2 * deep
    first_last = first_out + deep

    def put(source, e, tile, value):
        tiles_ref[source, tile // share, e * share + tile % share] = value

    def x_copies(chip, e):
        copies = []
        for step in range(1, ctx_n):
            peer = lax.rem(ctx + step, ctx_n)
            here = pl.ds(e * share, share)
            copies.append(
                remote(
                    tiles_ref.at[pl.ds(2 * chip, 2), peer, here],
                    arrived_x.at[step - 1, pl.ds(2 * chip, 2), here],
                    x_send.at[step - 1, chip, e], x_recv.at[step - 1, chip, e], "context", peer,
                )
            )
        return copies

    def work(chip, e):
        names = [ids_ref[first_seq + 2 * chip + core] for core in range(2)]

        def stack(ref, cols=slice(None)):
            return jnp.concatenate([ref[name, e, :, cols] for name in names], 0)

        rows = arrived_rows[chip, e].reshape(both, model)
        in_down = stack(in_down_ref)
        out_up = stack(out_up_ref)
        gate = []
        for core in range(2):
            piece = arrived_gates[chip, e, core].astype(F32)
            total = piece[0:1] + piece[1:2] + piece[2:3]
            gate.append(jnp.transpose(jnp.broadcast_to(total, (128, capacity)))[:, 0:1])
        gate = jnp.concatenate(gate, 0)
        d_out = (gate * arrived_dy[chip, e].reshape(both, model).astype(F32)).astype(BF)
        ranks = jnp.where(mine64, nt(rows, in_down), 0.0).astype(BF)
        twice = ADAPT_SCALE * ranks.astype(F32)
        twice_gate = jnp.where(is_gate, twice, 0.0).astype(BF)
        twice_up = jnp.where(is_gate, 0.0, twice).astype(BF)
        d_mid_rank = jnp.where(mine32, ADAPT_SCALE * nt(d_out, out_up), 0.0).astype(BF)

        def chunk(i, carry):
            rank_mid, d_rank = carry
            start = pl.multiple_of(i * step_cols, step_cols)
            cols = pl.ds(start, step_cols)
            up_cols = pl.ds(pl.multiple_of(width + i * step_cols, step_cols), step_cols)
            in_up = stack(in_up_ref, cols)
            out_down = stack(out_down_ref, cols)
            gate_pre = nn(rows, gate_up_ref[e, :, cols]) + nn(twice_gate, in_up)
            up_pre = nn(rows, gate_up_ref[e, :, up_cols]) + nn(twice_up, in_up)
            d_act = (nt(d_out, w_down_ref[e, cols, :]) + nn(d_mid_rank, out_down)).astype(BF).astype(F32)
            sigma = 1.0 / (1.0 + jnp.exp(-gate_pre))
            silu = gate_pre * sigma
            act = (silu * up_pre).astype(BF)
            d_gate = (d_act * up_pre * sigma * (1.0 + gate_pre * (1.0 - sigma))).astype(BF)
            d_up = (d_act * silu).astype(BF)
            act_ref[:, cols] = act
            d_pre_ref[:, cols] = d_gate
            d_pre_ref[:, up_cols] = d_up
            rank_mid = rank_mid + nt(act, out_down)
            d_rank = d_rank + jnp.where(is_gate, nt(d_gate, in_up), nt(d_up, in_up))
            grad_up = (tn(twice_gate, d_gate) + tn(twice_up, d_up)).astype(BF)
            grad_out = tn(d_mid_rank, act).astype(BF)
            for core in range(2):
                for t in range(per_step):
                    here = slice(t * 128, t * 128 + 128)
                    tile = i * per_step + t
                    for which in range(2):
                        first = (2 * core + which) * rank
                        put(
                            2 * chip + core, e, first_up + which * deep + tile,
                            grad_up[first : first + rank, here],
                        )
                    put(
                        2 * chip + core, e, first_out + tile,
                        grad_out[core * rank : (core + 1) * rank, here],
                    )
            return rank_mid, d_rank

        rank_mid, d_rank = lax.fori_loop(
            0, width // step_cols, chunk,
            (jnp.zeros((both, 2 * rank), F32), jnp.zeros((both, 4 * rank), F32)),
        )
        twice_mid = jnp.where(
            mine32, ADAPT_SCALE * rank_mid.astype(BF).astype(F32), 0.0
        ).astype(BF)

        def out_chunk(i, carry):
            cols = pl.ds(pl.multiple_of(i * 256, 256), 256)
            value = nn(act_ref[...], w_down_ref[e, :, cols]) + nn(twice_mid, stack(out_up_ref, cols))
            for core in range(2):
                done_out[chip, e, core, :, cols] = value[core * capacity : (core + 1) * capacity].astype(BF)
            return carry

        lax.fori_loop(0, model // 256, out_chunk, 0)
        give_back(chip, e, done_out, back_out, out_send, out_recv)
        d_rank_in = jnp.where(mine64, ADAPT_SCALE * d_rank, 0.0).astype(BF)

        def in_chunk(i, carry):
            cols = pl.ds(pl.multiple_of(i * 256, 256), 256)
            value = nt(d_pre_ref[...], gate_up_ref[e, cols, :]) + nn(d_rank_in, stack(in_down_ref, cols))
            for core in range(2):
                done_rows[chip, e, core, :, cols] = value[core * capacity : (core + 1) * capacity].astype(BF)
            return carry

        lax.fori_loop(0, model // 256, in_chunk, 0)
        give_back(chip, e, done_rows, back_rows, in_send, in_recv)
        grad_last = tn(twice_mid, d_out).astype(BF)
        grad_first = tn(d_rank_in, rows).astype(BF)
        for core in range(2):
            for t in range(across):
                here = slice(t * 128, t * 128 + 128)
                for which in range(2):
                    first = (2 * core + which) * rank
                    put(
                        2 * chip + core, e, which * across + t, grad_first[first : first + rank, here]
                    )
                put(
                    2 * chip + core, e, first_last + t,
                    grad_last[core * rank : (core + 1) * rank, here],
                )
        for copy in x_copies(chip, e):
            copy.start()

    def give_back(chip, e, done, back, send, recv):
        for core in range(2):
            target = 2 * chip + core
            copy = remote(
                done.at[chip, e, core], back.at[me * experts + e], send.at[target, e], recv.at[me, e],
                "expert", target,
            )

            @pl.when(target == me)
            def _(core=core):
                back[me * experts + e] = done[chip, e, core]

            @pl.when(target != me)
            def _(copy=copy):
                copy.start()

    for load in loads[:2]:
        load.wait()
    arrive(others[-1])
    work(my_chip, 0)
    far_chips = [lax.rem(my_chip + step, exp_n // 2) for step in range(1, exp_n // 2)]
    for load in loads[2:]:
        load.wait()
    for i, chip in enumerate(far_chips):
        arrive(others[2 * i])
        arrive(others[2 * i + 1])
        for e in range(experts):
            work(chip, e)
    for e in range(1, experts):
        work(my_chip, e)

    def collect(done, back, send, recv):
        for owner in others:
            for e in range(experts):
                remote(
                    done.at[0, e, 0], back.at[owner * experts + e], send.at[owner, e], recv.at[owner, e],
                    "expert", owner,
                ).wait_recv()

    slots_total = exp_n * per_owner
    block = 256

    def hot_cols(rows):
        target = lax.broadcasted_iota(jnp.int32, (block, slots_total), 1)
        return [target == cols_ref[rows, 2 + k : 3 + k].astype(jnp.int32) for k in range(2)]

    gain = gain_ref[...].astype(F32)
    lanes = lax.broadcasted_iota(jnp.int32, (block, 128), 1)
    ffn_kinds = exp_n * experts

    def outward(i, carry):
        rows = pl.ds(pl.multiple_of(i * block, block), block)
        hots = hot_cols(rows)
        table = back_out[...].reshape(slots_total, model)
        mid = mid_ref[rows]
        dy = dy_ref[rows].astype(F32)
        normed = mid * lax.rsqrt(jnp.mean(mid * mid, -1, keepdims=True) + EPSILON) * gain
        logits = logits_ref[rows]
        masked = jnp.where(lanes < kinds, logits, NEG)
        exps = jnp.exp(masked - jnp.max(masked, -1, keepdims=True))
        probs = exps / jnp.sum(exps, -1, keepdims=True)
        pairs = []
        for c in range(2):
            one, two = logits[:, kinds + 2 * c : kinds + 2 * c + 1], logits[:, kinds + 2 * c + 1 : kinds + 2 * c + 2]
            pairs.append((1.0 / (1.0 + jnp.exp(two - one)), 1.0 / (1.0 + jnp.exp(one - two))))
        total = mid
        d_kinds = jnp.zeros((block, 128), F32)
        dy_scale = jnp.zeros((block, 1), F32)
        weights = [jnp.zeros((block, 1), F32)] * 2
        for k in range(2):
            kind = cols_ref[rows, k : k + 1].astype(jnp.int32)
            gate = gates_ref[rows, k : k + 1]
            scale = jnp.where(kind == ffn_kinds + 1, 1.0, 0.0)
            term = nn(jnp.where(hots[k], 1.0, 0.0).astype(BF), table)
            for c in range(2):
                here = jnp.where(kind == ffn_kinds + 2 + c, 1.0, 0.0)
                scale = scale + here * pairs[c][0]
                term = term + (here * pairs[c][1]) * vec_ref[c : c + 1].astype(F32)
                weights[c] = weights[c] + here * gate
            term = term + scale * normed
            dy_scale = dy_scale + gate * scale
            total = total + gate * term
            d_gate = jnp.sum(dy * term, -1, keepdims=True)
            d_kinds = d_kinds + jnp.where(lanes == kind, d_gate, 0.0)
        hidden_ref[rows] = total.astype(BF)
        d_logits = probs * (d_kinds - jnp.sum(probs * d_kinds, -1, keepdims=True))
        along = jnp.sum(dy * normed, -1, keepdims=True)
        for c in range(2):
            d_one = weights[c] * along
            d_two = weights[c] * jnp.sum(dy * vec_ref[c : c + 1].astype(F32), -1, keepdims=True)
            mean = pairs[c][0] * d_one + pairs[c][1] * d_two
            d_logits = jnp.where(lanes == kinds + 2 * c, pairs[c][0] * (d_one - mean), d_logits)
            d_logits = jnp.where(lanes == kinds + 2 * c + 1, pairs[c][1] * (d_two - mean), d_logits)
        d_logits_ref[rows] = d_logits
        high = d_logits.astype(BF)
        rest = d_logits - high.astype(F32)
        middle = rest.astype(BF)
        lowest = (rest - middle.astype(F32)).astype(BF)
        router = router_ref[...]
        d_mid_ref[rows] = dy_scale * dy + (nn(high, router) + nn(middle, router) + nn(lowest, router))
        return carry

    def inward(i, carry):
        rows = pl.ds(pl.multiple_of(i * block, block), block)
        hots = hot_cols(rows)
        table = back_rows[...].reshape(slots_total, model)
        hot = jnp.where(hots[0] | hots[1], 1.0, 0.0).astype(BF)
        scaled = (d_mid_ref[rows] + nn(hot, table)) * gain
        mid = mid_ref[rows]
        inv = lax.rsqrt(jnp.mean(mid * mid, -1, keepdims=True) + EPSILON)
        d_mid_ref[rows] = (
            dy_ref[rows].astype(F32)
            + inv * scaled
            - mid * (inv * inv * inv) * jnp.mean(scaled * mid, -1, keepdims=True)
        )
        return carry

    collect(done_out, back_out, out_send, out_recv)
    lax.fori_loop(0, tok // block, outward, 0)
    collect(done_rows, back_rows, in_send, in_recv)
    lax.fori_loop(0, tok // block, inward, 0)
    for chip in range(exp_n // 2):
        for e in range(experts):
            for copy in x_copies(chip, e):
                copy.wait()

    def add(tile, carry):
        total = tiles_ref[:, ctx, pl.ds(tile, 1)].astype(F32)
        for step in range(1, ctx_n):
            total = total + arrived_x[step - 1, :, pl.ds(tile, 1)].astype(F32)
        sums_ref[:, pl.ds(tile, 1)] = total.astype(BF)
        return carry

    lax.fori_loop(0, experts * share, add, 0)
    for copy in sends:
        copy.wait_send()
    for target in others:
        for e in range(experts):
            for done, back, send, recv in (
                (done_out, back_out, out_send, out_recv),
                (done_rows, back_rows, in_send, in_recv),
            ):
                remote(
                    done.at[0, e, 0], back.at[0], send.at[target, e], recv.at[target, e],
                    "expert", target,
                ).wait_send()


def expert_tiling(experts, model, width):
    share = pl.cdiv(3 * (model + width) // 128, lax.axis_size("context"))
    z_tiles = pl.cdiv(experts * share, lax.axis_size("dp"))
    return share, z_tiles * lax.axis_size("dp"), z_tiles


def attn_tiling(attn_tiles):
    own = attn_tiles // lax.axis_size("expert")
    x_tiles = pl.cdiv(own, lax.axis_size("context"))
    return own, x_tiles, pl.cdiv(x_tiles, lax.axis_size("dp"))


def expert_layer(rows, mid, logits, slots, dy, arrived_dy, ids, gain, router, vec, w_gate_up, w_down, tables, kinds):
    exp_n = lax.axis_size("expert")
    tok, model = rows.shape
    experts, width = w_down.shape[:2]
    capacity = tok // 4
    rank = tables[3].shape[2]
    ctx_n = lax.axis_size("context")
    share, x_tiles, _ = expert_tiling(experts, model, width)
    many = max(ctx_n - 1, 1)
    chips = exp_n // 2
    vmem = pl.BlockSpec(memory_space=pltpu.VMEM)
    hbm = pl.BlockSpec(memory_space=pl.ANY)
    dma = pltpu.SemaphoreType.DMA
    shape = jax.ShapeDtypeStruct
    block = (experts, capacity, model)
    return pl.pallas_call(
        functools.partial(moe_kernel, (ctx_n, exp_n, kinds, rank, share)),
        out_shape=(
            shape((tok, model), BF),
            shape((tok, model), F32),
            shape((tok, 128), F32),
            shape((exp_n, x_tiles, 16, 128), BF),
        ),
        in_specs=[pl.BlockSpec(memory_space=pltpu.SMEM)] + [vmem] * 9 + [hbm] * 2 + [vmem] * 4,
        out_specs=(vmem,) * 4,
        scratch_shapes=[
            pltpu.VMEM((exp_n, ctx_n, experts * share, 16, 128), BF),
            pltpu.VMEM((many, exp_n, experts * share, 16, 128), BF),
            pltpu.VMEM((experts, model, 2 * width), BF),
            pltpu.VMEM((experts, width, model), BF),
            pltpu.VMEM((exp_n - 1,) + block, BF),
            pltpu.VMEM((exp_n - 1, experts, 16, capacity), BF),
            pltpu.VMEM((chips, experts, 2, capacity, model), BF),
            pltpu.VMEM((chips, experts, 2, 16, capacity), BF),
            pltpu.VMEM((2 * capacity, width), BF),
            pltpu.VMEM((2 * capacity, 2 * width), BF),
            pltpu.VMEM((chips, experts, 2, capacity, model), BF),
            pltpu.VMEM((chips, experts, 2, capacity, model), BF),
            pltpu.VMEM((exp_n * experts, capacity, model), BF),
            pltpu.VMEM((exp_n * experts, capacity, model), BF),
            pltpu.VMEM((tok, 128), F32),
            pltpu.VMEM((tok, 128), F32),
            dma((experts, 2)), dma((exp_n - 1,)), dma((exp_n,)), dma((exp_n - 1,)), dma((exp_n,)),
            dma((exp_n, experts)), dma((exp_n, experts)), dma((exp_n, experts)), dma((exp_n, experts)),
            dma((many, chips, experts)), dma((many, chips, experts)),
        ],
        compiler_params=pltpu.CompilerParams(
            collective_id=4, has_side_effects=True, vmem_limit_bytes=VLIMIT
        ),
        name="expert_layer",
    )(
        ids, rows, mid, logits, slots, dy, arrived_dy, gain.reshape(1, model), router, vec, w_gate_up,
        w_down, *tables,
    )


class Sums:
    def __init__(self, sizes, ids_ref, sums_ref, attn_ref, table_ref, attn_table, scratch):
        self.ctx_n, self.dp_n, self.exp_n, self.adapters, self.attn_tiles = sizes
        self.ids_ref, self.sums_ref, self.attn_ref = ids_ref, sums_ref, attn_ref
        self.table_ref, self.attn_table = table_ref, attn_table
        self.ctx, self.dp, self.exp = (lax.axis_index(axis) for axis in ("context", "dp", "expert"))
        (
            self.arrived_z, self.held_a, self.arrived_xa, self.part_a, self.arrived_za,
            self.z_send, self.z_recv, self.az_send, self.az_recv, self.ax_send, self.ax_recv,
            self.r_send, self.r_recv, self.xa_send, self.xa_recv, self.za_send, self.za_recv,
            self.bz_send, self.bz_recv, self.bx_send, self.bx_recv, self.be_send, self.be_recv,
            self.keep_sem,
        ) = scratch
        self.waits = []

    def peer(self, axis, step):
        index, size = {
            "context": (self.ctx, self.ctx_n), "dp": (self.dp, self.dp_n), "expert": (self.exp, self.exp_n)
        }[axis]
        return lax.rem(index + step, size)

    def send(self, src, dst, send, recv, axis, target):
        copy = remote(src, dst, send, recv, axis, target)
        copy.start()
        self.waits.append(copy)
        return copy

    def weight(self, k, source):
        origin = lax.rem(self.dp - k + self.dp_n, self.dp_n)
        name = self.ids_ref[origin * self.exp_n + source]
        return [jnp.where(name == a, 1.0, 0.0).astype(F32) for a in range(self.adapters)]

    def merge(self, count, own, arrived, write):
        marks = [self.weight(k, source) for k in range(self.dp_n) for source in range(self.exp_n)]

        def tile_sums(tile, carry):
            totals = [jnp.zeros((16, 128), F32)] * self.adapters
            for k in range(self.dp_n):
                for source in range(self.exp_n):
                    value = (own(source, tile) if k == 0 else arrived[k - 1, source, tile]).astype(F32)
                    mark = marks[k * self.exp_n + source]
                    totals = [total + m * value for total, m in zip(totals, mark)]
            for a in range(self.adapters):
                write(a, tile, totals[a].astype(BF))
            return carry

        lax.fori_loop(0, count, tile_sums, 0)

    def start(self):
        z_tiles = self.arrived_z.shape[2]
        self.z_copies = [
            self.send(
                self.sums_ref.at[:, pl.ds(self.peer("dp", k) * z_tiles, z_tiles)], self.arrived_z.at[k - 1],
                self.z_send.at[k - 1], self.z_recv.at[k - 1], "dp", self.peer("dp", k),
            )
            for k in range(1, self.dp_n)
        ]

    def combine(self):
        z_tiles = self.arrived_z.shape[2]
        for copy in self.z_copies:
            copy.wait_recv()

        def write(a, tile, value):
            self.table_ref[self.ctx, self.dp, a, tile] = value

        self.merge(
            z_tiles, lambda source, tile: self.sums_ref[source, self.dp * z_tiles + tile], self.arrived_z, write
        )
        here = self.table_ref.at[self.ctx, self.dp]
        self.az_copies = [
            self.send(here, here, self.az_send.at[k - 1], self.az_recv.at[k - 1], "dp", self.peer("dp", k))
            for k in range(1, self.dp_n)
        ]
        self.ax_copies = []
        self.forward(0)

    def forward(self, k):
        if k > 0:
            self.az_copies[k - 1].wait_recv()
        origin = lax.rem(self.dp - k + self.dp_n, self.dp_n)
        here = self.table_ref.at[self.ctx, origin]
        for step in range(1, self.ctx_n):
            self.ax_copies.append(
                self.send(
                    here, here, self.ax_send.at[step - 1, k], self.ax_recv.at[step - 1, k], "context",
                    self.peer("context", step),
                )
            )

    def tail(self, between):
        between = list(between)

        def other():
            if between:
                between.pop(0)()

        own, x_tiles, z_tiles = attn_tiling(self.attn_tiles)
        real = pl.cdiv(x_tiles, z_tiles)
        keep = pltpu.make_async_copy(
            self.attn_ref.at[pl.ds(self.exp * own, own)], self.held_a.at[self.exp, pl.ds(0, own)], self.keep_sem
        )
        keep.start()
        copies = [
            self.send(
                self.attn_ref.at[pl.ds(self.peer("expert", k) * own, own)],
                self.held_a.at[self.exp, pl.ds(0, own)],
                self.r_send.at[k - 1], self.r_recv.at[k - 1], "expert", self.peer("expert", k),
            )
            for k in range(1, self.exp_n)
        ]
        other()
        keep.wait()
        for copy in copies:
            copy.wait_recv()
        copies = [
            self.send(
                self.held_a.at[:, pl.ds(self.peer("context", k) * x_tiles, x_tiles)], self.arrived_xa.at[k - 1],
                self.xa_send.at[k - 1], self.xa_recv.at[k - 1], "context", self.peer("context", k),
            )
            for k in range(1, self.ctx_n)
        ]
        for copy in copies:
            copy.wait_recv()
        total = self.held_a[:, pl.ds(self.ctx * x_tiles, x_tiles)].astype(F32)
        for k in range(1, self.ctx_n):
            total = total + self.arrived_xa[k - 1].astype(F32)
        self.part_a[:, 0:x_tiles] = total.astype(BF)
        copies = [
            self.send(
                self.part_a.at[:, pl.ds(self.peer("dp", k) * z_tiles, z_tiles)], self.arrived_za.at[k - 1],
                self.za_send.at[k - 1], self.za_recv.at[k - 1], "dp", self.peer("dp", k),
            )
            for k in range(1, self.dp_n)
        ]
        other()
        for copy in copies:
            copy.wait_recv()
        mine = self.attn_table.at[self.exp]

        def write(a, tile, value):
            self.attn_table[self.exp, self.ctx, self.dp, a, tile] = value

        self.merge(
            z_tiles, lambda source, tile: self.part_a[source, self.dp * z_tiles + tile], self.arrived_za, write
        )
        here = mine.at[self.ctx, self.dp]
        copies = [
            self.send(here, here, self.bz_send.at[k - 1], self.bz_recv.at[k - 1], "dp", self.peer("dp", k))
            for k in range(1, self.dp_n)
        ]
        other()
        for copy in copies:
            copy.wait_recv()
        here = mine.at[self.ctx, pl.ds(0, real)]
        copies = [
            self.send(
                here, here, self.bx_send.at[k - 1], self.bx_recv.at[k - 1], "context", self.peer("context", k)
            )
            for k in range(1, self.ctx_n)
        ]
        for copy in copies:
            copy.wait_recv()
        core = lax.rem(self.exp, 2)
        twin = self.exp + 1 - 2 * core
        chips = self.exp_n // 2

        def table_of(owner):
            return self.attn_table.at[owner, :, pl.ds(0, real)]

        far = [
            self.send(
                table_of(self.exp), table_of(self.exp), self.be_send.at[0, k - 1], self.be_recv.at[0, k - 1],
                "expert", self.peer("expert", 2 * k),
            )
            for k in range(1, chips)
        ]
        near = [
            self.send(
                table_of(self.exp), table_of(self.exp), self.be_send.at[1, 0], self.be_recv.at[1, 0], "expert", twin
            )
        ]
        while between:
            other()
        for k in range(1, chips):
            far[k - 1].wait_recv()
            owner = self.peer("expert", self.exp_n - 2 * k)
            near.append(
                self.send(
                    table_of(owner), table_of(owner), self.be_send.at[1, k], self.be_recv.at[1, k], "expert", twin
                )
            )
        for copy in near:
            copy.wait_recv()

    def finish(self):
        for copy in self.ax_copies:
            copy.wait_recv()
        for copy in self.waits:
            copy.wait_send()


def sums_shapes(experts, model, width, attn_tiles, adapters):
    ctx_n, dp_n, exp_n = (lax.axis_size(axis) for axis in ("context", "dp", "expert"))
    _, _, z_tiles = expert_tiling(experts, model, width)
    own, xa_tiles, za_tiles = attn_tiling(attn_tiles)
    many, deep, chips = max(ctx_n - 1, 1), max(dp_n - 1, 1), max(exp_n // 2, 1)
    dma = pltpu.SemaphoreType.DMA
    outs = (
        jax.ShapeDtypeStruct((ctx_n, dp_n, adapters, z_tiles, 16, 128), BF),
        jax.ShapeDtypeStruct((exp_n, ctx_n, dp_n, adapters, za_tiles, 16, 128), BF),
    )
    scratch = [
        pltpu.VMEM((deep, exp_n, z_tiles, 16, 128), BF),
        pltpu.VMEM((exp_n, max(ctx_n * xa_tiles, own), 16, 128), BF),
        pltpu.VMEM((many, exp_n, xa_tiles, 16, 128), BF),
        pltpu.VMEM((exp_n, dp_n * za_tiles, 16, 128), BF),
        pltpu.VMEM((deep, exp_n, za_tiles, 16, 128), BF),
        dma((deep,)), dma((deep,)), dma((deep,)), dma((deep,)), dma((many, dp_n)), dma((many, dp_n)),
        dma((exp_n,)), dma((exp_n,)), dma((many,)), dma((many,)), dma((deep,)), dma((deep,)),
        dma((deep,)), dma((deep,)), dma((many,)), dma((many,)), dma((2, chips)), dma((2, chips)),
        dma,
    ]
    return outs, scratch


ALL_AXES = ("context", "dp", "expert")


def sums_kernel(sizes, ids_ref, sums_ref, attn_ref, table_ref, attn_table, *scratch):
    entered = greet([(axis, lax.axis_size(axis)) for axis in ALL_AXES])
    entered()
    sums = Sums(sizes, ids_ref, sums_ref, attn_ref, table_ref, attn_table, scratch)
    sums.start()
    sums.combine()
    for k in range(1, sizes[1]):
        sums.forward(k)
    sums.tail([])
    sums.finish()


def add_up(ids, sums, attn, experts, width, adapters):
    model = attn.shape[0] * 16
    outs, scratch = sums_shapes(experts, model, width, attn.shape[0], adapters)
    vmem = pl.BlockSpec(memory_space=pltpu.VMEM)
    sizes = tuple(lax.axis_size(axis) for axis in ALL_AXES) + (adapters, attn.shape[0])
    return pl.pallas_call(
        functools.partial(sums_kernel, sizes),
        out_shape=outs,
        in_specs=[pl.BlockSpec(memory_space=pltpu.SMEM), vmem, vmem],
        out_specs=(vmem, vmem),
        scratch_shapes=scratch,
        compiler_params=pltpu.CompilerParams(
            collective_id=1, has_side_effects=True, vmem_limit_bytes=VLIMIT
        ),
        name="reduce_adapters",
    )(ids, sums, attn)


def unpack_kernel(sizes, table_ref, attn_ref, down_ref, up_ref, in_down_ref, in_up_ref, out_down_ref, out_up_ref):
    share, z_tiles, own, xa_tiles, za_tiles = sizes
    for expert in range(in_up_ref.shape[1]):
        tile = 0
        for out_ref in (in_down_ref, in_up_ref, out_down_ref, out_up_ref):
            rows, cols = out_ref.shape[2:]
            for row in range(rows // 16):
                for col in range(cols // 128):
                    place = expert * share + tile % share
                    out_ref[0, expert, row * 16 : row * 16 + 16, col * 128 : col * 128 + 128] = table_ref[
                        tile // share, place // z_tiles, 0, place % z_tiles
                    ].astype(F32)
                    tile += 1
    tile = 0
    for out_ref in (down_ref, up_ref):
        rows, cols = out_ref.shape[1:]
        for row in range(rows // 16):
            for col in range(cols // 128):
                place = tile % own
                out_ref[0, row * 16 : row * 16 + 16, col * 128 : col * 128 + 128] = attn_ref[
                    tile // own, place // xa_tiles, place % xa_tiles // za_tiles, 0, place % xa_tiles % za_tiles
                ].astype(F32)
                tile += 1


def unpack(table, attn_table, experts, width, table_shapes, attn_shape):
    adapters = table.shape[2]
    model = attn_shape[1]
    share, _, z_tiles = expert_tiling(experts, model, width)
    sizes = (share, z_tiles) + attn_tiling(8 * model // 128)
    shapes = [(adapters,) + attn_shape] * 2 + [(adapters,) + shape for shape in table_shapes]

    def by_adapter(array, axis):
        block = array.shape[:axis] + (1,) + array.shape[axis + 1 :]
        return pl.BlockSpec(block, lambda a, n=array.ndim: (0,) * axis + (a,) + (0,) * (n - axis - 1))

    return pl.pallas_call(
        functools.partial(unpack_kernel, sizes),
        grid=(adapters,),
        out_shape=tuple(jax.ShapeDtypeStruct(shape, F32) for shape in shapes),
        in_specs=[by_adapter(table, 2), by_adapter(attn_table, 3)],
        out_specs=tuple(
            pl.BlockSpec((1,) + shape[1:], lambda a, n=len(shape): (a,) + (0,) * (n - 1))
            for shape in shapes
        ),
        compiler_params=pltpu.CompilerParams(vmem_limit_bytes=VLIMIT),
        name="unpack_adapters",
    )(table, attn_table)


def local(
    hidden_in,
    prev_logits,
    segment_ids,
    routes,
    adapter_ids,
    attn_gain,
    w_qkv,
    w_out,
    attn_down,
    attn_up,
    ffn_gain,
    router_weight,
    gate_mix,
    const_mix,
    const_vec,
    w_gate_up,
    w_down,
    exp_in_down,
    exp_in_up,
    exp_out_down,
    exp_out_up,
    cotangent,
):
    model_dim = hidden_in.shape[2]
    kind_count = prev_logits.shape[2]
    local_experts, ffn_width = w_down.shape[:2]
    adapter_count = attn_down.shape[0]
    rank_dim = attn_up.shape[2]
    down_all = jnp.swapaxes(attn_down, 2, 3).reshape(adapter_count, 4 * rank_dim, model_dim)
    up_all = attn_up.reshape(adapter_count, 4 * rank_dim, model_dim)
    router_rows = jnp.concatenate(
        [router_weight.T, const_mix.transpose(0, 2, 1).reshape(4, model_dim)], 0
    )
    router_rows = jnp.pad(router_rows, ((0, 128 - router_rows.shape[0]), (0, 0)))
    mixed = jnp.pad(fdot("te,ef->tf", prev_logits[0], gate_mix), ((0, 0), (0, 128 - kind_count)))
    (
        q_pairs, k_pairs, v_pairs, normed_all, rank_all, log_cols, attn_flat, rank_out_all, mid_resid,
        rows_low, logits_all, seg_all, arrived_dy, slots,
    ) = attention_forward(
        hidden_in[0], segment_ids, mixed, adapter_ids, attn_gain, w_qkv, w_out, down_all, up_all,
        ffn_gain, router_rows, cotangent[0], routes[0].T, local_experts,
    )
    tables = (
        jnp.swapaxes(exp_in_down, 2, 3),
        exp_in_up.reshape(exp_in_up.shape[:2] + (2 * rank_dim, ffn_width)),
        jnp.swapaxes(exp_out_down, 2, 3),
        exp_out_up,
    )
    hidden_out, d_mid, d_logits, expert_sums = expert_layer(
        rows_low, mid_resid, logits_all, slots, cotangent[0], arrived_dy, adapter_ids, ffn_gain,
        router_rows, const_vec, w_gate_up, w_down, tables, kind_count,
    )
    grad_prev = fdot("tf,ef->te", d_logits[:, :kind_count], gate_mix)
    grad_in, table, attn_table = attention_backward(
        d_mid,
        (q_pairs, k_pairs, v_pairs, normed_all, rank_all, log_cols, attn_flat, rank_out_all, seg_all),
        hidden_in[0], adapter_ids, attn_gain, w_qkv, w_out, down_all, up_all, expert_sums,
        local_experts, ffn_width,
    )
    sums = unpack(
        table, attn_table, local_experts, ffn_width, [entry.shape[1:] for entry in tables],
        (4 * rank_dim, model_dim),
    )
    grad_attn_down = jnp.swapaxes(sums[0].reshape(adapter_count, 4, rank_dim, model_dim), 2, 3)
    grad_attn_up = sums[1].reshape(adapter_count, 4, rank_dim, model_dim)
    grad_in_down = jnp.swapaxes(sums[2], 2, 3)
    grad_in_up = sums[3].reshape(exp_in_up.shape)
    grad_out_down = jnp.swapaxes(sums[4], 2, 3)
    grad_out_up = sums[5]
    return (
        hidden_out[None],
        grad_in[None],
        grad_prev[None],
        grad_attn_down,
        grad_attn_up,
        grad_in_down,
        grad_in_up,
        grad_out_down,
        grad_out_up,
    )


def solution(mesh):
    return jax.shard_map(
        local,
        mesh=mesh,
        in_specs=(
            P(("dp", "expert"), "context", None),
            P(("dp", "expert"), "context", None),
            P(("dp", "expert"), "context"),
            P(("dp", "expert"), "context", None),
            P(),
            P(),
            P(),
            P(),
            P(),
            P(),
            P(),
            P(),
            P(),
            P(),
            P(),
            P("expert", None, None),
            P("expert", None, None),
            P(None, "expert", None, None),
            P(None, "expert", None, None, None),
            P(None, "expert", None, None),
            P(None, "expert", None, None),
            P(("dp", "expert"), "context", None),
        ),
        out_specs=(
            P(("dp", "expert"), "context", None),
            P(("dp", "expert"), "context", None),
            P(("dp", "expert"), "context", None),
            P(),
            P(),
            P(None, "expert", None, None),
            P(None, "expert", None, None, None),
            P(None, "expert", None, None),
            P(None, "expert", None, None),
        ),
        check_vma=False,
    )
```

```python
import functools
import math

import jax
import jax.numpy as jnp
import numpy as np
from jax import lax
from jax.experimental import pallas as pl
from jax.experimental.pallas import tpu as pltpu
from jax.sharding import PartitionSpec as P

MESH = pl.DeviceIdType.MESH
VLIMIT = 60 * 1024 * 1024
BF = jnp.bfloat16
F32 = jnp.float32

HEADS = 12


EPSILON = 1e-06
ADAPT_SCALE = 2.0
NEG = -1e30
HIGH = lax.Precision.HIGHEST


def nt(left, right):
    return lax.dot_general(left, right, (((1,), (1,)), ((), ())), preferred_element_type=F32)


def tn(left, right):
    return lax.dot_general(left, right, (((0,), (0,)), ((), ())), preferred_element_type=F32)


def nn(left, right):
    return jnp.dot(left, right, preferred_element_type=F32)


def rope_tables(positions, width):
    half = width // 2
    frequency = np.exp(np.arange(half) * (-2.0 * math.log(10000.0) / width))
    angles = np.arange(positions)[:, None] * frequency[None, :]
    cosine, sine = np.cos(angles), np.sin(angles)
    return (
        np.concatenate([cosine] * 4, 1).astype(np.float32),
        np.concatenate([-sine, sine] * 2, 1).astype(np.float32),
    )


def turn(block, cosine, sine, width):
    half = width // 2
    lane = lax.broadcasted_iota(jnp.int32, block.shape, 1)
    other = jnp.where(
        lane % width < half, pltpu.roll(block, 128 - half, 1), pltpu.roll(block, half, 1)
    )
    return block * cosine + other * sine


def greet(axes):
    barrier = pltpu.get_barrier_semaphore()
    count = 0
    for axis, size in axes:
        index = lax.axis_index(axis)
        for step in range(1, size):
            pl.semaphore_signal(
                barrier, inc=1, device_id={axis: lax.rem(index + step, size)}, device_id_type=MESH
            )
        count += size - 1
    return lambda: pl.semaphore_wait(barrier, count)


def remote(src, dst, send, recv, axis, target):
    return pltpu.make_async_remote_copy(
        src_ref=src, dst_ref=dst, send_sem=send, recv_sem=recv,
        device_id={axis: target}, device_id_type=MESH,
    )


def blocks_of(ctx_n, ctx, count):
    return [lax.rem(ctx + 1 + j, ctx_n) for j in range(count)]


def fill_bias(bias_ref, seg_all, ctx, tok, j, block):
    own = jnp.broadcast_to(seg_all[ctx, 0:1, :].astype(F32), (128, tok))
    query_seg = jnp.transpose(own)[:, 0:1]
    query_pos = ctx * tok + lax.broadcasted_iota(jnp.int32, (tok, tok), 0)
    key_seg = seg_all[block, 0:1, :].astype(F32)
    key_pos = block * tok + lax.broadcasted_iota(jnp.int32, (tok, tok), 1)
    allowed = (query_seg == key_seg) & (key_pos <= query_pos)
    bias_ref[j] = jnp.where(allowed, 0.0, NEG).astype(bias_ref.dtype)


def head_marks():
    lane = lax.broadcasted_iota(jnp.int32, (1, 128), 1)
    return lane, lane < 64


def stack_heads(value):
    _, first = head_marks()
    return jnp.concatenate([jnp.where(first, value, 0), jnp.where(first, 0, value)], 0)


def join_heads(value):
    _, first = head_marks()
    rows = value.shape[0] // 2
    return jnp.where(first, value[:rows], value[rows:])


def stack_columns(stats, i):
    lane, _ = head_marks()
    return jnp.concatenate(
        [jnp.sum(jnp.where(lane == 2 * i + head, stats, 0.0), -1, keepdims=True) for head in range(2)], 0
    )


def put_columns(stats, i, column):
    lane, _ = head_marks()
    rows = stats.shape[0]
    stats = jnp.where(lane == 2 * i, column[:rows], stats)
    return jnp.where(lane == 2 * i + 1, column[rows:], stats)


def biased(raw, bias):
    rows, keys = bias.shape
    return (raw.reshape(2, rows, keys) + bias[None]).reshape(2 * rows, keys)


def attention_kernel(
    sizes, ids_ref, x_hbm, seg_ref, prev_ref, mix_ref, w_qkv_hbm, w_out_hbm, down_hbm, up_hbm,
    router_ref, cos_hbm, sin_hbm, dy_hbm, routes_ref,
    q_out, k_out, v_out, normed_out, rank_ref, total_ref, flat_ref, rank_out_ref, mid_ref, rows_ref,
    logits_ref, seg_all, arrived_dy, slots_ref,
    x_all, bias_ref, sent_dy, acc_ref, top_ref, weight_ref, prev_pad, mix_pad, send_sem, recv_sem, seg_send, seg_recv, dy_send, dy_recv,
    q_ref, k_ref, v_ref, normed_ref, own_dy, out_sem, *staged,
):
    ctx_n, exp_n, rank = sizes
    dy_ref, x_ref, down_ref, up_ref, w_qkv_ref, cos_ref, sin_ref, w_out_ref, stage_sem = staged
    stages = stage_copies(
        (dy_hbm, x_hbm, down_hbm, up_hbm, w_qkv_hbm, cos_hbm, sin_hbm, w_out_hbm), staged, stage_sem
    )
    for stage in stages:
        stage.start()
    ctx = lax.axis_index("context")
    sequence = lax.axis_index("dp") * exp_n + lax.axis_index("expert")
    tok, model = x_ref.shape
    pairs, head_dim = model // 128, 64
    entered = greet([("context", ctx_n), ("expert", exp_n)])
    seg_all[ctx] = jnp.broadcast_to(seg_ref[...], (8, tok))
    me = lax.axis_index("expert")
    experts, capacity = arrived_dy.shape[1], arrived_dy.shape[3]
    others = partners(exp_n, me)
    entered()
    dy_copies = []
    if ctx_n > 1:
        copies = []
        for step in range(1, ctx_n):
            peer = lax.rem(ctx + step, ctx_n)
            copies.append(
                (
                    peer,
                    step,
                    remote(x_hbm, x_all.at[ctx], send_sem.at[step - 1], recv_sem.at[step - 1], "context", peer),
                    remote(seg_all.at[ctx], seg_all.at[ctx], seg_send.at[step - 1], seg_recv.at[step - 1], "context", peer),
                )
            )

        def to_later(peer):
            return ctx < peer if ctx_n == 2 else ctx < ctx_n

        def from_earlier(step):
            return lax.rem(ctx - step + ctx_n, ctx_n) < ctx if ctx_n == 2 else ctx < ctx_n

        for peer, step, rows_copy, seg_copy in copies:
            @pl.when(to_later(peer))
            def _(rows_copy=rows_copy, seg_copy=seg_copy):
                seg_copy.start()
                rows_copy.start()

    kind_rows = jnp.concatenate([routes_ref[...], jnp.full((6, tok), -1, jnp.int32)], 0)
    sub = lax.broadcasted_iota(jnp.int32, (16, tok), 0)
    uses = jnp.where((sub == kind_rows[0:1]) | (sub == kind_rows[1:2]), 1.0, 0.0).astype(BF)
    earlier = jnp.where(
        lax.broadcasted_iota(jnp.int32, (tok, tok), 0) < lax.broadcasted_iota(jnp.int32, (tok, tok), 1), 1.0, 0.0
    ).astype(BF)
    places = nn(uses, earlier) + (sub * capacity).astype(F32)
    slot_rows = []
    for j in range(2):
        kind = kind_rows[j : j + 1]
        place = jnp.sum(jnp.where(sub == kind, places, 0.0), 0, keepdims=True)
        slot_rows.append(jnp.where(kind < exp_n * experts, place, -1.0))
    row8 = lax.broadcasted_iota(jnp.int32, (8, tok), 0)
    slots_ref[...] = jnp.where(
        row8 < 2, kind_rows.astype(F32), jnp.where(row8 == 2, slot_rows[0], jnp.where(row8 == 3, slot_rows[1], 0.0))
    )
    slot_ints = [row.astype(jnp.int32) for row in slot_rows]

    def pick_dy(owner):
        hots = [hot_rows(row, owner * experts * capacity, experts * capacity) for row in slot_ints]
        hot = jnp.where(hots[0] | hots[1], 1.0, 0.0).astype(BF)
        return nn(hot, dy_ref[...]).astype(BF)

    stages[0].wait()
    for i, peer in enumerate(others):
        picked = pick_dy(peer)
        for e in range(experts):
            sent_dy[i, e] = picked[e * capacity : (e + 1) * capacity]
        copy = remote(
            sent_dy.at[i], arrived_dy.at[me // 2, :, lax.rem(me, 2)], dy_send.at[i], dy_recv.at[me], "expert", peer
        )
        copy.start()
        dy_copies.append(copy)
    picked = pick_dy(me)
    for e in range(experts):
        own_dy[e] = picked[e * capacity : (e + 1) * capacity]
    writes = [pltpu.make_async_copy(own_dy, arrived_dy.at[me // 2, :, lax.rem(me, 2)], out_sem.at[0])]
    writes[0].start()
    for stage in stages[1:]:
        stage.wait()
    adapter = ids_ref[sequence]
    down = down_ref[adapter]
    up = up_ref[adapter]
    gain_one = router_ref[16:17].astype(F32)
    column = lax.broadcasted_iota(jnp.int32, (tok, down.shape[0]), 1) // rank

    def project(values, block, first):
        wide = values.astype(F32)
        inv = lax.rsqrt(jnp.mean(wide * wide, -1, keepdims=True) + EPSILON)
        normed_ref[block] = (wide * inv * gain_one).astype(BF)
        normed = normed_ref[block]
        ranks = nt(normed, down).astype(BF)
        rank_ref[block] = ranks
        start = pl.multiple_of(block * tok, tok)
        for p in range(first, 3):
            part = jnp.where(column == p, ADAPT_SCALE * ranks.astype(F32), 0.0).astype(BF)

            def chunk(i, carry, p=p, part=part):
                wide_cols = pl.ds(pl.multiple_of(p * model + i * 256, 256), 256)
                cols = pl.ds(pl.multiple_of(i * 256, 256), 256)
                proj = nn(normed_ref[block], w_qkv_ref[:, wide_cols]) + nn(
                    part, up_cols[:, cols]
                )
                for half in range(2):
                    piece = proj[:, half * 128 : half * 128 + 128]
                    if p < 2:
                        piece = turn(
                            piece, cos_ref[pl.ds(start, tok)], sin_ref[pl.ds(start, tok)], head_dim
                        )
                    if p == 0:
                        q_ref[2 * i + half] = (piece * head_dim ** (-0.5)).astype(BF)
                    else:
                        (k_ref if p == 1 else v_ref)[block, 2 * i + half] = piece.astype(BF)
                return carry

            up_cols = up_ref.at[adapter]
            lax.fori_loop(0, model // 256, chunk, 0)

    project(x_ref[...], ctx, 0)
    half_rows = tok // 2
    halves = [slice(half * half_rows, (half + 1) * half_rows) for half in range(2)]

    def own_pair(i, carry):
        for half, rows in enumerate(halves):
            width = (half + 1) * half_rows
            scores = biased(
                nt(stack_heads(q_ref[i, rows]), k_ref[ctx, i, 0:width]), bias_ref[0, rows, 0:width]
            )
            top = jnp.max(scores, -1, keepdims=True)
            exps = jnp.exp(scores - top)
            acc_ref[i, rows] = join_heads(nn(exps.astype(BF), v_ref[ctx, i, 0:width]))
            top_ref[rows] = put_columns(top_ref[rows], i, top)
            weight_ref[rows] = put_columns(weight_ref[rows], i, jnp.sum(exps, -1, keepdims=True))
        return carry

    def close_pair(i, carry):
        for rows in halves:
            inv = 1.0 / stack_columns(weight_ref[rows], i)
            flat_ref[rows, pl.ds(pl.multiple_of(i * 128, 128), 128)] = (
                acc_ref[i, rows] * join_heads(inv)
            ).astype(BF)
        return carry

    def attend_others():
        others = blocks_of(ctx_n, ctx, ctx_n - 1)
        for j, block in enumerate(others):
            fill_bias(bias_ref, seg_all, ctx, tok, j + 1, block)

        def pair(i, carry):
            for rows in halves:
                q = stack_heads(q_ref[i, rows])
                scores = [
                    biased(nt(q, k_ref[block, i]), bias_ref[j + 1, rows]) for j, block in enumerate(others)
                ]
                before = stack_columns(top_ref[rows], i)
                top = functools.reduce(
                    jnp.maximum, [before] + [jnp.max(part, -1, keepdims=True) for part in scores]
                )
                keep = jnp.exp(before - top)
                exps = [jnp.exp(part - top) for part in scores]
                total = keep * stack_columns(weight_ref[rows], i)
                result = acc_ref[i, rows] * join_heads(keep)
                for part, block in zip(exps, others):
                    total = total + jnp.sum(part, -1, keepdims=True)
                    result = result + join_heads(nn(part.astype(BF), v_ref[block, i]))
                flat_ref[rows, pl.ds(pl.multiple_of(i * 128, 128), 128)] = (
                    result * join_heads(1.0 / total)
                ).astype(BF)
                top_ref[rows] = put_columns(top_ref[rows], i, top)
                weight_ref[rows] = put_columns(weight_ref[rows], i, total)
            return carry

        lax.fori_loop(0, pairs, pair, 0)

    top_ref[...] = jnp.zeros_like(top_ref)
    weight_ref[...] = jnp.ones_like(weight_ref)
    fill_bias(bias_ref, seg_all, ctx, tok, 0, ctx)
    lax.fori_loop(0, pairs, own_pair, 0)
    if ctx_n == 1:
        lax.fori_loop(0, pairs, close_pair, 0)
    else:
        for peer, step, rows_copy, seg_copy in copies:
            @pl.when(from_earlier(step))
            def _(step=step, rows_copy=rows_copy, seg_copy=seg_copy):
                rows_copy.wait_recv()
                seg_copy.wait_recv()
                block = lax.rem(ctx - step + ctx_n, ctx_n)
                project(x_all[block], block, 1)

        if ctx_n == 2:
            @pl.when(ctx == 0)
            def _():
                lax.fori_loop(0, pairs, close_pair, 0)

            pl.when(ctx == 1)(attend_others)
        else:
            attend_others()
        for peer, step, rows_copy, seg_copy in copies:
            @pl.when(to_later(peer))
            def _(rows_copy=rows_copy, seg_copy=seg_copy):
                seg_copy.wait_send()
                rows_copy.wait_send()

    for i, (src, dst) in enumerate(((q_ref, q_out), (k_ref, k_out), (v_ref, v_out), (normed_ref, normed_out))):
        writes.append(pltpu.make_async_copy(src, dst, out_sem.at[1 + i]))
        writes[-1].start()
    total_ref[...] = top_ref[...] + jnp.log(weight_ref[...])
    rank_out = nt(flat_ref[...], down).astype(BF)
    rank_out_ref[...] = rank_out
    part = jnp.where(column == 3, ADAPT_SCALE * rank_out.astype(F32), 0.0).astype(BF)

    def out_chunk(i, carry):
        cols = pl.ds(pl.multiple_of(i * 256, 256), 256)
        mid_ref[:, cols] = (
            x_ref[:, cols].astype(F32)
            + nn(flat_ref[...], w_out_ref[:, cols])
            + nn(part, up_ref[adapter, :, cols])
        )
        return carry

    lax.fori_loop(0, model // 256, out_chunk, 0)
    gain_two = router_ref[17:18].astype(F32)
    step_rows = 128

    def norm_rows(i, carry):
        rows = pl.ds(pl.multiple_of(i * step_rows, step_rows), step_rows)
        mid = mid_ref[rows]
        inv = lax.rsqrt(jnp.mean(mid * mid, -1, keepdims=True) + EPSILON)
        rows_ref[rows] = (mid * inv * gain_two).astype(BF)
        return carry

    lax.fori_loop(0, tok // step_rows, norm_rows, 0)
    kinds = mix_ref.shape[0]
    prev_pad[...] = jnp.zeros_like(prev_pad)
    mix_pad[...] = jnp.zeros_like(mix_pad)
    prev_pad[0:kinds] = prev_ref[...]
    mix_pad[0:kinds, 0:kinds] = mix_ref[...]
    logits_ref[...] = nt(rows_ref[...], router_ref[...]) + lax.dot_general(
        prev_pad[...], mix_pad[...], (((0,), (0,)), ((), ())), precision=HIGH, preferred_element_type=F32
    )
    for write in writes:
        write.wait()
    for copy in dy_copies:
        copy.wait_send()
    for peer in others:
        remote(
            sent_dy.at[0], arrived_dy.at[peer // 2, :, lax.rem(peer, 2)], dy_send.at[0], dy_recv.at[peer], "expert", peer
        ).wait_recv()


def attention_forward(hidden, segments, prev, mix, ids, w_qkv, w_out, down, up, router, dy, routes, experts):
    ctx_n, exp_n = lax.axis_size("context"), lax.axis_size("expert")
    tok, model = hidden.shape
    pairs = model // 128
    wide = down.shape[1]
    cos_table, sin_table = rope_tables(ctx_n * tok, 64)
    vmem, hbm = pl.BlockSpec(memory_space=pltpu.VMEM), pl.BlockSpec(memory_space=pl.ANY)
    dma = pltpu.SemaphoreType.DMA
    many = max(ctx_n - 1, 1)
    shape = jax.ShapeDtypeStruct
    cos_table, sin_table = jnp.asarray(cos_table), jnp.asarray(sin_table)
    return pl.pallas_call(
        functools.partial(attention_kernel, (ctx_n, exp_n, wide // 4)),
        out_shape=(
            shape((pairs, tok, 128), BF),
            shape((ctx_n, pairs, tok, 128), BF),
            shape((ctx_n, pairs, tok, 128), BF),
            shape((ctx_n, tok, model), BF),
            shape((ctx_n, tok, wide), BF),
            shape((tok, 128), F32),
            shape((tok, model), BF),
            shape((tok, wide), BF),
            shape((tok, model), F32),
            shape((tok, model), BF),
            shape((tok, 128), F32),
            shape((ctx_n, 8, tok), jnp.int32),
            shape((exp_n // 2, experts, 2, tok // 4, model), BF),
            shape((8, tok), F32),
        ),
        in_specs=[pl.BlockSpec(memory_space=pltpu.SMEM), hbm]
        + [vmem] * 3
        + [hbm] * 4
        + [vmem]
        + [hbm] * 3
        + [vmem],
        out_specs=(hbm,) * 4 + (vmem,) * 8 + (hbm, vmem),
        scratch_shapes=[
            pltpu.VMEM((ctx_n, tok, model), BF),
            pltpu.VMEM((ctx_n, tok, tok), BF if ctx_n > 2 else F32),
            pltpu.VMEM((exp_n - 1, experts, tok // 4, model), BF),
            pltpu.VMEM((pairs, tok, 128), F32),
            pltpu.VMEM((tok, 128), F32),
            pltpu.VMEM((tok, 128), F32),
            pltpu.VMEM((16, tok), F32),
            pltpu.VMEM((16, 128), F32),
            dma((many,)), dma((many,)), dma((many,)), dma((many,)), dma((exp_n - 1,)), dma((exp_n,)),
            pltpu.VMEM((pairs, tok, 128), BF),
            pltpu.VMEM((ctx_n, pairs, tok, 128), BF),
            pltpu.VMEM((ctx_n, pairs, tok, 128), BF),
            pltpu.VMEM((ctx_n, tok, model), BF),
            pltpu.VMEM((experts, tok // 4, model), BF),
            dma((5,)),
        ]
        + stage_scratch(dy, hidden, down, up, w_qkv, cos_table, sin_table, w_out),
        compiler_params=pltpu.CompilerParams(
            collective_id=2, has_side_effects=True, vmem_limit_bytes=VLIMIT + 5 * 2**19
        ),
        name="attention_forward",
    )(
        ids, hidden, segments, prev, mix, w_qkv, w_out, down, up, router, cos_table, sin_table, dy, routes,
    )


def put_tiles(tiles_ref, first, value):
    for col in range(value.shape[1] // 128):
        tiles_ref[first + col] = value[:, col * 128 : col * 128 + 128].astype(tiles_ref.dtype)


STAGED = 17


def backward_kernel(
    sizes, ids_ref, d_mid_hbm, q_hbm, k_hbm, v_hbm, normed_ref, rank_hbm, total_hbm, flat_hbm,
    rank_out_hbm, x_hbm, seg_hbm, router_hbm, w_qkv_hbm, w_out_hbm, down_hbm, up_hbm, cos_hbm,
    sin_hbm, *rest,
):
    ctx_n, exp_n, rank, fused = sizes
    staged, rest = rest[-STAGED - 1 :], rest[: -STAGED - 1]
    (
        d_mid_ref, up_ref, down_ref, w_out_ref, rank_out_ref, flat_ref, q_ref, k_ref, v_ref, total_ref,
        seg_all, cos_ref, sin_ref, w_qkv_ref, rank_ref, x_ref, router_ref, stage_sem,
    ) = staged
    stages = stage_copies(
        (
            d_mid_hbm, up_hbm, down_hbm, w_out_hbm, rank_out_hbm, flat_hbm, q_hbm, k_hbm, v_hbm,
            total_hbm, seg_hbm, cos_hbm, sin_hbm, w_qkv_hbm, rank_hbm, x_hbm, router_hbm,
        ),
        staged, stage_sem,
    )
    if fused:
        sums_ref, early_ref, done_ref, base_ref, cols_ref = rest[:5]
        grad_ref, table_ref, attn_table, hidden_ref, tiles_ref = rest[5:10]
        scratch, more, results_scratch = rest[10:-31], rest[-31:-5], rest[-5:]
        results = Results(exp_n, done_ref, base_ref, cols_ref, hidden_ref, results_scratch)
        sums = Sums(fused, ids_ref, sums_ref, early_ref, tiles_ref, table_ref, attn_table, more)
    else:
        grad_ref, tiles_ref = rest[:2]
        scratch = rest[2:]
    (
        recv_buf, do_ref, bias_ref, dk_acc, dv_acc, dq_all, dkv_all, send_buf, grad_up, grad_down,
        normed_buf, send_sem, recv_sem, load_sem,
    ) = scratch
    ctx = lax.axis_index("context")
    sequence = lax.axis_index("dp") * exp_n + lax.axis_index("expert")
    tok, model = x_ref.shape
    pairs, head_dim = model // 128, 64
    entered = greet([(axis, lax.axis_size(axis)) for axis in (ALL_AXES if fused else ("context",))])
    for stage in stages[:6]:
        stage.start()
    if fused:
        entered()
        sums.start()
        results.start()
    for stage in stages[6:]:
        stage.start()
    order = [ctx] + blocks_of(ctx_n, ctx, ctx_n - 1)

    def fetch(j):
        return pltpu.make_async_copy(
            normed_ref.at[order[j]], normed_buf.at[min(j, 1)], load_sem.at[min(j, 1)]
        )

    fetch(0).start()
    if ctx_n > 1:
        fetch(1).start()
    for stage in stages[:6]:
        stage.wait()
    adapter = ids_ref[sequence]
    down = down_ref[adapter]
    up = up_ref[adapter]
    wide = down.shape[0]
    column = lax.broadcasted_iota(jnp.int32, (tok, wide), 1) // rank
    d_branch = d_mid_ref[...].astype(BF)
    d_rank_out = jnp.where(column == 3, ADAPT_SCALE * nt(d_branch, up), 0.0).astype(BF)
    twice_out = jnp.where(column == 3, ADAPT_SCALE * rank_out_ref[...].astype(F32), 0.0).astype(BF)
    grad_up[...] = tn(twice_out, d_branch)
    grad_down[...] = tn(d_rank_out, flat_ref[...])

    def attn_chunk(i, carry):
        rows = pl.ds(pl.multiple_of(i * 256, 256), 256)
        d_attn = nt(d_branch, w_out_ref[rows, :]) + nn(d_rank_out, down_ref[adapter, :, rows])
        do_ref[2 * i] = d_attn[:, :128].astype(BF)
        do_ref[2 * i + 1] = d_attn[:, 128:].astype(BF)
        return carry

    lax.fori_loop(0, model // 256, attn_chunk, 0)
    for stage in stages[6:]:
        stage.wait()
    if fused:
        for e in range(sums.experts - 1):
            sums.combine(e)
    half_rows = tok // 2

    steps = []
    if fused:
        steps = [
            functools.partial(sums.forward, e, k) for e in range(sums.experts - 1) for k in range(1, sums.dp_n)
        ]

    def attend(count):
        others = blocks_of(ctx_n, ctx, count)
        for j, block in enumerate([ctx] + others):
            fill_bias(bias_ref, seg_all, ctx, tok, j, block)

        def pair(i, carry):
            cols = pl.ds(pl.multiple_of(i * 128, 128), 128)
            for half in (1, 0):
                rows = slice(half * half_rows, (half + 1) * half_rows)
                q = stack_heads(q_ref[i, rows])
                d_out = stack_heads(do_ref[i, rows])
                total = stack_columns(total_ref[rows], i)
                def terms(j, block, width, i=i, rows=rows, q=q, d_out=d_out, total=total):
                    probs = jnp.exp(
                        biased(nt(q, k_ref[block, i, 0:width]), bias_ref[j, rows, 0:width]) - total
                    )
                    return probs, nt(d_out, v_ref[block, i, 0:width])

                def use(j, block, width, probs, d_probs, delta, i=i, half=half, q=q, d_out=d_out):
                    d_scores = (probs * (d_probs - delta)).astype(BF)
                    d_key = tn(q, d_scores)
                    d_value = tn(d_out, probs.astype(BF))
                    if half == 1:
                        dk_acc[j] = d_key
                        dv_acc[j] = d_value
                    else:
                        dk_acc[j, :, 0:width] += d_key
                        dv_acc[j, :, 0:width] += d_value
                    return nn(d_scores, k_ref[block, i, 0:width])

                width = (half + 1) * half_rows
                own = terms(0, ctx, width)
                delta = jnp.sum(own[0] * own[1], -1, keepdims=True)
                if count < 2:
                    kept = [terms(j + 1, block, tok) for j, block in enumerate(others)]
                    for probs, d_probs in kept:
                        delta = delta + jnp.sum(probs * d_probs, -1, keepdims=True)
                    d_query = use(0, ctx, width, *own, delta)
                    for j, block in enumerate(others):
                        d_query = d_query + use(j + 1, block, tok, *kept[j], delta)
                else:

                    def more_delta(j, delta):
                        probs, d_probs = terms(j, lax.rem(ctx + j, ctx_n), tok)
                        return delta + jnp.sum(probs * d_probs, -1, keepdims=True)

                    delta = lax.fori_loop(1, ctx_n, more_delta, delta)

                    def more_query(j, d_query, delta=delta):
                        block = lax.rem(ctx + j, ctx_n)
                        return d_query + use(j, block, tok, *terms(j, block, tok), delta)

                    d_query = lax.fori_loop(1, ctx_n, more_query, use(0, ctx, width, *own, delta))
                start = pl.multiple_of(ctx * tok + half * half_rows, half_rows)
                d_query = join_heads(d_query) * head_dim ** (-0.5)
                dq_all[rows, cols] = turn(
                    d_query, cos_ref[pl.ds(start, half_rows)], -sin_ref[pl.ds(start, half_rows)], head_dim
                ).astype(BF)
            for j, block in enumerate([ctx] + others):
                start = pl.multiple_of(block * tok, tok)
                d_key = turn(
                    jnp.transpose(dk_acc[j]), cos_ref[pl.ds(start, tok)], -sin_ref[pl.ds(start, tok)], head_dim
                )
                dkv_all[j, 0, :, cols] = d_key.astype(BF)
                dkv_all[j, 1, :, cols] = jnp.transpose(dv_acc[j]).astype(BF)
            for n, step in enumerate(steps):
                pl.when(i == (n + 1) * pairs // (len(steps) + 1))(step)
            return carry

        lax.fori_loop(0, pairs, pair, 0)

    def fold(j, block, first, write):
        normed = normed_buf[min(j, 1)]
        ranks = rank_ref[block].astype(F32)
        d_ranks = jnp.zeros((tok, wide), F32)
        for p in range(first, 3):
            d_proj = dq_all[...] if p == 0 else dkv_all[j, p - 1]
            twice = jnp.where(column == p, ADAPT_SCALE * ranks, 0.0).astype(BF)
            grad_up[...] += tn(twice, d_proj)
            d_ranks = d_ranks + jnp.where(column == p, ADAPT_SCALE * nt(d_proj, up), 0.0)
        d_ranks = d_ranks.astype(BF)
        grad_down[...] += tn(d_ranks, normed)

        def chunk(i, carry):
            rows = pl.ds(pl.multiple_of(i * 256, 256), 256)
            value = nn(d_ranks, down_ref[adapter, :, rows])
            for p in range(first, 3):
                d_proj = dq_all[...] if p == 0 else dkv_all[j, p - 1]
                value = value + nt(d_proj, w_qkv_ref[rows, p * model : (p + 1) * model])
            write(rows, value)
            return carry

        lax.fori_loop(0, model // 256, chunk, 0)

    def write_own(cols, value):
        grad_ref[:, cols] = value

    copies = []
    for step in range(1, ctx_n):
        peer = lax.rem(ctx + step, ctx_n)
        copies.append(
            remote(send_buf, recv_buf.at[step - 1], send_sem.at[step - 1], recv_sem.at[step - 1], "context", peer)
        )

    if ctx_n == 1:
        attend(0)
        sums.combine(sums.experts - 1)
    elif ctx_n == 2:
        @pl.when(ctx == 0)
        def _():
            attend(0)
            sums.combine(sums.experts - 1)

    if not fused:
        entered()

    def spread():
        attend(ctx_n - 1)
        if fused:
            sums.combine(sums.experts - 1)
        for j, block in enumerate(blocks_of(ctx_n, ctx, ctx_n - 1)):
            def write(cols, value):
                send_buf[:, cols] = value.astype(BF)

            fetch(j + 1).wait()
            if j > 0:
                copies[j - 1].wait_send()
            fold(j + 1, block, 1, write)
            copies[j].start()
            if j + 2 < ctx_n:
                fetch(j + 2).start()

    if ctx_n == 2:
        pl.when(ctx == 1)(spread)
        pl.when(ctx == 0)(fetch(1).wait)
    elif ctx_n > 2:
        spread()
    fetch(0).wait()
    fold(0, ctx, 0, write_own)
    per = model // 128
    for p in range(4):
        put_tiles(tiles_ref, p * per, grad_down[p * rank : (p + 1) * rank])
        put_tiles(tiles_ref, (4 + p) * per, grad_up[p * rank : (p + 1) * rank])

    def settle():
        take_shares()
        lax.fori_loop(0, tok // 128, finish, 0)

    def take_shares():
        if ctx_n == 2:
            pl.when(ctx == 0)(copies[0].wait_recv)

            @pl.when(ctx == 1)
            def _():
                recv_buf[...] = jnp.zeros_like(recv_buf)

        elif ctx_n > 2:
            copies[-1].wait_send()
            for step, item in enumerate(copies):
                item.wait_recv()
                load = pltpu.make_async_copy(recv_buf.at[step], send_buf, load_sem.at[0])
                load.start()
                load.wait()
                grad_ref[...] += send_buf[...].astype(F32)

    gain_one = router_ref[16:17].astype(F32)

    def finish(i, carry):
        rows = pl.ds(pl.multiple_of(i * 128, 128), 128)
        value = grad_ref[rows]
        if ctx_n == 2:
            value = value + recv_buf[0, rows].astype(F32)
        x = x_ref[rows].astype(F32)
        inv = lax.rsqrt(jnp.mean(x * x, -1, keepdims=True) + EPSILON)
        scaled = value * gain_one
        grad_ref[rows] = (
            d_mid_ref[rows]
            + inv * scaled
            - x * (inv * inv * inv) * jnp.mean(scaled * x, -1, keepdims=True)
        )
        return carry

    if fused:
        last = sums.experts - 1
        sums.tail(
            [results.combine] + [functools.partial(sums.forward, last, k) for k in range(1, fused[1])] + [settle]
        )
        sums.finish()
        results.finish()
    else:
        settle()
    if ctx_n == 2:
        pl.when(ctx == 1)(copies[0].wait_send)


def attention_backward(d_mid, saved, hidden, ids, router, w_qkv, w_out, down, up, expert_sums, done, experts, width):
    ctx_n, exp_n = lax.axis_size("context"), lax.axis_size("expert")
    tok, model = hidden.shape
    pairs = model // 128
    wide = down.shape[1]
    cos_table, sin_table = rope_tables(ctx_n * tok, 64)
    vmem = pl.BlockSpec(memory_space=pltpu.VMEM)
    dma = pltpu.SemaphoreType.DMA
    many = max(ctx_n - 1, 1)
    shape = jax.ShapeDtypeStruct
    q, k, v, normed, ranks, totals, flat, rank_out, seg_all = saved
    cos_table, sin_table = jnp.asarray(cos_table), jnp.asarray(sin_table)
    staged = (
        d_mid, up, down, w_out, rank_out, flat, q, k, v, totals, seg_all, cos_table, sin_table, w_qkv,
        ranks, hidden, router,
    )
    hbm = pl.BlockSpec(memory_space=pl.ANY)
    spill = ctx_n > 2
    landing = ((many, tok, model), BF)
    attn_tiles, adapters = 8 * pairs, down.shape[0]
    sums_outs, sums_scratch = sums_shapes(experts, model, width, attn_tiles, adapters)
    fused = None
    if not spill:
        fused = tuple(lax.axis_size(axis) for axis in ALL_AXES) + (adapters, attn_tiles)
    tiles_shape = ((attn_tiles, 16, 128), BF)
    results = pl.pallas_call(
        functools.partial(backward_kernel, (ctx_n, exp_n, wide // 4, fused)),
        out_shape=(shape((tok, model), F32),)
        + ((shape(*tiles_shape), shape(*landing)) if spill else sums_outs + (shape((tok, model), BF),)),
        in_specs=[pl.BlockSpec(memory_space=pltpu.SMEM)] + [hbm] * 18 + ([] if spill else [hbm] * 4 + [vmem]),
        out_specs=(vmem, vmem) + ((pl.BlockSpec(memory_space=pl.ANY),) if spill else (vmem, vmem)),
        scratch_shapes=([] if spill else [pltpu.VMEM(*tiles_shape), pltpu.VMEM(*landing)])
        + [
            pltpu.VMEM((pairs, tok, 128), BF),
            pltpu.VMEM((ctx_n, tok, tok), BF if spill else F32),
            pltpu.VMEM((ctx_n, 128, tok), F32),
            pltpu.VMEM((ctx_n, 128, tok), F32),
            pltpu.VMEM((tok, model), BF),
            pltpu.VMEM((ctx_n, 2, tok, model), BF),
            pltpu.VMEM((tok, model), BF),
            pltpu.VMEM((wide, model), F32),
            pltpu.VMEM((wide, model), F32),
            pltpu.VMEM((min(ctx_n, 2), tok, model), BF),
            dma((many,)), dma((many,)), dma((2,)),
        ]
        + ([] if spill else sums_scratch + results_shapes(exp_n, done[0]))
        + stage_scratch(*staged),
        compiler_params=pltpu.CompilerParams(
            collective_id=3, has_side_effects=True, vmem_limit_bytes=VLIMIT + 5 * 2**19
        ),
        name="attention_backward",
    )(
        ids, d_mid, q, k, v, normed, ranks, totals, flat, rank_out, hidden, seg_all,
        router, w_qkv, w_out, down, up, cos_table, sin_table, *([] if spill else [*expert_sums, *done]),
    )
    if spill:
        sums = add_up(ids, expert_sums, results[1], experts, width, adapters)
        return (results[0],) + tuple(sums) + (return_results(done),)
    return results


def partners(exp_n, me):
    core = lax.rem(me, 2)
    twin = me + 1 - 2 * core
    far = []
    for step in range(2, exp_n, 2):
        far += [lax.rem(me + step, exp_n), lax.rem(twin + step, exp_n)]
    return far + [twin]


def hot_rows(slot_rows, first, count):
    target = first + lax.broadcasted_iota(jnp.int32, (count, slot_rows.shape[1]), 0)
    return target == slot_rows


def moe_kernel(
    sizes, ids_ref, rows_ref, mid_hbm, logits_ref, slots_ref, dy_hbm, arrived_hbm, router_ref, mix_ref,
    vec_ref, gate_up_hbm, down_hbm, in_down_hbm, in_up_hbm, out_down_hbm, out_up_hbm,
    base_ref, d_mid_ref, grad_prev_ref, sums_ref, early_ref, done_out, cols_ref, part_z,
    d_logits_ref, mix_pad, done_gate, back_gate, tiles_ref, arrived_x, gate_up_ref, w_down_ref, sent_rows, sent_gates, arrived_rows, arrived_gates, act_ref, d_pre_ref,
    done_rows, back_rows, gates_ref,
    weight_sem, row_send, row_recv, gate_send, gate_recv, out_send, out_recv, in_send, in_recv,
    x_send, x_recv, z_send, z_recv, *staged,
):
    in_down_ref, in_up_ref, out_down_ref, out_up_ref, arrived_dy, mid_ref, dy_ref, stage_sem = staged
    stages = stage_copies(
        (in_down_hbm, in_up_hbm, out_down_hbm, out_up_hbm, arrived_hbm, mid_hbm, dy_hbm), staged, stage_sem
    )
    ctx_n, dp_n, exp_n, kinds, rank, share = sizes
    ctx, dp = lax.axis_index("context"), lax.axis_index("dp")
    me = lax.axis_index("expert")
    my_chip, my_core = me // 2, lax.rem(me, 2)
    first_seq = lax.axis_index("dp") * exp_n
    tok, model = rows_ref.shape
    experts, width = w_down_ref.shape[:2]
    capacity = arrived_rows.shape[3]
    per_owner = experts * capacity
    both = 2 * capacity
    entered = greet([("expert", exp_n), ("context", ctx_n), ("dp", dp_n)])
    loads = []
    for e in range(experts):
        for hbm, ref, k in ((gate_up_hbm, gate_up_ref, 0), (down_hbm, w_down_ref, 1)):
            load = pltpu.make_async_copy(hbm.at[e], ref.at[e], weight_sem.at[e, k])
            load.start()
            loads.append(load)
        if e == 0:
            for stage in stages:
                stage.start()

    lane = lax.broadcasted_iota(jnp.int32, (tok, 128), 1)
    logits = logits_ref[...]
    masked = jnp.where(lane < kinds, logits, NEG)
    exps = jnp.exp(masked - jnp.max(masked, -1, keepdims=True))
    probs = exps / jnp.sum(exps, -1, keepdims=True)
    slot_cols = jnp.transpose(
        jnp.concatenate([slots_ref[...], jnp.zeros((120, tok), F32)], 0)
    )
    gates = [
        jnp.sum(jnp.where(lane == slot_cols[:, k : k + 1].astype(jnp.int32), probs, 0.0), -1, keepdims=True)
        for k in range(2)
    ]
    gates_ref[...] = jnp.where(lane == 0, gates[0], jnp.where(lane == 1, gates[1], 0.0))
    cols_ref[...] = jnp.where(lane == 4, gates[0], jnp.where(lane == 5, gates[1], slot_cols))
    gate_rows = jnp.transpose(gates_ref[...])
    parts = []
    sub = lax.broadcasted_iota(jnp.int32, (16, tok), 0)
    for k in range(2):
        whole = jnp.broadcast_to(gate_rows[k : k + 1], (16, tok))
        high = whole.astype(BF).astype(F32)
        middle = (whole - high).astype(BF).astype(F32)
        lowest = whole - high - middle
        parts.append(
            jnp.where(sub == 0, high, jnp.where(sub == 1, middle, jnp.where(sub == 2, lowest, 0.0))).astype(BF)
        )
    slot_rows = [slots_ref[2 + k : 3 + k].astype(jnp.int32) for k in range(2)]

    def pick(owner, e):
        hots = [hot_rows(slot_rows[k], owner * per_owner + e * capacity, capacity) for k in range(2)]
        hot = jnp.where(hots[0] | hots[1], 1.0, 0.0).astype(BF)
        gates = sum(nt(parts[k], jnp.where(hots[k], 1.0, 0.0).astype(BF)) for k in range(2))
        return gates.astype(BF), nn(hot, rows_ref[...]).astype(BF)

    entered()
    sends = []
    others = partners(exp_n, me)
    for e in range(experts):
        for i, peer in enumerate(others):
            sent_gates[i, e], sent_rows[i, e] = pick(peer, e)
            for src, dst, send, recv in (
                (sent_gates, arrived_gates, gate_send, gate_recv),
                (sent_rows, arrived_rows, row_send, row_recv),
            ):
                copy = remote(
                    src.at[i, e], dst.at[my_chip, e, my_core], send.at[i, e], recv.at[me, e], "expert", peer
                )
                copy.start()
                sends.append(copy)
        arrived_gates[my_chip, e, my_core], arrived_rows[my_chip, e, my_core] = pick(me, e)

    def arrive(source, e):
        for ref, src, send, recv in (
            (arrived_gates, sent_gates, gate_send, gate_recv),
            (arrived_rows, sent_rows, row_send, row_recv),
        ):
            remote(
                src.at[0, e], ref.at[source // 2, e, lax.rem(source, 2)], send.at[0, e], recv.at[source, e],
                "expert", source,
            ).wait_recv()

    row64 = lax.broadcasted_iota(jnp.int32, (both, 4 * rank), 0) // capacity
    col64 = lax.broadcasted_iota(jnp.int32, (both, 4 * rank), 1)
    mine64 = row64 == col64 // (2 * rank)
    is_gate = col64 % (2 * rank) < rank
    mine32 = lax.broadcasted_iota(jnp.int32, (both, 2 * rank), 0) // capacity == (
        lax.broadcasted_iota(jnp.int32, (both, 2 * rank), 1) // rank
    )
    step_cols = 512
    per_step = step_cols // 128
    across, deep = model // 128, width // 128
    first_up = 2 * across
    first_out = first_up + 2 * deep
    first_last = first_out + deep

    def put(source, e, tile, value):
        tiles_ref[source, tile // share, e * share + tile % share] = value

    def x_copies(chip, e):
        copies = []
        for step in range(1, ctx_n):
            peer = lax.rem(ctx + step, ctx_n)
            here = pl.ds(e * share, share)
            copies.append(
                remote(
                    tiles_ref.at[pl.ds(2 * chip, 2), peer, here],
                    arrived_x.at[step - 1, pl.ds(2 * chip, 2), here],
                    x_send.at[step - 1, chip, e], x_recv.at[step - 1, chip, e], "context", peer,
                )
            )
        return copies

    def work(chip, e):
        names = [ids_ref[first_seq + 2 * chip + core] for core in range(2)]

        def stack(ref, cols=slice(None)):
            return jnp.concatenate([ref[name, e, :, cols] for name in names], 0)

        rows = arrived_rows[chip, e].reshape(both, model)
        in_down = stack(in_down_ref)
        out_up = stack(out_up_ref)
        gate = []
        for core in range(2):
            piece = arrived_gates[chip, e, core].astype(F32)
            total = piece[0:1] + piece[1:2] + piece[2:3]
            gate.append(jnp.transpose(jnp.broadcast_to(total, (128, capacity)))[:, 0:1])
        gate = jnp.concatenate(gate, 0)
        d_out = (gate * arrived_dy[chip, e].reshape(both, model).astype(F32)).astype(BF)
        ranks = jnp.where(mine64, nt(rows, in_down), 0.0).astype(BF)
        twice = ADAPT_SCALE * ranks.astype(F32)
        twice_gate = jnp.where(is_gate, twice, 0.0).astype(BF)
        twice_up = jnp.where(is_gate, 0.0, twice).astype(BF)
        d_mid_rank = jnp.where(mine32, ADAPT_SCALE * nt(d_out, out_up), 0.0).astype(BF)

        def chunk(i, carry):
            rank_mid, d_rank = carry
            start = pl.multiple_of(i * step_cols, step_cols)
            cols = pl.ds(start, step_cols)
            up_cols = pl.ds(pl.multiple_of(width + i * step_cols, step_cols), step_cols)
            in_up = stack(in_up_ref, cols)
            out_down = stack(out_down_ref, cols)
            gate_pre = nn(rows, gate_up_ref[e, :, cols]) + nn(twice_gate, in_up)
            up_pre = nn(rows, gate_up_ref[e, :, up_cols]) + nn(twice_up, in_up)
            d_act = (nt(d_out, w_down_ref[e, cols, :]) + nn(d_mid_rank, out_down)).astype(BF).astype(F32)
            sigma = 1.0 / (1.0 + jnp.exp(-gate_pre))
            silu = gate_pre * sigma
            act = (silu * up_pre).astype(BF)
            d_gate = (d_act * up_pre * sigma * (1.0 + gate_pre * (1.0 - sigma))).astype(BF)
            d_up = (d_act * silu).astype(BF)
            act_ref[:, cols] = act
            d_pre_ref[:, cols] = d_gate
            d_pre_ref[:, up_cols] = d_up
            rank_mid = rank_mid + nt(act, out_down)
            d_rank = d_rank + jnp.where(is_gate, nt(d_gate, in_up), nt(d_up, in_up))
            grad_up = (tn(twice_gate, d_gate) + tn(twice_up, d_up)).astype(BF)
            grad_out = tn(d_mid_rank, act).astype(BF)
            for core in range(2):
                for t in range(per_step):
                    here = slice(t * 128, t * 128 + 128)
                    tile = i * per_step + t
                    for which in range(2):
                        first = (2 * core + which) * rank
                        put(
                            2 * chip + core, e, first_up + which * deep + tile,
                            grad_up[first : first + rank, here],
                        )
                    put(
                        2 * chip + core, e, first_out + tile,
                        grad_out[core * rank : (core + 1) * rank, here],
                    )
            return rank_mid, d_rank

        rank_mid, d_rank = lax.fori_loop(
            0, width // step_cols, chunk,
            (jnp.zeros((both, 2 * rank), F32), jnp.zeros((both, 4 * rank), F32)),
        )
        twice_mid = jnp.where(
            mine32, ADAPT_SCALE * rank_mid.astype(BF).astype(F32), 0.0
        ).astype(BF)

        def out_chunk(i, carry):
            cols = pl.ds(pl.multiple_of(i * 256, 256), 256)
            value = nn(act_ref[...], w_down_ref[e, :, cols]) + nn(twice_mid, stack(out_up_ref, cols))
            for core in range(2):
                done_out[chip, e, core, :, cols] = value[core * capacity : (core + 1) * capacity].astype(BF)
            return carry

        lax.fori_loop(0, model // 256, out_chunk, 0)
        for core in range(2):
            d_gate = jnp.sum(
                arrived_dy[chip, e, core].astype(F32) * done_out[chip, e, core].astype(F32), -1, keepdims=True
            )
            done_gate[chip, e, core] = jnp.transpose(jnp.broadcast_to(d_gate, (capacity, 128)))[0:8]
        give_back(chip, e, done_gate, back_gate, out_send, out_recv)
        d_rank_in = jnp.where(mine64, ADAPT_SCALE * d_rank, 0.0).astype(BF)

        def in_chunk(i, carry):
            cols = pl.ds(pl.multiple_of(i * 256, 256), 256)
            value = nt(d_pre_ref[...], gate_up_ref[e, cols, :]) + nn(d_rank_in, stack(in_down_ref, cols))
            for core in range(2):
                done_rows[chip, e, core, :, cols] = value[core * capacity : (core + 1) * capacity].astype(BF)
            return carry

        lax.fori_loop(0, model // 256, in_chunk, 0)
        give_back(chip, e, done_rows, back_rows, in_send, in_recv)
        grad_last = tn(twice_mid, d_out).astype(BF)
        grad_first = tn(d_rank_in, rows).astype(BF)
        for core in range(2):
            for t in range(across):
                here = slice(t * 128, t * 128 + 128)
                for which in range(2):
                    first = (2 * core + which) * rank
                    put(
                        2 * chip + core, e, which * across + t, grad_first[first : first + rank, here]
                    )
                put(
                    2 * chip + core, e, first_last + t,
                    grad_last[core * rank : (core + 1) * rank, here],
                )
        for copy in x_copies(chip, e):
            copy.start()

    def give_back(chip, e, done, back, send, recv):
        for core in range(2):
            target = 2 * chip + core
            copy = remote(
                done.at[chip, e, core], back.at[me * experts + e], send.at[target, e], recv.at[me, e],
                "expert", target,
            )

            @pl.when(target == me)
            def _(core=core):
                back[me * experts + e] = done[chip, e, core]

            @pl.when(target != me)
            def _(copy=copy):
                copy.start()

    def own_work(e):
        arrive(others[-1], e)
        work(my_chip, e)

    def gather(e, out_ref):
        for chip in range(exp_n // 2):
            for copy in x_copies(chip, e):
                copy.wait_recv()

        def add(tile, carry):
            here = pl.ds(e * share + tile, 1)
            total = tiles_ref[:, ctx, here].astype(F32)
            for step in range(1, ctx_n):
                total = total + arrived_x[step - 1, :, here].astype(F32)
            out_ref[:, pl.ds(tile, 1)] = total.astype(BF)
            return carry

        lax.fori_loop(0, share, add, 0)

    z_tiles = early_ref.shape[3]
    z_copies = []
    for load in loads[:2]:
        load.wait()
    for stage in stages[:5]:
        stage.wait()
    own_work(0)
    for e in range(experts):
        if e > 0:
            for load in loads[2 * e : 2 * e + 2]:
                load.wait()
        for step in range(1, exp_n // 2):
            arrive(others[2 * step - 2], e)
            arrive(others[2 * step - 1], e)
            work(lax.rem(my_chip + step, exp_n // 2), e)
    for e in range(experts - 1):
        if e > 0:
            own_work(e)
        gather(e, part_z.at[e])
        early_ref[e, 0] = part_z[e, :, pl.ds(dp * z_tiles, z_tiles)]
        for k in range(1, dp_n):
            peer = lax.rem(dp + k, dp_n)
            copy = remote(
                part_z.at[e, :, pl.ds(peer * z_tiles, z_tiles)], early_ref.at[e, k], z_send.at[e, k], z_recv.at[e, k],
                "dp", peer,
            )
            copy.start()
            z_copies.append(copy)

    if experts > 1:
        own_work(experts - 1)
    for stage in stages[5:]:
        stage.wait()

    def collect(done, back, send, recv):
        for owner in others:
            for e in range(experts):
                remote(
                    done.at[0, e, 0], back.at[owner * experts + e], send.at[owner, e], recv.at[owner, e],
                    "expert", owner,
                ).wait_recv()

    slots_total = exp_n * per_owner
    block = 256

    def hot_cols(rows):
        target = lax.broadcasted_iota(jnp.int32, (block, slots_total), 1)
        return [target == cols_ref[rows, 2 + k : 3 + k].astype(jnp.int32) for k in range(2)]

    gain = router_ref[17:18].astype(F32)
    lanes = lax.broadcasted_iota(jnp.int32, (block, 128), 1)
    ffn_kinds = exp_n * experts

    def outward(i, carry):
        rows = pl.ds(pl.multiple_of(i * block, block), block)
        hots = hot_cols(rows)
        mid = mid_ref[rows]
        dy = dy_ref[rows].astype(F32)
        normed = mid * lax.rsqrt(jnp.mean(mid * mid, -1, keepdims=True) + EPSILON) * gain
        logits = logits_ref[rows]
        masked = jnp.where(lanes < kinds, logits, NEG)
        exps = jnp.exp(masked - jnp.max(masked, -1, keepdims=True))
        probs = exps / jnp.sum(exps, -1, keepdims=True)
        pairs = []
        for c in range(2):
            one, two = logits[:, kinds + 2 * c : kinds + 2 * c + 1], logits[:, kinds + 2 * c + 1 : kinds + 2 * c + 2]
            pairs.append((1.0 / (1.0 + jnp.exp(two - one)), 1.0 / (1.0 + jnp.exp(one - two))))
        along = jnp.sum(dy * normed, -1, keepdims=True)
        across_vec = [jnp.sum(dy * vec_ref[c : c + 1].astype(F32), -1, keepdims=True) for c in range(2)]
        d_kinds = jnp.zeros((block, 128), F32)
        dy_scale = jnp.zeros((block, 1), F32)
        weights = [jnp.zeros((block, 1), F32)] * 2
        for k in range(2):
            kind = cols_ref[rows, k : k + 1].astype(jnp.int32)
            gate = gates_ref[rows, k : k + 1]
            scale = jnp.where(kind == ffn_kinds + 1, 1.0, 0.0)
            picked = jnp.zeros((block, 128), F32)
            for owner in range(exp_n * experts):
                hot = hots[k][:, owner * capacity : (owner + 1) * capacity]
                picked = picked + jnp.where(hot, back_gate[owner, 0:1], 0.0)
            d_gate = jnp.sum(picked, -1, keepdims=True)
            for c in range(2):
                here = jnp.where(kind == ffn_kinds + 2 + c, 1.0, 0.0)
                scale = scale + here * pairs[c][0]
                d_gate = d_gate + here * pairs[c][1] * across_vec[c]
                weights[c] = weights[c] + here * gate
            d_gate = d_gate + scale * along
            dy_scale = dy_scale + gate * scale
            d_kinds = d_kinds + jnp.where(lanes == kind, d_gate, 0.0)
        base = mid + dy_scale * normed
        for c in range(2):
            base = base + (weights[c] * pairs[c][1]) * vec_ref[c : c + 1].astype(F32)
        base_ref[rows] = base
        d_logits = probs * (d_kinds - jnp.sum(probs * d_kinds, -1, keepdims=True))
        for c in range(2):
            d_one = weights[c] * along
            d_two = weights[c] * across_vec[c]
            mean = pairs[c][0] * d_one + pairs[c][1] * d_two
            d_logits = jnp.where(lanes == kinds + 2 * c, pairs[c][0] * (d_one - mean), d_logits)
            d_logits = jnp.where(lanes == kinds + 2 * c + 1, pairs[c][1] * (d_two - mean), d_logits)
        d_logits_ref[rows] = d_logits
        high = d_logits.astype(BF)
        rest = d_logits - high.astype(F32)
        middle = rest.astype(BF)
        lowest = (rest - middle.astype(F32)).astype(BF)
        router = router_ref[...]
        d_mid_ref[rows] = dy_scale * dy + (nn(high, router) + nn(middle, router) + nn(lowest, router))
        return carry

    def inward(i, carry):
        rows = pl.ds(pl.multiple_of(i * block, block), block)
        hots = hot_cols(rows)
        table = back_rows[...].reshape(slots_total, model)
        hot = jnp.where(hots[0] | hots[1], 1.0, 0.0).astype(BF)
        scaled = (d_mid_ref[rows] + nn(hot, table)) * gain
        mid = mid_ref[rows]
        inv = lax.rsqrt(jnp.mean(mid * mid, -1, keepdims=True) + EPSILON)
        d_mid_ref[rows] = (
            dy_ref[rows].astype(F32)
            + inv * scaled
            - mid * (inv * inv * inv) * jnp.mean(scaled * mid, -1, keepdims=True)
        )
        return carry

    collect(done_gate, back_gate, out_send, out_recv)
    lax.fori_loop(0, tok // block, outward, 0)
    mix_pad[...] = jnp.zeros_like(mix_pad)
    mix_pad[0:kinds, 0:kinds] = mix_ref[...]
    grad_prev = lax.dot_general(
        mix_pad[...], d_logits_ref[...], (((1,), (1,)), ((), ())), precision=HIGH, preferred_element_type=F32
    )
    for kind in range(kinds):
        grad_prev_ref[kind] = grad_prev[kind : kind + 1]
    collect(done_rows, back_rows, in_send, in_recv)
    lax.fori_loop(0, tok // block, inward, 0)
    gather(experts - 1, sums_ref)
    for chip in range(exp_n // 2):
        for e in range(experts):
            for copy in x_copies(chip, e):
                copy.wait_send()
    for copy in z_copies:
        copy.wait()
    for copy in sends:
        copy.wait_send()
    for target in others:
        for e in range(experts):
            for done, back, send, recv in (
                (done_gate, back_gate, out_send, out_recv),
                (done_rows, back_rows, in_send, in_recv),
            ):
                remote(
                    done.at[0, e, 0], back.at[0], send.at[target, e], recv.at[target, e],
                    "expert", target,
                ).wait_send()


def expert_tiling(experts, model, width):
    share = pl.cdiv(3 * (model + width) // 128, lax.axis_size("context"))
    z_tiles = pl.cdiv(share, lax.axis_size("dp"))
    return share, z_tiles * lax.axis_size("dp"), z_tiles


def attn_tiling(attn_tiles):
    own = attn_tiles // lax.axis_size("expert")
    x_tiles = pl.cdiv(own, lax.axis_size("context"))
    return own, x_tiles, pl.cdiv(x_tiles, lax.axis_size("dp"))


def expert_layer(rows, mid, logits, slots, dy, arrived_dy, ids, router, mix, vec, w_gate_up, w_down, tables):
    exp_n = lax.axis_size("expert")
    tok, model = rows.shape
    experts, width = w_down.shape[:2]
    capacity = tok // 4
    rank = tables[3].shape[2]
    ctx_n = lax.axis_size("context")
    dp_n = lax.axis_size("dp")
    share, x_tiles, z_tiles = expert_tiling(experts, model, width)
    many, before = max(ctx_n - 1, 1), max(experts - 1, 1)
    chips = exp_n // 2
    vmem = pl.BlockSpec(memory_space=pltpu.VMEM)
    hbm = pl.BlockSpec(memory_space=pl.ANY)
    dma = pltpu.SemaphoreType.DMA
    shape = jax.ShapeDtypeStruct
    block = (experts, capacity, model)
    kinds = mix.shape[0]
    return pl.pallas_call(
        functools.partial(moe_kernel, (ctx_n, dp_n, exp_n, kinds, rank, share)),
        out_shape=(
            shape((tok, model), F32),
            shape((tok, model), F32),
            shape((kinds, 1, tok), F32),
            shape((exp_n, x_tiles, 16, 128), BF),
            shape((before, dp_n, exp_n, z_tiles, 16, 128), BF),
            shape((chips, experts, 2, capacity, model), BF),
            shape((tok, 128), F32),
        ),
        in_specs=[pl.BlockSpec(memory_space=pltpu.SMEM), vmem, hbm, vmem, vmem, hbm, hbm]
        + [vmem] * 3
        + [hbm] * 6,
        out_specs=(vmem,) * 7,
        scratch_shapes=[
            pltpu.VMEM((before, exp_n, x_tiles, 16, 128), BF),
            pltpu.VMEM((tok, 128), F32),
            pltpu.VMEM((16, 128), F32),
            pltpu.VMEM((chips, experts, 2, 8, 128), F32),
            pltpu.VMEM((exp_n * experts, 8, 128), F32),
            pltpu.VMEM((exp_n, ctx_n, experts * share, 16, 128), BF),
            pltpu.VMEM((many, exp_n, experts * share, 16, 128), BF),
            pltpu.VMEM((experts, model, 2 * width), BF),
            pltpu.VMEM((experts, width, model), BF),
            pltpu.VMEM((exp_n - 1,) + block, BF),
            pltpu.VMEM((exp_n - 1, experts, 16, capacity), BF),
            pltpu.VMEM((chips, experts, 2, capacity, model), BF),
            pltpu.VMEM((chips, experts, 2, 16, capacity), BF),
            pltpu.VMEM((2 * capacity, width), BF),
            pltpu.VMEM((2 * capacity, 2 * width), BF),
            pltpu.VMEM((chips, experts, 2, capacity, model), BF),
            pltpu.VMEM((exp_n * experts, capacity, model), BF),
            pltpu.VMEM((tok, 128), F32),
            dma((experts, 2)), dma((exp_n - 1, experts)), dma((exp_n, experts)), dma((exp_n - 1, experts)),
            dma((exp_n, experts)),
            dma((exp_n, experts)), dma((exp_n, experts)), dma((exp_n, experts)), dma((exp_n, experts)),
            dma((many, chips, experts)), dma((many, chips, experts)), dma((before, dp_n)), dma((before, dp_n)),
        ]
        + stage_scratch(*tables, arrived_dy, mid, dy),
        compiler_params=pltpu.CompilerParams(
            collective_id=4, has_side_effects=True, vmem_limit_bytes=VLIMIT
        ),
        name="expert_layer",
    )(
        ids, rows, mid, logits, slots, dy, arrived_dy, router, mix, vec, w_gate_up,
        w_down, *tables,
    )


def stage_copies(sources, targets, sem):
    return [
        pltpu.make_async_copy(src, dst, sem.at[i]) for i, (src, dst) in enumerate(zip(sources, targets))
    ]


def stage_scratch(*arrays):
    return [pltpu.VMEM(array.shape, array.dtype) for array in arrays] + [
        pltpu.SemaphoreType.DMA((len(arrays),))
    ]


class Results:
    def __init__(self, exp_n, done_ref, base_ref, cols_ref, hidden_ref, scratch):
        self.done_ref, self.base_ref, self.cols_ref, self.hidden_ref = done_ref, base_ref, cols_ref, hidden_ref
        self.back_ref, self.base_buf, self.send_sem, self.recv_sem, own_sem = scratch
        self.me = lax.axis_index("expert")
        self.experts = done_ref.shape[1]
        self.others = partners(exp_n, self.me)
        self.own = [
            pltpu.make_async_copy(
                done_ref.at[self.me // 2, e, lax.rem(self.me, 2)], self.back_ref.at[self.me * self.experts + e],
                own_sem.at[e],
            )
            for e in range(self.experts)
        ] + [pltpu.make_async_copy(base_ref, self.base_buf, own_sem.at[self.experts])]

    def copy(self, other, e, owner):
        return remote(
            self.done_ref.at[other // 2, e, lax.rem(other, 2)], self.back_ref.at[owner * self.experts + e],
            self.send_sem.at[other, e], self.recv_sem.at[owner, e], "expert", other,
        )

    def start(self):
        for other in self.others:
            for e in range(self.experts):
                self.copy(other, e, self.me).start()
        for copy in self.own:
            copy.start()

    def combine(self):
        for copy in self.own:
            copy.wait()
        for other in self.others:
            for e in range(self.experts):
                self.copy(other, e, other).wait_recv()
        tok, model = self.base_ref.shape
        slots = self.back_ref.shape[0] * self.back_ref.shape[1]
        block = 256

        def rows_out(i, carry):
            rows = pl.ds(pl.multiple_of(i * block, block), block)
            table = self.back_ref[...].reshape(slots, model)
            target = lax.broadcasted_iota(jnp.int32, (block, slots), 1)
            total = self.base_buf[rows]
            for k in range(2):
                slot = self.cols_ref[rows, 2 + k : 3 + k].astype(jnp.int32)
                gate = self.cols_ref[rows, 4 + k : 5 + k]
                total = total + gate * nn(jnp.where(target == slot, 1.0, 0.0).astype(BF), table)
            self.hidden_ref[rows] = total.astype(BF)
            return carry

        lax.fori_loop(0, tok // block, rows_out, 0)

    def finish(self):
        for other in self.others:
            for e in range(self.experts):
                self.copy(other, e, self.me).wait_send()


def results_shapes(exp_n, done):
    _, experts, _, capacity, model = done.shape
    dma = pltpu.SemaphoreType.DMA
    return [
        pltpu.VMEM((exp_n * experts, capacity, model), BF), pltpu.VMEM((4 * capacity, model), F32),
        dma((exp_n, experts)), dma((exp_n, experts)), dma((experts + 1,)),
    ]


def results_kernel(exp_n, done_ref, base_ref, cols_ref, hidden_ref, *scratch):
    greet([("expert", exp_n)])()
    results = Results(exp_n, done_ref, base_ref, cols_ref, hidden_ref, scratch)
    results.start()
    results.combine()
    results.finish()


def return_results(done):
    exp_n = lax.axis_size("expert")
    vmem = pl.BlockSpec(memory_space=pltpu.VMEM)
    return pl.pallas_call(
        functools.partial(results_kernel, exp_n),
        out_shape=jax.ShapeDtypeStruct(done[1].shape, BF),
        in_specs=[pl.BlockSpec(memory_space=pl.ANY)] * 2 + [vmem],
        out_specs=vmem,
        scratch_shapes=results_shapes(exp_n, done[0]),
        compiler_params=pltpu.CompilerParams(
            collective_id=5, has_side_effects=True, vmem_limit_bytes=VLIMIT
        ),
        name="return_results",
    )(*done)


class Sums:
    def __init__(self, sizes, ids_ref, sums_ref, early_ref, attn_ref, table_ref, attn_table, scratch):
        self.ctx_n, self.dp_n, self.exp_n, self.adapters, self.attn_tiles = sizes
        self.ids_ref, self.attn_ref = ids_ref, attn_ref
        self.table_ref, self.attn_table = table_ref, attn_table
        self.ctx, self.dp, self.exp = (lax.axis_index(axis) for axis in ALL_AXES)
        (
            self.arrived_z, self.early, self.held_a, self.arrived_xa, self.part_a, self.arrived_za,
            self.z_send, self.z_recv, self.az_send, self.az_recv, self.ax_send, self.ax_recv,
            self.r_send, self.r_recv, self.xa_send, self.xa_recv, self.za_send, self.za_recv,
            self.bz_send, self.bz_recv, self.bx_send, self.bx_recv, self.be_send, self.be_recv,
            self.keep_sem, load_sem,
        ) = scratch
        self.waits = []
        z_tiles = self.arrived_z.shape[2]
        self.experts = table_ref.shape[2]
        self.loads = [
            pltpu.make_async_copy(early_ref, self.early, load_sem.at[0]),
            pltpu.make_async_copy(
                sums_ref.at[:, pl.ds(self.dp * z_tiles, z_tiles)], self.arrived_z.at[0], load_sem.at[1]
            ),
        ]
        self.z_copies = [
            self.plan(
                sums_ref.at[:, pl.ds(self.peer("dp", k) * z_tiles, z_tiles)], self.arrived_z.at[k],
                self.z_send.at[k - 1], self.z_recv.at[k - 1], "dp", self.peer("dp", k),
            )
            for k in range(1, self.dp_n)
        ]
        self.az_copies, self.ax_copies = [], []
        for e in range(self.experts):
            here = table_ref.at[self.ctx, self.dp, e]
            self.az_copies.append(
                [
                    self.plan(
                        here, here, self.az_send.at[e, k - 1], self.az_recv.at[e, k - 1], "dp", self.peer("dp", k)
                    )
                    for k in range(1, self.dp_n)
                ]
            )
            self.ax_copies.append([])
            for k in range(self.dp_n):
                here = table_ref.at[self.ctx, lax.rem(self.dp - k + self.dp_n, self.dp_n), e]
                self.ax_copies[e].append(
                    [
                        self.plan(
                            here, here, self.ax_send.at[step - 1, e, k], self.ax_recv.at[step - 1, e, k],
                            "context", self.peer("context", step),
                        )
                        for step in range(1, self.ctx_n)
                    ]
                )

    def plan(self, src, dst, send, recv, axis, target):
        copy = remote(src, dst, send, recv, axis, target)
        self.waits.append(copy)
        return copy

    def peer(self, axis, step):
        index, size = {
            "context": (self.ctx, self.ctx_n), "dp": (self.dp, self.dp_n), "expert": (self.exp, self.exp_n)
        }[axis]
        return lax.rem(index + step, size)

    def send(self, src, dst, send, recv, axis, target):
        copy = self.plan(src, dst, send, recv, axis, target)
        copy.start()
        return copy

    def weight(self, k, source):
        origin = lax.rem(self.dp - k + self.dp_n, self.dp_n)
        name = self.ids_ref[origin * self.exp_n + source]
        return [jnp.where(name == a, 1.0, 0.0).astype(F32) for a in range(self.adapters)]

    def merge(self, count, read, write):
        marks = [self.weight(k, source) for k in range(self.dp_n) for source in range(self.exp_n)]

        def tile_sums(tile, carry):
            totals = [jnp.zeros((16, 128), F32)] * self.adapters
            for k in range(self.dp_n):
                for source in range(self.exp_n):
                    value = read(k, source, tile).astype(F32)
                    mark = marks[k * self.exp_n + source]
                    totals = [total + m * value for total, m in zip(totals, mark)]
            for a in range(self.adapters):
                write(a, tile, totals[a].astype(BF))
            return carry

        lax.fori_loop(0, count, tile_sums, 0)

    def start(self):
        for copy in self.loads + self.z_copies:
            copy.start()

    def combine(self, e):
        z_tiles = self.arrived_z.shape[2]
        if e < self.experts - 1:
            if e == 0:
                self.loads[0].wait()
            source_ref = self.early.at[e]
        else:
            if self.experts == 1:
                self.loads[0].wait()
            self.loads[1].wait()
            for copy in self.z_copies:
                copy.wait_recv()
            source_ref = self.arrived_z

        def write(a, tile, value):
            self.table_ref[self.ctx, self.dp, e, a, tile] = value

        self.merge(z_tiles, lambda k, source, tile: source_ref[k, source, tile], write)
        for copy in self.az_copies[e]:
            copy.start()
        self.forward(e, 0)

    def forward(self, e, k):
        if k > 0:
            self.az_copies[e][k - 1].wait_recv()
        for copy in self.ax_copies[e][k]:
            copy.start()

    def tail(self, between):
        between = list(between)

        def other():
            if between:
                between.pop(0)()

        own, x_tiles, z_tiles = attn_tiling(self.attn_tiles)
        real = pl.cdiv(x_tiles, z_tiles)
        keep = pltpu.make_async_copy(
            self.attn_ref.at[pl.ds(self.exp * own, own)], self.held_a.at[self.exp, pl.ds(0, own)], self.keep_sem
        )
        keep.start()
        copies = [
            self.send(
                self.attn_ref.at[pl.ds(self.peer("expert", k) * own, own)],
                self.held_a.at[self.exp, pl.ds(0, own)],
                self.r_send.at[k - 1], self.r_recv.at[k - 1], "expert", self.peer("expert", k),
            )
            for k in range(1, self.exp_n)
        ]
        other()
        keep.wait()
        for copy in copies:
            copy.wait_recv()
        copies = [
            self.send(
                self.held_a.at[:, pl.ds(self.peer("context", k) * x_tiles, x_tiles)], self.arrived_xa.at[k - 1],
                self.xa_send.at[k - 1], self.xa_recv.at[k - 1], "context", self.peer("context", k),
            )
            for k in range(1, self.ctx_n)
        ]
        for copy in copies:
            copy.wait_recv()
        total = self.held_a[:, pl.ds(self.ctx * x_tiles, x_tiles)].astype(F32)
        for k in range(1, self.ctx_n):
            total = total + self.arrived_xa[k - 1].astype(F32)
        self.part_a[:, 0:x_tiles] = total.astype(BF)
        copies = [
            self.send(
                self.part_a.at[:, pl.ds(self.peer("dp", k) * z_tiles, z_tiles)], self.arrived_za.at[k - 1],
                self.za_send.at[k - 1], self.za_recv.at[k - 1], "dp", self.peer("dp", k),
            )
            for k in range(1, self.dp_n)
        ]
        for copy in copies:
            copy.wait_recv()
        mine = self.attn_table.at[self.exp]

        def write(a, tile, value):
            self.attn_table[self.exp, self.ctx, self.dp, a, tile] = value

        def read(k, source, tile):
            if k == 0:
                return self.part_a[source, self.dp * z_tiles + tile]
            return self.arrived_za[k - 1, source, tile]

        self.merge(z_tiles, read, write)
        here = mine.at[self.ctx, self.dp]
        copies = [
            self.send(here, here, self.bz_send.at[k - 1], self.bz_recv.at[k - 1], "dp", self.peer("dp", k))
            for k in range(1, self.dp_n)
        ]
        other()
        for copy in copies:
            copy.wait_recv()
        here = mine.at[self.ctx, pl.ds(0, real)]
        copies = [
            self.send(
                here, here, self.bx_send.at[k - 1], self.bx_recv.at[k - 1], "context", self.peer("context", k)
            )
            for k in range(1, self.ctx_n)
        ]
        other()
        for copy in copies:
            copy.wait_recv()
        core = lax.rem(self.exp, 2)
        twin = self.exp + 1 - 2 * core
        chips = self.exp_n // 2

        def table_of(owner):
            return self.attn_table.at[owner, :, pl.ds(0, real)]

        far = [
            self.send(
                table_of(self.exp), table_of(self.exp), self.be_send.at[0, k - 1], self.be_recv.at[0, k - 1],
                "expert", self.peer("expert", 2 * k),
            )
            for k in range(1, chips)
        ]
        near = [
            self.send(
                table_of(self.exp), table_of(self.exp), self.be_send.at[1, 0], self.be_recv.at[1, 0], "expert", twin
            )
        ]
        while between:
            other()
        for k in range(1, chips):
            far[k - 1].wait_recv()
            owner = self.peer("expert", self.exp_n - 2 * k)
            near.append(
                self.send(
                    table_of(owner), table_of(owner), self.be_send.at[1, k], self.be_recv.at[1, k], "expert", twin
                )
            )
        for copy in near:
            copy.wait_recv()

    def finish(self):
        for by_expert in self.ax_copies:
            for copies in by_expert:
                for copy in copies:
                    copy.wait_recv()
        for copy in self.waits:
            copy.wait_send()


def sums_shapes(experts, model, width, attn_tiles, adapters):
    ctx_n, dp_n, exp_n = (lax.axis_size(axis) for axis in ("context", "dp", "expert"))
    _, _, z_tiles = expert_tiling(experts, model, width)
    own, xa_tiles, za_tiles = attn_tiling(attn_tiles)
    many, deep, chips = max(ctx_n - 1, 1), max(dp_n - 1, 1), max(exp_n // 2, 1)
    dma = pltpu.SemaphoreType.DMA
    outs = (
        jax.ShapeDtypeStruct((ctx_n, dp_n, experts, adapters, z_tiles, 16, 128), BF),
        jax.ShapeDtypeStruct((exp_n, ctx_n, dp_n, adapters, za_tiles, 16, 128), BF),
    )
    scratch = [
        pltpu.VMEM((dp_n, exp_n, z_tiles, 16, 128), BF),
        pltpu.VMEM((max(experts - 1, 1), dp_n, exp_n, z_tiles, 16, 128), BF),
        pltpu.VMEM((exp_n, max(ctx_n * xa_tiles, own), 16, 128), BF),
        pltpu.VMEM((many, exp_n, xa_tiles, 16, 128), BF),
        pltpu.VMEM((exp_n, dp_n * za_tiles, 16, 128), BF),
        pltpu.VMEM((deep, exp_n, za_tiles, 16, 128), BF),
        dma((deep,)), dma((deep,)), dma((experts, deep)), dma((experts, deep)),
        dma((many, experts, dp_n)), dma((many, experts, dp_n)),
        dma((exp_n,)), dma((exp_n,)), dma((many,)), dma((many,)), dma((deep,)), dma((deep,)),
        dma((deep,)), dma((deep,)), dma((many,)), dma((many,)), dma((2, chips)), dma((2, chips)),
        dma, dma((2,)),
    ]
    return outs, scratch


ALL_AXES = ("context", "dp", "expert")


def sums_kernel(sizes, ids_ref, sums_ref, early_ref, attn_ref, table_ref, attn_table, *scratch):
    greet([(axis, lax.axis_size(axis)) for axis in ALL_AXES])()
    sums = Sums(sizes, ids_ref, sums_ref, early_ref, attn_ref, table_ref, attn_table, scratch)
    sums.start()
    for e in range(sums.experts):
        sums.combine(e)
    for e in range(sums.experts):
        for k in range(1, sums.dp_n):
            sums.forward(e, k)
    sums.tail([])
    sums.finish()


def add_up(ids, sums, attn, experts, width, adapters):
    model = attn.shape[0] * 16
    outs, scratch = sums_shapes(experts, model, width, attn.shape[0], adapters)
    vmem, hbm = pl.BlockSpec(memory_space=pltpu.VMEM), pl.BlockSpec(memory_space=pl.ANY)
    sizes = tuple(lax.axis_size(axis) for axis in ALL_AXES) + (adapters, attn.shape[0])
    return pl.pallas_call(
        functools.partial(sums_kernel, sizes),
        out_shape=outs,
        in_specs=[pl.BlockSpec(memory_space=pltpu.SMEM), hbm, hbm, vmem],
        out_specs=(vmem, vmem),
        scratch_shapes=scratch,
        compiler_params=pltpu.CompilerParams(
            collective_id=1, has_side_effects=True, vmem_limit_bytes=VLIMIT
        ),
        name="reduce_adapters",
    )(ids, *sums, attn)


def unpack_kernel(sizes, table_ref, attn_ref, down_ref, up_ref, in_down_ref, in_up_ref, out_down_ref, out_up_ref):
    share, z_tiles, own, xa_tiles, za_tiles = sizes
    for expert in range(in_up_ref.shape[1]):
        tile = 0
        for out_ref in (in_down_ref, in_up_ref, out_down_ref, out_up_ref):
            rows, cols = out_ref.shape[2:]
            for row in range(rows // 16):
                for col in range(cols // 128):
                    place = tile % share
                    out_ref[0, expert, row * 16 : row * 16 + 16, col * 128 : col * 128 + 128] = table_ref[
                        tile // share, place // z_tiles, expert, 0, place % z_tiles
                    ].astype(F32)
                    tile += 1
    tile = 0
    for out_ref in (down_ref, up_ref):
        rows, cols = out_ref.shape[1:]
        for row in range(rows // 16):
            for col in range(cols // 128):
                place = tile % own
                out_ref[0, row * 16 : row * 16 + 16, col * 128 : col * 128 + 128] = attn_ref[
                    tile // own, place // xa_tiles, place % xa_tiles // za_tiles, 0, place % xa_tiles % za_tiles
                ].astype(F32)
                tile += 1


def unpack(table, attn_table, experts, width, table_shapes, attn_shape):
    adapters = table.shape[3]
    model = attn_shape[1]
    share, _, z_tiles = expert_tiling(experts, model, width)
    sizes = (share, z_tiles) + attn_tiling(8 * model // 128)
    shapes = [(adapters,) + attn_shape] * 2 + [(adapters,) + shape for shape in table_shapes]

    def by_adapter(array, axis):
        block = array.shape[:axis] + (1,) + array.shape[axis + 1 :]
        return pl.BlockSpec(block, lambda a, n=array.ndim: (0,) * axis + (a,) + (0,) * (n - axis - 1))

    return pl.pallas_call(
        functools.partial(unpack_kernel, sizes),
        grid=(adapters,),
        out_shape=tuple(jax.ShapeDtypeStruct(shape, F32) for shape in shapes),
        in_specs=[by_adapter(table, 3), by_adapter(attn_table, 3)],
        out_specs=tuple(
            pl.BlockSpec((1,) + shape[1:], lambda a, n=len(shape): (a,) + (0,) * (n - 1))
            for shape in shapes
        ),
        compiler_params=pltpu.CompilerParams(vmem_limit_bytes=VLIMIT),
        name="unpack_adapters",
    )(table, attn_table)


def local(
    hidden_in,
    prev_logits,
    segment_ids,
    routes,
    adapter_ids,
    attn_gain,
    w_qkv,
    w_out,
    attn_down,
    attn_up,
    ffn_gain,
    router_weight,
    gate_mix,
    const_mix,
    const_vec,
    w_gate_up,
    w_down,
    exp_in_down,
    exp_in_up,
    exp_out_down,
    exp_out_up,
    cotangent,
):
    model_dim = hidden_in.shape[2]
    local_experts, ffn_width = w_down.shape[:2]
    adapter_count = attn_down.shape[0]
    rank_dim = attn_up.shape[2]
    down_all = jnp.swapaxes(attn_down, 2, 3).reshape(adapter_count, 4 * rank_dim, model_dim)
    up_all = attn_up.reshape(adapter_count, 4 * rank_dim, model_dim)
    router_rows = jnp.concatenate(
        [
            router_weight.T,
            const_mix.transpose(0, 2, 1).reshape(4, model_dim),
            attn_gain[None],
            ffn_gain[None],
        ],
        0,
    )
    router_rows = jnp.pad(router_rows, ((0, 128 - router_rows.shape[0]), (0, 0)))
    (
        q_pairs, k_pairs, v_pairs, normed_all, rank_all, log_cols, attn_flat, rank_out_all, mid_resid,
        rows_low, logits_all, seg_all, arrived_dy, slots,
    ) = attention_forward(
        hidden_in[0], segment_ids, prev_logits[0].T, gate_mix, adapter_ids, w_qkv, w_out, down_all,
        up_all, router_rows, cotangent[0], routes[0].T, local_experts,
    )
    tables = (
        jnp.swapaxes(exp_in_down, 2, 3),
        exp_in_up.reshape(exp_in_up.shape[:2] + (2 * rank_dim, ffn_width)),
        jnp.swapaxes(exp_out_down, 2, 3),
        exp_out_up,
    )
    base, d_mid, grad_prev, *expert_sums, done_out, cols = expert_layer(
        rows_low, mid_resid, logits_all, slots, cotangent[0], arrived_dy, adapter_ids, router_rows,
        gate_mix, const_vec, w_gate_up, w_down, tables,
    )
    grad_in, table, attn_table, hidden_out = attention_backward(
        d_mid,
        (q_pairs, k_pairs, v_pairs, normed_all, rank_all, log_cols, attn_flat, rank_out_all, seg_all),
        hidden_in[0], adapter_ids, router_rows, w_qkv, w_out, down_all, up_all, expert_sums,
        (done_out, base, cols), local_experts, ffn_width,
    )
    sums = unpack(
        table, attn_table, local_experts, ffn_width, [entry.shape[1:] for entry in tables],
        (4 * rank_dim, model_dim),
    )
    grad_attn_down = jnp.swapaxes(sums[0].reshape(adapter_count, 4, rank_dim, model_dim), 2, 3)
    grad_attn_up = sums[1].reshape(adapter_count, 4, rank_dim, model_dim)
    grad_in_down = jnp.swapaxes(sums[2], 2, 3)
    grad_in_up = sums[3].reshape(exp_in_up.shape)
    grad_out_down = jnp.swapaxes(sums[4], 2, 3)
    grad_out_up = sums[5]
    return (
        hidden_out[None],
        grad_in[None],
        grad_prev.transpose(1, 2, 0),
        grad_attn_down,
        grad_attn_up,
        grad_in_down,
        grad_in_up,
        grad_out_down,
        grad_out_up,
    )


def solution(mesh):
    return jax.shard_map(
        local,
        mesh=mesh,
        in_specs=(
            P(("dp", "expert"), "context", None),
            P(("dp", "expert"), "context", None),
            P(("dp", "expert"), "context"),
            P(("dp", "expert"), "context", None),
            P(),
            P(),
            P(),
            P(),
            P(),
            P(),
            P(),
            P(),
            P(),
            P(),
            P(),
            P("expert", None, None),
            P("expert", None, None),
            P(None, "expert", None, None),
            P(None, "expert", None, None, None),
            P(None, "expert", None, None),
            P(None, "expert", None, None),
            P(("dp", "expert"), "context", None),
        ),
        out_specs=(
            P(("dp", "expert"), "context", None),
            P(("dp", "expert"), "context", None),
            P(("dp", "expert"), "context", None),
            P(),
            P(),
            P(None, "expert", None, None),
            P(None, "expert", None, None, None),
            P(None, "expert", None, None),
            P(None, "expert", None, None),
        ),
        check_vma=False,
    )
```

```python
import functools
import math

import jax
import jax.numpy as jnp
import numpy as np
from jax import lax
from jax.experimental import pallas as pl
from jax.experimental.pallas import tpu as pltpu
from jax.sharding import PartitionSpec as P

MESH = pl.DeviceIdType.MESH
VLIMIT = 60 * 1024 * 1024
BF = jnp.bfloat16
F32 = jnp.float32

HEADS = 12


EPSILON = 1e-06
ADAPT_SCALE = 2.0
NEG = -1e30
HIGH = lax.Precision.HIGHEST


def nt(left, right):
    return lax.dot_general(left, right, (((1,), (1,)), ((), ())), preferred_element_type=F32)


def tn(left, right):
    return lax.dot_general(left, right, (((0,), (0,)), ((), ())), preferred_element_type=F32)


def nn(left, right):
    return jnp.dot(left, right, preferred_element_type=F32)


def rope_tables(positions, width):
    half = width // 2
    frequency = np.exp(np.arange(half) * (-2.0 * math.log(10000.0) / width))
    angles = np.arange(positions)[:, None] * frequency[None, :]
    cosine, sine = np.cos(angles), np.sin(angles)
    return (
        np.concatenate([cosine] * 4, 1).astype(np.float32),
        np.concatenate([-sine, sine] * 2, 1).astype(np.float32),
    )


def turn(block, cosine, sine, width):
    half = width // 2
    lane = lax.broadcasted_iota(jnp.int32, block.shape, 1)
    other = jnp.where(
        lane % width < half, pltpu.roll(block, 128 - half, 1), pltpu.roll(block, half, 1)
    )
    return block * cosine + other * sine


def greet(axes):
    barrier = pltpu.get_barrier_semaphore()
    count = 0
    for axis, size in axes:
        index = lax.axis_index(axis)
        for step in range(1, size):
            pl.semaphore_signal(
                barrier, inc=1, device_id={axis: lax.rem(index + step, size)}, device_id_type=MESH
            )
        count += size - 1
    return lambda: pl.semaphore_wait(barrier, count)


def remote(src, dst, send, recv, axis, target):
    return pltpu.make_async_remote_copy(
        src_ref=src, dst_ref=dst, send_sem=send, recv_sem=recv,
        device_id={axis: target}, device_id_type=MESH,
    )


def blocks_of(ctx_n, ctx, count):
    return [lax.rem(ctx + 1 + j, ctx_n) for j in range(count)]


def fill_bias(bias_ref, seg_all, ctx, tok, j, block):
    own = jnp.broadcast_to(seg_all[ctx, 0:1, :].astype(F32), (128, tok))
    query_seg = jnp.transpose(own)[:, 0:1]
    query_pos = ctx * tok + lax.broadcasted_iota(jnp.int32, (tok, tok), 0)
    key_seg = seg_all[block, 0:1, :].astype(F32)
    key_pos = block * tok + lax.broadcasted_iota(jnp.int32, (tok, tok), 1)
    allowed = (query_seg == key_seg) & (key_pos <= query_pos)
    bias_ref[j] = jnp.where(allowed, 0.0, NEG).astype(bias_ref.dtype)


def head_marks():
    lane = lax.broadcasted_iota(jnp.int32, (1, 128), 1)
    return lane, lane < 64


def stack_heads(value):
    _, first = head_marks()
    return jnp.concatenate([jnp.where(first, value, 0), jnp.where(first, 0, value)], 0)


def join_heads(value):
    _, first = head_marks()
    rows = value.shape[0] // 2
    return jnp.where(first, value[:rows], value[rows:])


def stack_columns(stats, i):
    lane, _ = head_marks()
    return jnp.concatenate(
        [jnp.sum(jnp.where(lane == 2 * i + head, stats, 0.0), -1, keepdims=True) for head in range(2)], 0
    )


def put_columns(stats, i, column):
    lane, _ = head_marks()
    rows = stats.shape[0]
    stats = jnp.where(lane == 2 * i, column[:rows], stats)
    return jnp.where(lane == 2 * i + 1, column[rows:], stats)


def biased(raw, bias):
    rows, keys = bias.shape
    return (raw.reshape(2, rows, keys) + bias[None]).reshape(2 * rows, keys)


def attention_kernel(
    sizes, ids_ref, x_hbm, seg_ref, prev_ref, mix_ref, w_qkv_hbm, w_out_hbm, down_hbm, up_hbm,
    router_ref, cos_hbm, sin_hbm, dy_hbm, routes_ref,
    q_out, k_out, v_out, normed_out, rank_ref, total_ref, flat_ref, rank_out_ref, mid_ref, rows_ref,
    logits_ref, seg_all, arrived_dy, slots_ref,
    x_all, bias_ref, sent_dy, acc_ref, top_ref, weight_ref, prev_pad, mix_pad, send_sem, recv_sem, seg_send, seg_recv, dy_send, dy_recv,
    q_ref, k_ref, v_ref, normed_ref, own_dy, out_sem, *staged,
):
    ctx_n, exp_n, rank = sizes
    dy_ref, x_ref, down_ref, up_ref, w_qkv_ref, cos_ref, sin_ref, w_out_ref, stage_sem = staged
    stages = stage_copies(
        (dy_hbm, x_hbm, down_hbm, up_hbm, w_qkv_hbm, cos_hbm, sin_hbm, w_out_hbm), staged, stage_sem
    )
    for stage in stages:
        stage.start()
    ctx = lax.axis_index("context")
    sequence = lax.axis_index("dp") * exp_n + lax.axis_index("expert")
    tok, model = x_ref.shape
    pairs, head_dim = model // 128, 64
    entered = greet([("context", ctx_n), ("expert", exp_n)])
    seg_all[ctx] = jnp.broadcast_to(seg_ref[...], (8, tok))
    me = lax.axis_index("expert")
    experts, capacity = arrived_dy.shape[1], arrived_dy.shape[3]
    others = partners(exp_n, me)
    entered()
    dy_copies = []
    if ctx_n > 1:
        copies = []
        for step in range(1, ctx_n):
            peer = lax.rem(ctx + step, ctx_n)
            copies.append(
                (
                    peer,
                    step,
                    remote(x_hbm, x_all.at[ctx], send_sem.at[step - 1], recv_sem.at[step - 1], "context", peer),
                    remote(seg_all.at[ctx], seg_all.at[ctx], seg_send.at[step - 1], seg_recv.at[step - 1], "context", peer),
                )
            )

        def to_later(peer):
            return ctx < peer if ctx_n == 2 else ctx < ctx_n

        def from_earlier(step):
            return lax.rem(ctx - step + ctx_n, ctx_n) < ctx if ctx_n == 2 else ctx < ctx_n

        for peer, step, rows_copy, seg_copy in copies:
            @pl.when(to_later(peer))
            def _(rows_copy=rows_copy, seg_copy=seg_copy):
                seg_copy.start()
                rows_copy.start()

    kind_rows = jnp.concatenate([routes_ref[...], jnp.full((6, tok), -1, jnp.int32)], 0)
    sub = lax.broadcasted_iota(jnp.int32, (16, tok), 0)
    uses = jnp.where((sub == kind_rows[0:1]) | (sub == kind_rows[1:2]), 1.0, 0.0).astype(BF)
    earlier = jnp.where(
        lax.broadcasted_iota(jnp.int32, (tok, tok), 0) < lax.broadcasted_iota(jnp.int32, (tok, tok), 1), 1.0, 0.0
    ).astype(BF)
    places = nn(uses, earlier) + (sub * capacity).astype(F32)
    slot_rows = []
    for j in range(2):
        kind = kind_rows[j : j + 1]
        place = jnp.sum(jnp.where(sub == kind, places, 0.0), 0, keepdims=True)
        slot_rows.append(jnp.where(kind < exp_n * experts, place, -1.0))
    row8 = lax.broadcasted_iota(jnp.int32, (8, tok), 0)
    slots_ref[...] = jnp.where(
        row8 < 2, kind_rows.astype(F32), jnp.where(row8 == 2, slot_rows[0], jnp.where(row8 == 3, slot_rows[1], 0.0))
    )
    slot_ints = [row.astype(jnp.int32) for row in slot_rows]

    def pick_dy(owner):
        hots = [hot_rows(row, owner * experts * capacity, experts * capacity) for row in slot_ints]
        hot = jnp.where(hots[0] | hots[1], 1.0, 0.0).astype(BF)
        return nn(hot, dy_ref[...]).astype(BF)

    stages[0].wait()
    for i, peer in enumerate(others):
        picked = pick_dy(peer)
        for e in range(experts):
            sent_dy[i, e] = picked[e * capacity : (e + 1) * capacity]
        copy = remote(
            sent_dy.at[i], arrived_dy.at[me // 2, :, lax.rem(me, 2)], dy_send.at[i], dy_recv.at[me], "expert", peer
        )
        copy.start()
        dy_copies.append(copy)
    picked = pick_dy(me)
    for e in range(experts):
        own_dy[e] = picked[e * capacity : (e + 1) * capacity]
    writes = [pltpu.make_async_copy(own_dy, arrived_dy.at[me // 2, :, lax.rem(me, 2)], out_sem.at[0])]
    writes[0].start()
    for stage in stages[1:]:
        stage.wait()
    adapter = ids_ref[sequence]
    down = down_ref[adapter]
    up = up_ref[adapter]
    gain_one = router_ref[16:17].astype(F32)
    column = lax.broadcasted_iota(jnp.int32, (tok, down.shape[0]), 1) // rank

    def project(values, block, first):
        wide = values.astype(F32)
        inv = lax.rsqrt(jnp.mean(wide * wide, -1, keepdims=True) + EPSILON)
        normed_ref[block] = (wide * inv * gain_one).astype(BF)
        normed = normed_ref[block]
        ranks = nt(normed, down).astype(BF)
        rank_ref[block] = ranks
        start = pl.multiple_of(block * tok, tok)
        for p in range(first, 3):
            part = jnp.where(column == p, ADAPT_SCALE * ranks.astype(F32), 0.0).astype(BF)

            def chunk(i, carry, p=p, part=part):
                wide_cols = pl.ds(pl.multiple_of(p * model + i * 256, 256), 256)
                cols = pl.ds(pl.multiple_of(i * 256, 256), 256)
                proj = nn(normed_ref[block], w_qkv_ref[:, wide_cols]) + nn(
                    part, up_cols[:, cols]
                )
                for half in range(2):
                    piece = proj[:, half * 128 : half * 128 + 128]
                    if p < 2:
                        piece = turn(
                            piece, cos_ref[pl.ds(start, tok)], sin_ref[pl.ds(start, tok)], head_dim
                        )
                    if p == 0:
                        q_ref[2 * i + half] = (piece * head_dim ** (-0.5)).astype(BF)
                    else:
                        (k_ref if p == 1 else v_ref)[block, 2 * i + half] = piece.astype(BF)
                return carry

            up_cols = up_ref.at[adapter]
            lax.fori_loop(0, model // 256, chunk, 0)

    project(x_ref[...], ctx, 0)
    half_rows = tok // 2
    halves = [slice(half * half_rows, (half + 1) * half_rows) for half in range(2)]

    def own_pair(i, carry):
        for half, rows in enumerate(halves):
            width = (half + 1) * half_rows
            scores = biased(
                nt(stack_heads(q_ref[i, rows]), k_ref[ctx, i, 0:width]), bias_ref[0, rows, 0:width]
            )
            top = jnp.max(scores, -1, keepdims=True)
            exps = jnp.exp(scores - top)
            acc_ref[i, rows] = join_heads(nn(exps.astype(BF), v_ref[ctx, i, 0:width]))
            top_ref[rows] = put_columns(top_ref[rows], i, top)
            weight_ref[rows] = put_columns(weight_ref[rows], i, jnp.sum(exps, -1, keepdims=True))
        return carry

    def close_pair(i, carry):
        for rows in halves:
            inv = 1.0 / stack_columns(weight_ref[rows], i)
            flat_ref[rows, pl.ds(pl.multiple_of(i * 128, 128), 128)] = (
                acc_ref[i, rows] * join_heads(inv)
            ).astype(BF)
        return carry

    def attend_others():
        others = blocks_of(ctx_n, ctx, ctx_n - 1)
        for j, block in enumerate(others):
            fill_bias(bias_ref, seg_all, ctx, tok, j + 1, block)

        def pair(i, carry):
            for rows in halves:
                q = stack_heads(q_ref[i, rows])
                scores = [
                    biased(nt(q, k_ref[block, i]), bias_ref[j + 1, rows]) for j, block in enumerate(others)
                ]
                before = stack_columns(top_ref[rows], i)
                top = functools.reduce(
                    jnp.maximum, [before] + [jnp.max(part, -1, keepdims=True) for part in scores]
                )
                keep = jnp.exp(before - top)
                exps = [jnp.exp(part - top) for part in scores]
                total = keep * stack_columns(weight_ref[rows], i)
                result = acc_ref[i, rows] * join_heads(keep)
                for part, block in zip(exps, others):
                    total = total + jnp.sum(part, -1, keepdims=True)
                    result = result + join_heads(nn(part.astype(BF), v_ref[block, i]))
                flat_ref[rows, pl.ds(pl.multiple_of(i * 128, 128), 128)] = (
                    result * join_heads(1.0 / total)
                ).astype(BF)
                top_ref[rows] = put_columns(top_ref[rows], i, top)
                weight_ref[rows] = put_columns(weight_ref[rows], i, total)
            return carry

        lax.fori_loop(0, pairs, pair, 0)

    top_ref[...] = jnp.zeros_like(top_ref)
    weight_ref[...] = jnp.ones_like(weight_ref)
    fill_bias(bias_ref, seg_all, ctx, tok, 0, ctx)
    lax.fori_loop(0, pairs, own_pair, 0)
    if ctx_n == 1:
        lax.fori_loop(0, pairs, close_pair, 0)
    else:
        for peer, step, rows_copy, seg_copy in copies:
            @pl.when(from_earlier(step))
            def _(step=step, rows_copy=rows_copy, seg_copy=seg_copy):
                rows_copy.wait_recv()
                seg_copy.wait_recv()
                block = lax.rem(ctx - step + ctx_n, ctx_n)
                project(x_all[block], block, 1)

        if ctx_n == 2:
            @pl.when(ctx == 0)
            def _():
                lax.fori_loop(0, pairs, close_pair, 0)

            pl.when(ctx == 1)(attend_others)
        else:
            attend_others()
        for peer, step, rows_copy, seg_copy in copies:
            @pl.when(to_later(peer))
            def _(rows_copy=rows_copy, seg_copy=seg_copy):
                seg_copy.wait_send()
                rows_copy.wait_send()

    for i, (src, dst) in enumerate(((q_ref, q_out), (k_ref, k_out), (v_ref, v_out), (normed_ref, normed_out))):
        writes.append(pltpu.make_async_copy(src, dst, out_sem.at[1 + i]))
        writes[-1].start()
    total_ref[...] = top_ref[...] + jnp.log(weight_ref[...])
    rank_out = nt(flat_ref[...], down).astype(BF)
    rank_out_ref[...] = rank_out
    part = jnp.where(column == 3, ADAPT_SCALE * rank_out.astype(F32), 0.0).astype(BF)

    def out_chunk(i, carry):
        cols = pl.ds(pl.multiple_of(i * 256, 256), 256)
        mid_ref[:, cols] = (
            x_ref[:, cols].astype(F32)
            + nn(flat_ref[...], w_out_ref[:, cols])
            + nn(part, up_ref[adapter, :, cols])
        )
        return carry

    lax.fori_loop(0, model // 256, out_chunk, 0)
    gain_two = router_ref[17:18].astype(F32)
    step_rows = 128

    def norm_rows(i, carry):
        rows = pl.ds(pl.multiple_of(i * step_rows, step_rows), step_rows)
        mid = mid_ref[rows]
        inv = lax.rsqrt(jnp.mean(mid * mid, -1, keepdims=True) + EPSILON)
        rows_ref[rows] = (mid * inv * gain_two).astype(BF)
        return carry

    lax.fori_loop(0, tok // step_rows, norm_rows, 0)
    kinds = mix_ref.shape[0]
    prev_pad[...] = jnp.zeros_like(prev_pad)
    mix_pad[...] = jnp.zeros_like(mix_pad)
    prev_pad[0:kinds] = prev_ref[...]
    mix_pad[0:kinds, 0:kinds] = mix_ref[...]
    logits_ref[...] = nt(rows_ref[...], router_ref[...]) + lax.dot_general(
        prev_pad[...], mix_pad[...], (((0,), (0,)), ((), ())), precision=HIGH, preferred_element_type=F32
    )
    for write in writes:
        write.wait()
    for copy in dy_copies:
        copy.wait_send()
    for peer in others:
        remote(
            sent_dy.at[0], arrived_dy.at[peer // 2, :, lax.rem(peer, 2)], dy_send.at[0], dy_recv.at[peer], "expert", peer
        ).wait_recv()


def attention_forward(hidden, segments, prev, mix, ids, w_qkv, w_out, down, up, router, dy, routes, experts):
    ctx_n, exp_n = lax.axis_size("context"), lax.axis_size("expert")
    tok, model = hidden.shape
    pairs = model // 128
    wide = down.shape[1]
    cos_table, sin_table = rope_tables(ctx_n * tok, 64)
    vmem, hbm = pl.BlockSpec(memory_space=pltpu.VMEM), pl.BlockSpec(memory_space=pl.ANY)
    dma = pltpu.SemaphoreType.DMA
    many = max(ctx_n - 1, 1)
    shape = jax.ShapeDtypeStruct
    cos_table, sin_table = jnp.asarray(cos_table), jnp.asarray(sin_table)
    return pl.pallas_call(
        functools.partial(attention_kernel, (ctx_n, exp_n, wide // 4)),
        out_shape=(
            shape((pairs, tok, 128), BF),
            shape((ctx_n, pairs, tok, 128), BF),
            shape((ctx_n, pairs, tok, 128), BF),
            shape((ctx_n, tok, model), BF),
            shape((ctx_n, tok, wide), BF),
            shape((tok, 128), F32),
            shape((tok, model), BF),
            shape((tok, wide), BF),
            shape((tok, model), F32),
            shape((tok, model), BF),
            shape((tok, 128), F32),
            shape((ctx_n, 8, tok), jnp.int32),
            shape((exp_n // 2, experts, 2, tok // 4, model), BF),
            shape((8, tok), F32),
        ),
        in_specs=[pl.BlockSpec(memory_space=pltpu.SMEM), hbm]
        + [vmem] * 3
        + [hbm] * 4
        + [vmem]
        + [hbm] * 3
        + [vmem],
        out_specs=(hbm,) * 4 + (vmem,) * 8 + (hbm, vmem),
        scratch_shapes=[
            pltpu.VMEM((ctx_n, tok, model), BF),
            pltpu.VMEM((ctx_n, tok, tok), BF if ctx_n > 2 else F32),
            pltpu.VMEM((exp_n - 1, experts, tok // 4, model), BF),
            pltpu.VMEM((pairs, tok, 128), F32),
            pltpu.VMEM((tok, 128), F32),
            pltpu.VMEM((tok, 128), F32),
            pltpu.VMEM((16, tok), F32),
            pltpu.VMEM((16, 128), F32),
            dma((many,)), dma((many,)), dma((many,)), dma((many,)), dma((exp_n - 1,)), dma((exp_n,)),
            pltpu.VMEM((pairs, tok, 128), BF),
            pltpu.VMEM((ctx_n, pairs, tok, 128), BF),
            pltpu.VMEM((ctx_n, pairs, tok, 128), BF),
            pltpu.VMEM((ctx_n, tok, model), BF),
            pltpu.VMEM((experts, tok // 4, model), BF),
            dma((5,)),
        ]
        + stage_scratch(dy, hidden, down, up, w_qkv, cos_table, sin_table, w_out),
        compiler_params=pltpu.CompilerParams(
            collective_id=2, has_side_effects=True, vmem_limit_bytes=VLIMIT + 5 * 2**19
        ),
        name="attention_forward",
    )(
        ids, hidden, segments, prev, mix, w_qkv, w_out, down, up, router, cos_table, sin_table, dy, routes,
    )


def put_tiles(tiles_ref, first, value):
    for col in range(value.shape[1] // 128):
        tiles_ref[first + col] = value[:, col * 128 : col * 128 + 128].astype(tiles_ref.dtype)


STAGED = 17


def backward_kernel(
    sizes, ids_ref, d_mid_hbm, q_hbm, k_hbm, v_hbm, normed_ref, rank_hbm, total_hbm, flat_hbm,
    rank_out_hbm, x_hbm, seg_hbm, router_hbm, w_qkv_hbm, w_out_hbm, down_hbm, up_hbm, cos_hbm,
    sin_hbm, *rest,
):
    ctx_n, exp_n, rank, fused = sizes
    staged, rest = rest[-STAGED - 1 :], rest[: -STAGED - 1]
    (
        d_mid_ref, up_ref, down_ref, w_out_ref, rank_out_ref, flat_ref, q_ref, k_ref, v_ref, total_ref,
        seg_all, cos_ref, sin_ref, w_qkv_ref, rank_ref, x_ref, router_ref, stage_sem,
    ) = staged
    stages = stage_copies(
        (
            d_mid_hbm, up_hbm, down_hbm, w_out_hbm, rank_out_hbm, flat_hbm, q_hbm, k_hbm, v_hbm,
            total_hbm, seg_hbm, cos_hbm, sin_hbm, w_qkv_hbm, rank_hbm, x_hbm, router_hbm,
        ),
        staged, stage_sem,
    )
    if fused:
        sums_ref, early_ref, done_ref, base_ref, cols_ref = rest[:5]
        grad_ref, table_ref, attn_table, hidden_ref, tiles_ref = rest[5:10]
        scratch, more, results_scratch = rest[10:-31], rest[-31:-5], rest[-5:]
        results = Results(exp_n, done_ref, base_ref, cols_ref, hidden_ref, results_scratch)
        sums = Sums(fused, ids_ref, sums_ref, early_ref, tiles_ref, table_ref, attn_table, more)
    else:
        grad_ref, tiles_ref = rest[:2]
        scratch = rest[2:]
    (
        recv_buf, do_ref, bias_ref, dk_acc, dv_acc, dq_all, dkv_all, send_buf, grad_up, grad_down,
        normed_buf, send_sem, recv_sem, load_sem,
    ) = scratch
    ctx = lax.axis_index("context")
    sequence = lax.axis_index("dp") * exp_n + lax.axis_index("expert")
    tok, model = x_ref.shape
    pairs, head_dim = model // 128, 64
    entered = greet([(axis, lax.axis_size(axis)) for axis in (ALL_AXES if fused else ("context",))])
    for stage in stages[:6]:
        stage.start()
    if fused:
        entered()
        sums.start()
        results.start()
    for stage in stages[6:]:
        stage.start()
    order = [ctx] + blocks_of(ctx_n, ctx, ctx_n - 1)

    def fetch(j):
        return pltpu.make_async_copy(
            normed_ref.at[order[j]], normed_buf.at[min(j, 1)], load_sem.at[min(j, 1)]
        )

    fetch(0).start()
    if ctx_n > 1:
        fetch(1).start()
    if fused:
        for e in range(sums.experts - 1):
            sums.combine(e)
    for stage in stages[:6]:
        stage.wait()
    adapter = ids_ref[sequence]
    down = down_ref[adapter]
    up = up_ref[adapter]
    wide = down.shape[0]
    column = lax.broadcasted_iota(jnp.int32, (tok, wide), 1) // rank
    d_branch = d_mid_ref[...].astype(BF)
    d_rank_out = jnp.where(column == 3, ADAPT_SCALE * nt(d_branch, up), 0.0).astype(BF)
    twice_out = jnp.where(column == 3, ADAPT_SCALE * rank_out_ref[...].astype(F32), 0.0).astype(BF)
    grad_up[...] = tn(twice_out, d_branch)
    grad_down[...] = tn(d_rank_out, flat_ref[...])

    def attn_chunk(i, carry):
        rows = pl.ds(pl.multiple_of(i * 256, 256), 256)
        d_attn = nt(d_branch, w_out_ref[rows, :]) + nn(d_rank_out, down_ref[adapter, :, rows])
        do_ref[2 * i] = d_attn[:, :128].astype(BF)
        do_ref[2 * i + 1] = d_attn[:, 128:].astype(BF)
        return carry

    lax.fori_loop(0, model // 256, attn_chunk, 0)
    for stage in stages[6:]:
        stage.wait()
    half_rows = tok // 2

    steps = {}
    if fused and sums.experts > 1:
        earlier = range(sums.experts - 1)

        def first_step():
            for e in earlier:
                sums.advance(e, 1)
            sums.exchange()

        def second_step():
            for e in earlier:
                sums.advance(e, 2)

        steps = {0: first_step, 3: second_step}

    def attend(count):
        others = blocks_of(ctx_n, ctx, count)
        for j, block in enumerate([ctx] + others):
            fill_bias(bias_ref, seg_all, ctx, tok, j, block)

        def pair(i, carry):
            cols = pl.ds(pl.multiple_of(i * 128, 128), 128)
            for half in (1, 0):
                rows = slice(half * half_rows, (half + 1) * half_rows)
                q = stack_heads(q_ref[i, rows])
                d_out = stack_heads(do_ref[i, rows])
                total = stack_columns(total_ref[rows], i)
                def terms(j, block, width, i=i, rows=rows, q=q, d_out=d_out, total=total):
                    probs = jnp.exp(
                        biased(nt(q, k_ref[block, i, 0:width]), bias_ref[j, rows, 0:width]) - total
                    )
                    return probs, nt(d_out, v_ref[block, i, 0:width])

                def use(j, block, width, probs, d_probs, delta, i=i, half=half, q=q, d_out=d_out):
                    d_scores = (probs * (d_probs - delta)).astype(BF)
                    d_key = tn(q, d_scores)
                    d_value = tn(d_out, probs.astype(BF))
                    if half == 1:
                        dk_acc[j] = d_key
                        dv_acc[j] = d_value
                    else:
                        dk_acc[j, :, 0:width] += d_key
                        dv_acc[j, :, 0:width] += d_value
                    return nn(d_scores, k_ref[block, i, 0:width])

                width = (half + 1) * half_rows
                own = terms(0, ctx, width)
                delta = jnp.sum(own[0] * own[1], -1, keepdims=True)
                if count < 2:
                    kept = [terms(j + 1, block, tok) for j, block in enumerate(others)]
                    for probs, d_probs in kept:
                        delta = delta + jnp.sum(probs * d_probs, -1, keepdims=True)
                    d_query = use(0, ctx, width, *own, delta)
                    for j, block in enumerate(others):
                        d_query = d_query + use(j + 1, block, tok, *kept[j], delta)
                else:

                    def more_delta(j, delta):
                        probs, d_probs = terms(j, lax.rem(ctx + j, ctx_n), tok)
                        return delta + jnp.sum(probs * d_probs, -1, keepdims=True)

                    delta = lax.fori_loop(1, ctx_n, more_delta, delta)

                    def more_query(j, d_query, delta=delta):
                        block = lax.rem(ctx + j, ctx_n)
                        return d_query + use(j, block, tok, *terms(j, block, tok), delta)

                    d_query = lax.fori_loop(1, ctx_n, more_query, use(0, ctx, width, *own, delta))
                start = pl.multiple_of(ctx * tok + half * half_rows, half_rows)
                d_query = join_heads(d_query) * head_dim ** (-0.5)
                dq_all[rows, cols] = turn(
                    d_query, cos_ref[pl.ds(start, half_rows)], -sin_ref[pl.ds(start, half_rows)], head_dim
                ).astype(BF)
            for j, block in enumerate([ctx] + others):
                start = pl.multiple_of(block * tok, tok)
                d_key = turn(
                    jnp.transpose(dk_acc[j]), cos_ref[pl.ds(start, tok)], -sin_ref[pl.ds(start, tok)], head_dim
                )
                dkv_all[j, 0, :, cols] = d_key.astype(BF)
                dkv_all[j, 1, :, cols] = jnp.transpose(dv_acc[j]).astype(BF)
            for turn_of, step in steps.items():
                pl.when(i == turn_of)(step)
            return carry

        lax.fori_loop(0, pairs, pair, 0)

    def fold(j, block, first, write):
        normed = normed_buf[min(j, 1)]
        ranks = rank_ref[block].astype(F32)
        d_ranks = jnp.zeros((tok, wide), F32)
        for p in range(first, 3):
            d_proj = dq_all[...] if p == 0 else dkv_all[j, p - 1]
            twice = jnp.where(column == p, ADAPT_SCALE * ranks, 0.0).astype(BF)
            grad_up[...] += tn(twice, d_proj)
            d_ranks = d_ranks + jnp.where(column == p, ADAPT_SCALE * nt(d_proj, up), 0.0)
        d_ranks = d_ranks.astype(BF)
        grad_down[...] += tn(d_ranks, normed)

        def chunk(i, carry):
            rows = pl.ds(pl.multiple_of(i * 256, 256), 256)
            value = nn(d_ranks, down_ref[adapter, :, rows])
            for p in range(first, 3):
                d_proj = dq_all[...] if p == 0 else dkv_all[j, p - 1]
                value = value + nt(d_proj, w_qkv_ref[rows, p * model : (p + 1) * model])
            write(rows, value)
            return carry

        lax.fori_loop(0, model // 256, chunk, 0)

    def write_own(cols, value):
        grad_ref[:, cols] = value

    class Share:
        def __init__(self, step):
            peer = lax.rem(ctx + step, ctx_n)
            self.halves = [
                remote(
                    send_buf.at[pl.ds(half * half_rows, half_rows)],
                    recv_buf.at[step - 1, pl.ds(half * half_rows, half_rows)],
                    send_sem.at[step - 1, half], recv_sem.at[step - 1, half], "context", peer,
                )
                for half in range(2)
            ]

        def start(self):
            self.halves[0].start()
            if not fused:
                self.halves[1].start()

        def start_rest(self):
            self.halves[1].start()

        def wait_recv(self):
            for half in self.halves:
                half.wait_recv()

        def wait_send(self):
            for half in self.halves:
                half.wait_send()

    copies = [Share(step) for step in range(1, ctx_n)]

    def share_rest():
        if ctx_n == 2:
            pl.when(ctx == 1)(copies[0].start_rest)

    if ctx_n == 1:
        attend(0)
        sums.combine(sums.experts - 1)
    elif ctx_n == 2:
        @pl.when(ctx == 0)
        def _():
            attend(0)
            sums.combine(sums.experts - 1)

    if not fused:
        entered()

    def spread():
        attend(ctx_n - 1)
        if fused:
            sums.combine(sums.experts - 1)
        for j, block in enumerate(blocks_of(ctx_n, ctx, ctx_n - 1)):
            def write(cols, value):
                send_buf[:, cols] = value.astype(BF)

            fetch(j + 1).wait()
            if j > 0:
                copies[j - 1].wait_send()
            fold(j + 1, block, 1, write)
            copies[j].start()
            if j + 2 < ctx_n:
                fetch(j + 2).start()

    if ctx_n == 2:
        pl.when(ctx == 1)(spread)
        pl.when(ctx == 0)(fetch(1).wait)
    elif ctx_n > 2:
        spread()
    fetch(0).wait()
    fold(0, ctx, 0, write_own)
    per = model // 128
    for p in range(4):
        put_tiles(tiles_ref, p * per, grad_down[p * rank : (p + 1) * rank])
        put_tiles(tiles_ref, (4 + p) * per, grad_up[p * rank : (p + 1) * rank])

    def settle():
        take_shares()
        lax.fori_loop(0, tok // 128, finish, 0)

    def take_shares():
        if ctx_n == 2:
            pl.when(ctx == 0)(copies[0].wait_recv)

            @pl.when(ctx == 1)
            def _():
                recv_buf[...] = jnp.zeros_like(recv_buf)

        elif ctx_n > 2:
            copies[-1].wait_send()
            for step, item in enumerate(copies):
                item.wait_recv()
                load = pltpu.make_async_copy(recv_buf.at[step], send_buf, load_sem.at[0])
                load.start()
                load.wait()
                grad_ref[...] += send_buf[...].astype(F32)

    gain_one = router_ref[16:17].astype(F32)

    def finish(i, carry):
        rows = pl.ds(pl.multiple_of(i * 128, 128), 128)
        value = grad_ref[rows]
        if ctx_n == 2:
            value = value + recv_buf[0, rows].astype(F32)
        x = x_ref[rows].astype(F32)
        inv = lax.rsqrt(jnp.mean(x * x, -1, keepdims=True) + EPSILON)
        scaled = value * gain_one
        grad_ref[rows] = (
            d_mid_ref[rows]
            + inv * scaled
            - x * (inv * inv * inv) * jnp.mean(scaled * x, -1, keepdims=True)
        )
        return carry

    if fused:
        last = sums.experts - 1

        for e in range(last):
            for s in range(3, sums.dp_n):
                sums.advance(e, s)
        sums.advance(last, 1)

        def rest():
            for s in range(3, sums.dp_n):
                sums.advance(last, s)

        sums.tail(
            {
                "sources": results.combine,
                "context": share_rest,
                "dp": functools.partial(sums.advance, last, 2),
                "context_back": rest,
                "last": settle,
            }
        )
        sums.finish()
        results.finish()
    else:
        settle()
    if ctx_n == 2:
        pl.when(ctx == 1)(copies[0].wait_send)


def attention_backward(d_mid, saved, hidden, ids, router, w_qkv, w_out, down, up, expert_sums, done, experts, width):
    ctx_n, exp_n = lax.axis_size("context"), lax.axis_size("expert")
    tok, model = hidden.shape
    pairs = model // 128
    wide = down.shape[1]
    cos_table, sin_table = rope_tables(ctx_n * tok, 64)
    vmem = pl.BlockSpec(memory_space=pltpu.VMEM)
    dma = pltpu.SemaphoreType.DMA
    many = max(ctx_n - 1, 1)
    shape = jax.ShapeDtypeStruct
    q, k, v, normed, ranks, totals, flat, rank_out, seg_all = saved
    cos_table, sin_table = jnp.asarray(cos_table), jnp.asarray(sin_table)
    staged = (
        d_mid, up, down, w_out, rank_out, flat, q, k, v, totals, seg_all, cos_table, sin_table, w_qkv,
        ranks, hidden, router,
    )
    hbm = pl.BlockSpec(memory_space=pl.ANY)
    spill = ctx_n > 2
    landing = ((many, tok, model), BF)
    attn_tiles, adapters = 8 * pairs, down.shape[0]
    sums_outs, sums_scratch = sums_shapes(experts, model, width, attn_tiles, adapters)
    fused = None
    if not spill:
        fused = tuple(lax.axis_size(axis) for axis in ALL_AXES) + (adapters, attn_tiles)
    tiles_shape = ((attn_tiles, 16, 128), BF)
    results = pl.pallas_call(
        functools.partial(backward_kernel, (ctx_n, exp_n, wide // 4, fused)),
        out_shape=(shape((tok, model), F32),)
        + ((shape(*tiles_shape), shape(*landing)) if spill else sums_outs + (shape((tok, model), BF),)),
        in_specs=[pl.BlockSpec(memory_space=pltpu.SMEM)] + [hbm] * 18 + ([] if spill else [hbm] * 4 + [vmem]),
        out_specs=(vmem, vmem) + ((pl.BlockSpec(memory_space=pl.ANY),) if spill else (vmem, vmem)),
        scratch_shapes=([] if spill else [pltpu.VMEM(*tiles_shape), pltpu.VMEM(*landing)])
        + [
            pltpu.VMEM((pairs, tok, 128), BF),
            pltpu.VMEM((ctx_n, tok, tok), BF if spill else F32),
            pltpu.VMEM((ctx_n, 128, tok), F32),
            pltpu.VMEM((ctx_n, 128, tok), F32),
            pltpu.VMEM((tok, model), BF),
            pltpu.VMEM((ctx_n, 2, tok, model), BF),
            pltpu.VMEM((tok, model), BF),
            pltpu.VMEM((wide, model), F32),
            pltpu.VMEM((wide, model), F32),
            pltpu.VMEM((min(ctx_n, 2), tok, model), BF),
            dma((many, 2)), dma((many, 2)), dma((2,)),
        ]
        + ([] if spill else sums_scratch + results_shapes(exp_n, done[0]))
        + stage_scratch(*staged),
        compiler_params=pltpu.CompilerParams(
            collective_id=3, has_side_effects=True, vmem_limit_bytes=VLIMIT + 5 * 2**19
        ),
        name="attention_backward",
    )(
        ids, d_mid, q, k, v, normed, ranks, totals, flat, rank_out, hidden, seg_all,
        router, w_qkv, w_out, down, up, cos_table, sin_table, *([] if spill else [*expert_sums, *done]),
    )
    if spill:
        sums = add_up(ids, expert_sums, results[1], experts, width, adapters)
        return (results[0],) + tuple(sums) + (return_results(done),)
    return results


def partners(exp_n, me):
    core = lax.rem(me, 2)
    twin = me + 1 - 2 * core
    far = []
    for step in range(2, exp_n, 2):
        far += [lax.rem(me + step, exp_n), lax.rem(twin + step, exp_n)]
    return far + [twin]


def hot_rows(slot_rows, first, count):
    target = first + lax.broadcasted_iota(jnp.int32, (count, slot_rows.shape[1]), 0)
    return target == slot_rows


def moe_kernel(
    sizes, ids_ref, rows_ref, mid_hbm, logits_ref, slots_ref, dy_hbm, arrived_hbm, router_ref, mix_ref,
    vec_ref, gate_up_hbm, down_hbm, in_down_hbm, in_up_hbm, out_down_hbm, out_up_hbm,
    base_ref, d_mid_ref, grad_prev_ref, sums_ref, early_ref, done_out, cols_ref, part_z,
    d_logits_ref, mix_pad, done_gate, back_gate, tiles_ref, arrived_x, gate_up_ref, w_down_ref, sent_rows, sent_gates, arrived_rows, arrived_gates, act_ref, d_pre_ref,
    done_rows, back_rows, gates_ref,
    weight_sem, row_send, row_recv, gate_send, gate_recv, out_send, out_recv, in_send, in_recv,
    x_send, x_recv, z_send, z_recv, *staged,
):
    in_down_ref, in_up_ref, out_down_ref, out_up_ref, arrived_dy, mid_ref, dy_ref, stage_sem = staged
    stages = stage_copies(
        (in_down_hbm, in_up_hbm, out_down_hbm, out_up_hbm, arrived_hbm, mid_hbm, dy_hbm), staged, stage_sem
    )
    ctx_n, dp_n, exp_n, kinds, rank, share = sizes
    ctx, dp = lax.axis_index("context"), lax.axis_index("dp")
    me = lax.axis_index("expert")
    my_chip, my_core = me // 2, lax.rem(me, 2)
    first_seq = lax.axis_index("dp") * exp_n
    tok, model = rows_ref.shape
    experts, width = w_down_ref.shape[:2]
    capacity = arrived_rows.shape[3]
    per_owner = experts * capacity
    both = 2 * capacity
    entered = greet([("expert", exp_n), ("context", ctx_n), ("dp", dp_n)])
    loads = []
    for e in range(experts):
        for hbm, ref, k in ((gate_up_hbm, gate_up_ref, 0), (down_hbm, w_down_ref, 1)):
            load = pltpu.make_async_copy(hbm.at[e], ref.at[e], weight_sem.at[e, k])
            load.start()
            loads.append(load)
        if e == 0:
            for stage in stages:
                stage.start()

    lane = lax.broadcasted_iota(jnp.int32, (tok, 128), 1)
    logits = logits_ref[...]
    masked = jnp.where(lane < kinds, logits, NEG)
    exps = jnp.exp(masked - jnp.max(masked, -1, keepdims=True))
    probs = exps / jnp.sum(exps, -1, keepdims=True)
    slot_cols = jnp.transpose(
        jnp.concatenate([slots_ref[...], jnp.zeros((120, tok), F32)], 0)
    )
    gates = [
        jnp.sum(jnp.where(lane == slot_cols[:, k : k + 1].astype(jnp.int32), probs, 0.0), -1, keepdims=True)
        for k in range(2)
    ]
    gates_ref[...] = jnp.where(lane == 0, gates[0], jnp.where(lane == 1, gates[1], 0.0))
    cols_ref[...] = jnp.where(lane == 4, gates[0], jnp.where(lane == 5, gates[1], slot_cols))
    gate_rows = jnp.transpose(gates_ref[...])
    parts = []
    sub = lax.broadcasted_iota(jnp.int32, (16, tok), 0)
    for k in range(2):
        whole = jnp.broadcast_to(gate_rows[k : k + 1], (16, tok))
        high = whole.astype(BF).astype(F32)
        middle = (whole - high).astype(BF).astype(F32)
        lowest = whole - high - middle
        parts.append(
            jnp.where(sub == 0, high, jnp.where(sub == 1, middle, jnp.where(sub == 2, lowest, 0.0))).astype(BF)
        )
    slot_rows = [slots_ref[2 + k : 3 + k].astype(jnp.int32) for k in range(2)]

    def pick(owner, e):
        hots = [hot_rows(slot_rows[k], owner * per_owner + e * capacity, capacity) for k in range(2)]
        hot = jnp.where(hots[0] | hots[1], 1.0, 0.0).astype(BF)
        gates = sum(nt(parts[k], jnp.where(hots[k], 1.0, 0.0).astype(BF)) for k in range(2))
        return gates.astype(BF), nn(hot, rows_ref[...]).astype(BF)

    entered()
    sends = []
    others = partners(exp_n, me)
    for e in range(experts):
        for i, peer in enumerate(others):
            sent_gates[i, e], sent_rows[i, e] = pick(peer, e)
            for src, dst, send, recv in (
                (sent_gates, arrived_gates, gate_send, gate_recv),
                (sent_rows, arrived_rows, row_send, row_recv),
            ):
                copy = remote(
                    src.at[i, e], dst.at[my_chip, e, my_core], send.at[i, e], recv.at[me, e], "expert", peer
                )
                copy.start()
                sends.append(copy)
        arrived_gates[my_chip, e, my_core], arrived_rows[my_chip, e, my_core] = pick(me, e)

    def arrive(source, e):
        for ref, src, send, recv in (
            (arrived_gates, sent_gates, gate_send, gate_recv),
            (arrived_rows, sent_rows, row_send, row_recv),
        ):
            remote(
                src.at[0, e], ref.at[source // 2, e, lax.rem(source, 2)], send.at[0, e], recv.at[source, e],
                "expert", source,
            ).wait_recv()

    row64 = lax.broadcasted_iota(jnp.int32, (both, 4 * rank), 0) // capacity
    col64 = lax.broadcasted_iota(jnp.int32, (both, 4 * rank), 1)
    mine64 = row64 == col64 // (2 * rank)
    is_gate = col64 % (2 * rank) < rank
    mine32 = lax.broadcasted_iota(jnp.int32, (both, 2 * rank), 0) // capacity == (
        lax.broadcasted_iota(jnp.int32, (both, 2 * rank), 1) // rank
    )
    step_cols = 512
    per_step = step_cols // 128
    across, deep = model // 128, width // 128
    first_up = 2 * across
    first_out = first_up + 2 * deep
    first_last = first_out + deep

    def put(source, e, tile, value):
        tiles_ref[source, tile // share, e * share + tile % share] = value

    def x_copies(chip, e):
        copies = []
        for step in range(1, ctx_n):
            peer = lax.rem(ctx + step, ctx_n)
            here = pl.ds(e * share, share)
            copies.append(
                remote(
                    tiles_ref.at[pl.ds(2 * chip, 2), peer, here],
                    arrived_x.at[step - 1, pl.ds(2 * chip, 2), here],
                    x_send.at[step - 1, chip, e], x_recv.at[step - 1, chip, e], "context", peer,
                )
            )
        return copies

    def work(chip, e):
        names = [ids_ref[first_seq + 2 * chip + core] for core in range(2)]

        def stack(ref, cols=slice(None)):
            return jnp.concatenate([ref[name, e, :, cols] for name in names], 0)

        rows = arrived_rows[chip, e].reshape(both, model)
        in_down = stack(in_down_ref)
        out_up = stack(out_up_ref)
        gate = []
        for core in range(2):
            piece = arrived_gates[chip, e, core].astype(F32)
            total = piece[0:1] + piece[1:2] + piece[2:3]
            gate.append(jnp.transpose(jnp.broadcast_to(total, (128, capacity)))[:, 0:1])
        gate = jnp.concatenate(gate, 0)
        d_out = (gate * arrived_dy[chip, e].reshape(both, model).astype(F32)).astype(BF)
        ranks = jnp.where(mine64, nt(rows, in_down), 0.0).astype(BF)
        twice = ADAPT_SCALE * ranks.astype(F32)
        twice_gate = jnp.where(is_gate, twice, 0.0).astype(BF)
        twice_up = jnp.where(is_gate, 0.0, twice).astype(BF)
        d_mid_rank = jnp.where(mine32, ADAPT_SCALE * nt(d_out, out_up), 0.0).astype(BF)

        def chunk(i, carry):
            rank_mid, d_rank = carry
            start = pl.multiple_of(i * step_cols, step_cols)
            cols = pl.ds(start, step_cols)
            up_cols = pl.ds(pl.multiple_of(width + i * step_cols, step_cols), step_cols)
            in_up = stack(in_up_ref, cols)
            out_down = stack(out_down_ref, cols)
            gate_pre = nn(rows, gate_up_ref[e, :, cols]) + nn(twice_gate, in_up)
            up_pre = nn(rows, gate_up_ref[e, :, up_cols]) + nn(twice_up, in_up)
            d_act = (nt(d_out, w_down_ref[e, cols, :]) + nn(d_mid_rank, out_down)).astype(BF).astype(F32)
            sigma = 1.0 / (1.0 + jnp.exp(-gate_pre))
            silu = gate_pre * sigma
            act = (silu * up_pre).astype(BF)
            d_gate = (d_act * up_pre * sigma * (1.0 + gate_pre * (1.0 - sigma))).astype(BF)
            d_up = (d_act * silu).astype(BF)
            act_ref[:, cols] = act
            d_pre_ref[:, cols] = d_gate
            d_pre_ref[:, up_cols] = d_up
            rank_mid = rank_mid + nt(act, out_down)
            d_rank = d_rank + jnp.where(is_gate, nt(d_gate, in_up), nt(d_up, in_up))
            grad_up = (tn(twice_gate, d_gate) + tn(twice_up, d_up)).astype(BF)
            grad_out = tn(d_mid_rank, act).astype(BF)
            for core in range(2):
                for t in range(per_step):
                    here = slice(t * 128, t * 128 + 128)
                    tile = i * per_step + t
                    for which in range(2):
                        first = (2 * core + which) * rank
                        put(
                            2 * chip + core, e, first_up + which * deep + tile,
                            grad_up[first : first + rank, here],
                        )
                    put(
                        2 * chip + core, e, first_out + tile,
                        grad_out[core * rank : (core + 1) * rank, here],
                    )
            return rank_mid, d_rank

        rank_mid, d_rank = lax.fori_loop(
            0, width // step_cols, chunk,
            (jnp.zeros((both, 2 * rank), F32), jnp.zeros((both, 4 * rank), F32)),
        )
        twice_mid = jnp.where(
            mine32, ADAPT_SCALE * rank_mid.astype(BF).astype(F32), 0.0
        ).astype(BF)

        def out_chunk(i, carry):
            cols = pl.ds(pl.multiple_of(i * 256, 256), 256)
            value = nn(act_ref[...], w_down_ref[e, :, cols]) + nn(twice_mid, stack(out_up_ref, cols))
            for core in range(2):
                done_out[chip, e, core, :, cols] = value[core * capacity : (core + 1) * capacity].astype(BF)
            return carry

        lax.fori_loop(0, model // 256, out_chunk, 0)
        for core in range(2):
            d_gate = jnp.sum(
                arrived_dy[chip, e, core].astype(F32) * done_out[chip, e, core].astype(F32), -1, keepdims=True
            )
            done_gate[chip, e, core] = jnp.transpose(jnp.broadcast_to(d_gate, (capacity, 128)))[0:8]
        give_back(chip, e, done_gate, back_gate, out_send, out_recv)
        d_rank_in = jnp.where(mine64, ADAPT_SCALE * d_rank, 0.0).astype(BF)

        def in_chunk(i, carry):
            cols = pl.ds(pl.multiple_of(i * 256, 256), 256)
            value = nt(d_pre_ref[...], gate_up_ref[e, cols, :]) + nn(d_rank_in, stack(in_down_ref, cols))
            for core in range(2):
                done_rows[chip, e, core, :, cols] = value[core * capacity : (core + 1) * capacity].astype(BF)
            return carry

        lax.fori_loop(0, model // 256, in_chunk, 0)
        give_back(chip, e, done_rows, back_rows, in_send, in_recv)
        grad_last = tn(twice_mid, d_out).astype(BF)
        grad_first = tn(d_rank_in, rows).astype(BF)
        for core in range(2):
            for t in range(across):
                here = slice(t * 128, t * 128 + 128)
                for which in range(2):
                    first = (2 * core + which) * rank
                    put(
                        2 * chip + core, e, which * across + t, grad_first[first : first + rank, here]
                    )
                put(
                    2 * chip + core, e, first_last + t,
                    grad_last[core * rank : (core + 1) * rank, here],
                )
        for copy in x_copies(chip, e):
            copy.start()

    def give_back(chip, e, done, back, send, recv):
        for core in range(2):
            target = 2 * chip + core
            copy = remote(
                done.at[chip, e, core], back.at[me * experts + e], send.at[target, e], recv.at[me, e],
                "expert", target,
            )

            @pl.when(target == me)
            def _(core=core):
                back[me * experts + e] = done[chip, e, core]

            @pl.when(target != me)
            def _(copy=copy):
                copy.start()

    def own_work(e):
        arrive(others[-1], e)
        work(my_chip, e)

    def gather(e, out_ref):
        for chip in range(exp_n // 2):
            for copy in x_copies(chip, e):
                copy.wait_recv()

        def add(tile, carry):
            here = pl.ds(e * share + tile, 1)
            total = tiles_ref[:, ctx, here].astype(F32)
            for step in range(1, ctx_n):
                total = total + arrived_x[step - 1, :, here].astype(F32)
            out_ref[:, pl.ds(tile, 1)] = total.astype(BF)
            return carry

        lax.fori_loop(0, share, add, 0)

    z_tiles = early_ref.shape[3]
    z_copies = []
    for load in loads[:2]:
        load.wait()
    for stage in stages[:5]:
        stage.wait()
    own_work(0)
    for e in range(experts):
        if e > 0:
            for load in loads[2 * e : 2 * e + 2]:
                load.wait()
        for step in range(1, exp_n // 2):
            arrive(others[2 * step - 2], e)
            arrive(others[2 * step - 1], e)
            work(lax.rem(my_chip + step, exp_n // 2), e)
    for e in range(experts - 1):
        if e > 0:
            own_work(e)
        gather(e, part_z.at[e])
        early_ref[e, 0] = part_z[e, :, pl.ds(dp * z_tiles, z_tiles)]
        for k in range(1, dp_n):
            peer = lax.rem(dp + k, dp_n)
            copy = remote(
                part_z.at[e, :, pl.ds(peer * z_tiles, z_tiles)], early_ref.at[e, k], z_send.at[e, k], z_recv.at[e, k],
                "dp", peer,
            )
            copy.start()
            z_copies.append(copy)

    if experts > 1:
        own_work(experts - 1)
    for stage in stages[5:]:
        stage.wait()

    def collect(done, back, send, recv):
        for owner in others:
            for e in range(experts):
                remote(
                    done.at[0, e, 0], back.at[owner * experts + e], send.at[owner, e], recv.at[owner, e],
                    "expert", owner,
                ).wait_recv()

    slots_total = exp_n * per_owner
    block = 256

    def hot_cols(rows):
        target = lax.broadcasted_iota(jnp.int32, (block, slots_total), 1)
        return [target == cols_ref[rows, 2 + k : 3 + k].astype(jnp.int32) for k in range(2)]

    gain = router_ref[17:18].astype(F32)
    lanes = lax.broadcasted_iota(jnp.int32, (block, 128), 1)
    ffn_kinds = exp_n * experts

    def outward(i, carry):
        rows = pl.ds(pl.multiple_of(i * block, block), block)
        hots = hot_cols(rows)
        mid = mid_ref[rows]
        dy = dy_ref[rows].astype(F32)
        normed = mid * lax.rsqrt(jnp.mean(mid * mid, -1, keepdims=True) + EPSILON) * gain
        logits = logits_ref[rows]
        masked = jnp.where(lanes < kinds, logits, NEG)
        exps = jnp.exp(masked - jnp.max(masked, -1, keepdims=True))
        probs = exps / jnp.sum(exps, -1, keepdims=True)
        pairs = []
        for c in range(2):
            one, two = logits[:, kinds + 2 * c : kinds + 2 * c + 1], logits[:, kinds + 2 * c + 1 : kinds + 2 * c + 2]
            pairs.append((1.0 / (1.0 + jnp.exp(two - one)), 1.0 / (1.0 + jnp.exp(one - two))))
        along = jnp.sum(dy * normed, -1, keepdims=True)
        across_vec = [jnp.sum(dy * vec_ref[c : c + 1].astype(F32), -1, keepdims=True) for c in range(2)]
        d_kinds = jnp.zeros((block, 128), F32)
        dy_scale = jnp.zeros((block, 1), F32)
        weights = [jnp.zeros((block, 1), F32)] * 2
        for k in range(2):
            kind = cols_ref[rows, k : k + 1].astype(jnp.int32)
            gate = gates_ref[rows, k : k + 1]
            scale = jnp.where(kind == ffn_kinds + 1, 1.0, 0.0)
            picked = jnp.zeros((block, 128), F32)
            for owner in range(exp_n * experts):
                hot = hots[k][:, owner * capacity : (owner + 1) * capacity]
                picked = picked + jnp.where(hot, back_gate[owner, 0:1], 0.0)
            d_gate = jnp.sum(picked, -1, keepdims=True)
            for c in range(2):
                here = jnp.where(kind == ffn_kinds + 2 + c, 1.0, 0.0)
                scale = scale + here * pairs[c][0]
                d_gate = d_gate + here * pairs[c][1] * across_vec[c]
                weights[c] = weights[c] + here * gate
            d_gate = d_gate + scale * along
            dy_scale = dy_scale + gate * scale
            d_kinds = d_kinds + jnp.where(lanes == kind, d_gate, 0.0)
        base = mid + dy_scale * normed
        for c in range(2):
            base = base + (weights[c] * pairs[c][1]) * vec_ref[c : c + 1].astype(F32)
        base_ref[rows] = base
        d_logits = probs * (d_kinds - jnp.sum(probs * d_kinds, -1, keepdims=True))
        for c in range(2):
            d_one = weights[c] * along
            d_two = weights[c] * across_vec[c]
            mean = pairs[c][0] * d_one + pairs[c][1] * d_two
            d_logits = jnp.where(lanes == kinds + 2 * c, pairs[c][0] * (d_one - mean), d_logits)
            d_logits = jnp.where(lanes == kinds + 2 * c + 1, pairs[c][1] * (d_two - mean), d_logits)
        d_logits_ref[rows] = d_logits
        high = d_logits.astype(BF)
        rest = d_logits - high.astype(F32)
        middle = rest.astype(BF)
        lowest = (rest - middle.astype(F32)).astype(BF)
        router = router_ref[...]
        d_mid_ref[rows] = dy_scale * dy + (nn(high, router) + nn(middle, router) + nn(lowest, router))
        return carry

    def inward(i, carry):
        rows = pl.ds(pl.multiple_of(i * block, block), block)
        hots = hot_cols(rows)
        table = back_rows[...].reshape(slots_total, model)
        hot = jnp.where(hots[0] | hots[1], 1.0, 0.0).astype(BF)
        scaled = (d_mid_ref[rows] + nn(hot, table)) * gain
        mid = mid_ref[rows]
        inv = lax.rsqrt(jnp.mean(mid * mid, -1, keepdims=True) + EPSILON)
        d_mid_ref[rows] = (
            dy_ref[rows].astype(F32)
            + inv * scaled
            - mid * (inv * inv * inv) * jnp.mean(scaled * mid, -1, keepdims=True)
        )
        return carry

    collect(done_gate, back_gate, out_send, out_recv)
    lax.fori_loop(0, tok // block, outward, 0)
    mix_pad[...] = jnp.zeros_like(mix_pad)
    mix_pad[0:kinds, 0:kinds] = mix_ref[...]
    grad_prev = lax.dot_general(
        mix_pad[...], d_logits_ref[...], (((1,), (1,)), ((), ())), precision=HIGH, preferred_element_type=F32
    )
    for kind in range(kinds):
        grad_prev_ref[kind] = grad_prev[kind : kind + 1]
    collect(done_rows, back_rows, in_send, in_recv)
    lax.fori_loop(0, tok // block, inward, 0)
    gather(experts - 1, sums_ref)
    for chip in range(exp_n // 2):
        for e in range(experts):
            for copy in x_copies(chip, e):
                copy.wait_send()
    for copy in z_copies:
        copy.wait()
    for copy in sends:
        copy.wait_send()
    for target in others:
        for e in range(experts):
            for done, back, send, recv in (
                (done_gate, back_gate, out_send, out_recv),
                (done_rows, back_rows, in_send, in_recv),
            ):
                remote(
                    done.at[0, e, 0], back.at[0], send.at[target, e], recv.at[target, e],
                    "expert", target,
                ).wait_send()


def expert_tiling(experts, model, width):
    share = pl.cdiv(3 * (model + width) // 128, lax.axis_size("context"))
    z_tiles = pl.cdiv(share, lax.axis_size("dp"))
    return share, z_tiles * lax.axis_size("dp"), z_tiles


def attn_tiling(attn_tiles):
    own = attn_tiles // lax.axis_size("expert")
    x_tiles = pl.cdiv(own, lax.axis_size("context"))
    return own, x_tiles, pl.cdiv(x_tiles, lax.axis_size("dp"))


def expert_layer(rows, mid, logits, slots, dy, arrived_dy, ids, router, mix, vec, w_gate_up, w_down, tables):
    exp_n = lax.axis_size("expert")
    tok, model = rows.shape
    experts, width = w_down.shape[:2]
    capacity = tok // 4
    rank = tables[3].shape[2]
    ctx_n = lax.axis_size("context")
    dp_n = lax.axis_size("dp")
    share, x_tiles, z_tiles = expert_tiling(experts, model, width)
    many, before = max(ctx_n - 1, 1), max(experts - 1, 1)
    chips = exp_n // 2
    vmem = pl.BlockSpec(memory_space=pltpu.VMEM)
    hbm = pl.BlockSpec(memory_space=pl.ANY)
    dma = pltpu.SemaphoreType.DMA
    shape = jax.ShapeDtypeStruct
    block = (experts, capacity, model)
    kinds = mix.shape[0]
    return pl.pallas_call(
        functools.partial(moe_kernel, (ctx_n, dp_n, exp_n, kinds, rank, share)),
        out_shape=(
            shape((tok, model), F32),
            shape((tok, model), F32),
            shape((kinds, 1, tok), F32),
            shape((exp_n, x_tiles, 16, 128), BF),
            shape((before, dp_n, exp_n, z_tiles, 16, 128), BF),
            shape((chips, experts, 2, capacity, model), BF),
            shape((tok, 128), F32),
        ),
        in_specs=[pl.BlockSpec(memory_space=pltpu.SMEM), vmem, hbm, vmem, vmem, hbm, hbm]
        + [vmem] * 3
        + [hbm] * 6,
        out_specs=(vmem,) * 7,
        scratch_shapes=[
            pltpu.VMEM((before, exp_n, x_tiles, 16, 128), BF),
            pltpu.VMEM((tok, 128), F32),
            pltpu.VMEM((16, 128), F32),
            pltpu.VMEM((chips, experts, 2, 8, 128), F32),
            pltpu.VMEM((exp_n * experts, 8, 128), F32),
            pltpu.VMEM((exp_n, ctx_n, experts * share, 16, 128), BF),
            pltpu.VMEM((many, exp_n, experts * share, 16, 128), BF),
            pltpu.VMEM((experts, model, 2 * width), BF),
            pltpu.VMEM((experts, width, model), BF),
            pltpu.VMEM((exp_n - 1,) + block, BF),
            pltpu.VMEM((exp_n - 1, experts, 16, capacity), BF),
            pltpu.VMEM((chips, experts, 2, capacity, model), BF),
            pltpu.VMEM((chips, experts, 2, 16, capacity), BF),
            pltpu.VMEM((2 * capacity, width), BF),
            pltpu.VMEM((2 * capacity, 2 * width), BF),
            pltpu.VMEM((chips, experts, 2, capacity, model), BF),
            pltpu.VMEM((exp_n * experts, capacity, model), BF),
            pltpu.VMEM((tok, 128), F32),
            dma((experts, 2)), dma((exp_n - 1, experts)), dma((exp_n, experts)), dma((exp_n - 1, experts)),
            dma((exp_n, experts)),
            dma((exp_n, experts)), dma((exp_n, experts)), dma((exp_n, experts)), dma((exp_n, experts)),
            dma((many, chips, experts)), dma((many, chips, experts)), dma((before, dp_n)), dma((before, dp_n)),
        ]
        + stage_scratch(*tables, arrived_dy, mid, dy),
        compiler_params=pltpu.CompilerParams(
            collective_id=4, has_side_effects=True, vmem_limit_bytes=VLIMIT
        ),
        name="expert_layer",
    )(
        ids, rows, mid, logits, slots, dy, arrived_dy, router, mix, vec, w_gate_up,
        w_down, *tables,
    )


def stage_copies(sources, targets, sem):
    return [
        pltpu.make_async_copy(src, dst, sem.at[i]) for i, (src, dst) in enumerate(zip(sources, targets))
    ]


def stage_scratch(*arrays):
    return [pltpu.VMEM(array.shape, array.dtype) for array in arrays] + [
        pltpu.SemaphoreType.DMA((len(arrays),))
    ]


class Results:
    def __init__(self, exp_n, done_ref, base_ref, cols_ref, hidden_ref, scratch):
        self.done_ref, self.base_ref, self.cols_ref, self.hidden_ref = done_ref, base_ref, cols_ref, hidden_ref
        self.back_ref, self.base_buf, self.send_sem, self.recv_sem, own_sem = scratch
        self.me = lax.axis_index("expert")
        self.experts = done_ref.shape[1]
        self.others = partners(exp_n, self.me)
        self.own = [
            pltpu.make_async_copy(
                done_ref.at[self.me // 2, e, lax.rem(self.me, 2)], self.back_ref.at[self.me * self.experts + e],
                own_sem.at[e],
            )
            for e in range(self.experts)
        ] + [pltpu.make_async_copy(base_ref, self.base_buf, own_sem.at[self.experts])]

    def copy(self, other, e, owner):
        return remote(
            self.done_ref.at[other // 2, e, lax.rem(other, 2)], self.back_ref.at[owner * self.experts + e],
            self.send_sem.at[other, e], self.recv_sem.at[owner, e], "expert", other,
        )

    def start(self):
        for other in self.others:
            for e in range(self.experts):
                self.copy(other, e, self.me).start()
        for copy in self.own:
            copy.start()

    def combine(self):
        for copy in self.own:
            copy.wait()
        for other in self.others:
            for e in range(self.experts):
                self.copy(other, e, other).wait_recv()
        tok, model = self.base_ref.shape
        slots = self.back_ref.shape[0] * self.back_ref.shape[1]
        block = 256

        def rows_out(i, carry):
            rows = pl.ds(pl.multiple_of(i * block, block), block)
            table = self.back_ref[...].reshape(slots, model)
            target = lax.broadcasted_iota(jnp.int32, (block, slots), 1)
            total = self.base_buf[rows]
            for k in range(2):
                slot = self.cols_ref[rows, 2 + k : 3 + k].astype(jnp.int32)
                gate = self.cols_ref[rows, 4 + k : 5 + k]
                total = total + gate * nn(jnp.where(target == slot, 1.0, 0.0).astype(BF), table)
            self.hidden_ref[rows] = total.astype(BF)
            return carry

        lax.fori_loop(0, tok // block, rows_out, 0)

    def finish(self):
        for other in self.others:
            for e in range(self.experts):
                self.copy(other, e, self.me).wait_send()


def results_shapes(exp_n, done):
    _, experts, _, capacity, model = done.shape
    dma = pltpu.SemaphoreType.DMA
    return [
        pltpu.VMEM((exp_n * experts, capacity, model), BF), pltpu.VMEM((4 * capacity, model), F32),
        dma((exp_n, experts)), dma((exp_n, experts)), dma((experts + 1,)),
    ]


def results_kernel(exp_n, done_ref, base_ref, cols_ref, hidden_ref, *scratch):
    greet([("expert", exp_n)])()
    results = Results(exp_n, done_ref, base_ref, cols_ref, hidden_ref, scratch)
    results.start()
    results.combine()
    results.finish()


def return_results(done):
    exp_n = lax.axis_size("expert")
    vmem = pl.BlockSpec(memory_space=pltpu.VMEM)
    return pl.pallas_call(
        functools.partial(results_kernel, exp_n),
        out_shape=jax.ShapeDtypeStruct(done[1].shape, BF),
        in_specs=[pl.BlockSpec(memory_space=pl.ANY)] * 2 + [vmem],
        out_specs=vmem,
        scratch_shapes=results_shapes(exp_n, done[0]),
        compiler_params=pltpu.CompilerParams(
            collective_id=5, has_side_effects=True, vmem_limit_bytes=VLIMIT
        ),
        name="return_results",
    )(*done)


class Sums:
    def __init__(self, sizes, ids_ref, sums_ref, early_ref, attn_ref, table_ref, attn_table, scratch):
        self.ctx_n, self.dp_n, self.exp_n, self.adapters, self.attn_tiles = sizes
        self.ids_ref, self.attn_ref = ids_ref, attn_ref
        self.table_ref, self.attn_table = table_ref, attn_table
        self.ctx, self.dp, self.exp = (lax.axis_index(axis) for axis in ALL_AXES)
        (
            self.arrived_z, self.early, self.held_a, self.arrived_xa, self.part_a, self.arrived_za,
            self.z_send, self.z_recv, self.az_send, self.az_recv, self.ax_send, self.ax_recv,
            self.r_send, self.r_recv, self.xa_send, self.xa_recv, self.za_send, self.za_recv,
            self.bz_send, self.bz_recv, self.bx_send, self.bx_recv, self.be_send, self.be_recv,
            self.keep_sem, load_sem,
        ) = scratch
        self.waits = []
        z_tiles = self.arrived_z.shape[2]
        self.experts = table_ref.shape[2]
        self.loads = [
            pltpu.make_async_copy(early_ref, self.early, load_sem.at[0]),
            pltpu.make_async_copy(
                sums_ref.at[:, pl.ds(self.dp * z_tiles, z_tiles)], self.arrived_z.at[0], load_sem.at[1]
            ),
        ]
        self.z_copies = [
            self.plan(
                sums_ref.at[:, pl.ds(self.peer("dp", k) * z_tiles, z_tiles)], self.arrived_z.at[k],
                self.z_send.at[k - 1], self.z_recv.at[k - 1], "dp", self.peer("dp", k),
            )
            for k in range(1, self.dp_n)
        ]
        self.lines, self.ax_copies = [], []
        for e in range(self.experts):
            self.lines.append([self.line(e, s) for s in range(1, self.dp_n)])
            self.ax_copies.append([self.across(e, origin) for origin in range(self.dp_n)])

    def slot(self, e, origin):
        return self.table_ref.at[self.ctx, lax.rem(origin + self.dp_n, self.dp_n), e]

    def line(self, e, s):
        ways = []
        for way, sign in enumerate((1, -1)):
            mine, landing = self.slot(e, self.dp - sign * (s - 1)), self.slot(e, self.dp - sign * s)
            target = lax.rem(self.dp + sign + self.dp_n, self.dp_n)
            send_sem, recv_sem = self.az_send.at[e, way, s - 1], self.az_recv.at[e, way, s - 1]
            edge, origin, source = self.dp + sign, self.dp - sign * (s - 1), self.dp - sign * s
            ways.append(
                (
                    remote(mine, mine, send_sem, recv_sem, "dp", target),
                    (edge >= 0) & (edge < self.dp_n) & (origin >= 0) & (origin < self.dp_n),
                    remote(landing, landing, send_sem, recv_sem, "dp", target),
                    (source >= 0) & (source < self.dp_n),
                )
            )
        return ways

    def across(self, e, origin):
        here = self.slot(e, origin)
        at = lax.rem(origin + self.dp_n, self.dp_n)
        return [
            remote(
                here, here, self.ax_send.at[step - 1, e, at], self.ax_recv.at[step - 1, e, at], "context",
                self.peer("context", step),
            )
            for step in range(1, self.ctx_n)
        ]

    def plan(self, src, dst, send, recv, axis, target):
        copy = remote(src, dst, send, recv, axis, target)
        self.waits.append(copy)
        return copy

    def peer(self, axis, step):
        index, size = {
            "context": (self.ctx, self.ctx_n), "dp": (self.dp, self.dp_n), "expert": (self.exp, self.exp_n)
        }[axis]
        return lax.rem(index + step, size)

    def send(self, src, dst, send, recv, axis, target):
        copy = self.plan(src, dst, send, recv, axis, target)
        copy.start()
        return copy

    def weight(self, k, source):
        origin = lax.rem(self.dp - k + self.dp_n, self.dp_n)
        name = self.ids_ref[origin * self.exp_n + source]
        return [jnp.where(name == a, 1.0, 0.0).astype(F32) for a in range(self.adapters)]

    def merge(self, count, read, write):
        marks = [self.weight(k, source) for k in range(self.dp_n) for source in range(self.exp_n)]

        def tile_sums(tile, carry):
            totals = [jnp.zeros((16, 128), F32)] * self.adapters
            for k in range(self.dp_n):
                for source in range(self.exp_n):
                    value = read(k, source, tile).astype(F32)
                    mark = marks[k * self.exp_n + source]
                    totals = [total + m * value for total, m in zip(totals, mark)]
            for a in range(self.adapters):
                write(a, tile, totals[a].astype(BF))
            return carry

        lax.fori_loop(0, count, tile_sums, 0)

    def start(self):
        for copy in self.loads:
            copy.start()
        if self.experts == 1:
            self.exchange()

    def exchange(self):
        for copy in self.z_copies:
            copy.start()

    def combine(self, e):
        z_tiles = self.arrived_z.shape[2]
        if e < self.experts - 1:
            if e == 0:
                self.loads[0].wait()
            source_ref = self.early.at[e]
        else:
            if self.experts == 1:
                self.loads[0].wait()
            self.loads[1].wait()
            for copy in self.z_copies:
                copy.wait_recv()
            source_ref = self.arrived_z

        def write(a, tile, value):
            self.table_ref[self.ctx, self.dp, e, a, tile] = value

        self.merge(z_tiles, lambda k, source, tile: source_ref[k, source, tile], write)
        self.push(e, 1)
        for copy in self.across(e, self.dp):
            copy.start()

    def push(self, e, s):
        if s < self.dp_n:
            for send, whether, _, _ in self.lines[e][s - 1]:
                pl.when(whether)(send.start)

    def advance(self, e, s):
        if s >= self.dp_n:
            return
        for _, _, receive, whether in self.lines[e][s - 1]:
            pl.when(whether)(receive.wait_recv)
        self.push(e, s + 1)
        for sign, (_, _, _, whether) in zip((1, -1), self.lines[e][s - 1]):
            @pl.when(whether)
            def _(sign=sign):
                for copy in self.across(e, self.dp - sign * s):
                    copy.start()

    def tail(self, between):
        def other(step):
            if step in between:
                between[step]()

        own, x_tiles, z_tiles = attn_tiling(self.attn_tiles)
        real = pl.cdiv(x_tiles, z_tiles)
        keep = pltpu.make_async_copy(
            self.attn_ref.at[pl.ds(self.exp * own, own)], self.held_a.at[self.exp, pl.ds(0, own)], self.keep_sem
        )
        keep.start()
        copies = [
            self.send(
                self.attn_ref.at[pl.ds(self.peer("expert", k) * own, own)],
                self.held_a.at[self.exp, pl.ds(0, own)],
                self.r_send.at[k - 1], self.r_recv.at[k - 1], "expert", self.peer("expert", k),
            )
            for k in range(1, self.exp_n)
        ]
        other("sources")
        keep.wait()
        for copy in copies:
            copy.wait_recv()
        copies = [
            self.send(
                self.held_a.at[:, pl.ds(self.peer("context", k) * x_tiles, x_tiles)], self.arrived_xa.at[k - 1],
                self.xa_send.at[k - 1], self.xa_recv.at[k - 1], "context", self.peer("context", k),
            )
            for k in range(1, self.ctx_n)
        ]
        other("context")
        for copy in copies:
            copy.wait_recv()
        total = self.held_a[:, pl.ds(self.ctx * x_tiles, x_tiles)].astype(F32)
        for k in range(1, self.ctx_n):
            total = total + self.arrived_xa[k - 1].astype(F32)
        self.part_a[:, 0:x_tiles] = total.astype(BF)
        copies = [
            self.send(
                self.part_a.at[:, pl.ds(self.peer("dp", k) * z_tiles, z_tiles)], self.arrived_za.at[k - 1],
                self.za_send.at[k - 1], self.za_recv.at[k - 1], "dp", self.peer("dp", k),
            )
            for k in range(1, self.dp_n)
        ]
        other("dp")
        for copy in copies:
            copy.wait_recv()
        mine = self.attn_table.at[self.exp]

        def write(a, tile, value):
            self.attn_table[self.exp, self.ctx, self.dp, a, tile] = value

        def read(k, source, tile):
            if k == 0:
                return self.part_a[source, self.dp * z_tiles + tile]
            return self.arrived_za[k - 1, source, tile]

        self.merge(z_tiles, read, write)
        here = mine.at[self.ctx, self.dp]
        copies = [
            self.send(here, here, self.bz_send.at[k - 1], self.bz_recv.at[k - 1], "dp", self.peer("dp", k))
            for k in range(1, self.dp_n)
        ]
        other("dp_back")
        for copy in copies:
            copy.wait_recv()
        here = mine.at[self.ctx, pl.ds(0, real)]
        copies = [
            self.send(
                here, here, self.bx_send.at[k - 1], self.bx_recv.at[k - 1], "context", self.peer("context", k)
            )
            for k in range(1, self.ctx_n)
        ]
        other("context_back")
        for copy in copies:
            copy.wait_recv()
        core = lax.rem(self.exp, 2)
        twin = self.exp + 1 - 2 * core
        chips = self.exp_n // 2

        def table_of(owner):
            return self.attn_table.at[owner, :, pl.ds(0, real)]

        far = [
            self.send(
                table_of(self.exp), table_of(self.exp), self.be_send.at[0, k - 1], self.be_recv.at[0, k - 1],
                "expert", self.peer("expert", 2 * k),
            )
            for k in range(1, chips)
        ]
        near = [
            self.send(
                table_of(self.exp), table_of(self.exp), self.be_send.at[1, 0], self.be_recv.at[1, 0], "expert", twin
            )
        ]
        for k in range(1, chips):
            far[k - 1].wait_recv()
            owner = self.peer("expert", self.exp_n - 2 * k)
            near.append(
                self.send(
                    table_of(owner), table_of(owner), self.be_send.at[1, k], self.be_recv.at[1, k], "expert", twin
                )
            )
        other("last")
        for copy in near:
            copy.wait_recv()

    def finish(self):
        for by_expert in self.ax_copies:
            for copies in by_expert:
                for copy in copies:
                    copy.wait()
        for by_expert in self.lines:
            for ways in by_expert:
                for send, whether, _, _ in ways:
                    pl.when(whether)(send.wait_send)
        for copy in self.waits:
            copy.wait_send()


def sums_shapes(experts, model, width, attn_tiles, adapters):
    ctx_n, dp_n, exp_n = (lax.axis_size(axis) for axis in ("context", "dp", "expert"))
    _, _, z_tiles = expert_tiling(experts, model, width)
    own, xa_tiles, za_tiles = attn_tiling(attn_tiles)
    many, deep, chips = max(ctx_n - 1, 1), max(dp_n - 1, 1), max(exp_n // 2, 1)
    dma = pltpu.SemaphoreType.DMA
    outs = (
        jax.ShapeDtypeStruct((ctx_n, dp_n, experts, adapters, z_tiles, 16, 128), BF),
        jax.ShapeDtypeStruct((exp_n, ctx_n, dp_n, adapters, za_tiles, 16, 128), BF),
    )
    scratch = [
        pltpu.VMEM((dp_n, exp_n, z_tiles, 16, 128), BF),
        pltpu.VMEM((max(experts - 1, 1), dp_n, exp_n, z_tiles, 16, 128), BF),
        pltpu.VMEM((exp_n, max(ctx_n * xa_tiles, own), 16, 128), BF),
        pltpu.VMEM((many, exp_n, xa_tiles, 16, 128), BF),
        pltpu.VMEM((exp_n, dp_n * za_tiles, 16, 128), BF),
        pltpu.VMEM((deep, exp_n, za_tiles, 16, 128), BF),
        dma((deep,)), dma((deep,)), dma((experts, 2, deep)), dma((experts, 2, deep)),
        dma((many, experts, dp_n)), dma((many, experts, dp_n)),
        dma((exp_n,)), dma((exp_n,)), dma((many,)), dma((many,)), dma((deep,)), dma((deep,)),
        dma((deep,)), dma((deep,)), dma((many,)), dma((many,)), dma((2, chips)), dma((2, chips)),
        dma, dma((2,)),
    ]
    return outs, scratch


ALL_AXES = ("context", "dp", "expert")


def sums_kernel(sizes, ids_ref, sums_ref, early_ref, attn_ref, table_ref, attn_table, *scratch):
    greet([(axis, lax.axis_size(axis)) for axis in ALL_AXES])()
    sums = Sums(sizes, ids_ref, sums_ref, early_ref, attn_ref, table_ref, attn_table, scratch)
    sums.start()
    for e in range(sums.experts):
        if e > 0 and e == sums.experts - 1:
            sums.exchange()
        sums.combine(e)
    for e in range(sums.experts):
        for s in range(1, sums.dp_n):
            sums.advance(e, s)
    sums.tail({})
    sums.finish()


def add_up(ids, sums, attn, experts, width, adapters):
    model = attn.shape[0] * 16
    outs, scratch = sums_shapes(experts, model, width, attn.shape[0], adapters)
    vmem, hbm = pl.BlockSpec(memory_space=pltpu.VMEM), pl.BlockSpec(memory_space=pl.ANY)
    sizes = tuple(lax.axis_size(axis) for axis in ALL_AXES) + (adapters, attn.shape[0])
    return pl.pallas_call(
        functools.partial(sums_kernel, sizes),
        out_shape=outs,
        in_specs=[pl.BlockSpec(memory_space=pltpu.SMEM), hbm, hbm, vmem],
        out_specs=(vmem, vmem),
        scratch_shapes=scratch,
        compiler_params=pltpu.CompilerParams(
            collective_id=1, has_side_effects=True, vmem_limit_bytes=VLIMIT
        ),
        name="reduce_adapters",
    )(ids, *sums, attn)


def unpack_kernel(sizes, table_ref, attn_ref, down_ref, up_ref, in_down_ref, in_up_ref, out_down_ref, out_up_ref):
    share, z_tiles, own, xa_tiles, za_tiles = sizes
    for expert in range(in_up_ref.shape[1]):
        tile = 0
        for out_ref in (in_down_ref, in_up_ref, out_down_ref, out_up_ref):
            rows, cols = out_ref.shape[2:]
            for row in range(rows // 16):
                for col in range(cols // 128):
                    place = tile % share
                    out_ref[0, expert, row * 16 : row * 16 + 16, col * 128 : col * 128 + 128] = table_ref[
                        tile // share, place // z_tiles, expert, 0, place % z_tiles
                    ].astype(F32)
                    tile += 1
    tile = 0
    for out_ref in (down_ref, up_ref):
        rows, cols = out_ref.shape[1:]
        for row in range(rows // 16):
            for col in range(cols // 128):
                place = tile % own
                out_ref[0, row * 16 : row * 16 + 16, col * 128 : col * 128 + 128] = attn_ref[
                    tile // own, place // xa_tiles, place % xa_tiles // za_tiles, 0, place % xa_tiles % za_tiles
                ].astype(F32)
                tile += 1


def unpack(table, attn_table, experts, width, table_shapes, attn_shape):
    adapters = table.shape[3]
    model = attn_shape[1]
    share, _, z_tiles = expert_tiling(experts, model, width)
    sizes = (share, z_tiles) + attn_tiling(8 * model // 128)
    shapes = [(adapters,) + attn_shape] * 2 + [(adapters,) + shape for shape in table_shapes]

    def by_adapter(array, axis):
        block = array.shape[:axis] + (1,) + array.shape[axis + 1 :]
        return pl.BlockSpec(block, lambda a, n=array.ndim: (0,) * axis + (a,) + (0,) * (n - axis - 1))

    return pl.pallas_call(
        functools.partial(unpack_kernel, sizes),
        grid=(adapters,),
        out_shape=tuple(jax.ShapeDtypeStruct(shape, F32) for shape in shapes),
        in_specs=[by_adapter(table, 3), by_adapter(attn_table, 3)],
        out_specs=tuple(
            pl.BlockSpec((1,) + shape[1:], lambda a, n=len(shape): (a,) + (0,) * (n - 1))
            for shape in shapes
        ),
        compiler_params=pltpu.CompilerParams(vmem_limit_bytes=VLIMIT),
        name="unpack_adapters",
    )(table, attn_table)


def local(
    hidden_in,
    prev_logits,
    segment_ids,
    routes,
    adapter_ids,
    attn_gain,
    w_qkv,
    w_out,
    attn_down,
    attn_up,
    ffn_gain,
    router_weight,
    gate_mix,
    const_mix,
    const_vec,
    w_gate_up,
    w_down,
    exp_in_down,
    exp_in_up,
    exp_out_down,
    exp_out_up,
    cotangent,
):
    model_dim = hidden_in.shape[2]
    local_experts, ffn_width = w_down.shape[:2]
    adapter_count = attn_down.shape[0]
    rank_dim = attn_up.shape[2]
    down_all = jnp.swapaxes(attn_down, 2, 3).reshape(adapter_count, 4 * rank_dim, model_dim)
    up_all = attn_up.reshape(adapter_count, 4 * rank_dim, model_dim)
    router_rows = jnp.concatenate(
        [
            router_weight.T,
            const_mix.transpose(0, 2, 1).reshape(4, model_dim),
            attn_gain[None],
            ffn_gain[None],
        ],
        0,
    )
    router_rows = jnp.pad(router_rows, ((0, 128 - router_rows.shape[0]), (0, 0)))
    (
        q_pairs, k_pairs, v_pairs, normed_all, rank_all, log_cols, attn_flat, rank_out_all, mid_resid,
        rows_low, logits_all, seg_all, arrived_dy, slots,
    ) = attention_forward(
        hidden_in[0], segment_ids, prev_logits[0].T, gate_mix, adapter_ids, w_qkv, w_out, down_all,
        up_all, router_rows, cotangent[0], routes[0].T, local_experts,
    )
    tables = (
        jnp.swapaxes(exp_in_down, 2, 3),
        exp_in_up.reshape(exp_in_up.shape[:2] + (2 * rank_dim, ffn_width)),
        jnp.swapaxes(exp_out_down, 2, 3),
        exp_out_up,
    )
    base, d_mid, grad_prev, *expert_sums, done_out, cols = expert_layer(
        rows_low, mid_resid, logits_all, slots, cotangent[0], arrived_dy, adapter_ids, router_rows,
        gate_mix, const_vec, w_gate_up, w_down, tables,
    )
    grad_in, table, attn_table, hidden_out = attention_backward(
        d_mid,
        (q_pairs, k_pairs, v_pairs, normed_all, rank_all, log_cols, attn_flat, rank_out_all, seg_all),
        hidden_in[0], adapter_ids, router_rows, w_qkv, w_out, down_all, up_all, expert_sums,
        (done_out, base, cols), local_experts, ffn_width,
    )
    sums = unpack(
        table, attn_table, local_experts, ffn_width, [entry.shape[1:] for entry in tables],
        (4 * rank_dim, model_dim),
    )
    grad_attn_down = jnp.swapaxes(sums[0].reshape(adapter_count, 4, rank_dim, model_dim), 2, 3)
    grad_attn_up = sums[1].reshape(adapter_count, 4, rank_dim, model_dim)
    grad_in_down = jnp.swapaxes(sums[2], 2, 3)
    grad_in_up = sums[3].reshape(exp_in_up.shape)
    grad_out_down = jnp.swapaxes(sums[4], 2, 3)
    grad_out_up = sums[5]
    return (
        hidden_out[None],
        grad_in[None],
        grad_prev.transpose(1, 2, 0),
        grad_attn_down,
        grad_attn_up,
        grad_in_down,
        grad_in_up,
        grad_out_down,
        grad_out_up,
    )


def solution(mesh):
    return jax.shard_map(
        local,
        mesh=mesh,
        in_specs=(
            P(("dp", "expert"), "context", None),
            P(("dp", "expert"), "context", None),
            P(("dp", "expert"), "context"),
            P(("dp", "expert"), "context", None),
            P(),
            P(),
            P(),
            P(),
            P(),
            P(),
            P(),
            P(),
            P(),
            P(),
            P(),
            P("expert", None, None),
            P("expert", None, None),
            P(None, "expert", None, None),
            P(None, "expert", None, None, None),
            P(None, "expert", None, None),
            P(None, "expert", None, None),
            P(("dp", "expert"), "context", None),
        ),
        out_specs=(
            P(("dp", "expert"), "context", None),
            P(("dp", "expert"), "context", None),
            P(("dp", "expert"), "context", None),
            P(),
            P(),
            P(None, "expert", None, None),
            P(None, "expert", None, None, None),
            P(None, "expert", None, None),
            P(None, "expert", None, None),
        ),
        check_vma=False,
    )
```

```python
import functools
import math

import jax
import jax.numpy as jnp
import numpy as np
from jax import lax
from jax.experimental import pallas as pl
from jax.experimental.pallas import tpu as pltpu
from jax.sharding import PartitionSpec as P

MESH = pl.DeviceIdType.MESH
VLIMIT = 60 * 1024 * 1024
BF = jnp.bfloat16
F32 = jnp.float32

HEADS = 12


EPSILON = 1e-06
ADAPT_SCALE = 2.0
NEG = -1e30
HIGH = lax.Precision.HIGHEST


def nt(left, right):
    return lax.dot_general(left, right, (((1,), (1,)), ((), ())), preferred_element_type=F32)


def tn(left, right):
    return lax.dot_general(left, right, (((0,), (0,)), ((), ())), preferred_element_type=F32)


def nn(left, right):
    return jnp.dot(left, right, preferred_element_type=F32)


def rope_tables(positions, width):
    half = width // 2
    frequency = np.exp(np.arange(half) * (-2.0 * math.log(10000.0) / width))
    angles = np.arange(positions)[:, None] * frequency[None, :]
    cosine, sine = np.cos(angles), np.sin(angles)
    return (
        np.concatenate([cosine] * 4, 1).astype(np.float32),
        np.concatenate([-sine, sine] * 2, 1).astype(np.float32),
    )


def turn(block, cosine, sine, width):
    half = width // 2
    lane = lax.broadcasted_iota(jnp.int32, block.shape, 1)
    other = jnp.where(
        lane % width < half, pltpu.roll(block, 128 - half, 1), pltpu.roll(block, half, 1)
    )
    return block * cosine + other * sine


def greet(axes):
    barrier = pltpu.get_barrier_semaphore()
    count = 0
    for axis, size in axes:
        index = lax.axis_index(axis)
        for step in range(1, size):
            pl.semaphore_signal(
                barrier, inc=1, device_id={axis: lax.rem(index + step, size)}, device_id_type=MESH
            )
        count += size - 1
    return lambda: pl.semaphore_wait(barrier, count)


def remote(src, dst, send, recv, axis, target):
    return pltpu.make_async_remote_copy(
        src_ref=src, dst_ref=dst, send_sem=send, recv_sem=recv,
        device_id={axis: target}, device_id_type=MESH,
    )


def blocks_of(ctx_n, ctx, count):
    return [lax.rem(ctx + 1 + j, ctx_n) for j in range(count)]


def fill_bias(bias_ref, seg_all, ctx, tok, j, block):
    own = jnp.broadcast_to(seg_all[ctx, 0:1, :].astype(F32), (128, tok))
    query_seg = jnp.transpose(own)[:, 0:1]
    query_pos = ctx * tok + lax.broadcasted_iota(jnp.int32, (tok, tok), 0)
    key_seg = seg_all[block, 0:1, :].astype(F32)
    key_pos = block * tok + lax.broadcasted_iota(jnp.int32, (tok, tok), 1)
    allowed = (query_seg == key_seg) & (key_pos <= query_pos)
    bias_ref[j] = jnp.where(allowed, 0.0, NEG).astype(bias_ref.dtype)


def head_marks():
    lane = lax.broadcasted_iota(jnp.int32, (1, 128), 1)
    return lane, lane < 64


def stack_heads(value):
    _, first = head_marks()
    return jnp.concatenate([jnp.where(first, value, 0), jnp.where(first, 0, value)], 0)


def join_heads(value):
    _, first = head_marks()
    rows = value.shape[0] // 2
    return jnp.where(first, value[:rows], value[rows:])


def stack_columns(stats, i):
    lane, _ = head_marks()
    return jnp.concatenate(
        [jnp.sum(jnp.where(lane == 2 * i + head, stats, 0.0), -1, keepdims=True) for head in range(2)], 0
    )


def put_columns(stats, i, column):
    lane, _ = head_marks()
    rows = stats.shape[0]
    stats = jnp.where(lane == 2 * i, column[:rows], stats)
    return jnp.where(lane == 2 * i + 1, column[rows:], stats)


def biased(raw, bias):
    rows, keys = bias.shape
    return (raw.reshape(2, rows, keys) + bias[None]).reshape(2 * rows, keys)


def attention_kernel(
    sizes, ids_ref, x_hbm, seg_ref, prev_ref, mix_ref, w_qkv_hbm, w_out_hbm, down_hbm, up_hbm,
    kind_ref, const_ref, gain_one_ref, gain_two_ref, cos_hbm, sin_hbm, dy_hbm, routes_ref,
    q_out, k_out, v_out, normed_out, rank_ref, total_ref, flat_ref, rank_out_ref, mid_ref, rows_ref,
    logits_ref, seg_all, arrived_dy, slots_ref, router_ref,
    x_all, bias_ref, sent_dy, acc_ref, top_ref, weight_ref, prev_pad, mix_pad, send_sem, recv_sem, seg_send, seg_recv, dy_send, dy_recv,
    q_ref, k_ref, v_ref, normed_ref, own_dy, out_sem, rows_f32, *staged,
):
    ctx_n, exp_n, rank = sizes
    dy_ref, x_ref, down_ref, up_ref, w_qkv_ref, cos_ref, sin_ref, w_out_ref, stage_sem = staged
    stages = stage_copies(
        (dy_hbm, x_hbm, down_hbm, up_hbm, w_qkv_hbm, cos_hbm, sin_hbm, w_out_hbm), staged, stage_sem
    )
    for stage in stages:
        stage.start()
    ctx = lax.axis_index("context")
    sequence = lax.axis_index("dp") * exp_n + lax.axis_index("expert")
    tok, model = x_ref.shape
    pairs, head_dim = model // 128, 64
    entered = greet([("context", ctx_n), ("expert", exp_n)])
    seg_all[ctx] = jnp.broadcast_to(seg_ref[...], (8, tok))
    me = lax.axis_index("expert")
    experts, capacity = arrived_dy.shape[1], arrived_dy.shape[3]
    others = partners(exp_n, me)
    entered()
    dy_copies = []
    if ctx_n > 1:
        copies = []
        for step in range(1, ctx_n):
            peer = lax.rem(ctx + step, ctx_n)
            copies.append(
                (
                    peer,
                    step,
                    remote(x_hbm, x_all.at[ctx], send_sem.at[step - 1], recv_sem.at[step - 1], "context", peer),
                    remote(seg_all.at[ctx], seg_all.at[ctx], seg_send.at[step - 1], seg_recv.at[step - 1], "context", peer),
                )
            )

        def to_later(peer):
            return ctx < peer if ctx_n == 2 else ctx < ctx_n

        def from_earlier(step):
            return lax.rem(ctx - step + ctx_n, ctx_n) < ctx if ctx_n == 2 else ctx < ctx_n

        for peer, step, rows_copy, seg_copy in copies:
            @pl.when(to_later(peer))
            def _(rows_copy=rows_copy, seg_copy=seg_copy):
                seg_copy.start()
                rows_copy.start()

    kind_rows = jnp.concatenate([routes_ref[...], jnp.full((6, tok), -1, jnp.int32)], 0)
    sub = lax.broadcasted_iota(jnp.int32, (16, tok), 0)
    uses = jnp.where((sub == kind_rows[0:1]) | (sub == kind_rows[1:2]), 1.0, 0.0).astype(BF)
    earlier = jnp.where(
        lax.broadcasted_iota(jnp.int32, (tok, tok), 0) < lax.broadcasted_iota(jnp.int32, (tok, tok), 1), 1.0, 0.0
    ).astype(BF)
    places = nn(uses, earlier) + (sub * capacity).astype(F32)
    slot_rows = []
    for j in range(2):
        kind = kind_rows[j : j + 1]
        place = jnp.sum(jnp.where(sub == kind, places, 0.0), 0, keepdims=True)
        slot_rows.append(jnp.where(kind < exp_n * experts, place, -1.0))
    row8 = lax.broadcasted_iota(jnp.int32, (8, tok), 0)
    slots_ref[...] = jnp.where(
        row8 < 2, kind_rows.astype(F32), jnp.where(row8 == 2, slot_rows[0], jnp.where(row8 == 3, slot_rows[1], 0.0))
    )
    slot_ints = [row.astype(jnp.int32) for row in slot_rows]

    def pick_dy(owner):
        hots = [hot_rows(row, owner * experts * capacity, experts * capacity) for row in slot_ints]
        hot = jnp.where(hots[0] | hots[1], 1.0, 0.0).astype(BF)
        return nn(hot, dy_ref[...]).astype(BF)

    stages[0].wait()
    for i, peer in enumerate(others):
        picked = pick_dy(peer)
        for e in range(experts):
            sent_dy[i, e] = picked[e * capacity : (e + 1) * capacity]
        copy = remote(
            sent_dy.at[i], arrived_dy.at[me // 2, :, lax.rem(me, 2)], dy_send.at[i], dy_recv.at[me], "expert", peer
        )
        copy.start()
        dy_copies.append(copy)
    picked = pick_dy(me)
    for e in range(experts):
        own_dy[e] = picked[e * capacity : (e + 1) * capacity]
    writes = [pltpu.make_async_copy(own_dy, arrived_dy.at[me // 2, :, lax.rem(me, 2)], out_sem.at[0])]
    writes[0].start()
    for stage in stages[1:]:
        stage.wait()
    adapter = ids_ref[sequence]
    down = down_ref[adapter]
    up = up_ref[adapter]
    kinds = mix_ref.shape[0]
    rows_f32[...] = jnp.zeros_like(rows_f32)
    rows_f32[0:kinds] = kind_ref[...].astype(F32)
    for c in range(2):
        rows_f32[kinds + 2 * c : kinds + 2 * c + 2] = const_ref[c].astype(F32)
    rows_f32[16:17] = gain_one_ref[...].astype(F32).reshape(1, model)
    rows_f32[17:18] = gain_two_ref[...].astype(F32).reshape(1, model)
    router_ref[...] = jnp.zeros_like(router_ref)
    router_ref[0:32] = rows_f32[...].astype(BF)
    gain_one = rows_f32[16:17]
    column = lax.broadcasted_iota(jnp.int32, (tok, down.shape[0]), 1) // rank

    def project(values, block, first):
        wide = values.astype(F32)
        inv = lax.rsqrt(jnp.mean(wide * wide, -1, keepdims=True) + EPSILON)
        normed_ref[block] = (wide * inv * gain_one).astype(BF)
        normed = normed_ref[block]
        ranks = nt(normed, down).astype(BF)
        rank_ref[block] = ranks
        start = pl.multiple_of(block * tok, tok)
        for p in range(first, 3):
            part = jnp.where(column == p, ADAPT_SCALE * ranks.astype(F32), 0.0).astype(BF)

            def chunk(i, carry, p=p, part=part):
                wide_cols = pl.ds(pl.multiple_of(p * model + i * 256, 256), 256)
                cols = pl.ds(pl.multiple_of(i * 256, 256), 256)
                proj = nn(normed_ref[block], w_qkv_ref[:, wide_cols]) + nn(
                    part, up_cols[:, cols]
                )
                for half in range(2):
                    piece = proj[:, half * 128 : half * 128 + 128]
                    if p < 2:
                        piece = turn(
                            piece, cos_ref[pl.ds(start, tok)], sin_ref[pl.ds(start, tok)], head_dim
                        )
                    if p == 0:
                        q_ref[2 * i + half] = (piece * head_dim ** (-0.5)).astype(BF)
                    else:
                        (k_ref if p == 1 else v_ref)[block, 2 * i + half] = piece.astype(BF)
                return carry

            up_cols = up_ref.at[adapter]
            lax.fori_loop(0, model // 256, chunk, 0)

    project(x_ref[...], ctx, 0)
    half_rows = tok // 2
    halves = [slice(half * half_rows, (half + 1) * half_rows) for half in range(2)]

    def own_pair(i, carry):
        for half, rows in enumerate(halves):
            width = (half + 1) * half_rows
            scores = biased(
                nt(stack_heads(q_ref[i, rows]), k_ref[ctx, i, 0:width]), bias_ref[0, rows, 0:width]
            )
            top = jnp.max(scores, -1, keepdims=True)
            exps = jnp.exp(scores - top)
            acc_ref[i, rows] = join_heads(nn(exps.astype(BF), v_ref[ctx, i, 0:width]))
            top_ref[rows] = put_columns(top_ref[rows], i, top)
            weight_ref[rows] = put_columns(weight_ref[rows], i, jnp.sum(exps, -1, keepdims=True))
        return carry

    def close_pair(i, carry):
        for rows in halves:
            inv = 1.0 / stack_columns(weight_ref[rows], i)
            flat_ref[rows, pl.ds(pl.multiple_of(i * 128, 128), 128)] = (
                acc_ref[i, rows] * join_heads(inv)
            ).astype(BF)
        return carry

    def attend_others():
        others = blocks_of(ctx_n, ctx, ctx_n - 1)
        for j, block in enumerate(others):
            fill_bias(bias_ref, seg_all, ctx, tok, j + 1, block)

        def pair(i, carry):
            for rows in halves:
                q = stack_heads(q_ref[i, rows])
                scores = [
                    biased(nt(q, k_ref[block, i]), bias_ref[j + 1, rows]) for j, block in enumerate(others)
                ]
                before = stack_columns(top_ref[rows], i)
                top = functools.reduce(
                    jnp.maximum, [before] + [jnp.max(part, -1, keepdims=True) for part in scores]
                )
                keep = jnp.exp(before - top)
                exps = [jnp.exp(part - top) for part in scores]
                total = keep * stack_columns(weight_ref[rows], i)
                result = acc_ref[i, rows] * join_heads(keep)
                for part, block in zip(exps, others):
                    total = total + jnp.sum(part, -1, keepdims=True)
                    result = result + join_heads(nn(part.astype(BF), v_ref[block, i]))
                flat_ref[rows, pl.ds(pl.multiple_of(i * 128, 128), 128)] = (
                    result * join_heads(1.0 / total)
                ).astype(BF)
                top_ref[rows] = put_columns(top_ref[rows], i, top)
                weight_ref[rows] = put_columns(weight_ref[rows], i, total)
            return carry

        lax.fori_loop(0, pairs, pair, 0)

    top_ref[...] = jnp.zeros_like(top_ref)
    weight_ref[...] = jnp.ones_like(weight_ref)
    fill_bias(bias_ref, seg_all, ctx, tok, 0, ctx)
    lax.fori_loop(0, pairs, own_pair, 0)
    if ctx_n == 1:
        lax.fori_loop(0, pairs, close_pair, 0)
    else:
        for peer, step, rows_copy, seg_copy in copies:
            @pl.when(from_earlier(step))
            def _(step=step, rows_copy=rows_copy, seg_copy=seg_copy):
                rows_copy.wait_recv()
                seg_copy.wait_recv()
                block = lax.rem(ctx - step + ctx_n, ctx_n)
                project(x_all[block], block, 1)

        if ctx_n == 2:
            @pl.when(ctx == 0)
            def _():
                lax.fori_loop(0, pairs, close_pair, 0)

            pl.when(ctx == 1)(attend_others)
        else:
            attend_others()
        for peer, step, rows_copy, seg_copy in copies:
            @pl.when(to_later(peer))
            def _(rows_copy=rows_copy, seg_copy=seg_copy):
                seg_copy.wait_send()
                rows_copy.wait_send()

    for i, (src, dst) in enumerate(((q_ref, q_out), (k_ref, k_out), (v_ref, v_out), (normed_ref, normed_out))):
        writes.append(pltpu.make_async_copy(src, dst, out_sem.at[1 + i]))
        writes[-1].start()
    total_ref[...] = top_ref[...] + jnp.log(weight_ref[...])
    rank_out = nt(flat_ref[...], down).astype(BF)
    rank_out_ref[...] = rank_out
    part = jnp.where(column == 3, ADAPT_SCALE * rank_out.astype(F32), 0.0).astype(BF)

    def out_chunk(i, carry):
        cols = pl.ds(pl.multiple_of(i * 256, 256), 256)
        mid_ref[:, cols] = (
            x_ref[:, cols].astype(F32)
            + nn(flat_ref[...], w_out_ref[:, cols])
            + nn(part, up_ref[adapter, :, cols])
        )
        return carry

    lax.fori_loop(0, model // 256, out_chunk, 0)
    gain_two = rows_f32[17:18]
    step_rows = 128

    def norm_rows(i, carry):
        rows = pl.ds(pl.multiple_of(i * step_rows, step_rows), step_rows)
        mid = mid_ref[rows]
        inv = lax.rsqrt(jnp.mean(mid * mid, -1, keepdims=True) + EPSILON)
        rows_ref[rows] = (mid * inv * gain_two).astype(BF)
        return carry

    lax.fori_loop(0, tok // step_rows, norm_rows, 0)
    prev_pad[...] = jnp.zeros_like(prev_pad)
    mix_pad[...] = jnp.zeros_like(mix_pad)
    for kind in range(kinds):
        prev_pad[kind : kind + 1] = prev_ref[kind]
    mix_pad[0:kinds, 0:kinds] = mix_ref[...]
    logits_ref[...] = nt(rows_ref[...], router_ref[...]) + lax.dot_general(
        prev_pad[...], mix_pad[...], (((0,), (0,)), ((), ())), precision=HIGH, preferred_element_type=F32
    )
    for write in writes:
        write.wait()
    for copy in dy_copies:
        copy.wait_send()
    for peer in others:
        remote(
            sent_dy.at[0], arrived_dy.at[peer // 2, :, lax.rem(peer, 2)], dy_send.at[0], dy_recv.at[peer], "expert", peer
        ).wait_recv()


def attention_forward(hidden, segments, prev, mix, ids, w_qkv, w_out, down, up, small, dy, routes, experts):
    ctx_n, exp_n = lax.axis_size("context"), lax.axis_size("expert")
    tok, model = hidden.shape
    pairs = model // 128
    wide = down.shape[1]
    cos_table, sin_table = rope_tables(ctx_n * tok, 64)
    vmem, hbm = pl.BlockSpec(memory_space=pltpu.VMEM), pl.BlockSpec(memory_space=pl.ANY)
    dma = pltpu.SemaphoreType.DMA
    many = max(ctx_n - 1, 1)
    shape = jax.ShapeDtypeStruct
    cos_table, sin_table = jnp.asarray(cos_table), jnp.asarray(sin_table)
    return pl.pallas_call(
        functools.partial(attention_kernel, (ctx_n, exp_n, wide // 4)),
        out_shape=(
            shape((pairs, tok, 128), BF),
            shape((ctx_n, pairs, tok, 128), BF),
            shape((ctx_n, pairs, tok, 128), BF),
            shape((ctx_n, tok, model), BF),
            shape((ctx_n, tok, wide), BF),
            shape((tok, 128), F32),
            shape((tok, model), BF),
            shape((tok, wide), BF),
            shape((tok, model), F32),
            shape((tok, model), BF),
            shape((tok, 128), F32),
            shape((ctx_n, 8, tok), jnp.int32),
            shape((exp_n // 2, experts, 2, tok // 4, model), BF),
            shape((8, tok), F32),
            shape((128, model), BF),
        ),
        in_specs=[pl.BlockSpec(memory_space=pltpu.SMEM), hbm]
        + [vmem] * 3
        + [hbm] * 4
        + [vmem] * 4
        + [hbm] * 3
        + [vmem],
        out_specs=(hbm,) * 4 + (vmem,) * 8 + (hbm, vmem, vmem),
        scratch_shapes=[
            pltpu.VMEM((ctx_n, tok, model), BF),
            pltpu.VMEM((ctx_n, tok, tok), BF if ctx_n > 2 else F32),
            pltpu.VMEM((exp_n - 1, experts, tok // 4, model), BF),
            pltpu.VMEM((pairs, tok, 128), F32),
            pltpu.VMEM((tok, 128), F32),
            pltpu.VMEM((tok, 128), F32),
            pltpu.VMEM((16, tok), F32),
            pltpu.VMEM((16, 128), F32),
            dma((many,)), dma((many,)), dma((many,)), dma((many,)), dma((exp_n - 1,)), dma((exp_n,)),
            pltpu.VMEM((pairs, tok, 128), BF),
            pltpu.VMEM((ctx_n, pairs, tok, 128), BF),
            pltpu.VMEM((ctx_n, pairs, tok, 128), BF),
            pltpu.VMEM((ctx_n, tok, model), BF),
            pltpu.VMEM((experts, tok // 4, model), BF),
            dma((5,)),
            pltpu.VMEM((32, model), F32),
        ]
        + stage_scratch(dy, hidden, down, up, w_qkv, cos_table, sin_table, w_out),
        compiler_params=pltpu.CompilerParams(
            collective_id=2, has_side_effects=True, vmem_limit_bytes=VLIMIT + 5 * 2**19
        ),
        name="attention_forward",
    )(
        ids, hidden, segments, prev, mix, w_qkv, w_out, down, up, *small, cos_table, sin_table, dy, routes,
    )


def put_tiles(tiles_ref, first, value):
    for col in range(value.shape[1] // 128):
        tiles_ref[first + col] = value[:, col * 128 : col * 128 + 128].astype(tiles_ref.dtype)


STAGED = 17


def backward_kernel(
    sizes, ids_ref, d_mid_hbm, q_hbm, k_hbm, v_hbm, normed_ref, rank_hbm, total_hbm, flat_hbm,
    rank_out_hbm, x_hbm, seg_hbm, router_hbm, w_qkv_hbm, w_out_hbm, down_hbm, up_hbm, cos_hbm,
    sin_hbm, *rest,
):
    ctx_n, exp_n, rank, fused = sizes
    staged, rest = rest[-STAGED - 1 :], rest[: -STAGED - 1]
    (
        d_mid_ref, up_ref, down_ref, w_out_ref, rank_out_ref, flat_ref, q_ref, k_ref, v_ref, total_ref,
        seg_all, cos_ref, sin_ref, w_qkv_ref, rank_ref, x_ref, router_ref, stage_sem,
    ) = staged
    stages = stage_copies(
        (
            d_mid_hbm, up_hbm, down_hbm, w_out_hbm, rank_out_hbm, flat_hbm, q_hbm, k_hbm, v_hbm,
            total_hbm, seg_hbm, cos_hbm, sin_hbm, w_qkv_hbm, rank_hbm, x_hbm, router_hbm,
        ),
        staged, stage_sem,
    )
    if fused:
        sums_ref, early_ref, done_ref, base_ref, cols_ref = rest[:5]
        grad_ref, table_ref, attn_table, hidden_ref, tiles_ref = rest[5:10]
        scratch, more, results_scratch = rest[10:-31], rest[-31:-5], rest[-5:]
        results = Results(exp_n, done_ref, base_ref, cols_ref, hidden_ref, results_scratch)
        sums = Sums(fused, ids_ref, sums_ref, early_ref, tiles_ref, table_ref, attn_table, more)
    else:
        grad_ref, tiles_ref = rest[:2]
        scratch = rest[2:]
    (
        recv_buf, do_ref, bias_ref, dk_acc, dv_acc, dq_all, dkv_all, send_buf, grad_up, grad_down,
        normed_buf, send_sem, recv_sem, load_sem,
    ) = scratch
    ctx = lax.axis_index("context")
    sequence = lax.axis_index("dp") * exp_n + lax.axis_index("expert")
    tok, model = x_ref.shape
    pairs, head_dim = model // 128, 64
    entered = greet([(axis, lax.axis_size(axis)) for axis in (ALL_AXES if fused else ("context",))])
    for stage in stages[:6]:
        stage.start()
    if fused:
        entered()
        sums.start()
        results.start()
    for stage in stages[6:]:
        stage.start()
    order = [ctx] + blocks_of(ctx_n, ctx, ctx_n - 1)

    def fetch(j):
        return pltpu.make_async_copy(
            normed_ref.at[order[j]], normed_buf.at[min(j, 1)], load_sem.at[min(j, 1)]
        )

    fetch(0).start()
    if ctx_n > 1:
        fetch(1).start()
    if fused:
        for e in range(sums.experts - 1):
            sums.combine(e)
    for stage in stages[:6]:
        stage.wait()
    adapter = ids_ref[sequence]
    down = down_ref[adapter]
    up = up_ref[adapter]
    wide = down.shape[0]
    column = lax.broadcasted_iota(jnp.int32, (tok, wide), 1) // rank
    d_branch = d_mid_ref[...].astype(BF)
    d_rank_out = jnp.where(column == 3, ADAPT_SCALE * nt(d_branch, up), 0.0).astype(BF)
    twice_out = jnp.where(column == 3, ADAPT_SCALE * rank_out_ref[...].astype(F32), 0.0).astype(BF)
    grad_up[...] = tn(twice_out, d_branch)
    grad_down[...] = tn(d_rank_out, flat_ref[...])

    def attn_chunk(i, carry):
        rows = pl.ds(pl.multiple_of(i * 256, 256), 256)
        d_attn = nt(d_branch, w_out_ref[rows, :]) + nn(d_rank_out, down_ref[adapter, :, rows])
        do_ref[2 * i] = d_attn[:, :128].astype(BF)
        do_ref[2 * i + 1] = d_attn[:, 128:].astype(BF)
        return carry

    lax.fori_loop(0, model // 256, attn_chunk, 0)
    for stage in stages[6:]:
        stage.wait()
    half_rows = tok // 2

    steps = {}
    if fused and sums.experts > 1:
        earlier = range(sums.experts - 1)

        def first_step():
            for e in earlier:
                sums.advance(e, 1)
            sums.exchange()

        def second_step():
            for e in earlier:
                sums.advance(e, 2)

        steps = {0: first_step, 3: second_step}

    def attend(count):
        others = blocks_of(ctx_n, ctx, count)
        for j, block in enumerate([ctx] + others):
            fill_bias(bias_ref, seg_all, ctx, tok, j, block)

        def pair(i, carry):
            cols = pl.ds(pl.multiple_of(i * 128, 128), 128)
            for half in (1, 0):
                rows = slice(half * half_rows, (half + 1) * half_rows)
                q = stack_heads(q_ref[i, rows])
                d_out = stack_heads(do_ref[i, rows])
                total = stack_columns(total_ref[rows], i)
                def terms(j, block, width, i=i, rows=rows, q=q, d_out=d_out, total=total):
                    probs = jnp.exp(
                        biased(nt(q, k_ref[block, i, 0:width]), bias_ref[j, rows, 0:width]) - total
                    )
                    return probs, nt(d_out, v_ref[block, i, 0:width])

                def use(j, block, width, probs, d_probs, delta, i=i, half=half, q=q, d_out=d_out):
                    d_scores = (probs * (d_probs - delta)).astype(BF)
                    d_key = tn(q, d_scores)
                    d_value = tn(d_out, probs.astype(BF))
                    if half == 1:
                        dk_acc[j] = d_key
                        dv_acc[j] = d_value
                    else:
                        dk_acc[j, :, 0:width] += d_key
                        dv_acc[j, :, 0:width] += d_value
                    return nn(d_scores, k_ref[block, i, 0:width])

                width = (half + 1) * half_rows
                own = terms(0, ctx, width)
                delta = jnp.sum(own[0] * own[1], -1, keepdims=True)
                if count < 2:
                    kept = [terms(j + 1, block, tok) for j, block in enumerate(others)]
                    for probs, d_probs in kept:
                        delta = delta + jnp.sum(probs * d_probs, -1, keepdims=True)
                    d_query = use(0, ctx, width, *own, delta)
                    for j, block in enumerate(others):
                        d_query = d_query + use(j + 1, block, tok, *kept[j], delta)
                else:

                    def more_delta(j, delta):
                        probs, d_probs = terms(j, lax.rem(ctx + j, ctx_n), tok)
                        return delta + jnp.sum(probs * d_probs, -1, keepdims=True)

                    delta = lax.fori_loop(1, ctx_n, more_delta, delta)

                    def more_query(j, d_query, delta=delta):
                        block = lax.rem(ctx + j, ctx_n)
                        return d_query + use(j, block, tok, *terms(j, block, tok), delta)

                    d_query = lax.fori_loop(1, ctx_n, more_query, use(0, ctx, width, *own, delta))
                start = pl.multiple_of(ctx * tok + half * half_rows, half_rows)
                d_query = join_heads(d_query) * head_dim ** (-0.5)
                dq_all[rows, cols] = turn(
                    d_query, cos_ref[pl.ds(start, half_rows)], -sin_ref[pl.ds(start, half_rows)], head_dim
                ).astype(BF)
            for j, block in enumerate([ctx] + others):
                start = pl.multiple_of(block * tok, tok)
                d_key = turn(
                    jnp.transpose(dk_acc[j]), cos_ref[pl.ds(start, tok)], -sin_ref[pl.ds(start, tok)], head_dim
                )
                dkv_all[j, 0, :, cols] = d_key.astype(BF)
                dkv_all[j, 1, :, cols] = jnp.transpose(dv_acc[j]).astype(BF)
            for turn_of, step in steps.items():
                pl.when(i == turn_of)(step)
            return carry

        lax.fori_loop(0, pairs, pair, 0)

    def fold(j, block, first, write):
        normed = normed_buf[min(j, 1)]
        ranks = rank_ref[block].astype(F32)
        d_ranks = jnp.zeros((tok, wide), F32)
        for p in range(first, 3):
            d_proj = dq_all[...] if p == 0 else dkv_all[j, p - 1]
            twice = jnp.where(column == p, ADAPT_SCALE * ranks, 0.0).astype(BF)
            grad_up[...] += tn(twice, d_proj)
            d_ranks = d_ranks + jnp.where(column == p, ADAPT_SCALE * nt(d_proj, up), 0.0)
        d_ranks = d_ranks.astype(BF)
        grad_down[...] += tn(d_ranks, normed)

        def chunk(i, carry):
            rows = pl.ds(pl.multiple_of(i * 256, 256), 256)
            value = nn(d_ranks, down_ref[adapter, :, rows])
            for p in range(first, 3):
                d_proj = dq_all[...] if p == 0 else dkv_all[j, p - 1]
                value = value + nt(d_proj, w_qkv_ref[rows, p * model : (p + 1) * model])
            write(rows, value)
            return carry

        lax.fori_loop(0, model // 256, chunk, 0)

    def write_own(cols, value):
        grad_ref[:, cols] = value

    class Share:
        def __init__(self, step):
            peer = lax.rem(ctx + step, ctx_n)
            self.halves = [
                remote(
                    send_buf.at[pl.ds(half * half_rows, half_rows)],
                    recv_buf.at[step - 1, pl.ds(half * half_rows, half_rows)],
                    send_sem.at[step - 1, half], recv_sem.at[step - 1, half], "context", peer,
                )
                for half in range(2)
            ]

        def start(self):
            self.halves[0].start()
            if not fused:
                self.halves[1].start()

        def start_rest(self):
            self.halves[1].start()

        def wait_recv(self):
            for half in self.halves:
                half.wait_recv()

        def wait_send(self):
            for half in self.halves:
                half.wait_send()

    copies = [Share(step) for step in range(1, ctx_n)]

    def share_rest():
        if ctx_n == 2:
            pl.when(ctx == 1)(copies[0].start_rest)

    if ctx_n == 1:
        attend(0)
        sums.combine(sums.experts - 1)
    elif ctx_n == 2:
        @pl.when(ctx == 0)
        def _():
            attend(0)
            sums.combine(sums.experts - 1)

    if not fused:
        entered()

    def spread():
        attend(ctx_n - 1)
        if fused:
            sums.combine(sums.experts - 1)
        for j, block in enumerate(blocks_of(ctx_n, ctx, ctx_n - 1)):
            def write(cols, value):
                send_buf[:, cols] = value.astype(BF)

            fetch(j + 1).wait()
            if j > 0:
                copies[j - 1].wait_send()
            fold(j + 1, block, 1, write)
            copies[j].start()
            if j + 2 < ctx_n:
                fetch(j + 2).start()

    if ctx_n == 2:
        pl.when(ctx == 1)(spread)
        pl.when(ctx == 0)(fetch(1).wait)
    elif ctx_n > 2:
        spread()
    fetch(0).wait()
    fold(0, ctx, 0, write_own)
    per = model // 128
    for p in range(4):
        put_tiles(tiles_ref, p * per, grad_down[p * rank : (p + 1) * rank])
        put_tiles(tiles_ref, (4 + p) * per, grad_up[p * rank : (p + 1) * rank])

    def settle():
        take_shares()
        lax.fori_loop(0, tok // 128, finish, 0)

    def take_shares():
        if ctx_n == 2:
            pl.when(ctx == 0)(copies[0].wait_recv)

            @pl.when(ctx == 1)
            def _():
                recv_buf[...] = jnp.zeros_like(recv_buf)

        elif ctx_n > 2:
            copies[-1].wait_send()
            for step, item in enumerate(copies):
                item.wait_recv()
                load = pltpu.make_async_copy(recv_buf.at[step], send_buf, load_sem.at[0])
                load.start()
                load.wait()
                grad_ref[...] += send_buf[...].astype(F32)

    gain_one = router_ref[16:17].astype(F32)

    def finish(i, carry):
        rows = pl.ds(pl.multiple_of(i * 128, 128), 128)
        value = grad_ref[rows]
        if ctx_n == 2:
            value = value + recv_buf[0, rows].astype(F32)
        x = x_ref[rows].astype(F32)
        inv = lax.rsqrt(jnp.mean(x * x, -1, keepdims=True) + EPSILON)
        scaled = value * gain_one
        grad_ref[rows] = (
            d_mid_ref[rows]
            + inv * scaled
            - x * (inv * inv * inv) * jnp.mean(scaled * x, -1, keepdims=True)
        )
        return carry

    if fused:
        last = sums.experts - 1

        for e in range(last):
            for s in range(3, sums.dp_n):
                sums.advance(e, s)
        sums.take(last, 1)

        def rest():
            share_rest()
            sums.hand(last, 2)

        def end():
            for s in range(3, sums.dp_n):
                sums.advance(last, s)
            settle()

        sums.tail(
            {
                "sources": results.combine,
                "context": functools.partial(sums.hand, last, 1),
                "dp_back": functools.partial(sums.take, last, 2),
                "context_back": rest,
                "last": end,
            }
        )
        sums.finish()
        results.finish()
    else:
        settle()
    if ctx_n == 2:
        pl.when(ctx == 1)(copies[0].wait_send)


def attention_backward(d_mid, saved, hidden, ids, router, w_qkv, w_out, down, up, expert_sums, done, experts, width):
    ctx_n, exp_n = lax.axis_size("context"), lax.axis_size("expert")
    tok, model = hidden.shape
    pairs = model // 128
    wide = down.shape[1]
    cos_table, sin_table = rope_tables(ctx_n * tok, 64)
    vmem = pl.BlockSpec(memory_space=pltpu.VMEM)
    dma = pltpu.SemaphoreType.DMA
    many = max(ctx_n - 1, 1)
    shape = jax.ShapeDtypeStruct
    q, k, v, normed, ranks, totals, flat, rank_out, seg_all = saved
    cos_table, sin_table = jnp.asarray(cos_table), jnp.asarray(sin_table)
    staged = (
        d_mid, up, down, w_out, rank_out, flat, q, k, v, totals, seg_all, cos_table, sin_table, w_qkv,
        ranks, hidden, router,
    )
    hbm = pl.BlockSpec(memory_space=pl.ANY)
    spill = ctx_n > 2
    landing = ((many, tok, model), BF)
    attn_tiles, adapters = 8 * pairs, down.shape[0]
    sums_outs, sums_scratch = sums_shapes(experts, model, width, attn_tiles, adapters)
    fused = None
    if not spill:
        fused = tuple(lax.axis_size(axis) for axis in ALL_AXES) + (adapters, attn_tiles)
    tiles_shape = ((attn_tiles, 16, 128), BF)
    results = pl.pallas_call(
        functools.partial(backward_kernel, (ctx_n, exp_n, wide // 4, fused)),
        out_shape=(shape((tok, model), F32),)
        + ((shape(*tiles_shape), shape(*landing)) if spill else sums_outs + (shape((tok, model), BF),)),
        in_specs=[pl.BlockSpec(memory_space=pltpu.SMEM)] + [hbm] * 18 + ([] if spill else [hbm] * 4 + [vmem]),
        out_specs=(vmem, vmem) + ((pl.BlockSpec(memory_space=pl.ANY),) if spill else (vmem, vmem)),
        scratch_shapes=([] if spill else [pltpu.VMEM(*tiles_shape), pltpu.VMEM(*landing)])
        + [
            pltpu.VMEM((pairs, tok, 128), BF),
            pltpu.VMEM((ctx_n, tok, tok), BF if spill else F32),
            pltpu.VMEM((ctx_n, 128, tok), F32),
            pltpu.VMEM((ctx_n, 128, tok), F32),
            pltpu.VMEM((tok, model), BF),
            pltpu.VMEM((ctx_n, 2, tok, model), BF),
            pltpu.VMEM((tok, model), BF),
            pltpu.VMEM((wide, model), F32),
            pltpu.VMEM((wide, model), F32),
            pltpu.VMEM((min(ctx_n, 2), tok, model), BF),
            dma((many, 2)), dma((many, 2)), dma((2,)),
        ]
        + ([] if spill else sums_scratch + results_shapes(exp_n, done[0]))
        + stage_scratch(*staged),
        compiler_params=pltpu.CompilerParams(
            collective_id=3, has_side_effects=True, vmem_limit_bytes=VLIMIT + 5 * 2**19
        ),
        name="attention_backward",
    )(
        ids, d_mid, q, k, v, normed, ranks, totals, flat, rank_out, hidden, seg_all,
        router, w_qkv, w_out, down, up, cos_table, sin_table, *([] if spill else [*expert_sums, *done]),
    )
    if spill:
        sums = add_up(ids, expert_sums, results[1], experts, width, adapters)
        return (results[0],) + tuple(sums) + (return_results(done),)
    return results


def partners(exp_n, me):
    core = lax.rem(me, 2)
    twin = me + 1 - 2 * core
    far = []
    for step in range(2, exp_n, 2):
        far += [lax.rem(me + step, exp_n), lax.rem(twin + step, exp_n)]
    return far + [twin]


def hot_rows(slot_rows, first, count):
    target = first + lax.broadcasted_iota(jnp.int32, (count, slot_rows.shape[1]), 0)
    return target == slot_rows


def moe_kernel(
    sizes, ids_ref, rows_ref, mid_hbm, logits_ref, slots_ref, dy_hbm, arrived_hbm, router_ref, mix_ref,
    vec_ref, gate_up_hbm, down_hbm, in_down_hbm, in_up_hbm, out_down_hbm, out_up_hbm,
    base_ref, d_mid_ref, grad_prev_ref, sums_ref, early_ref, done_out, cols_ref, part_z,
    d_logits_ref, mix_pad, done_gate, back_gate, tiles_ref, arrived_x, gate_up_ref, w_down_ref, sent_rows, sent_gates, arrived_rows, arrived_gates, act_ref, d_pre_ref,
    done_rows, back_rows, gates_ref,
    weight_sem, row_send, row_recv, gate_send, gate_recv, out_send, out_recv, in_send, in_recv,
    x_send, x_recv, z_send, z_recv, *staged,
):
    in_down_ref, in_up_ref, out_down_ref, out_up_ref, arrived_dy, mid_ref, dy_ref, stage_sem = staged
    stages = stage_copies(
        (in_down_hbm, in_up_hbm, out_down_hbm, out_up_hbm, arrived_hbm, mid_hbm, dy_hbm), staged, stage_sem
    )
    ctx_n, dp_n, exp_n, kinds, rank, share = sizes
    ctx, dp = lax.axis_index("context"), lax.axis_index("dp")
    me = lax.axis_index("expert")
    my_chip, my_core = me // 2, lax.rem(me, 2)
    first_seq = lax.axis_index("dp") * exp_n
    tok, model = rows_ref.shape
    experts, width = w_down_ref.shape[:2]
    capacity = arrived_rows.shape[3]
    per_owner = experts * capacity
    both = 2 * capacity
    entered = greet([("expert", exp_n), ("context", ctx_n), ("dp", dp_n)])
    loads = []
    for e in range(experts):
        for hbm, ref, k in ((gate_up_hbm, gate_up_ref, 0), (down_hbm, w_down_ref, 1)):
            load = pltpu.make_async_copy(hbm.at[e], ref.at[e], weight_sem.at[e, k])
            load.start()
            loads.append(load)
        if e == 0:
            for stage in stages:
                stage.start()

    lane = lax.broadcasted_iota(jnp.int32, (tok, 128), 1)
    logits = logits_ref[...]
    masked = jnp.where(lane < kinds, logits, NEG)
    exps = jnp.exp(masked - jnp.max(masked, -1, keepdims=True))
    probs = exps / jnp.sum(exps, -1, keepdims=True)
    slot_cols = jnp.transpose(
        jnp.concatenate([slots_ref[...], jnp.zeros((120, tok), F32)], 0)
    )
    gates = [
        jnp.sum(jnp.where(lane == slot_cols[:, k : k + 1].astype(jnp.int32), probs, 0.0), -1, keepdims=True)
        for k in range(2)
    ]
    gates_ref[...] = jnp.where(lane == 0, gates[0], jnp.where(lane == 1, gates[1], 0.0))
    cols_ref[...] = jnp.where(lane == 4, gates[0], jnp.where(lane == 5, gates[1], slot_cols))
    gate_rows = jnp.transpose(gates_ref[...])
    parts = []
    sub = lax.broadcasted_iota(jnp.int32, (16, tok), 0)
    for k in range(2):
        whole = jnp.broadcast_to(gate_rows[k : k + 1], (16, tok))
        high = whole.astype(BF).astype(F32)
        middle = (whole - high).astype(BF).astype(F32)
        lowest = whole - high - middle
        parts.append(
            jnp.where(sub == 0, high, jnp.where(sub == 1, middle, jnp.where(sub == 2, lowest, 0.0))).astype(BF)
        )
    slot_rows = [slots_ref[2 + k : 3 + k].astype(jnp.int32) for k in range(2)]

    def pick(owner, e):
        hots = [hot_rows(slot_rows[k], owner * per_owner + e * capacity, capacity) for k in range(2)]
        hot = jnp.where(hots[0] | hots[1], 1.0, 0.0).astype(BF)
        gates = sum(nt(parts[k], jnp.where(hots[k], 1.0, 0.0).astype(BF)) for k in range(2))
        return gates.astype(BF), nn(hot, rows_ref[...]).astype(BF)

    entered()
    sends = []
    others = partners(exp_n, me)
    for e in range(experts):
        for i, peer in enumerate(others):
            sent_gates[i, e], sent_rows[i, e] = pick(peer, e)
            for src, dst, send, recv in (
                (sent_gates, arrived_gates, gate_send, gate_recv),
                (sent_rows, arrived_rows, row_send, row_recv),
            ):
                copy = remote(
                    src.at[i, e], dst.at[my_chip, e, my_core], send.at[i, e], recv.at[me, e], "expert", peer
                )
                copy.start()
                sends.append(copy)
        arrived_gates[my_chip, e, my_core], arrived_rows[my_chip, e, my_core] = pick(me, e)

    def arrive(source, e):
        for ref, src, send, recv in (
            (arrived_gates, sent_gates, gate_send, gate_recv),
            (arrived_rows, sent_rows, row_send, row_recv),
        ):
            remote(
                src.at[0, e], ref.at[source // 2, e, lax.rem(source, 2)], send.at[0, e], recv.at[source, e],
                "expert", source,
            ).wait_recv()

    row64 = lax.broadcasted_iota(jnp.int32, (both, 4 * rank), 0) // capacity
    col64 = lax.broadcasted_iota(jnp.int32, (both, 4 * rank), 1)
    mine64 = row64 == col64 // (2 * rank)
    is_gate = col64 % (2 * rank) < rank
    mine32 = lax.broadcasted_iota(jnp.int32, (both, 2 * rank), 0) // capacity == (
        lax.broadcasted_iota(jnp.int32, (both, 2 * rank), 1) // rank
    )
    step_cols = 512
    per_step = step_cols // 128
    across, deep = model // 128, width // 128
    first_up = 2 * across
    first_out = first_up + 2 * deep
    first_last = first_out + deep

    def put(source, e, tile, value):
        tiles_ref[source, tile // share, e * share + tile % share] = value

    def x_copies(chip, e):
        copies = []
        for step in range(1, ctx_n):
            peer = lax.rem(ctx + step, ctx_n)
            here = pl.ds(e * share, share)
            copies.append(
                remote(
                    tiles_ref.at[pl.ds(2 * chip, 2), peer, here],
                    arrived_x.at[step - 1, pl.ds(2 * chip, 2), here],
                    x_send.at[step - 1, chip, e], x_recv.at[step - 1, chip, e], "context", peer,
                )
            )
        return copies

    def work(chip, e):
        names = [ids_ref[first_seq + 2 * chip + core] for core in range(2)]

        def stack(ref, cols=slice(None)):
            return jnp.concatenate([ref[name, e, :, cols] for name in names], 0)

        rows = arrived_rows[chip, e].reshape(both, model)
        in_down = stack(in_down_ref)
        out_up = stack(out_up_ref)
        gate = []
        for core in range(2):
            piece = arrived_gates[chip, e, core].astype(F32)
            total = piece[0:1] + piece[1:2] + piece[2:3]
            gate.append(jnp.transpose(jnp.broadcast_to(total, (128, capacity)))[:, 0:1])
        gate = jnp.concatenate(gate, 0)
        d_out = (gate * arrived_dy[chip, e].reshape(both, model).astype(F32)).astype(BF)
        ranks = jnp.where(mine64, nt(rows, in_down), 0.0).astype(BF)
        twice = ADAPT_SCALE * ranks.astype(F32)
        twice_gate = jnp.where(is_gate, twice, 0.0).astype(BF)
        twice_up = jnp.where(is_gate, 0.0, twice).astype(BF)
        d_mid_rank = jnp.where(mine32, ADAPT_SCALE * nt(d_out, out_up), 0.0).astype(BF)

        def chunk(i, carry):
            rank_mid, d_rank = carry
            start = pl.multiple_of(i * step_cols, step_cols)
            cols = pl.ds(start, step_cols)
            up_cols = pl.ds(pl.multiple_of(width + i * step_cols, step_cols), step_cols)
            in_up = stack(in_up_ref, cols)
            out_down = stack(out_down_ref, cols)
            gate_pre = nn(rows, gate_up_ref[e, :, cols]) + nn(twice_gate, in_up)
            up_pre = nn(rows, gate_up_ref[e, :, up_cols]) + nn(twice_up, in_up)
            d_act = (nt(d_out, w_down_ref[e, cols, :]) + nn(d_mid_rank, out_down)).astype(BF).astype(F32)
            sigma = 1.0 / (1.0 + jnp.exp(-gate_pre))
            silu = gate_pre * sigma
            act = (silu * up_pre).astype(BF)
            d_gate = (d_act * up_pre * sigma * (1.0 + gate_pre * (1.0 - sigma))).astype(BF)
            d_up = (d_act * silu).astype(BF)
            act_ref[:, cols] = act
            d_pre_ref[:, cols] = d_gate
            d_pre_ref[:, up_cols] = d_up
            rank_mid = rank_mid + nt(act, out_down)
            d_rank = d_rank + jnp.where(is_gate, nt(d_gate, in_up), nt(d_up, in_up))
            grad_up = (tn(twice_gate, d_gate) + tn(twice_up, d_up)).astype(BF)
            grad_out = tn(d_mid_rank, act).astype(BF)
            for core in range(2):
                for t in range(per_step):
                    here = slice(t * 128, t * 128 + 128)
                    tile = i * per_step + t
                    for which in range(2):
                        first = (2 * core + which) * rank
                        put(
                            2 * chip + core, e, first_up + which * deep + tile,
                            grad_up[first : first + rank, here],
                        )
                    put(
                        2 * chip + core, e, first_out + tile,
                        grad_out[core * rank : (core + 1) * rank, here],
                    )
            return rank_mid, d_rank

        rank_mid, d_rank = lax.fori_loop(
            0, width // step_cols, chunk,
            (jnp.zeros((both, 2 * rank), F32), jnp.zeros((both, 4 * rank), F32)),
        )
        twice_mid = jnp.where(
            mine32, ADAPT_SCALE * rank_mid.astype(BF).astype(F32), 0.0
        ).astype(BF)

        def out_chunk(i, carry):
            cols = pl.ds(pl.multiple_of(i * 256, 256), 256)
            value = nn(act_ref[...], w_down_ref[e, :, cols]) + nn(twice_mid, stack(out_up_ref, cols))
            for core in range(2):
                done_out[chip, e, core, :, cols] = value[core * capacity : (core + 1) * capacity].astype(BF)
            return carry

        lax.fori_loop(0, model // 256, out_chunk, 0)
        for core in range(2):
            d_gate = jnp.sum(
                arrived_dy[chip, e, core].astype(F32) * done_out[chip, e, core].astype(F32), -1, keepdims=True
            )
            done_gate[chip, e, core] = jnp.transpose(jnp.broadcast_to(d_gate, (capacity, 128)))[0:8]
        give_back(chip, e, done_gate, back_gate, out_send, out_recv)
        d_rank_in = jnp.where(mine64, ADAPT_SCALE * d_rank, 0.0).astype(BF)

        def in_chunk(i, carry):
            cols = pl.ds(pl.multiple_of(i * 256, 256), 256)
            value = nt(d_pre_ref[...], gate_up_ref[e, cols, :]) + nn(d_rank_in, stack(in_down_ref, cols))
            for core in range(2):
                done_rows[chip, e, core, :, cols] = value[core * capacity : (core + 1) * capacity].astype(BF)
            return carry

        lax.fori_loop(0, model // 256, in_chunk, 0)
        give_back(chip, e, done_rows, back_rows, in_send, in_recv)
        grad_last = tn(twice_mid, d_out).astype(BF)
        grad_first = tn(d_rank_in, rows).astype(BF)
        for core in range(2):
            for t in range(across):
                here = slice(t * 128, t * 128 + 128)
                for which in range(2):
                    first = (2 * core + which) * rank
                    put(
                        2 * chip + core, e, which * across + t, grad_first[first : first + rank, here]
                    )
                put(
                    2 * chip + core, e, first_last + t,
                    grad_last[core * rank : (core + 1) * rank, here],
                )
        for copy in x_copies(chip, e):
            copy.start()

    def give_back(chip, e, done, back, send, recv):
        for core in range(2):
            target = 2 * chip + core
            copy = remote(
                done.at[chip, e, core], back.at[me * experts + e], send.at[target, e], recv.at[me, e],
                "expert", target,
            )

            @pl.when(target == me)
            def _(core=core):
                back[me * experts + e] = done[chip, e, core]

            @pl.when(target != me)
            def _(copy=copy):
                copy.start()

    def own_work(e):
        arrive(others[-1], e)
        work(my_chip, e)

    def gather(e, out_ref):
        for chip in range(exp_n // 2):
            for copy in x_copies(chip, e):
                copy.wait_recv()

        def add(tile, carry):
            here = pl.ds(e * share + tile, 1)
            total = tiles_ref[:, ctx, here].astype(F32)
            for step in range(1, ctx_n):
                total = total + arrived_x[step - 1, :, here].astype(F32)
            out_ref[:, pl.ds(tile, 1)] = total.astype(BF)
            return carry

        lax.fori_loop(0, share, add, 0)

    z_tiles = early_ref.shape[3]
    z_copies = []
    for load in loads[:2]:
        load.wait()
    for stage in stages[:5]:
        stage.wait()
    own_work(0)
    for e in range(experts):
        if e > 0:
            for load in loads[2 * e : 2 * e + 2]:
                load.wait()
        for step in range(1, exp_n // 2):
            arrive(others[2 * step - 2], e)
            arrive(others[2 * step - 1], e)
            work(lax.rem(my_chip + step, exp_n // 2), e)
    for e in range(experts - 1):
        if e > 0:
            own_work(e)
        gather(e, part_z.at[e])
        early_ref[e, 0] = part_z[e, :, pl.ds(dp * z_tiles, z_tiles)]
        for k in range(1, dp_n):
            peer = lax.rem(dp + k, dp_n)
            copy = remote(
                part_z.at[e, :, pl.ds(peer * z_tiles, z_tiles)], early_ref.at[e, k], z_send.at[e, k], z_recv.at[e, k],
                "dp", peer,
            )
            copy.start()
            z_copies.append(copy)

    if experts > 1:
        own_work(experts - 1)
    for stage in stages[5:]:
        stage.wait()

    def collect(done, back, send, recv):
        for owner in others:
            for e in range(experts):
                remote(
                    done.at[0, e, 0], back.at[owner * experts + e], send.at[owner, e], recv.at[owner, e],
                    "expert", owner,
                ).wait_recv()

    slots_total = exp_n * per_owner
    block = 256

    def hot_cols(rows):
        target = lax.broadcasted_iota(jnp.int32, (block, slots_total), 1)
        return [target == cols_ref[rows, 2 + k : 3 + k].astype(jnp.int32) for k in range(2)]

    gain = router_ref[17:18].astype(F32)
    lanes = lax.broadcasted_iota(jnp.int32, (block, 128), 1)
    ffn_kinds = exp_n * experts

    def outward(i, carry):
        rows = pl.ds(pl.multiple_of(i * block, block), block)
        hots = hot_cols(rows)
        mid = mid_ref[rows]
        dy = dy_ref[rows].astype(F32)
        normed = mid * lax.rsqrt(jnp.mean(mid * mid, -1, keepdims=True) + EPSILON) * gain
        logits = logits_ref[rows]
        masked = jnp.where(lanes < kinds, logits, NEG)
        exps = jnp.exp(masked - jnp.max(masked, -1, keepdims=True))
        probs = exps / jnp.sum(exps, -1, keepdims=True)
        pairs = []
        for c in range(2):
            one, two = logits[:, kinds + 2 * c : kinds + 2 * c + 1], logits[:, kinds + 2 * c + 1 : kinds + 2 * c + 2]
            pairs.append((1.0 / (1.0 + jnp.exp(two - one)), 1.0 / (1.0 + jnp.exp(one - two))))
        along = jnp.sum(dy * normed, -1, keepdims=True)
        across_vec = [jnp.sum(dy * vec_ref[c : c + 1].astype(F32), -1, keepdims=True) for c in range(2)]
        d_kinds = jnp.zeros((block, 128), F32)
        dy_scale = jnp.zeros((block, 1), F32)
        weights = [jnp.zeros((block, 1), F32)] * 2
        for k in range(2):
            kind = cols_ref[rows, k : k + 1].astype(jnp.int32)
            gate = gates_ref[rows, k : k + 1]
            scale = jnp.where(kind == ffn_kinds + 1, 1.0, 0.0)
            picked = jnp.zeros((block, 128), F32)
            for owner in range(exp_n * experts):
                hot = hots[k][:, owner * capacity : (owner + 1) * capacity]
                picked = picked + jnp.where(hot, back_gate[owner, 0:1], 0.0)
            d_gate = jnp.sum(picked, -1, keepdims=True)
            for c in range(2):
                here = jnp.where(kind == ffn_kinds + 2 + c, 1.0, 0.0)
                scale = scale + here * pairs[c][0]
                d_gate = d_gate + here * pairs[c][1] * across_vec[c]
                weights[c] = weights[c] + here * gate
            d_gate = d_gate + scale * along
            dy_scale = dy_scale + gate * scale
            d_kinds = d_kinds + jnp.where(lanes == kind, d_gate, 0.0)
        base = mid + dy_scale * normed
        for c in range(2):
            base = base + (weights[c] * pairs[c][1]) * vec_ref[c : c + 1].astype(F32)
        base_ref[rows] = base
        d_logits = probs * (d_kinds - jnp.sum(probs * d_kinds, -1, keepdims=True))
        for c in range(2):
            d_one = weights[c] * along
            d_two = weights[c] * across_vec[c]
            mean = pairs[c][0] * d_one + pairs[c][1] * d_two
            d_logits = jnp.where(lanes == kinds + 2 * c, pairs[c][0] * (d_one - mean), d_logits)
            d_logits = jnp.where(lanes == kinds + 2 * c + 1, pairs[c][1] * (d_two - mean), d_logits)
        d_logits_ref[rows] = d_logits
        high = d_logits.astype(BF)
        rest = d_logits - high.astype(F32)
        middle = rest.astype(BF)
        lowest = (rest - middle.astype(F32)).astype(BF)
        router = router_ref[...]
        d_mid_ref[rows] = dy_scale * dy + (nn(high, router) + nn(middle, router) + nn(lowest, router))
        return carry

    def inward(i, carry):
        rows = pl.ds(pl.multiple_of(i * block, block), block)
        hots = hot_cols(rows)
        table = back_rows[...].reshape(slots_total, model)
        hot = jnp.where(hots[0] | hots[1], 1.0, 0.0).astype(BF)
        scaled = (d_mid_ref[rows] + nn(hot, table)) * gain
        mid = mid_ref[rows]
        inv = lax.rsqrt(jnp.mean(mid * mid, -1, keepdims=True) + EPSILON)
        d_mid_ref[rows] = (
            dy_ref[rows].astype(F32)
            + inv * scaled
            - mid * (inv * inv * inv) * jnp.mean(scaled * mid, -1, keepdims=True)
        )
        return carry

    collect(done_gate, back_gate, out_send, out_recv)
    lax.fori_loop(0, tok // block, outward, 0)
    mix_pad[...] = jnp.zeros_like(mix_pad)
    mix_pad[0:kinds, 0:kinds] = mix_ref[...]
    grad_prev = lax.dot_general(
        mix_pad[...], d_logits_ref[...], (((1,), (1,)), ((), ())), precision=HIGH, preferred_element_type=F32
    )
    for kind in range(kinds):
        grad_prev_ref[kind] = grad_prev[kind : kind + 1]
    collect(done_rows, back_rows, in_send, in_recv)
    lax.fori_loop(0, tok // block, inward, 0)
    gather(experts - 1, sums_ref)
    for chip in range(exp_n // 2):
        for e in range(experts):
            for copy in x_copies(chip, e):
                copy.wait_send()
    for copy in z_copies:
        copy.wait()
    for copy in sends:
        copy.wait_send()
    for target in others:
        for e in range(experts):
            for done, back, send, recv in (
                (done_gate, back_gate, out_send, out_recv),
                (done_rows, back_rows, in_send, in_recv),
            ):
                remote(
                    done.at[0, e, 0], back.at[0], send.at[target, e], recv.at[target, e],
                    "expert", target,
                ).wait_send()


def expert_tiling(experts, model, width):
    share = pl.cdiv(3 * (model + width) // 128, lax.axis_size("context"))
    z_tiles = pl.cdiv(share, lax.axis_size("dp"))
    return share, z_tiles * lax.axis_size("dp"), z_tiles


def attn_tiling(attn_tiles):
    own = attn_tiles // lax.axis_size("expert")
    x_tiles = pl.cdiv(own, lax.axis_size("context"))
    return own, x_tiles, pl.cdiv(x_tiles, lax.axis_size("dp"))


def expert_layer(rows, mid, logits, slots, dy, arrived_dy, ids, router, mix, vec, w_gate_up, w_down, tables):
    exp_n = lax.axis_size("expert")
    tok, model = rows.shape
    experts, width = w_down.shape[:2]
    capacity = tok // 4
    rank = tables[3].shape[2]
    ctx_n = lax.axis_size("context")
    dp_n = lax.axis_size("dp")
    share, x_tiles, z_tiles = expert_tiling(experts, model, width)
    many, before = max(ctx_n - 1, 1), max(experts - 1, 1)
    chips = exp_n // 2
    vmem = pl.BlockSpec(memory_space=pltpu.VMEM)
    hbm = pl.BlockSpec(memory_space=pl.ANY)
    dma = pltpu.SemaphoreType.DMA
    shape = jax.ShapeDtypeStruct
    block = (experts, capacity, model)
    kinds = mix.shape[0]
    return pl.pallas_call(
        functools.partial(moe_kernel, (ctx_n, dp_n, exp_n, kinds, rank, share)),
        out_shape=(
            shape((tok, model), F32),
            shape((tok, model), F32),
            shape((kinds, 1, tok), F32),
            shape((exp_n, x_tiles, 16, 128), BF),
            shape((before, dp_n, exp_n, z_tiles, 16, 128), BF),
            shape((chips, experts, 2, capacity, model), BF),
            shape((tok, 128), F32),
        ),
        in_specs=[pl.BlockSpec(memory_space=pltpu.SMEM), vmem, hbm, vmem, vmem, hbm, hbm]
        + [vmem] * 3
        + [hbm] * 6,
        out_specs=(vmem,) * 7,
        scratch_shapes=[
            pltpu.VMEM((before, exp_n, x_tiles, 16, 128), BF),
            pltpu.VMEM((tok, 128), F32),
            pltpu.VMEM((16, 128), F32),
            pltpu.VMEM((chips, experts, 2, 8, 128), F32),
            pltpu.VMEM((exp_n * experts, 8, 128), F32),
            pltpu.VMEM((exp_n, ctx_n, experts * share, 16, 128), BF),
            pltpu.VMEM((many, exp_n, experts * share, 16, 128), BF),
            pltpu.VMEM((experts, model, 2 * width), BF),
            pltpu.VMEM((experts, width, model), BF),
            pltpu.VMEM((exp_n - 1,) + block, BF),
            pltpu.VMEM((exp_n - 1, experts, 16, capacity), BF),
            pltpu.VMEM((chips, experts, 2, capacity, model), BF),
            pltpu.VMEM((chips, experts, 2, 16, capacity), BF),
            pltpu.VMEM((2 * capacity, width), BF),
            pltpu.VMEM((2 * capacity, 2 * width), BF),
            pltpu.VMEM((chips, experts, 2, capacity, model), BF),
            pltpu.VMEM((exp_n * experts, capacity, model), BF),
            pltpu.VMEM((tok, 128), F32),
            dma((experts, 2)), dma((exp_n - 1, experts)), dma((exp_n, experts)), dma((exp_n - 1, experts)),
            dma((exp_n, experts)),
            dma((exp_n, experts)), dma((exp_n, experts)), dma((exp_n, experts)), dma((exp_n, experts)),
            dma((many, chips, experts)), dma((many, chips, experts)), dma((before, dp_n)), dma((before, dp_n)),
        ]
        + stage_scratch(*tables, arrived_dy, mid, dy),
        compiler_params=pltpu.CompilerParams(
            collective_id=4, has_side_effects=True, vmem_limit_bytes=VLIMIT
        ),
        name="expert_layer",
    )(
        ids, rows, mid, logits, slots, dy, arrived_dy, router, mix, vec, w_gate_up,
        w_down, *tables,
    )


def stage_copies(sources, targets, sem):
    return [
        pltpu.make_async_copy(src, dst, sem.at[i]) for i, (src, dst) in enumerate(zip(sources, targets))
    ]


def stage_scratch(*arrays):
    return [pltpu.VMEM(array.shape, array.dtype) for array in arrays] + [
        pltpu.SemaphoreType.DMA((len(arrays),))
    ]


class Results:
    def __init__(self, exp_n, done_ref, base_ref, cols_ref, hidden_ref, scratch):
        self.done_ref, self.base_ref, self.cols_ref, self.hidden_ref = done_ref, base_ref, cols_ref, hidden_ref
        self.back_ref, self.base_buf, self.send_sem, self.recv_sem, own_sem = scratch
        self.me = lax.axis_index("expert")
        self.experts = done_ref.shape[1]
        self.others = partners(exp_n, self.me)
        self.own = [
            pltpu.make_async_copy(
                done_ref.at[self.me // 2, e, lax.rem(self.me, 2)], self.back_ref.at[self.me * self.experts + e],
                own_sem.at[e],
            )
            for e in range(self.experts)
        ] + [pltpu.make_async_copy(base_ref, self.base_buf, own_sem.at[self.experts])]

    def copy(self, other, e, owner):
        return remote(
            self.done_ref.at[other // 2, e, lax.rem(other, 2)], self.back_ref.at[owner * self.experts + e],
            self.send_sem.at[other, e], self.recv_sem.at[owner, e], "expert", other,
        )

    def start(self):
        for other in self.others:
            for e in range(self.experts):
                self.copy(other, e, self.me).start()
        for copy in self.own:
            copy.start()

    def combine(self):
        for copy in self.own:
            copy.wait()
        for other in self.others:
            for e in range(self.experts):
                self.copy(other, e, other).wait_recv()
        tok, model = self.base_ref.shape
        slots = self.back_ref.shape[0] * self.back_ref.shape[1]
        block = 256

        def rows_out(i, carry):
            rows = pl.ds(pl.multiple_of(i * block, block), block)
            table = self.back_ref[...].reshape(slots, model)
            target = lax.broadcasted_iota(jnp.int32, (block, slots), 1)
            total = self.base_buf[rows]
            for k in range(2):
                slot = self.cols_ref[rows, 2 + k : 3 + k].astype(jnp.int32)
                gate = self.cols_ref[rows, 4 + k : 5 + k]
                total = total + gate * nn(jnp.where(target == slot, 1.0, 0.0).astype(BF), table)
            self.hidden_ref[rows] = total.astype(BF)
            return carry

        lax.fori_loop(0, tok // block, rows_out, 0)

    def finish(self):
        for other in self.others:
            for e in range(self.experts):
                self.copy(other, e, self.me).wait_send()


def results_shapes(exp_n, done):
    _, experts, _, capacity, model = done.shape
    dma = pltpu.SemaphoreType.DMA
    return [
        pltpu.VMEM((exp_n * experts, capacity, model), BF), pltpu.VMEM((4 * capacity, model), F32),
        dma((exp_n, experts)), dma((exp_n, experts)), dma((experts + 1,)),
    ]


def results_kernel(exp_n, done_ref, base_ref, cols_ref, hidden_ref, *scratch):
    greet([("expert", exp_n)])()
    results = Results(exp_n, done_ref, base_ref, cols_ref, hidden_ref, scratch)
    results.start()
    results.combine()
    results.finish()


def return_results(done):
    exp_n = lax.axis_size("expert")
    vmem = pl.BlockSpec(memory_space=pltpu.VMEM)
    return pl.pallas_call(
        functools.partial(results_kernel, exp_n),
        out_shape=jax.ShapeDtypeStruct(done[1].shape, BF),
        in_specs=[pl.BlockSpec(memory_space=pl.ANY)] * 2 + [vmem],
        out_specs=vmem,
        scratch_shapes=results_shapes(exp_n, done[0]),
        compiler_params=pltpu.CompilerParams(
            collective_id=5, has_side_effects=True, vmem_limit_bytes=VLIMIT
        ),
        name="return_results",
    )(*done)


class Sums:
    def __init__(self, sizes, ids_ref, sums_ref, early_ref, attn_ref, table_ref, attn_table, scratch):
        self.ctx_n, self.dp_n, self.exp_n, self.adapters, self.attn_tiles = sizes
        self.ids_ref, self.attn_ref = ids_ref, attn_ref
        self.table_ref, self.attn_table = table_ref, attn_table
        self.ctx, self.dp, self.exp = (lax.axis_index(axis) for axis in ALL_AXES)
        (
            self.arrived_z, self.early, self.held_a, self.arrived_xa, self.part_a, self.arrived_za,
            self.z_send, self.z_recv, self.az_send, self.az_recv, self.ax_send, self.ax_recv,
            self.r_send, self.r_recv, self.xa_send, self.xa_recv, self.za_send, self.za_recv,
            self.bz_send, self.bz_recv, self.bx_send, self.bx_recv, self.be_send, self.be_recv,
            self.keep_sem, load_sem,
        ) = scratch
        self.waits = []
        z_tiles = self.arrived_z.shape[2]
        self.experts = table_ref.shape[2]
        self.loads = [
            pltpu.make_async_copy(early_ref, self.early, load_sem.at[0]),
            pltpu.make_async_copy(
                sums_ref.at[:, pl.ds(self.dp * z_tiles, z_tiles)], self.arrived_z.at[0], load_sem.at[1]
            ),
        ]
        self.z_copies = [
            self.plan(
                sums_ref.at[:, pl.ds(self.peer("dp", k) * z_tiles, z_tiles)], self.arrived_z.at[k],
                self.z_send.at[k - 1], self.z_recv.at[k - 1], "dp", self.peer("dp", k),
            )
            for k in range(1, self.dp_n)
        ]
        self.lines, self.ax_copies = [], []
        for e in range(self.experts):
            self.lines.append([self.line(e, s) for s in range(1, self.dp_n)])
            self.ax_copies.append([self.across(e, origin) for origin in range(self.dp_n)])

    def slot(self, e, origin):
        return self.table_ref.at[self.ctx, lax.rem(origin + self.dp_n, self.dp_n), e]

    def line(self, e, s):
        ways = []
        for way, sign in enumerate((1, -1)):
            mine, landing = self.slot(e, self.dp - sign * (s - 1)), self.slot(e, self.dp - sign * s)
            target = lax.rem(self.dp + sign + self.dp_n, self.dp_n)
            send_sem, recv_sem = self.az_send.at[e, way, s - 1], self.az_recv.at[e, way, s - 1]
            edge, origin, source = self.dp + sign, self.dp - sign * (s - 1), self.dp - sign * s
            ways.append(
                (
                    remote(mine, mine, send_sem, recv_sem, "dp", target),
                    (edge >= 0) & (edge < self.dp_n) & (origin >= 0) & (origin < self.dp_n),
                    remote(landing, landing, send_sem, recv_sem, "dp", target),
                    (source >= 0) & (source < self.dp_n),
                )
            )
        return ways

    def across(self, e, origin):
        here = self.slot(e, origin)
        at = lax.rem(origin + self.dp_n, self.dp_n)
        return [
            remote(
                here, here, self.ax_send.at[step - 1, e, at], self.ax_recv.at[step - 1, e, at], "context",
                self.peer("context", step),
            )
            for step in range(1, self.ctx_n)
        ]

    def plan(self, src, dst, send, recv, axis, target):
        copy = remote(src, dst, send, recv, axis, target)
        self.waits.append(copy)
        return copy

    def peer(self, axis, step):
        index, size = {
            "context": (self.ctx, self.ctx_n), "dp": (self.dp, self.dp_n), "expert": (self.exp, self.exp_n)
        }[axis]
        return lax.rem(index + step, size)

    def send(self, src, dst, send, recv, axis, target):
        copy = self.plan(src, dst, send, recv, axis, target)
        copy.start()
        return copy

    def weight(self, k, source):
        origin = lax.rem(self.dp - k + self.dp_n, self.dp_n)
        name = self.ids_ref[origin * self.exp_n + source]
        return [jnp.where(name == a, 1.0, 0.0).astype(F32) for a in range(self.adapters)]

    def merge(self, count, read, write):
        marks = [self.weight(k, source) for k in range(self.dp_n) for source in range(self.exp_n)]

        def tile_sums(tile, carry):
            totals = [jnp.zeros((16, 128), F32)] * self.adapters
            for k in range(self.dp_n):
                for source in range(self.exp_n):
                    value = read(k, source, tile).astype(F32)
                    mark = marks[k * self.exp_n + source]
                    totals = [total + m * value for total, m in zip(totals, mark)]
            for a in range(self.adapters):
                write(a, tile, totals[a].astype(BF))
            return carry

        lax.fori_loop(0, count, tile_sums, 0)

    def start(self):
        for copy in self.loads:
            copy.start()
        if self.experts == 1:
            self.exchange()

    def exchange(self):
        for copy in self.z_copies:
            copy.start()

    def combine(self, e):
        z_tiles = self.arrived_z.shape[2]
        if e < self.experts - 1:
            if e == 0:
                self.loads[0].wait()
            source_ref = self.early.at[e]
        else:
            if self.experts == 1:
                self.loads[0].wait()
            self.loads[1].wait()
            for copy in self.z_copies:
                copy.wait_recv()
            source_ref = self.arrived_z

        def write(a, tile, value):
            self.table_ref[self.ctx, self.dp, e, a, tile] = value

        self.merge(z_tiles, lambda k, source, tile: source_ref[k, source, tile], write)
        self.push(e, 1)
        for copy in self.across(e, self.dp):
            copy.start()

    def push(self, e, s):
        if s < self.dp_n:
            for send, whether, _, _ in self.lines[e][s - 1]:
                pl.when(whether)(send.start)

    def advance(self, e, s):
        self.take(e, s)
        self.hand(e, s)

    def take(self, e, s):
        if s < self.dp_n:
            for _, _, receive, whether in self.lines[e][s - 1]:
                pl.when(whether)(receive.wait_recv)
            self.push(e, s + 1)

    def hand(self, e, s):
        if s >= self.dp_n:
            return
        for sign, (_, _, _, whether) in zip((1, -1), self.lines[e][s - 1]):
            @pl.when(whether)
            def _(sign=sign):
                for copy in self.across(e, self.dp - sign * s):
                    copy.start()

    def tail(self, between):
        def other(step):
            if step in between:
                between[step]()

        own, x_tiles, z_tiles = attn_tiling(self.attn_tiles)
        real = pl.cdiv(x_tiles, z_tiles)
        keep = pltpu.make_async_copy(
            self.attn_ref.at[pl.ds(self.exp * own, own)], self.held_a.at[self.exp, pl.ds(0, own)], self.keep_sem
        )
        keep.start()
        copies = [
            self.send(
                self.attn_ref.at[pl.ds(self.peer("expert", k) * own, own)],
                self.held_a.at[self.exp, pl.ds(0, own)],
                self.r_send.at[k - 1], self.r_recv.at[k - 1], "expert", self.peer("expert", k),
            )
            for k in range(1, self.exp_n)
        ]
        other("sources")
        keep.wait()
        for copy in copies:
            copy.wait_recv()
        copies = [
            self.send(
                self.held_a.at[:, pl.ds(self.peer("context", k) * x_tiles, x_tiles)], self.arrived_xa.at[k - 1],
                self.xa_send.at[k - 1], self.xa_recv.at[k - 1], "context", self.peer("context", k),
            )
            for k in range(1, self.ctx_n)
        ]
        other("context")
        for copy in copies:
            copy.wait_recv()
        total = self.held_a[:, pl.ds(self.ctx * x_tiles, x_tiles)].astype(F32)
        for k in range(1, self.ctx_n):
            total = total + self.arrived_xa[k - 1].astype(F32)
        self.part_a[:, 0:x_tiles] = total.astype(BF)
        copies = [
            self.send(
                self.part_a.at[:, pl.ds(self.peer("dp", k) * z_tiles, z_tiles)], self.arrived_za.at[k - 1],
                self.za_send.at[k - 1], self.za_recv.at[k - 1], "dp", self.peer("dp", k),
            )
            for k in range(1, self.dp_n)
        ]
        other("dp")
        for copy in copies:
            copy.wait_recv()
        mine = self.attn_table.at[self.exp]

        def write(a, tile, value):
            self.attn_table[self.exp, self.ctx, self.dp, a, tile] = value

        def read(k, source, tile):
            if k == 0:
                return self.part_a[source, self.dp * z_tiles + tile]
            return self.arrived_za[k - 1, source, tile]

        self.merge(z_tiles, read, write)
        here = mine.at[self.ctx, self.dp]
        copies = [
            self.send(here, here, self.bz_send.at[k - 1], self.bz_recv.at[k - 1], "dp", self.peer("dp", k))
            for k in range(1, self.dp_n)
        ]
        other("dp_back")
        for copy in copies:
            copy.wait_recv()
        here = mine.at[self.ctx, pl.ds(0, real)]
        copies = [
            self.send(
                here, here, self.bx_send.at[k - 1], self.bx_recv.at[k - 1], "context", self.peer("context", k)
            )
            for k in range(1, self.ctx_n)
        ]
        x_back = copies
        core = lax.rem(self.exp, 2)
        twin = self.exp + 1 - 2 * core
        chips = self.exp_n // 2

        def table_of(owner, j):
            return self.attn_table.at[owner, lax.rem(self.ctx + j, self.ctx_n), pl.ds(0, real)]

        far, near = [], []

        def along(j):
            for k in range(1, chips):
                here = table_of(self.exp, j)
                far.append(
                    self.send(
                        here, here, self.be_send.at[0, k - 1, j], self.be_recv.at[0, k - 1, j], "expert",
                        self.peer("expert", 2 * k),
                    )
                )
            near.append(self.to_twin(table_of(self.exp, j), 0, j, twin))

        along(0)
        other("context_back")
        for copy in x_back:
            copy.wait_recv()
        for j in range(1, self.ctx_n):
            along(j)
        for j in range(self.ctx_n):
            for k in range(1, chips):
                far[j * (chips - 1) + k - 1].wait_recv()
                owner = self.peer("expert", self.exp_n - 2 * k)
                near.append(self.to_twin(table_of(owner, j), k, j, twin))
        other("last")
        for copy in near:
            copy.wait_recv()

    def to_twin(self, here, k, j, twin):
        return self.send(here, here, self.be_send.at[1, k, j], self.be_recv.at[1, k, j], "expert", twin)

    def finish(self):
        for by_expert in self.ax_copies:
            for copies in by_expert:
                for copy in copies:
                    copy.wait()
        for by_expert in self.lines:
            for ways in by_expert:
                for send, whether, _, _ in ways:
                    pl.when(whether)(send.wait_send)
        for copy in self.waits:
            copy.wait_send()


def sums_shapes(experts, model, width, attn_tiles, adapters):
    ctx_n, dp_n, exp_n = (lax.axis_size(axis) for axis in ("context", "dp", "expert"))
    _, _, z_tiles = expert_tiling(experts, model, width)
    own, xa_tiles, za_tiles = attn_tiling(attn_tiles)
    many, deep, chips = max(ctx_n - 1, 1), max(dp_n - 1, 1), max(exp_n // 2, 1)
    dma = pltpu.SemaphoreType.DMA
    outs = (
        jax.ShapeDtypeStruct((ctx_n, dp_n, experts, adapters, z_tiles, 16, 128), BF),
        jax.ShapeDtypeStruct((exp_n, ctx_n, dp_n, adapters, za_tiles, 16, 128), BF),
    )
    scratch = [
        pltpu.VMEM((dp_n, exp_n, z_tiles, 16, 128), BF),
        pltpu.VMEM((max(experts - 1, 1), dp_n, exp_n, z_tiles, 16, 128), BF),
        pltpu.VMEM((exp_n, max(ctx_n * xa_tiles, own), 16, 128), BF),
        pltpu.VMEM((many, exp_n, xa_tiles, 16, 128), BF),
        pltpu.VMEM((exp_n, dp_n * za_tiles, 16, 128), BF),
        pltpu.VMEM((deep, exp_n, za_tiles, 16, 128), BF),
        dma((deep,)), dma((deep,)), dma((experts, 2, deep)), dma((experts, 2, deep)),
        dma((many, experts, dp_n)), dma((many, experts, dp_n)),
        dma((exp_n,)), dma((exp_n,)), dma((many,)), dma((many,)), dma((deep,)), dma((deep,)),
        dma((deep,)), dma((deep,)), dma((many,)), dma((many,)), dma((2, chips, ctx_n)), dma((2, chips, ctx_n)),
        dma, dma((2,)),
    ]
    return outs, scratch


ALL_AXES = ("context", "dp", "expert")


def sums_kernel(sizes, ids_ref, sums_ref, early_ref, attn_ref, table_ref, attn_table, *scratch):
    greet([(axis, lax.axis_size(axis)) for axis in ALL_AXES])()
    sums = Sums(sizes, ids_ref, sums_ref, early_ref, attn_ref, table_ref, attn_table, scratch)
    sums.start()
    for e in range(sums.experts):
        if e > 0 and e == sums.experts - 1:
            sums.exchange()
        sums.combine(e)
    for e in range(sums.experts):
        for s in range(1, sums.dp_n):
            sums.advance(e, s)
    sums.tail({})
    sums.finish()


def add_up(ids, sums, attn, experts, width, adapters):
    model = attn.shape[0] * 16
    outs, scratch = sums_shapes(experts, model, width, attn.shape[0], adapters)
    vmem, hbm = pl.BlockSpec(memory_space=pltpu.VMEM), pl.BlockSpec(memory_space=pl.ANY)
    sizes = tuple(lax.axis_size(axis) for axis in ALL_AXES) + (adapters, attn.shape[0])
    return pl.pallas_call(
        functools.partial(sums_kernel, sizes),
        out_shape=outs,
        in_specs=[pl.BlockSpec(memory_space=pltpu.SMEM), hbm, hbm, vmem],
        out_specs=(vmem, vmem),
        scratch_shapes=scratch,
        compiler_params=pltpu.CompilerParams(
            collective_id=1, has_side_effects=True, vmem_limit_bytes=VLIMIT
        ),
        name="reduce_adapters",
    )(ids, *sums, attn)


def unpack_kernel(sizes, table_ref, attn_ref, hidden_in, grad_in, prev_in, hidden_ref, grad_ref, prev_ref, down_ref, up_ref, in_down_ref, in_up_ref, out_down_ref, out_up_ref):
    share, z_tiles, own, xa_tiles, za_tiles = sizes
    hidden_ref[...] = hidden_in[...]
    grad_ref[...] = grad_in[...]
    prev_ref[...] = prev_in[...]
    for expert in range(in_up_ref.shape[1]):
        tile = 0
        for out_ref in (in_down_ref, in_up_ref, out_down_ref, out_up_ref):
            rows, cols = out_ref.shape[2:]
            for row in range(rows // 16):
                for col in range(cols // 128):
                    place = tile % share
                    out_ref[0, expert, row * 16 : row * 16 + 16, col * 128 : col * 128 + 128] = table_ref[
                        tile // share, place // z_tiles, expert, 0, place % z_tiles
                    ].astype(F32)
                    tile += 1
    tile = 0
    for out_ref in (down_ref, up_ref):
        rows, cols = out_ref.shape[1:]
        for row in range(rows // 16):
            for col in range(cols // 128):
                place = tile % own
                out_ref[0, row * 16 : row * 16 + 16, col * 128 : col * 128 + 128] = attn_ref[
                    tile // own, place // xa_tiles, place % xa_tiles // za_tiles, 0, place % xa_tiles % za_tiles
                ].astype(F32)
                tile += 1


def unpack(table, attn_table, by_token, experts, width, table_shapes, attn_shape):
    adapters = table.shape[3]
    model = attn_shape[1]
    share, _, z_tiles = expert_tiling(experts, model, width)
    sizes = (share, z_tiles) + attn_tiling(8 * model // 128)
    shapes = [(adapters,) + attn_shape] * 2 + [(adapters,) + shape for shape in table_shapes]

    def by_adapter(array, axis):
        block = array.shape[:axis] + (1,) + array.shape[axis + 1 :]
        return pl.BlockSpec(block, lambda a, n=array.ndim: (0,) * axis + (a,) + (0,) * (n - axis - 1))

    hidden, grad, prev = by_token
    part = pl.BlockSpec((hidden.shape[0] // adapters, model), lambda a: (a, 0))
    passed = [part, part, pl.BlockSpec(prev.shape, lambda a: (0, 0, 0))]
    return pl.pallas_call(
        functools.partial(unpack_kernel, sizes),
        grid=(adapters,),
        out_shape=tuple(jax.ShapeDtypeStruct(entry.shape, entry.dtype) for entry in by_token)
        + tuple(jax.ShapeDtypeStruct(shape, F32) for shape in shapes),
        in_specs=[by_adapter(table, 3), by_adapter(attn_table, 3), *passed],
        out_specs=tuple(passed)
        + tuple(
            pl.BlockSpec((1,) + shape[1:], lambda a, n=len(shape): (a,) + (0,) * (n - 1))
            for shape in shapes
        ),
        compiler_params=pltpu.CompilerParams(vmem_limit_bytes=VLIMIT),
        name="unpack_adapters",
    )(table, attn_table, *by_token)


def local(
    hidden_in,
    prev_logits,
    segment_ids,
    routes,
    adapter_ids,
    attn_gain,
    w_qkv,
    w_out,
    attn_down,
    attn_up,
    ffn_gain,
    router_weight,
    gate_mix,
    const_mix,
    const_vec,
    w_gate_up,
    w_down,
    exp_in_down,
    exp_in_up,
    exp_out_down,
    exp_out_up,
    cotangent,
):
    model_dim = hidden_in.shape[2]
    local_experts, ffn_width = w_down.shape[:2]
    adapter_count = attn_down.shape[0]
    rank_dim = attn_up.shape[2]
    down_all = jnp.swapaxes(attn_down, 2, 3).reshape(adapter_count, 4 * rank_dim, model_dim)
    up_all = attn_up.reshape(adapter_count, 4 * rank_dim, model_dim)
    small = (router_weight.T, const_mix.transpose(0, 2, 1), attn_gain, ffn_gain)
    (
        q_pairs, k_pairs, v_pairs, normed_all, rank_all, log_cols, attn_flat, rank_out_all, mid_resid,
        rows_low, logits_all, seg_all, arrived_dy, slots, router_rows,
    ) = attention_forward(
        hidden_in[0], segment_ids, prev_logits.transpose(2, 0, 1), gate_mix, adapter_ids, w_qkv, w_out, down_all,
        up_all, small, cotangent[0], routes[0].T, local_experts,
    )
    tables = (
        jnp.swapaxes(exp_in_down, 2, 3),
        exp_in_up.reshape(exp_in_up.shape[:2] + (2 * rank_dim, ffn_width)),
        jnp.swapaxes(exp_out_down, 2, 3),
        exp_out_up,
    )
    base, d_mid, grad_prev, *expert_sums, done_out, cols = expert_layer(
        rows_low, mid_resid, logits_all, slots, cotangent[0], arrived_dy, adapter_ids, router_rows,
        gate_mix, const_vec, w_gate_up, w_down, tables,
    )
    grad_in, table, attn_table, hidden_out = attention_backward(
        d_mid,
        (q_pairs, k_pairs, v_pairs, normed_all, rank_all, log_cols, attn_flat, rank_out_all, seg_all),
        hidden_in[0], adapter_ids, router_rows, w_qkv, w_out, down_all, up_all, expert_sums,
        (done_out, base, cols), local_experts, ffn_width,
    )
    hidden_out, grad_in, grad_prev, *sums = unpack(
        table, attn_table, (hidden_out, grad_in, grad_prev), local_experts, ffn_width, [entry.shape[1:] for entry in tables],
        (4 * rank_dim, model_dim),
    )
    grad_attn_down = jnp.swapaxes(sums[0].reshape(adapter_count, 4, rank_dim, model_dim), 2, 3)
    grad_attn_up = sums[1].reshape(adapter_count, 4, rank_dim, model_dim)
    grad_in_down = jnp.swapaxes(sums[2], 2, 3)
    grad_in_up = sums[3].reshape(exp_in_up.shape)
    grad_out_down = jnp.swapaxes(sums[4], 2, 3)
    grad_out_up = sums[5]
    return (
        hidden_out[None],
        grad_in[None],
        grad_prev.transpose(1, 2, 0),
        grad_attn_down,
        grad_attn_up,
        grad_in_down,
        grad_in_up,
        grad_out_down,
        grad_out_up,
    )


def solution(mesh):
    return jax.shard_map(
        local,
        mesh=mesh,
        in_specs=(
            P(("dp", "expert"), "context", None),
            P(("dp", "expert"), "context", None),
            P(("dp", "expert"), "context"),
            P(("dp", "expert"), "context", None),
            P(),
            P(),
            P(),
            P(),
            P(),
            P(),
            P(),
            P(),
            P(),
            P(),
            P(),
            P("expert", None, None),
            P("expert", None, None),
            P(None, "expert", None, None),
            P(None, "expert", None, None, None),
            P(None, "expert", None, None),
            P(None, "expert", None, None),
            P(("dp", "expert"), "context", None),
        ),
        out_specs=(
            P(("dp", "expert"), "context", None),
            P(("dp", "expert"), "context", None),
            P(("dp", "expert"), "context", None),
            P(),
            P(),
            P(None, "expert", None, None),
            P(None, "expert", None, None, None),
            P(None, "expert", None, None),
            P(None, "expert", None, None),
        ),
        check_vma=False,
    )
```

```python
import functools
import math

import jax
import jax.numpy as jnp
import numpy as np
from jax import lax
from jax.experimental import pallas as pl
from jax.experimental.pallas import tpu as pltpu
from jax.sharding import PartitionSpec as P

MESH = pl.DeviceIdType.MESH
VLIMIT = 60 * 1024 * 1024
BF = jnp.bfloat16
F32 = jnp.float32

HEADS = 12


EPSILON = 1e-06
ADAPT_SCALE = 2.0
NEG = -1e30
HIGH = lax.Precision.HIGHEST


def nt(left, right):
    return lax.dot_general(left, right, (((1,), (1,)), ((), ())), preferred_element_type=F32)


def tn(left, right):
    return lax.dot_general(left, right, (((0,), (0,)), ((), ())), preferred_element_type=F32)


def nn(left, right):
    return jnp.dot(left, right, preferred_element_type=F32)


def rope_tables(positions, width):
    half = width // 2
    frequency = np.exp(np.arange(half) * (-2.0 * math.log(10000.0) / width))
    angles = np.arange(positions)[:, None] * frequency[None, :]
    cosine, sine = np.cos(angles), np.sin(angles)
    return (
        np.concatenate([cosine] * 4, 1).astype(np.float32),
        np.concatenate([-sine, sine] * 2, 1).astype(np.float32),
    )


def turn(block, cosine, sine, width):
    half = width // 2
    lane = lax.broadcasted_iota(jnp.int32, block.shape, 1)
    other = jnp.where(
        lane % width < half, pltpu.roll(block, 128 - half, 1), pltpu.roll(block, half, 1)
    )
    return block * cosine + other * sine


def greet(axes):
    barrier = pltpu.get_barrier_semaphore()
    count = 0
    for axis, size in axes:
        index = lax.axis_index(axis)
        for step in range(1, size):
            pl.semaphore_signal(
                barrier, inc=1, device_id={axis: lax.rem(index + step, size)}, device_id_type=MESH
            )
        count += size - 1
    return lambda: pl.semaphore_wait(barrier, count)


def remote(src, dst, send, recv, axis, target):
    return pltpu.make_async_remote_copy(
        src_ref=src, dst_ref=dst, send_sem=send, recv_sem=recv,
        device_id={axis: target}, device_id_type=MESH,
    )


def blocks_of(ctx_n, ctx, count):
    return [lax.rem(ctx + 1 + j, ctx_n) for j in range(count)]


def fill_bias(bias_ref, seg_all, ctx, tok, j, block):
    own = jnp.broadcast_to(seg_all[ctx, 0:1, :].astype(F32), (128, tok))
    query_seg = jnp.transpose(own)[:, 0:1]
    query_pos = ctx * tok + lax.broadcasted_iota(jnp.int32, (tok, tok), 0)
    key_seg = seg_all[block, 0:1, :].astype(F32)
    key_pos = block * tok + lax.broadcasted_iota(jnp.int32, (tok, tok), 1)
    allowed = (query_seg == key_seg) & (key_pos <= query_pos)
    bias_ref[j] = jnp.where(allowed, 0.0, NEG).astype(bias_ref.dtype)


def head_marks():
    lane = lax.broadcasted_iota(jnp.int32, (1, 128), 1)
    return lane, lane < 64


def stack_heads(value):
    _, first = head_marks()
    return jnp.concatenate([jnp.where(first, value, 0), jnp.where(first, 0, value)], 0)


def join_heads(value):
    _, first = head_marks()
    rows = value.shape[0] // 2
    return jnp.where(first, value[:rows], value[rows:])


def stack_columns(stats, i):
    lane, _ = head_marks()
    return jnp.concatenate(
        [jnp.sum(jnp.where(lane == 2 * i + head, stats, 0.0), -1, keepdims=True) for head in range(2)], 0
    )


def put_columns(stats, i, column):
    lane, _ = head_marks()
    rows = stats.shape[0]
    stats = jnp.where(lane == 2 * i, column[:rows], stats)
    return jnp.where(lane == 2 * i + 1, column[rows:], stats)


def biased(raw, bias):
    rows, keys = bias.shape
    return (raw.reshape(2, rows, keys) + bias[None]).reshape(2 * rows, keys)


def attention_kernel(
    sizes, ids_ref, x_hbm, seg_ref, prev_ref, mix_ref, w_qkv_hbm, w_out_hbm, down_hbm, up_hbm,
    kind_ref, const_ref, gain_one_ref, gain_two_ref, cos_hbm, sin_hbm, dy_hbm, routes_ref,
    q_out, k_out, v_out, normed_out, rank_ref, total_ref, flat_ref, rank_out_ref, mid_ref, rows_ref,
    logits_ref, seg_all, arrived_dy, slots_ref, router_ref,
    x_all, bias_ref, sent_dy, acc_ref, top_ref, weight_ref, prev_pad, mix_pad, send_sem, recv_sem, seg_send, seg_recv, dy_send, dy_recv,
    q_ref, k_ref, v_ref, normed_ref, own_dy, out_sem, rows_f32, *staged,
):
    ctx_n, exp_n, rank = sizes
    dy_ref, x_ref, down_ref, up_ref, w_qkv_ref, cos_ref, sin_ref, w_out_ref, stage_sem = staged
    stages = stage_copies(
        (dy_hbm, x_hbm, down_hbm, up_hbm, w_qkv_hbm, cos_hbm, sin_hbm, w_out_hbm), staged, stage_sem
    )
    for stage in stages:
        stage.start()
    ctx = lax.axis_index("context")
    sequence = lax.axis_index("dp") * exp_n + lax.axis_index("expert")
    tok, model = x_ref.shape
    pairs, head_dim = model // 128, 64
    entered = greet([("context", ctx_n), ("expert", exp_n)])
    seg_all[ctx] = jnp.broadcast_to(seg_ref[...], (8, tok))
    me = lax.axis_index("expert")
    experts, capacity = arrived_dy.shape[1], arrived_dy.shape[3]
    others = partners(exp_n, me)
    entered()
    dy_copies = []
    if ctx_n > 1:
        copies = []
        for step in range(1, ctx_n):
            peer = lax.rem(ctx + step, ctx_n)
            copies.append(
                (
                    peer,
                    step,
                    remote(x_hbm, x_all.at[ctx], send_sem.at[step - 1], recv_sem.at[step - 1], "context", peer),
                    remote(seg_all.at[ctx], seg_all.at[ctx], seg_send.at[step - 1], seg_recv.at[step - 1], "context", peer),
                )
            )

        def to_later(peer):
            return ctx < peer if ctx_n == 2 else ctx < ctx_n

        def from_earlier(step):
            return lax.rem(ctx - step + ctx_n, ctx_n) < ctx if ctx_n == 2 else ctx < ctx_n

        for peer, step, rows_copy, seg_copy in copies:
            @pl.when(to_later(peer))
            def _(rows_copy=rows_copy, seg_copy=seg_copy):
                seg_copy.start()
                rows_copy.start()

    kind_rows = jnp.concatenate([routes_ref[...], jnp.full((6, tok), -1, jnp.int32)], 0)
    sub = lax.broadcasted_iota(jnp.int32, (16, tok), 0)
    uses = jnp.where((sub == kind_rows[0:1]) | (sub == kind_rows[1:2]), 1.0, 0.0).astype(BF)
    earlier = jnp.where(
        lax.broadcasted_iota(jnp.int32, (tok, tok), 0) < lax.broadcasted_iota(jnp.int32, (tok, tok), 1), 1.0, 0.0
    ).astype(BF)
    places = nn(uses, earlier) + (sub * capacity).astype(F32)
    slot_rows = []
    for j in range(2):
        kind = kind_rows[j : j + 1]
        place = jnp.sum(jnp.where(sub == kind, places, 0.0), 0, keepdims=True)
        slot_rows.append(jnp.where(kind < exp_n * experts, place, -1.0))
    row8 = lax.broadcasted_iota(jnp.int32, (8, tok), 0)
    slots_ref[...] = jnp.where(
        row8 < 2, kind_rows.astype(F32), jnp.where(row8 == 2, slot_rows[0], jnp.where(row8 == 3, slot_rows[1], 0.0))
    )
    slot_ints = [row.astype(jnp.int32) for row in slot_rows]

    def pick_dy(owner):
        hots = [hot_rows(row, owner * experts * capacity, experts * capacity) for row in slot_ints]
        hot = jnp.where(hots[0] | hots[1], 1.0, 0.0).astype(BF)
        return nn(hot, dy_ref[...]).astype(BF)

    stages[0].wait()
    for i, peer in enumerate(others):
        picked = pick_dy(peer)
        for e in range(experts):
            sent_dy[i, e] = picked[e * capacity : (e + 1) * capacity]
        copy = remote(
            sent_dy.at[i], arrived_dy.at[me // 2, :, lax.rem(me, 2)], dy_send.at[i], dy_recv.at[me], "expert", peer
        )
        copy.start()
        dy_copies.append(copy)
    picked = pick_dy(me)
    for e in range(experts):
        own_dy[e] = picked[e * capacity : (e + 1) * capacity]
    writes = [pltpu.make_async_copy(own_dy, arrived_dy.at[me // 2, :, lax.rem(me, 2)], out_sem.at[0])]
    writes[0].start()
    for stage in stages[1:]:
        stage.wait()
    adapter = ids_ref[sequence]
    down = down_ref[adapter]
    up = up_ref[adapter]
    kinds = mix_ref.shape[0]
    rows_f32[...] = jnp.zeros_like(rows_f32)
    rows_f32[0:kinds] = kind_ref[...].astype(F32)
    for c in range(2):
        rows_f32[kinds + 2 * c : kinds + 2 * c + 2] = const_ref[c].astype(F32)
    rows_f32[16:17] = gain_one_ref[...].astype(F32).reshape(1, model)
    rows_f32[17:18] = gain_two_ref[...].astype(F32).reshape(1, model)
    router_ref[...] = jnp.zeros_like(router_ref)
    router_ref[0:32] = rows_f32[...].astype(BF)
    gain_one = rows_f32[16:17]
    column = lax.broadcasted_iota(jnp.int32, (tok, down.shape[0]), 1) // rank

    def project(values, block, first):
        wide = values.astype(F32)
        inv = lax.rsqrt(jnp.mean(wide * wide, -1, keepdims=True) + EPSILON)
        normed_ref[block] = (wide * inv * gain_one).astype(BF)
        normed = normed_ref[block]
        ranks = nt(normed, down).astype(BF)
        rank_ref[block] = ranks
        start = pl.multiple_of(block * tok, tok)
        for p in range(first, 3):
            part = jnp.where(column == p, ADAPT_SCALE * ranks.astype(F32), 0.0).astype(BF)

            def chunk(i, carry, p=p, part=part):
                wide_cols = pl.ds(pl.multiple_of(p * model + i * 256, 256), 256)
                cols = pl.ds(pl.multiple_of(i * 256, 256), 256)
                proj = nn(normed_ref[block], w_qkv_ref[:, wide_cols]) + nn(
                    part, up_cols[:, cols]
                )
                for half in range(2):
                    piece = proj[:, half * 128 : half * 128 + 128]
                    if p < 2:
                        piece = turn(
                            piece, cos_ref[pl.ds(start, tok)], sin_ref[pl.ds(start, tok)], head_dim
                        )
                    if p == 0:
                        q_ref[2 * i + half] = (piece * head_dim ** (-0.5)).astype(BF)
                    else:
                        (k_ref if p == 1 else v_ref)[block, 2 * i + half] = piece.astype(BF)
                return carry

            up_cols = up_ref.at[adapter]
            lax.fori_loop(0, model // 256, chunk, 0, unroll=True)

    project(x_ref[...], ctx, 0)
    half_rows = tok // 2
    halves = [slice(half * half_rows, (half + 1) * half_rows) for half in range(2)]

    def own_pair(i, carry):
        for half, rows in enumerate(halves):
            width = (half + 1) * half_rows
            scores = biased(
                nt(stack_heads(q_ref[i, rows]), k_ref[ctx, i, 0:width]), bias_ref[0, rows, 0:width]
            )
            top = jnp.max(scores, -1, keepdims=True)
            exps = jnp.exp(scores - top)
            acc_ref[i, rows] = join_heads(nn(exps.astype(BF), v_ref[ctx, i, 0:width]))
            top_ref[rows] = put_columns(top_ref[rows], i, top)
            weight_ref[rows] = put_columns(weight_ref[rows], i, jnp.sum(exps, -1, keepdims=True))
        return carry

    def close_pair(i, carry):
        for rows in halves:
            inv = 1.0 / stack_columns(weight_ref[rows], i)
            flat_ref[rows, pl.ds(pl.multiple_of(i * 128, 128), 128)] = (
                acc_ref[i, rows] * join_heads(inv)
            ).astype(BF)
        return carry

    def attend_others():
        others = blocks_of(ctx_n, ctx, ctx_n - 1)
        for j, block in enumerate(others):
            fill_bias(bias_ref, seg_all, ctx, tok, j + 1, block)

        def pair(i, carry):
            for rows in halves:
                q = stack_heads(q_ref[i, rows])
                scores = [
                    biased(nt(q, k_ref[block, i]), bias_ref[j + 1, rows]) for j, block in enumerate(others)
                ]
                before = stack_columns(top_ref[rows], i)
                top = functools.reduce(
                    jnp.maximum, [before] + [jnp.max(part, -1, keepdims=True) for part in scores]
                )
                keep = jnp.exp(before - top)
                exps = [jnp.exp(part - top) for part in scores]
                total = keep * stack_columns(weight_ref[rows], i)
                result = acc_ref[i, rows] * join_heads(keep)
                for part, block in zip(exps, others):
                    total = total + jnp.sum(part, -1, keepdims=True)
                    result = result + join_heads(nn(part.astype(BF), v_ref[block, i]))
                flat_ref[rows, pl.ds(pl.multiple_of(i * 128, 128), 128)] = (
                    result * join_heads(1.0 / total)
                ).astype(BF)
                top_ref[rows] = put_columns(top_ref[rows], i, top)
                weight_ref[rows] = put_columns(weight_ref[rows], i, total)
            return carry

        lax.fori_loop(0, pairs, pair, 0, unroll=2 if ctx_n == 2 else 1)

    top_ref[...] = jnp.zeros_like(top_ref)
    weight_ref[...] = jnp.ones_like(weight_ref)
    fill_bias(bias_ref, seg_all, ctx, tok, 0, ctx)
    lax.fori_loop(0, pairs, own_pair, 0, unroll=2)
    if ctx_n == 1:
        lax.fori_loop(0, pairs, close_pair, 0)
    else:
        for peer, step, rows_copy, seg_copy in copies:
            @pl.when(from_earlier(step))
            def _(step=step, rows_copy=rows_copy, seg_copy=seg_copy):
                rows_copy.wait_recv()
                seg_copy.wait_recv()
                block = lax.rem(ctx - step + ctx_n, ctx_n)
                project(x_all[block], block, 1)

        if ctx_n == 2:
            @pl.when(ctx == 0)
            def _():
                lax.fori_loop(0, pairs, close_pair, 0)

            pl.when(ctx == 1)(attend_others)
        else:
            attend_others()
        for peer, step, rows_copy, seg_copy in copies:
            @pl.when(to_later(peer))
            def _(rows_copy=rows_copy, seg_copy=seg_copy):
                seg_copy.wait_send()
                rows_copy.wait_send()

    for i, (src, dst) in enumerate(((q_ref, q_out), (k_ref, k_out), (v_ref, v_out), (normed_ref, normed_out))):
        writes.append(pltpu.make_async_copy(src, dst, out_sem.at[1 + i]))
        writes[-1].start()
    total_ref[...] = top_ref[...] + jnp.log(weight_ref[...])
    rank_out = nt(flat_ref[...], down).astype(BF)
    rank_out_ref[...] = rank_out
    part = jnp.where(column == 3, ADAPT_SCALE * rank_out.astype(F32), 0.0).astype(BF)

    def out_chunk(i, carry):
        cols = pl.ds(pl.multiple_of(i * 256, 256), 256)
        mid_ref[:, cols] = (
            x_ref[:, cols].astype(F32)
            + nn(flat_ref[...], w_out_ref[:, cols])
            + nn(part, up_ref[adapter, :, cols])
        )
        return carry

    lax.fori_loop(0, model // 256, out_chunk, 0, unroll=True)
    gain_two = rows_f32[17:18]
    step_rows = 128

    def norm_rows(i, carry):
        rows = pl.ds(pl.multiple_of(i * step_rows, step_rows), step_rows)
        mid = mid_ref[rows]
        inv = lax.rsqrt(jnp.mean(mid * mid, -1, keepdims=True) + EPSILON)
        rows_ref[rows] = (mid * inv * gain_two).astype(BF)
        return carry

    lax.fori_loop(0, tok // step_rows, norm_rows, 0, unroll=True)
    prev_pad[...] = jnp.zeros_like(prev_pad)
    mix_pad[...] = jnp.zeros_like(mix_pad)
    for kind in range(kinds):
        prev_pad[kind : kind + 1] = prev_ref[kind]
    mix_pad[0:kinds, 0:kinds] = mix_ref[...]
    logits_ref[...] = nt(rows_ref[...], router_ref[...]) + lax.dot_general(
        prev_pad[...], mix_pad[...], (((0,), (0,)), ((), ())), precision=HIGH, preferred_element_type=F32
    )
    for write in writes:
        write.wait()
    for copy in dy_copies:
        copy.wait_send()
    for peer in others:
        remote(
            sent_dy.at[0], arrived_dy.at[peer // 2, :, lax.rem(peer, 2)], dy_send.at[0], dy_recv.at[peer], "expert", peer
        ).wait_recv()


def attention_forward(hidden, segments, prev, mix, ids, w_qkv, w_out, down, up, small, dy, routes, experts):
    ctx_n, exp_n = lax.axis_size("context"), lax.axis_size("expert")
    tok, model = hidden.shape
    pairs = model // 128
    wide = down.shape[1]
    cos_table, sin_table = rope_tables(ctx_n * tok, 64)
    vmem, hbm = pl.BlockSpec(memory_space=pltpu.VMEM), pl.BlockSpec(memory_space=pl.ANY)
    dma = pltpu.SemaphoreType.DMA
    many = max(ctx_n - 1, 1)
    shape = jax.ShapeDtypeStruct
    cos_table, sin_table = jnp.asarray(cos_table), jnp.asarray(sin_table)
    return pl.pallas_call(
        functools.partial(attention_kernel, (ctx_n, exp_n, wide // 4)),
        out_shape=(
            shape((pairs, tok, 128), BF),
            shape((ctx_n, pairs, tok, 128), BF),
            shape((ctx_n, pairs, tok, 128), BF),
            shape((ctx_n, tok, model), BF),
            shape((ctx_n, tok, wide), BF),
            shape((tok, 128), F32),
            shape((tok, model), BF),
            shape((tok, wide), BF),
            shape((tok, model), F32),
            shape((tok, model), BF),
            shape((tok, 128), F32),
            shape((ctx_n, 8, tok), jnp.int32),
            shape((exp_n // 2, experts, 2, tok // 4, model), BF),
            shape((8, tok), F32),
            shape((128, model), BF),
        ),
        in_specs=[pl.BlockSpec(memory_space=pltpu.SMEM), hbm]
        + [vmem] * 3
        + [hbm] * 4
        + [vmem] * 4
        + [hbm] * 3
        + [vmem],
        out_specs=(hbm,) * 4 + (vmem,) * 8 + (hbm, vmem, vmem),
        scratch_shapes=[
            pltpu.VMEM((ctx_n, tok, model), BF),
            pltpu.VMEM((ctx_n, tok, tok), BF if ctx_n > 2 else F32),
            pltpu.VMEM((exp_n - 1, experts, tok // 4, model), BF),
            pltpu.VMEM((pairs, tok, 128), F32),
            pltpu.VMEM((tok, 128), F32),
            pltpu.VMEM((tok, 128), F32),
            pltpu.VMEM((16, tok), F32),
            pltpu.VMEM((16, 128), F32),
            dma((many,)), dma((many,)), dma((many,)), dma((many,)), dma((exp_n - 1,)), dma((exp_n,)),
            pltpu.VMEM((pairs, tok, 128), BF),
            pltpu.VMEM((ctx_n, pairs, tok, 128), BF),
            pltpu.VMEM((ctx_n, pairs, tok, 128), BF),
            pltpu.VMEM((ctx_n, tok, model), BF),
            pltpu.VMEM((experts, tok // 4, model), BF),
            dma((5,)),
            pltpu.VMEM((32, model), F32),
        ]
        + stage_scratch(dy, hidden, down, up, w_qkv, cos_table, sin_table, w_out),
        compiler_params=pltpu.CompilerParams(
            collective_id=2, has_side_effects=True, vmem_limit_bytes=VLIMIT + 5 * 2**19
        ),
        name="attention_forward",
    )(
        ids, hidden, segments, prev, mix, w_qkv, w_out, down, up, *small, cos_table, sin_table, dy, routes,
    )


def put_tiles(tiles_ref, first, value):
    for col in range(value.shape[1] // 128):
        tiles_ref[first + col] = value[:, col * 128 : col * 128 + 128].astype(tiles_ref.dtype)


STAGED = 17


def backward_kernel(
    sizes, ids_ref, d_mid_hbm, q_hbm, k_hbm, v_hbm, normed_ref, rank_hbm, total_hbm, flat_hbm,
    rank_out_hbm, x_hbm, seg_hbm, router_hbm, w_qkv_hbm, w_out_hbm, down_hbm, up_hbm, cos_hbm,
    sin_hbm, *rest,
):
    ctx_n, exp_n, rank, fused = sizes
    staged, rest = rest[-STAGED - 1 :], rest[: -STAGED - 1]
    (
        d_mid_ref, up_ref, down_ref, w_out_ref, rank_out_ref, flat_ref, q_ref, k_ref, v_ref, total_ref,
        seg_all, cos_ref, sin_ref, w_qkv_ref, rank_ref, x_ref, router_ref, stage_sem,
    ) = staged
    stages = stage_copies(
        (
            d_mid_hbm, up_hbm, down_hbm, w_out_hbm, rank_out_hbm, flat_hbm, q_hbm, k_hbm, v_hbm,
            total_hbm, seg_hbm, cos_hbm, sin_hbm, w_qkv_hbm, rank_hbm, x_hbm, router_hbm,
        ),
        staged, stage_sem,
    )
    if fused:
        sums_ref, early_ref, done_ref, base_ref, cols_ref = rest[:5]
        grad_ref, table_ref, attn_table, hidden_ref, tiles_ref = rest[5:10]
        scratch, more, results_scratch = rest[10:-31], rest[-31:-5], rest[-5:]
        results = Results(exp_n, done_ref, base_ref, cols_ref, hidden_ref, results_scratch)
        sums = Sums(fused, ids_ref, sums_ref, early_ref, tiles_ref, table_ref, attn_table, more)
    else:
        grad_ref, tiles_ref = rest[:2]
        scratch = rest[2:]
    (
        recv_buf, do_ref, bias_ref, dk_acc, dv_acc, dq_all, dkv_all, send_buf, grad_up, grad_down,
        normed_buf, send_sem, recv_sem, load_sem,
    ) = scratch
    ctx = lax.axis_index("context")
    sequence = lax.axis_index("dp") * exp_n + lax.axis_index("expert")
    tok, model = x_ref.shape
    pairs, head_dim = model // 128, 64
    entered = greet([(axis, lax.axis_size(axis)) for axis in (ALL_AXES if fused else ("context",))])
    for stage in stages[:6]:
        stage.start()
    if fused:
        entered()
        sums.start()
        results.start()
    for stage in stages[6:]:
        stage.start()
    order = [ctx] + blocks_of(ctx_n, ctx, ctx_n - 1)

    def fetch(j):
        return pltpu.make_async_copy(
            normed_ref.at[order[j]], normed_buf.at[min(j, 1)], load_sem.at[min(j, 1)]
        )

    fetch(0).start()
    if ctx_n > 1:
        fetch(1).start()
    if fused:
        for e in range(sums.experts - 1):
            sums.combine(e)
    for stage in stages[:6]:
        stage.wait()
    adapter = ids_ref[sequence]
    down = down_ref[adapter]
    up = up_ref[adapter]
    wide = down.shape[0]
    column = lax.broadcasted_iota(jnp.int32, (tok, wide), 1) // rank
    d_branch = d_mid_ref[...].astype(BF)
    d_rank_out = jnp.where(column == 3, ADAPT_SCALE * nt(d_branch, up), 0.0).astype(BF)
    twice_out = jnp.where(column == 3, ADAPT_SCALE * rank_out_ref[...].astype(F32), 0.0).astype(BF)
    grad_up[...] = tn(twice_out, d_branch)
    grad_down[...] = tn(d_rank_out, flat_ref[...])

    def attn_chunk(i, carry):
        rows = pl.ds(pl.multiple_of(i * 256, 256), 256)
        d_attn = nt(d_branch, w_out_ref[rows, :]) + nn(d_rank_out, down_ref[adapter, :, rows])
        do_ref[2 * i] = d_attn[:, :128].astype(BF)
        do_ref[2 * i + 1] = d_attn[:, 128:].astype(BF)
        return carry

    lax.fori_loop(0, model // 256, attn_chunk, 0)
    for stage in stages[6:]:
        stage.wait()
    half_rows = tok // 2

    steps = {}
    if fused and sums.experts > 1:
        earlier = range(sums.experts - 1)

        def first_step():
            for e in earlier:
                sums.advance(e, 1)
            sums.exchange()

        def second_step():
            for e in earlier:
                sums.advance(e, 2)

        steps = {0: first_step, 3: second_step}

    def attend(count):
        others = blocks_of(ctx_n, ctx, count)
        for j, block in enumerate([ctx] + others):
            fill_bias(bias_ref, seg_all, ctx, tok, j, block)

        def pair(i, carry):
            cols = pl.ds(pl.multiple_of(i * 128, 128), 128)
            for half in (1, 0):
                rows = slice(half * half_rows, (half + 1) * half_rows)
                q = stack_heads(q_ref[i, rows])
                d_out = stack_heads(do_ref[i, rows])
                total = stack_columns(total_ref[rows], i)
                def terms(j, block, width, i=i, rows=rows, q=q, d_out=d_out, total=total):
                    probs = jnp.exp(
                        biased(nt(q, k_ref[block, i, 0:width]), bias_ref[j, rows, 0:width]) - total
                    )
                    return probs, nt(d_out, v_ref[block, i, 0:width])

                def use(j, block, width, probs, d_probs, delta, i=i, half=half, q=q, d_out=d_out):
                    d_scores = (probs * (d_probs - delta)).astype(BF)
                    d_key = tn(q, d_scores)
                    d_value = tn(d_out, probs.astype(BF))
                    if half == 1:
                        dk_acc[j] = d_key
                        dv_acc[j] = d_value
                    else:
                        dk_acc[j, :, 0:width] += d_key
                        dv_acc[j, :, 0:width] += d_value
                    return nn(d_scores, k_ref[block, i, 0:width])

                width = (half + 1) * half_rows
                own = terms(0, ctx, width)
                delta = jnp.sum(own[0] * own[1], -1, keepdims=True)
                if count < 2:
                    kept = [terms(j + 1, block, tok) for j, block in enumerate(others)]
                    for probs, d_probs in kept:
                        delta = delta + jnp.sum(probs * d_probs, -1, keepdims=True)
                    d_query = use(0, ctx, width, *own, delta)
                    for j, block in enumerate(others):
                        d_query = d_query + use(j + 1, block, tok, *kept[j], delta)
                else:

                    def more_delta(j, delta):
                        probs, d_probs = terms(j, lax.rem(ctx + j, ctx_n), tok)
                        return delta + jnp.sum(probs * d_probs, -1, keepdims=True)

                    delta = lax.fori_loop(1, ctx_n, more_delta, delta)

                    def more_query(j, d_query, delta=delta):
                        block = lax.rem(ctx + j, ctx_n)
                        return d_query + use(j, block, tok, *terms(j, block, tok), delta)

                    d_query = lax.fori_loop(1, ctx_n, more_query, use(0, ctx, width, *own, delta))
                start = pl.multiple_of(ctx * tok + half * half_rows, half_rows)
                d_query = join_heads(d_query) * head_dim ** (-0.5)
                dq_all[rows, cols] = turn(
                    d_query, cos_ref[pl.ds(start, half_rows)], -sin_ref[pl.ds(start, half_rows)], head_dim
                ).astype(BF)
            for j, block in enumerate([ctx] + others):
                start = pl.multiple_of(block * tok, tok)
                d_key = turn(
                    jnp.transpose(dk_acc[j]), cos_ref[pl.ds(start, tok)], -sin_ref[pl.ds(start, tok)], head_dim
                )
                dkv_all[j, 0, :, cols] = d_key.astype(BF)
                dkv_all[j, 1, :, cols] = jnp.transpose(dv_acc[j]).astype(BF)
            for turn_of, step in steps.items():
                pl.when(i == turn_of)(step)
            return carry

        lax.fori_loop(0, pairs, pair, 0)

    def fold(j, block, first, write):
        normed = normed_buf[min(j, 1)]
        ranks = rank_ref[block].astype(F32)
        d_ranks = jnp.zeros((tok, wide), F32)
        for p in range(first, 3):
            d_proj = dq_all[...] if p == 0 else dkv_all[j, p - 1]
            twice = jnp.where(column == p, ADAPT_SCALE * ranks, 0.0).astype(BF)
            grad_up[...] += tn(twice, d_proj)
            d_ranks = d_ranks + jnp.where(column == p, ADAPT_SCALE * nt(d_proj, up), 0.0)
        d_ranks = d_ranks.astype(BF)
        grad_down[...] += tn(d_ranks, normed)

        def chunk(i, carry):
            rows = pl.ds(pl.multiple_of(i * 256, 256), 256)
            value = nn(d_ranks, down_ref[adapter, :, rows])
            for p in range(first, 3):
                d_proj = dq_all[...] if p == 0 else dkv_all[j, p - 1]
                value = value + nt(d_proj, w_qkv_ref[rows, p * model : (p + 1) * model])
            write(rows, value)
            return carry

        lax.fori_loop(0, model // 256, chunk, 0)

    def write_own(cols, value):
        grad_ref[:, cols] = value

    class Share:
        def __init__(self, step):
            peer = lax.rem(ctx + step, ctx_n)
            self.halves = [
                remote(
                    send_buf.at[pl.ds(half * half_rows, half_rows)],
                    recv_buf.at[step - 1, pl.ds(half * half_rows, half_rows)],
                    send_sem.at[step - 1, half], recv_sem.at[step - 1, half], "context", peer,
                )
                for half in range(2)
            ]

        def start(self):
            self.halves[0].start()
            if not fused:
                self.halves[1].start()

        def start_rest(self):
            self.halves[1].start()

        def wait_recv(self):
            for half in self.halves:
                half.wait_recv()

        def wait_send(self):
            for half in self.halves:
                half.wait_send()

    copies = [Share(step) for step in range(1, ctx_n)]

    def share_rest():
        if ctx_n == 2:
            pl.when(ctx == 1)(copies[0].start_rest)

    if ctx_n == 1:
        attend(0)
        sums.combine(sums.experts - 1)
    elif ctx_n == 2:
        @pl.when(ctx == 0)
        def _():
            attend(0)
            sums.combine(sums.experts - 1)

    if not fused:
        entered()

    def spread():
        attend(ctx_n - 1)
        if fused:
            sums.combine(sums.experts - 1)
        for j, block in enumerate(blocks_of(ctx_n, ctx, ctx_n - 1)):
            def write(cols, value):
                send_buf[:, cols] = value.astype(BF)

            fetch(j + 1).wait()
            if j > 0:
                copies[j - 1].wait_send()
            fold(j + 1, block, 1, write)
            copies[j].start()
            if j + 2 < ctx_n:
                fetch(j + 2).start()

    if ctx_n == 2:
        pl.when(ctx == 1)(spread)
        pl.when(ctx == 0)(fetch(1).wait)
    elif ctx_n > 2:
        spread()
    fetch(0).wait()
    fold(0, ctx, 0, write_own)
    per = model // 128
    for p in range(4):
        put_tiles(tiles_ref, p * per, grad_down[p * rank : (p + 1) * rank])
        put_tiles(tiles_ref, (4 + p) * per, grad_up[p * rank : (p + 1) * rank])

    def settle():
        take_shares()
        lax.fori_loop(0, tok // 128, finish, 0)

    def take_shares():
        if ctx_n == 2:
            pl.when(ctx == 0)(copies[0].wait_recv)

            @pl.when(ctx == 1)
            def _():
                recv_buf[...] = jnp.zeros_like(recv_buf)

        elif ctx_n > 2:
            copies[-1].wait_send()
            for step, item in enumerate(copies):
                item.wait_recv()
                load = pltpu.make_async_copy(recv_buf.at[step], send_buf, load_sem.at[0])
                load.start()
                load.wait()
                grad_ref[...] += send_buf[...].astype(F32)

    gain_one = router_ref[16:17].astype(F32)

    def finish(i, carry):
        rows = pl.ds(pl.multiple_of(i * 128, 128), 128)
        value = grad_ref[rows]
        if ctx_n == 2:
            value = value + recv_buf[0, rows].astype(F32)
        x = x_ref[rows].astype(F32)
        inv = lax.rsqrt(jnp.mean(x * x, -1, keepdims=True) + EPSILON)
        scaled = value * gain_one
        grad_ref[rows] = (
            d_mid_ref[rows]
            + inv * scaled
            - x * (inv * inv * inv) * jnp.mean(scaled * x, -1, keepdims=True)
        )
        return carry

    if fused:
        last = sums.experts - 1

        for e in range(last):
            for s in range(3, sums.dp_n):
                sums.advance(e, s)
        sums.take(last, 1)

        def rest():
            share_rest()
            sums.hand(last, 2)

        def end():
            for s in range(3, sums.dp_n):
                sums.advance(last, s)
            settle()

        sums.tail(
            {
                "sources": results.combine,
                "context": functools.partial(sums.hand, last, 1),
                "dp_back": functools.partial(sums.take, last, 2),
                "context_back": rest,
                "last": end,
            }
        )
        sums.finish()
        results.finish()
    else:
        settle()
    if ctx_n == 2:
        pl.when(ctx == 1)(copies[0].wait_send)


def attention_backward(d_mid, saved, hidden, ids, router, w_qkv, w_out, down, up, expert_sums, done, experts, width):
    ctx_n, exp_n = lax.axis_size("context"), lax.axis_size("expert")
    tok, model = hidden.shape
    pairs = model // 128
    wide = down.shape[1]
    cos_table, sin_table = rope_tables(ctx_n * tok, 64)
    vmem = pl.BlockSpec(memory_space=pltpu.VMEM)
    dma = pltpu.SemaphoreType.DMA
    many = max(ctx_n - 1, 1)
    shape = jax.ShapeDtypeStruct
    q, k, v, normed, ranks, totals, flat, rank_out, seg_all = saved
    cos_table, sin_table = jnp.asarray(cos_table), jnp.asarray(sin_table)
    staged = (
        d_mid, up, down, w_out, rank_out, flat, q, k, v, totals, seg_all, cos_table, sin_table, w_qkv,
        ranks, hidden, router,
    )
    hbm = pl.BlockSpec(memory_space=pl.ANY)
    spill = ctx_n > 2
    landing = ((many, tok, model), BF)
    attn_tiles, adapters = 8 * pairs, down.shape[0]
    sums_outs, sums_scratch = sums_shapes(experts, model, width, attn_tiles, adapters)
    fused = None
    if not spill:
        fused = tuple(lax.axis_size(axis) for axis in ALL_AXES) + (adapters, attn_tiles)
    tiles_shape = ((attn_tiles, 16, 128), BF)
    results = pl.pallas_call(
        functools.partial(backward_kernel, (ctx_n, exp_n, wide // 4, fused)),
        out_shape=(shape((tok, model), F32),)
        + ((shape(*tiles_shape), shape(*landing)) if spill else sums_outs + (shape((tok, model), BF),)),
        in_specs=[pl.BlockSpec(memory_space=pltpu.SMEM)] + [hbm] * 18 + ([] if spill else [hbm] * 4 + [vmem]),
        out_specs=(vmem, vmem) + ((pl.BlockSpec(memory_space=pl.ANY),) if spill else (vmem, vmem)),
        scratch_shapes=([] if spill else [pltpu.VMEM(*tiles_shape), pltpu.VMEM(*landing)])
        + [
            pltpu.VMEM((pairs, tok, 128), BF),
            pltpu.VMEM((ctx_n, tok, tok), BF if spill else F32),
            pltpu.VMEM((ctx_n, 128, tok), F32),
            pltpu.VMEM((ctx_n, 128, tok), F32),
            pltpu.VMEM((tok, model), BF),
            pltpu.VMEM((ctx_n, 2, tok, model), BF),
            pltpu.VMEM((tok, model), BF),
            pltpu.VMEM((wide, model), F32),
            pltpu.VMEM((wide, model), F32),
            pltpu.VMEM((min(ctx_n, 2), tok, model), BF),
            dma((many, 2)), dma((many, 2)), dma((2,)),
        ]
        + ([] if spill else sums_scratch + results_shapes(exp_n, done[0]))
        + stage_scratch(*staged),
        compiler_params=pltpu.CompilerParams(
            collective_id=3, has_side_effects=True, vmem_limit_bytes=VLIMIT + 5 * 2**19
        ),
        name="attention_backward",
    )(
        ids, d_mid, q, k, v, normed, ranks, totals, flat, rank_out, hidden, seg_all,
        router, w_qkv, w_out, down, up, cos_table, sin_table, *([] if spill else [*expert_sums, *done]),
    )
    if spill:
        sums = add_up(ids, expert_sums, results[1], experts, width, adapters)
        return (results[0],) + tuple(sums) + (return_results(done),)
    return results


def partners(exp_n, me):
    core = lax.rem(me, 2)
    twin = me + 1 - 2 * core
    far = []
    for step in range(2, exp_n, 2):
        far += [lax.rem(me + step, exp_n), lax.rem(twin + step, exp_n)]
    return far + [twin]


def hot_rows(slot_rows, first, count):
    target = first + lax.broadcasted_iota(jnp.int32, (count, slot_rows.shape[1]), 0)
    return target == slot_rows


def moe_kernel(
    sizes, ids_ref, rows_ref, mid_hbm, logits_ref, slots_ref, dy_hbm, arrived_hbm, router_ref, mix_ref,
    vec_ref, gate_up_hbm, down_hbm, in_down_hbm, in_up_hbm, out_down_hbm, out_up_hbm,
    base_ref, d_mid_ref, grad_prev_ref, sums_ref, early_ref, done_out, cols_ref, part_z,
    d_logits_ref, mix_pad, done_gate, back_gate, tiles_ref, arrived_x, gate_up_ref, w_down_ref, sent_rows, sent_gates, arrived_rows, arrived_gates, act_ref, d_pre_ref,
    done_rows, back_rows, gates_ref,
    weight_sem, row_send, row_recv, gate_send, gate_recv, out_send, out_recv, in_send, in_recv,
    x_send, x_recv, z_send, z_recv, *staged,
):
    in_down_ref, in_up_ref, out_down_ref, out_up_ref, arrived_dy, mid_ref, dy_ref, stage_sem = staged
    stages = stage_copies(
        (in_down_hbm, in_up_hbm, out_down_hbm, out_up_hbm, arrived_hbm, mid_hbm, dy_hbm), staged, stage_sem
    )
    ctx_n, dp_n, exp_n, kinds, rank, share = sizes
    ctx, dp = lax.axis_index("context"), lax.axis_index("dp")
    me = lax.axis_index("expert")
    my_chip, my_core = me // 2, lax.rem(me, 2)
    first_seq = lax.axis_index("dp") * exp_n
    tok, model = rows_ref.shape
    experts, width = w_down_ref.shape[:2]
    capacity = arrived_rows.shape[3]
    per_owner = experts * capacity
    both = 2 * capacity
    entered = greet([("expert", exp_n), ("context", ctx_n), ("dp", dp_n)])
    loads = []
    for e in range(experts):
        for hbm, ref, k in ((gate_up_hbm, gate_up_ref, 0), (down_hbm, w_down_ref, 1)):
            load = pltpu.make_async_copy(hbm.at[e], ref.at[e], weight_sem.at[e, k])
            load.start()
            loads.append(load)
        if e == 0:
            for stage in stages:
                stage.start()

    lane = lax.broadcasted_iota(jnp.int32, (tok, 128), 1)
    logits = logits_ref[...]
    masked = jnp.where(lane < kinds, logits, NEG)
    exps = jnp.exp(masked - jnp.max(masked, -1, keepdims=True))
    probs = exps / jnp.sum(exps, -1, keepdims=True)
    slot_cols = jnp.transpose(
        jnp.concatenate([slots_ref[...], jnp.zeros((120, tok), F32)], 0)
    )
    gates = [
        jnp.sum(jnp.where(lane == slot_cols[:, k : k + 1].astype(jnp.int32), probs, 0.0), -1, keepdims=True)
        for k in range(2)
    ]
    gates_ref[...] = jnp.where(lane == 0, gates[0], jnp.where(lane == 1, gates[1], 0.0))
    cols_ref[...] = jnp.where(lane == 4, gates[0], jnp.where(lane == 5, gates[1], slot_cols))
    gate_rows = jnp.transpose(gates_ref[...])
    parts = []
    sub = lax.broadcasted_iota(jnp.int32, (16, tok), 0)
    for k in range(2):
        whole = jnp.broadcast_to(gate_rows[k : k + 1], (16, tok))
        high = whole.astype(BF).astype(F32)
        middle = (whole - high).astype(BF).astype(F32)
        lowest = whole - high - middle
        parts.append(
            jnp.where(sub == 0, high, jnp.where(sub == 1, middle, jnp.where(sub == 2, lowest, 0.0))).astype(BF)
        )
    slot_rows = [slots_ref[2 + k : 3 + k].astype(jnp.int32) for k in range(2)]

    def pick(owner, e):
        hots = [hot_rows(slot_rows[k], owner * per_owner + e * capacity, capacity) for k in range(2)]
        hot = jnp.where(hots[0] | hots[1], 1.0, 0.0).astype(BF)
        gates = sum(nt(parts[k], jnp.where(hots[k], 1.0, 0.0).astype(BF)) for k in range(2))
        return gates.astype(BF), nn(hot, rows_ref[...]).astype(BF)

    entered()
    sends = []
    others = partners(exp_n, me)
    for e in range(experts):
        for i, peer in enumerate(others):
            sent_gates[i, e], sent_rows[i, e] = pick(peer, e)
            for src, dst, send, recv in (
                (sent_gates, arrived_gates, gate_send, gate_recv),
                (sent_rows, arrived_rows, row_send, row_recv),
            ):
                copy = remote(
                    src.at[i, e], dst.at[my_chip, e, my_core], send.at[i, e], recv.at[me, e], "expert", peer
                )
                copy.start()
                sends.append(copy)
        arrived_gates[my_chip, e, my_core], arrived_rows[my_chip, e, my_core] = pick(me, e)

    def arrive(source, e):
        for ref, src, send, recv in (
            (arrived_gates, sent_gates, gate_send, gate_recv),
            (arrived_rows, sent_rows, row_send, row_recv),
        ):
            remote(
                src.at[0, e], ref.at[source // 2, e, lax.rem(source, 2)], send.at[0, e], recv.at[source, e],
                "expert", source,
            ).wait_recv()

    row64 = lax.broadcasted_iota(jnp.int32, (both, 4 * rank), 0) // capacity
    col64 = lax.broadcasted_iota(jnp.int32, (both, 4 * rank), 1)
    mine64 = row64 == col64 // (2 * rank)
    is_gate = col64 % (2 * rank) < rank
    mine32 = lax.broadcasted_iota(jnp.int32, (both, 2 * rank), 0) // capacity == (
        lax.broadcasted_iota(jnp.int32, (both, 2 * rank), 1) // rank
    )
    step_cols = 1024
    per_step = step_cols // 128
    across, deep = model // 128, width // 128
    first_up = 2 * across
    first_out = first_up + 2 * deep
    first_last = first_out + deep

    def put(source, e, tile, value):
        tiles_ref[source, tile // share, e * share + tile % share] = value

    def x_copies(chip, e):
        copies = []
        for step in range(1, ctx_n):
            peer = lax.rem(ctx + step, ctx_n)
            here = pl.ds(e * share, share)
            copies.append(
                remote(
                    tiles_ref.at[pl.ds(2 * chip, 2), peer, here],
                    arrived_x.at[step - 1, pl.ds(2 * chip, 2), here],
                    x_send.at[step - 1, chip, e], x_recv.at[step - 1, chip, e], "context", peer,
                )
            )
        return copies

    def work(chip, e):
        names = [ids_ref[first_seq + 2 * chip + core] for core in range(2)]

        def stack(ref, cols=slice(None)):
            return jnp.concatenate([ref[name, e, :, cols] for name in names], 0)

        rows = arrived_rows[chip, e].reshape(both, model)
        in_down = stack(in_down_ref)
        out_up = stack(out_up_ref)
        gate = []
        for core in range(2):
            piece = arrived_gates[chip, e, core].astype(F32)
            total = piece[0:1] + piece[1:2] + piece[2:3]
            gate.append(jnp.transpose(jnp.broadcast_to(total, (128, capacity)))[:, 0:1])
        gate = jnp.concatenate(gate, 0)
        d_out = (gate * arrived_dy[chip, e].reshape(both, model).astype(F32)).astype(BF)
        ranks = jnp.where(mine64, nt(rows, in_down), 0.0).astype(BF)
        twice = ADAPT_SCALE * ranks.astype(F32)
        twice_gate = jnp.where(is_gate, twice, 0.0).astype(BF)
        twice_up = jnp.where(is_gate, 0.0, twice).astype(BF)
        d_mid_rank = jnp.where(mine32, ADAPT_SCALE * nt(d_out, out_up), 0.0).astype(BF)

        def chunk(i, carry):
            rank_mid, d_rank = carry
            start = pl.multiple_of(i * step_cols, step_cols)
            cols = pl.ds(start, step_cols)
            up_cols = pl.ds(pl.multiple_of(width + i * step_cols, step_cols), step_cols)
            in_up = stack(in_up_ref, cols)
            out_down = stack(out_down_ref, cols)
            gate_pre = nn(rows, gate_up_ref[e, :, cols]) + nn(twice_gate, in_up)
            up_pre = nn(rows, gate_up_ref[e, :, up_cols]) + nn(twice_up, in_up)
            d_act = (nt(d_out, w_down_ref[e, cols, :]) + nn(d_mid_rank, out_down)).astype(BF).astype(F32)
            sigma = 1.0 / (1.0 + jnp.exp(-gate_pre))
            silu = gate_pre * sigma
            act = (silu * up_pre).astype(BF)
            d_gate = (d_act * up_pre * sigma * (1.0 + gate_pre * (1.0 - sigma))).astype(BF)
            d_up = (d_act * silu).astype(BF)
            act_ref[:, cols] = act
            d_pre_ref[:, cols] = d_gate
            d_pre_ref[:, up_cols] = d_up
            rank_mid = rank_mid + nt(act, out_down)
            d_rank = d_rank + jnp.where(is_gate, nt(d_gate, in_up), nt(d_up, in_up))
            grad_up = (tn(twice_gate, d_gate) + tn(twice_up, d_up)).astype(BF)
            grad_out = tn(d_mid_rank, act).astype(BF)
            for core in range(2):
                for t in range(per_step):
                    here = slice(t * 128, t * 128 + 128)
                    tile = i * per_step + t
                    for which in range(2):
                        first = (2 * core + which) * rank
                        put(
                            2 * chip + core, e, first_up + which * deep + tile,
                            grad_up[first : first + rank, here],
                        )
                    put(
                        2 * chip + core, e, first_out + tile,
                        grad_out[core * rank : (core + 1) * rank, here],
                    )
            return rank_mid, d_rank

        rank_mid, d_rank = lax.fori_loop(
            0, width // step_cols, chunk,
            (jnp.zeros((both, 2 * rank), F32), jnp.zeros((both, 4 * rank), F32)),
        )
        twice_mid = jnp.where(
            mine32, ADAPT_SCALE * rank_mid.astype(BF).astype(F32), 0.0
        ).astype(BF)

        d_rank_in = jnp.where(mine64, ADAPT_SCALE * d_rank, 0.0).astype(BF)
        grad_last = tn(twice_mid, d_out).astype(BF)
        grad_first = tn(d_rank_in, rows).astype(BF)
        for core in range(2):
            for t in range(across):
                here = slice(t * 128, t * 128 + 128)
                for which in range(2):
                    first = (2 * core + which) * rank
                    put(
                        2 * chip + core, e, which * across + t, grad_first[first : first + rank, here]
                    )
                put(
                    2 * chip + core, e, first_last + t,
                    grad_last[core * rank : (core + 1) * rank, here],
                )
        for copy in x_copies(chip, e):
            copy.start()

        def out_chunk(i, carry):
            cols = pl.ds(pl.multiple_of(i * 256, 256), 256)
            value = nn(act_ref[...], w_down_ref[e, :, cols]) + nn(twice_mid, stack(out_up_ref, cols))
            for core in range(2):
                done_out[chip, e, core, :, cols] = value[core * capacity : (core + 1) * capacity].astype(BF)
            return carry

        lax.fori_loop(0, model // 256, out_chunk, 0)
        for core in range(2):
            d_gate = jnp.sum(
                arrived_dy[chip, e, core].astype(F32) * done_out[chip, e, core].astype(F32), -1, keepdims=True
            )
            done_gate[chip, e, core] = jnp.transpose(jnp.broadcast_to(d_gate, (capacity, 128)))[0:8]
        give_back(chip, e, done_gate, back_gate, out_send, out_recv)

        def in_chunk(i, carry):
            cols = pl.ds(pl.multiple_of(i * 256, 256), 256)
            value = nt(d_pre_ref[...], gate_up_ref[e, cols, :]) + nn(d_rank_in, stack(in_down_ref, cols))
            for core in range(2):
                done_rows[chip, e, core, :, cols] = value[core * capacity : (core + 1) * capacity].astype(BF)
            return carry

        lax.fori_loop(0, model // 256, in_chunk, 0)
        give_back(chip, e, done_rows, back_rows, in_send, in_recv)

    def give_back(chip, e, done, back, send, recv):
        for core in range(2):
            target = 2 * chip + core
            copy = remote(
                done.at[chip, e, core], back.at[me * experts + e], send.at[target, e], recv.at[me, e],
                "expert", target,
            )

            @pl.when(target == me)
            def _(core=core):
                back[me * experts + e] = done[chip, e, core]

            @pl.when(target != me)
            def _(copy=copy):
                copy.start()

    def own_work(e):
        arrive(others[-1], e)
        work(my_chip, e)

    def gather(e, out_ref):
        for chip in range(exp_n // 2):
            for copy in x_copies(chip, e):
                copy.wait_recv()

        def add(tile, carry):
            here = pl.ds(e * share + tile, 1)
            total = tiles_ref[:, ctx, here].astype(F32)
            for step in range(1, ctx_n):
                total = total + arrived_x[step - 1, :, here].astype(F32)
            out_ref[:, pl.ds(tile, 1)] = total.astype(BF)
            return carry

        lax.fori_loop(0, share, add, 0)

    z_tiles = early_ref.shape[3]
    z_copies = []
    for load in loads[:2]:
        load.wait()
    for stage in stages[:5]:
        stage.wait()
    own_work(0)
    for e in range(experts):
        if e > 0:
            for load in loads[2 * e : 2 * e + 2]:
                load.wait()
        for step in range(1, exp_n // 2):
            arrive(others[2 * step - 2], e)
            arrive(others[2 * step - 1], e)
            work(lax.rem(my_chip + step, exp_n // 2), e)
    for e in range(experts - 1):
        if e > 0:
            own_work(e)
        gather(e, part_z.at[e])
        early_ref[e, 0] = part_z[e, :, pl.ds(dp * z_tiles, z_tiles)]
        for k in range(1, dp_n):
            peer = lax.rem(dp + k, dp_n)
            copy = remote(
                part_z.at[e, :, pl.ds(peer * z_tiles, z_tiles)], early_ref.at[e, k], z_send.at[e, k], z_recv.at[e, k],
                "dp", peer,
            )
            copy.start()
            z_copies.append(copy)

    if experts > 1:
        own_work(experts - 1)
    for stage in stages[5:]:
        stage.wait()

    def collect(done, back, send, recv):
        for owner in others:
            for e in range(experts):
                remote(
                    done.at[0, e, 0], back.at[owner * experts + e], send.at[owner, e], recv.at[owner, e],
                    "expert", owner,
                ).wait_recv()

    slots_total = exp_n * per_owner
    block = 256

    def hot_cols(rows):
        target = lax.broadcasted_iota(jnp.int32, (block, slots_total), 1)
        return [target == cols_ref[rows, 2 + k : 3 + k].astype(jnp.int32) for k in range(2)]

    gain = router_ref[17:18].astype(F32)
    lanes = lax.broadcasted_iota(jnp.int32, (block, 128), 1)
    ffn_kinds = exp_n * experts

    def outward(i, carry):
        rows = pl.ds(pl.multiple_of(i * block, block), block)
        hots = hot_cols(rows)
        mid = mid_ref[rows]
        dy = dy_ref[rows].astype(F32)
        normed = mid * lax.rsqrt(jnp.mean(mid * mid, -1, keepdims=True) + EPSILON) * gain
        logits = logits_ref[rows]
        masked = jnp.where(lanes < kinds, logits, NEG)
        exps = jnp.exp(masked - jnp.max(masked, -1, keepdims=True))
        probs = exps / jnp.sum(exps, -1, keepdims=True)
        pairs = []
        for c in range(2):
            one, two = logits[:, kinds + 2 * c : kinds + 2 * c + 1], logits[:, kinds + 2 * c + 1 : kinds + 2 * c + 2]
            pairs.append((1.0 / (1.0 + jnp.exp(two - one)), 1.0 / (1.0 + jnp.exp(one - two))))
        along = jnp.sum(dy * normed, -1, keepdims=True)
        across_vec = [jnp.sum(dy * vec_ref[c : c + 1].astype(F32), -1, keepdims=True) for c in range(2)]
        d_kinds = jnp.zeros((block, 128), F32)
        dy_scale = jnp.zeros((block, 1), F32)
        weights = [jnp.zeros((block, 1), F32)] * 2
        for k in range(2):
            kind = cols_ref[rows, k : k + 1].astype(jnp.int32)
            gate = gates_ref[rows, k : k + 1]
            scale = jnp.where(kind == ffn_kinds + 1, 1.0, 0.0)
            picked = jnp.zeros((block, 128), F32)
            for owner in range(exp_n * experts):
                hot = hots[k][:, owner * capacity : (owner + 1) * capacity]
                picked = picked + jnp.where(hot, back_gate[owner, 0:1], 0.0)
            d_gate = jnp.sum(picked, -1, keepdims=True)
            for c in range(2):
                here = jnp.where(kind == ffn_kinds + 2 + c, 1.0, 0.0)
                scale = scale + here * pairs[c][0]
                d_gate = d_gate + here * pairs[c][1] * across_vec[c]
                weights[c] = weights[c] + here * gate
            d_gate = d_gate + scale * along
            dy_scale = dy_scale + gate * scale
            d_kinds = d_kinds + jnp.where(lanes == kind, d_gate, 0.0)
        base = mid + dy_scale * normed
        for c in range(2):
            base = base + (weights[c] * pairs[c][1]) * vec_ref[c : c + 1].astype(F32)
        base_ref[rows] = base
        d_logits = probs * (d_kinds - jnp.sum(probs * d_kinds, -1, keepdims=True))
        for c in range(2):
            d_one = weights[c] * along
            d_two = weights[c] * across_vec[c]
            mean = pairs[c][0] * d_one + pairs[c][1] * d_two
            d_logits = jnp.where(lanes == kinds + 2 * c, pairs[c][0] * (d_one - mean), d_logits)
            d_logits = jnp.where(lanes == kinds + 2 * c + 1, pairs[c][1] * (d_two - mean), d_logits)
        d_logits_ref[rows] = d_logits
        high = d_logits.astype(BF)
        rest = d_logits - high.astype(F32)
        middle = rest.astype(BF)
        lowest = (rest - middle.astype(F32)).astype(BF)
        router = router_ref[...]
        d_mid_ref[rows] = dy_scale * dy + (nn(high, router) + nn(middle, router) + nn(lowest, router))
        return carry

    def inward(i, carry):
        rows = pl.ds(pl.multiple_of(i * block, block), block)
        hots = hot_cols(rows)
        table = back_rows[...].reshape(slots_total, model)
        hot = jnp.where(hots[0] | hots[1], 1.0, 0.0).astype(BF)
        scaled = (d_mid_ref[rows] + nn(hot, table)) * gain
        mid = mid_ref[rows]
        inv = lax.rsqrt(jnp.mean(mid * mid, -1, keepdims=True) + EPSILON)
        d_mid_ref[rows] = (
            dy_ref[rows].astype(F32)
            + inv * scaled
            - mid * (inv * inv * inv) * jnp.mean(scaled * mid, -1, keepdims=True)
        )
        return carry

    collect(done_gate, back_gate, out_send, out_recv)
    lax.fori_loop(0, tok // block, outward, 0)
    mix_pad[...] = jnp.zeros_like(mix_pad)
    mix_pad[0:kinds, 0:kinds] = mix_ref[...]
    grad_prev = lax.dot_general(
        mix_pad[...], d_logits_ref[...], (((1,), (1,)), ((), ())), precision=HIGH, preferred_element_type=F32
    )
    for kind in range(kinds):
        grad_prev_ref[kind] = grad_prev[kind : kind + 1]
    collect(done_rows, back_rows, in_send, in_recv)
    lax.fori_loop(0, tok // block, inward, 0)
    gather(experts - 1, sums_ref)
    for chip in range(exp_n // 2):
        for e in range(experts):
            for copy in x_copies(chip, e):
                copy.wait_send()
    for copy in z_copies:
        copy.wait()
    for copy in sends:
        copy.wait_send()
    for target in others:
        for e in range(experts):
            for done, back, send, recv in (
                (done_gate, back_gate, out_send, out_recv),
                (done_rows, back_rows, in_send, in_recv),
            ):
                remote(
                    done.at[0, e, 0], back.at[0], send.at[target, e], recv.at[target, e],
                    "expert", target,
                ).wait_send()


def expert_tiling(experts, model, width):
    share = pl.cdiv(3 * (model + width) // 128, lax.axis_size("context"))
    z_tiles = pl.cdiv(share, lax.axis_size("dp"))
    return share, z_tiles * lax.axis_size("dp"), z_tiles


def attn_tiling(attn_tiles):
    own = attn_tiles // lax.axis_size("expert")
    x_tiles = pl.cdiv(own, lax.axis_size("context"))
    return own, x_tiles, pl.cdiv(x_tiles, lax.axis_size("dp"))


def expert_layer(rows, mid, logits, slots, dy, arrived_dy, ids, router, mix, vec, w_gate_up, w_down, tables):
    exp_n = lax.axis_size("expert")
    tok, model = rows.shape
    experts, width = w_down.shape[:2]
    capacity = tok // 4
    rank = tables[3].shape[2]
    ctx_n = lax.axis_size("context")
    dp_n = lax.axis_size("dp")
    share, x_tiles, z_tiles = expert_tiling(experts, model, width)
    many, before = max(ctx_n - 1, 1), max(experts - 1, 1)
    chips = exp_n // 2
    vmem = pl.BlockSpec(memory_space=pltpu.VMEM)
    hbm = pl.BlockSpec(memory_space=pl.ANY)
    dma = pltpu.SemaphoreType.DMA
    shape = jax.ShapeDtypeStruct
    block = (experts, capacity, model)
    kinds = mix.shape[0]
    return pl.pallas_call(
        functools.partial(moe_kernel, (ctx_n, dp_n, exp_n, kinds, rank, share)),
        out_shape=(
            shape((tok, model), F32),
            shape((tok, model), F32),
            shape((kinds, 1, tok), F32),
            shape((exp_n, x_tiles, 16, 128), BF),
            shape((before, dp_n, exp_n, z_tiles, 16, 128), BF),
            shape((chips, experts, 2, capacity, model), BF),
            shape((tok, 128), F32),
        ),
        in_specs=[pl.BlockSpec(memory_space=pltpu.SMEM), vmem, hbm, vmem, vmem, hbm, hbm]
        + [vmem] * 3
        + [hbm] * 6,
        out_specs=(vmem,) * 7,
        scratch_shapes=[
            pltpu.VMEM((before, exp_n, x_tiles, 16, 128), BF),
            pltpu.VMEM((tok, 128), F32),
            pltpu.VMEM((16, 128), F32),
            pltpu.VMEM((chips, experts, 2, 8, 128), F32),
            pltpu.VMEM((exp_n * experts, 8, 128), F32),
            pltpu.VMEM((exp_n, ctx_n, experts * share, 16, 128), BF),
            pltpu.VMEM((many, exp_n, experts * share, 16, 128), BF),
            pltpu.VMEM((experts, model, 2 * width), BF),
            pltpu.VMEM((experts, width, model), BF),
            pltpu.VMEM((exp_n - 1,) + block, BF),
            pltpu.VMEM((exp_n - 1, experts, 16, capacity), BF),
            pltpu.VMEM((chips, experts, 2, capacity, model), BF),
            pltpu.VMEM((chips, experts, 2, 16, capacity), BF),
            pltpu.VMEM((2 * capacity, width), BF),
            pltpu.VMEM((2 * capacity, 2 * width), BF),
            pltpu.VMEM((chips, experts, 2, capacity, model), BF),
            pltpu.VMEM((exp_n * experts, capacity, model), BF),
            pltpu.VMEM((tok, 128), F32),
            dma((experts, 2)), dma((exp_n - 1, experts)), dma((exp_n, experts)), dma((exp_n - 1, experts)),
            dma((exp_n, experts)),
            dma((exp_n, experts)), dma((exp_n, experts)), dma((exp_n, experts)), dma((exp_n, experts)),
            dma((many, chips, experts)), dma((many, chips, experts)), dma((before, dp_n)), dma((before, dp_n)),
        ]
        + stage_scratch(*tables, arrived_dy, mid, dy),
        compiler_params=pltpu.CompilerParams(
            collective_id=4, has_side_effects=True, vmem_limit_bytes=VLIMIT
        ),
        name="expert_layer",
    )(
        ids, rows, mid, logits, slots, dy, arrived_dy, router, mix, vec, w_gate_up,
        w_down, *tables,
    )


def stage_copies(sources, targets, sem):
    return [
        pltpu.make_async_copy(src, dst, sem.at[i]) for i, (src, dst) in enumerate(zip(sources, targets))
    ]


def stage_scratch(*arrays):
    return [pltpu.VMEM(array.shape, array.dtype) for array in arrays] + [
        pltpu.SemaphoreType.DMA((len(arrays),))
    ]


class Results:
    def __init__(self, exp_n, done_ref, base_ref, cols_ref, hidden_ref, scratch):
        self.done_ref, self.base_ref, self.cols_ref, self.hidden_ref = done_ref, base_ref, cols_ref, hidden_ref
        self.back_ref, self.base_buf, self.send_sem, self.recv_sem, own_sem = scratch
        self.me = lax.axis_index("expert")
        self.experts = done_ref.shape[1]
        self.others = partners(exp_n, self.me)
        self.own = [
            pltpu.make_async_copy(
                done_ref.at[self.me // 2, e, lax.rem(self.me, 2)], self.back_ref.at[self.me * self.experts + e],
                own_sem.at[e],
            )
            for e in range(self.experts)
        ] + [pltpu.make_async_copy(base_ref, self.base_buf, own_sem.at[self.experts])]

    def copy(self, other, e, owner):
        return remote(
            self.done_ref.at[other // 2, e, lax.rem(other, 2)], self.back_ref.at[owner * self.experts + e],
            self.send_sem.at[other, e], self.recv_sem.at[owner, e], "expert", other,
        )

    def start(self):
        for other in self.others:
            for e in range(self.experts):
                self.copy(other, e, self.me).start()
        for copy in self.own:
            copy.start()

    def combine(self):
        for copy in self.own:
            copy.wait()
        for other in self.others:
            for e in range(self.experts):
                self.copy(other, e, other).wait_recv()
        tok, model = self.base_ref.shape
        slots = self.back_ref.shape[0] * self.back_ref.shape[1]
        block = 256

        def rows_out(i, carry):
            rows = pl.ds(pl.multiple_of(i * block, block), block)
            table = self.back_ref[...].reshape(slots, model)
            target = lax.broadcasted_iota(jnp.int32, (block, slots), 1)
            total = self.base_buf[rows]
            for k in range(2):
                slot = self.cols_ref[rows, 2 + k : 3 + k].astype(jnp.int32)
                gate = self.cols_ref[rows, 4 + k : 5 + k]
                total = total + gate * nn(jnp.where(target == slot, 1.0, 0.0).astype(BF), table)
            self.hidden_ref[rows] = total.astype(BF)
            return carry

        lax.fori_loop(0, tok // block, rows_out, 0)

    def finish(self):
        for other in self.others:
            for e in range(self.experts):
                self.copy(other, e, self.me).wait_send()


def results_shapes(exp_n, done):
    _, experts, _, capacity, model = done.shape
    dma = pltpu.SemaphoreType.DMA
    return [
        pltpu.VMEM((exp_n * experts, capacity, model), BF), pltpu.VMEM((4 * capacity, model), F32),
        dma((exp_n, experts)), dma((exp_n, experts)), dma((experts + 1,)),
    ]


def results_kernel(exp_n, done_ref, base_ref, cols_ref, hidden_ref, *scratch):
    greet([("expert", exp_n)])()
    results = Results(exp_n, done_ref, base_ref, cols_ref, hidden_ref, scratch)
    results.start()
    results.combine()
    results.finish()


def return_results(done):
    exp_n = lax.axis_size("expert")
    vmem = pl.BlockSpec(memory_space=pltpu.VMEM)
    return pl.pallas_call(
        functools.partial(results_kernel, exp_n),
        out_shape=jax.ShapeDtypeStruct(done[1].shape, BF),
        in_specs=[pl.BlockSpec(memory_space=pl.ANY)] * 2 + [vmem],
        out_specs=vmem,
        scratch_shapes=results_shapes(exp_n, done[0]),
        compiler_params=pltpu.CompilerParams(
            collective_id=5, has_side_effects=True, vmem_limit_bytes=VLIMIT
        ),
        name="return_results",
    )(*done)


class Sums:
    def __init__(self, sizes, ids_ref, sums_ref, early_ref, attn_ref, table_ref, attn_table, scratch):
        self.ctx_n, self.dp_n, self.exp_n, self.adapters, self.attn_tiles = sizes
        self.ids_ref, self.attn_ref = ids_ref, attn_ref
        self.table_ref, self.attn_table = table_ref, attn_table
        self.ctx, self.dp, self.exp = (lax.axis_index(axis) for axis in ALL_AXES)
        (
            self.arrived_z, self.early, self.held_a, self.arrived_xa, self.part_a, self.arrived_za,
            self.z_send, self.z_recv, self.az_send, self.az_recv, self.ax_send, self.ax_recv,
            self.r_send, self.r_recv, self.xa_send, self.xa_recv, self.za_send, self.za_recv,
            self.bz_send, self.bz_recv, self.bx_send, self.bx_recv, self.be_send, self.be_recv,
            self.keep_sem, load_sem,
        ) = scratch
        self.waits = []
        z_tiles = self.arrived_z.shape[2]
        self.experts = table_ref.shape[2]
        self.loads = [
            pltpu.make_async_copy(early_ref, self.early, load_sem.at[0]),
            pltpu.make_async_copy(
                sums_ref.at[:, pl.ds(self.dp * z_tiles, z_tiles)], self.arrived_z.at[0], load_sem.at[1]
            ),
        ]
        self.z_copies = [
            self.plan(
                sums_ref.at[:, pl.ds(self.peer("dp", k) * z_tiles, z_tiles)], self.arrived_z.at[k],
                self.z_send.at[k - 1], self.z_recv.at[k - 1], "dp", self.peer("dp", k),
            )
            for k in range(1, self.dp_n)
        ]
        self.lines, self.ax_copies = [], []
        for e in range(self.experts):
            self.lines.append([self.line(e, s) for s in range(1, self.dp_n)])
            self.ax_copies.append([self.across(e, origin) for origin in range(self.dp_n)])

    def slot(self, e, origin):
        return self.table_ref.at[self.ctx, lax.rem(origin + self.dp_n, self.dp_n), e]

    def line(self, e, s):
        ways = []
        for way, sign in enumerate((1, -1)):
            mine, landing = self.slot(e, self.dp - sign * (s - 1)), self.slot(e, self.dp - sign * s)
            target = lax.rem(self.dp + sign + self.dp_n, self.dp_n)
            send_sem, recv_sem = self.az_send.at[e, way, s - 1], self.az_recv.at[e, way, s - 1]
            edge, origin, source = self.dp + sign, self.dp - sign * (s - 1), self.dp - sign * s
            ways.append(
                (
                    remote(mine, mine, send_sem, recv_sem, "dp", target),
                    (edge >= 0) & (edge < self.dp_n) & (origin >= 0) & (origin < self.dp_n),
                    remote(landing, landing, send_sem, recv_sem, "dp", target),
                    (source >= 0) & (source < self.dp_n),
                )
            )
        return ways

    def across(self, e, origin):
        here = self.slot(e, origin)
        at = lax.rem(origin + self.dp_n, self.dp_n)
        return [
            remote(
                here, here, self.ax_send.at[step - 1, e, at], self.ax_recv.at[step - 1, e, at], "context",
                self.peer("context", step),
            )
            for step in range(1, self.ctx_n)
        ]

    def plan(self, src, dst, send, recv, axis, target):
        copy = remote(src, dst, send, recv, axis, target)
        self.waits.append(copy)
        return copy

    def peer(self, axis, step):
        index, size = {
            "context": (self.ctx, self.ctx_n), "dp": (self.dp, self.dp_n), "expert": (self.exp, self.exp_n)
        }[axis]
        return lax.rem(index + step, size)

    def send(self, src, dst, send, recv, axis, target):
        copy = self.plan(src, dst, send, recv, axis, target)
        copy.start()
        return copy

    def weight(self, k, source):
        origin = lax.rem(self.dp - k + self.dp_n, self.dp_n)
        name = self.ids_ref[origin * self.exp_n + source]
        return [jnp.where(name == a, 1.0, 0.0).astype(F32) for a in range(self.adapters)]

    def merge(self, count, read, write):
        marks = [self.weight(k, source) for k in range(self.dp_n) for source in range(self.exp_n)]

        def tile_sums(tile, carry):
            totals = [jnp.zeros((16, 128), F32)] * self.adapters
            for k in range(self.dp_n):
                for source in range(self.exp_n):
                    value = read(k, source, tile).astype(F32)
                    mark = marks[k * self.exp_n + source]
                    totals = [total + m * value for total, m in zip(totals, mark)]
            for a in range(self.adapters):
                write(a, tile, totals[a].astype(BF))
            return carry

        lax.fori_loop(0, count, tile_sums, 0)

    def start(self):
        for copy in self.loads:
            copy.start()
        if self.experts == 1:
            self.exchange()

    def exchange(self):
        for copy in self.z_copies:
            copy.start()

    def combine(self, e):
        z_tiles = self.arrived_z.shape[2]
        if e < self.experts - 1:
            if e == 0:
                self.loads[0].wait()
            source_ref = self.early.at[e]
        else:
            if self.experts == 1:
                self.loads[0].wait()
            self.loads[1].wait()
            for copy in self.z_copies:
                copy.wait_recv()
            source_ref = self.arrived_z

        def write(a, tile, value):
            self.table_ref[self.ctx, self.dp, e, a, tile] = value

        self.merge(z_tiles, lambda k, source, tile: source_ref[k, source, tile], write)
        self.push(e, 1)
        for copy in self.across(e, self.dp):
            copy.start()

    def push(self, e, s):
        if s < self.dp_n:
            for send, whether, _, _ in self.lines[e][s - 1]:
                pl.when(whether)(send.start)

    def advance(self, e, s):
        self.take(e, s)
        self.hand(e, s)

    def take(self, e, s):
        if s < self.dp_n:
            for _, _, receive, whether in self.lines[e][s - 1]:
                pl.when(whether)(receive.wait_recv)
            self.push(e, s + 1)

    def hand(self, e, s):
        if s >= self.dp_n:
            return
        for sign, (_, _, _, whether) in zip((1, -1), self.lines[e][s - 1]):
            @pl.when(whether)
            def _(sign=sign):
                for copy in self.across(e, self.dp - sign * s):
                    copy.start()

    def tail(self, between):
        def other(step):
            if step in between:
                between[step]()

        own, x_tiles, z_tiles = attn_tiling(self.attn_tiles)
        real = pl.cdiv(x_tiles, z_tiles)
        keep = pltpu.make_async_copy(
            self.attn_ref.at[pl.ds(self.exp * own, own)], self.held_a.at[self.exp, pl.ds(0, own)], self.keep_sem
        )
        keep.start()
        copies = [
            self.send(
                self.attn_ref.at[pl.ds(self.peer("expert", k) * own, own)],
                self.held_a.at[self.exp, pl.ds(0, own)],
                self.r_send.at[k - 1], self.r_recv.at[k - 1], "expert", self.peer("expert", k),
            )
            for k in range(1, self.exp_n)
        ]
        other("sources")
        keep.wait()
        for copy in copies:
            copy.wait_recv()
        copies = [
            self.send(
                self.held_a.at[:, pl.ds(self.peer("context", k) * x_tiles, x_tiles)], self.arrived_xa.at[k - 1],
                self.xa_send.at[k - 1], self.xa_recv.at[k - 1], "context", self.peer("context", k),
            )
            for k in range(1, self.ctx_n)
        ]
        other("context")
        for copy in copies:
            copy.wait_recv()
        total = self.held_a[:, pl.ds(self.ctx * x_tiles, x_tiles)].astype(F32)
        for k in range(1, self.ctx_n):
            total = total + self.arrived_xa[k - 1].astype(F32)
        self.part_a[:, 0:x_tiles] = total.astype(BF)
        copies = [
            self.send(
                self.part_a.at[:, pl.ds(self.peer("dp", k) * z_tiles, z_tiles)], self.arrived_za.at[k - 1],
                self.za_send.at[k - 1], self.za_recv.at[k - 1], "dp", self.peer("dp", k),
            )
            for k in range(1, self.dp_n)
        ]
        other("dp")
        for copy in copies:
            copy.wait_recv()
        mine = self.attn_table.at[self.exp]

        def write(a, tile, value):
            self.attn_table[self.exp, self.ctx, self.dp, a, tile] = value

        def read(k, source, tile):
            if k == 0:
                return self.part_a[source, self.dp * z_tiles + tile]
            return self.arrived_za[k - 1, source, tile]

        self.merge(z_tiles, read, write)
        here = mine.at[self.ctx, self.dp]
        copies = [
            self.send(here, here, self.bz_send.at[k - 1], self.bz_recv.at[k - 1], "dp", self.peer("dp", k))
            for k in range(1, self.dp_n)
        ]
        other("dp_back")
        for copy in copies:
            copy.wait_recv()
        here = mine.at[self.ctx, pl.ds(0, real)]
        copies = [
            self.send(
                here, here, self.bx_send.at[k - 1], self.bx_recv.at[k - 1], "context", self.peer("context", k)
            )
            for k in range(1, self.ctx_n)
        ]
        x_back = copies
        core = lax.rem(self.exp, 2)
        twin = self.exp + 1 - 2 * core
        chips = self.exp_n // 2

        def table_of(owner, j):
            return self.attn_table.at[owner, lax.rem(self.ctx + j, self.ctx_n), pl.ds(0, real)]

        far, near = [], []

        def along(j):
            for k in range(1, chips):
                here = table_of(self.exp, j)
                far.append(
                    self.send(
                        here, here, self.be_send.at[0, k - 1, j], self.be_recv.at[0, k - 1, j], "expert",
                        self.peer("expert", 2 * k),
                    )
                )
            near.append(self.to_twin(table_of(self.exp, j), 0, j, twin))

        along(0)
        other("context_back")
        for copy in x_back:
            copy.wait_recv()
        for j in range(1, self.ctx_n):
            along(j)
        for j in range(self.ctx_n):
            for k in range(1, chips):
                far[j * (chips - 1) + k - 1].wait_recv()
                owner = self.peer("expert", self.exp_n - 2 * k)
                near.append(self.to_twin(table_of(owner, j), k, j, twin))
        other("last")
        for copy in near:
            copy.wait_recv()

    def to_twin(self, here, k, j, twin):
        return self.send(here, here, self.be_send.at[1, k, j], self.be_recv.at[1, k, j], "expert", twin)

    def finish(self):
        for by_expert in self.ax_copies:
            for copies in by_expert:
                for copy in copies:
                    copy.wait()
        for by_expert in self.lines:
            for ways in by_expert:
                for send, whether, _, _ in ways:
                    pl.when(whether)(send.wait_send)
        for copy in self.waits:
            copy.wait_send()


def sums_shapes(experts, model, width, attn_tiles, adapters):
    ctx_n, dp_n, exp_n = (lax.axis_size(axis) for axis in ("context", "dp", "expert"))
    _, _, z_tiles = expert_tiling(experts, model, width)
    own, xa_tiles, za_tiles = attn_tiling(attn_tiles)
    many, deep, chips = max(ctx_n - 1, 1), max(dp_n - 1, 1), max(exp_n // 2, 1)
    dma = pltpu.SemaphoreType.DMA
    outs = (
        jax.ShapeDtypeStruct((ctx_n, dp_n, experts, adapters, z_tiles, 16, 128), BF),
        jax.ShapeDtypeStruct((exp_n, ctx_n, dp_n, adapters, za_tiles, 16, 128), BF),
    )
    scratch = [
        pltpu.VMEM((dp_n, exp_n, z_tiles, 16, 128), BF),
        pltpu.VMEM((max(experts - 1, 1), dp_n, exp_n, z_tiles, 16, 128), BF),
        pltpu.VMEM((exp_n, max(ctx_n * xa_tiles, own), 16, 128), BF),
        pltpu.VMEM((many, exp_n, xa_tiles, 16, 128), BF),
        pltpu.VMEM((exp_n, dp_n * za_tiles, 16, 128), BF),
        pltpu.VMEM((deep, exp_n, za_tiles, 16, 128), BF),
        dma((deep,)), dma((deep,)), dma((experts, 2, deep)), dma((experts, 2, deep)),
        dma((many, experts, dp_n)), dma((many, experts, dp_n)),
        dma((exp_n,)), dma((exp_n,)), dma((many,)), dma((many,)), dma((deep,)), dma((deep,)),
        dma((deep,)), dma((deep,)), dma((many,)), dma((many,)), dma((2, chips, ctx_n)), dma((2, chips, ctx_n)),
        dma, dma((2,)),
    ]
    return outs, scratch


ALL_AXES = ("context", "dp", "expert")


def sums_kernel(sizes, ids_ref, sums_ref, early_ref, attn_ref, table_ref, attn_table, *scratch):
    greet([(axis, lax.axis_size(axis)) for axis in ALL_AXES])()
    sums = Sums(sizes, ids_ref, sums_ref, early_ref, attn_ref, table_ref, attn_table, scratch)
    sums.start()
    for e in range(sums.experts):
        if e > 0 and e == sums.experts - 1:
            sums.exchange()
        sums.combine(e)
    for e in range(sums.experts):
        for s in range(1, sums.dp_n):
            sums.advance(e, s)
    sums.tail({})
    sums.finish()


def add_up(ids, sums, attn, experts, width, adapters):
    model = attn.shape[0] * 16
    outs, scratch = sums_shapes(experts, model, width, attn.shape[0], adapters)
    vmem, hbm = pl.BlockSpec(memory_space=pltpu.VMEM), pl.BlockSpec(memory_space=pl.ANY)
    sizes = tuple(lax.axis_size(axis) for axis in ALL_AXES) + (adapters, attn.shape[0])
    return pl.pallas_call(
        functools.partial(sums_kernel, sizes),
        out_shape=outs,
        in_specs=[pl.BlockSpec(memory_space=pltpu.SMEM), hbm, hbm, vmem],
        out_specs=(vmem, vmem),
        scratch_shapes=scratch,
        compiler_params=pltpu.CompilerParams(
            collective_id=1, has_side_effects=True, vmem_limit_bytes=VLIMIT
        ),
        name="reduce_adapters",
    )(ids, *sums, attn)


def unpack_kernel(sizes, *refs):
    table_ref, attn_ref, *passed = refs[:8]
    for ref_in, ref_out in zip(passed[:3], passed[3:]):
        ref_out[...] = ref_in[...]
    for a in range(table_ref.shape[3]):
        unpack_one(sizes, a, table_ref, attn_ref, *refs[8:])


def unpack_one(sizes, a, table_ref, attn_ref, down_ref, up_ref, in_down_ref, in_up_ref, out_down_ref, out_up_ref):
    share, z_tiles, own, xa_tiles, za_tiles = sizes
    for expert in range(in_up_ref.shape[1]):
        tile = 0
        for out_ref in (in_down_ref, in_up_ref, out_down_ref, out_up_ref):
            rows, cols = out_ref.shape[2:]
            for row in range(rows // 16):
                for col in range(cols // 128):
                    place = tile % share
                    out_ref[a, expert, row * 16 : row * 16 + 16, col * 128 : col * 128 + 128] = table_ref[
                        tile // share, place // z_tiles, expert, a, place % z_tiles
                    ].astype(F32)
                    tile += 1
    tile = 0
    for out_ref in (down_ref, up_ref):
        rows, cols = out_ref.shape[1:]
        for row in range(rows // 16):
            for col in range(cols // 128):
                place = tile % own
                out_ref[a, row * 16 : row * 16 + 16, col * 128 : col * 128 + 128] = attn_ref[
                    tile // own, place // xa_tiles, place % xa_tiles // za_tiles, a, place % xa_tiles % za_tiles
                ].astype(F32)
                tile += 1


def unpack(table, attn_table, by_token, experts, width, table_shapes, attn_shape):
    adapters = table.shape[3]
    each = adapters // 2
    model = attn_shape[1]
    share, _, z_tiles = expert_tiling(experts, model, width)
    sizes = (share, z_tiles) + attn_tiling(8 * model // 128)
    shapes = [(adapters,) + attn_shape] * 2 + [(adapters,) + shape for shape in table_shapes]

    def by_adapter(array, axis):
        block = array.shape[:axis] + (each,) + array.shape[axis + 1 :]
        return pl.BlockSpec(block, lambda a, n=array.ndim: (0,) * axis + (a,) + (0,) * (n - axis - 1))

    hidden, grad, prev = by_token
    part = pl.BlockSpec((hidden.shape[0] * each // adapters, model), lambda a: (a, 0))
    passed = [part, part, pl.BlockSpec(prev.shape, lambda a: (0, 0, 0))]
    return pl.pallas_call(
        functools.partial(unpack_kernel, sizes),
        grid=(adapters // each,),
        out_shape=tuple(jax.ShapeDtypeStruct(entry.shape, entry.dtype) for entry in by_token)
        + tuple(jax.ShapeDtypeStruct(shape, F32) for shape in shapes),
        in_specs=[by_adapter(table, 3), by_adapter(attn_table, 3), *passed],
        out_specs=tuple(passed)
        + tuple(
            pl.BlockSpec((each,) + shape[1:], lambda a, n=len(shape): (a,) + (0,) * (n - 1))
            for shape in shapes
        ),
        compiler_params=pltpu.CompilerParams(vmem_limit_bytes=VLIMIT),
        name="unpack_adapters",
    )(table, attn_table, *by_token)


def local(
    hidden_in,
    prev_logits,
    segment_ids,
    routes,
    adapter_ids,
    attn_gain,
    w_qkv,
    w_out,
    attn_down,
    attn_up,
    ffn_gain,
    router_weight,
    gate_mix,
    const_mix,
    const_vec,
    w_gate_up,
    w_down,
    exp_in_down,
    exp_in_up,
    exp_out_down,
    exp_out_up,
    cotangent,
):
    model_dim = hidden_in.shape[2]
    local_experts, ffn_width = w_down.shape[:2]
    adapter_count = attn_down.shape[0]
    rank_dim = attn_up.shape[2]
    down_all = jnp.swapaxes(attn_down, 2, 3).reshape(adapter_count, 4 * rank_dim, model_dim)
    up_all = attn_up.reshape(adapter_count, 4 * rank_dim, model_dim)
    small = (router_weight.T, const_mix.transpose(0, 2, 1), attn_gain, ffn_gain)
    (
        q_pairs, k_pairs, v_pairs, normed_all, rank_all, log_cols, attn_flat, rank_out_all, mid_resid,
        rows_low, logits_all, seg_all, arrived_dy, slots, router_rows,
    ) = attention_forward(
        hidden_in[0], segment_ids, prev_logits.transpose(2, 0, 1), gate_mix, adapter_ids, w_qkv, w_out, down_all,
        up_all, small, cotangent[0], routes[0].T, local_experts,
    )
    tables = (
        jnp.swapaxes(exp_in_down, 2, 3),
        exp_in_up.reshape(exp_in_up.shape[:2] + (2 * rank_dim, ffn_width)),
        jnp.swapaxes(exp_out_down, 2, 3),
        exp_out_up,
    )
    base, d_mid, grad_prev, *expert_sums, done_out, cols = expert_layer(
        rows_low, mid_resid, logits_all, slots, cotangent[0], arrived_dy, adapter_ids, router_rows,
        gate_mix, const_vec, w_gate_up, w_down, tables,
    )
    grad_in, table, attn_table, hidden_out = attention_backward(
        d_mid,
        (q_pairs, k_pairs, v_pairs, normed_all, rank_all, log_cols, attn_flat, rank_out_all, seg_all),
        hidden_in[0], adapter_ids, router_rows, w_qkv, w_out, down_all, up_all, expert_sums,
        (done_out, base, cols), local_experts, ffn_width,
    )
    hidden_out, grad_in, grad_prev, *sums = unpack(
        table, attn_table, (hidden_out, grad_in, grad_prev), local_experts, ffn_width, [entry.shape[1:] for entry in tables],
        (4 * rank_dim, model_dim),
    )
    grad_attn_down = jnp.swapaxes(sums[0].reshape(adapter_count, 4, rank_dim, model_dim), 2, 3)
    grad_attn_up = sums[1].reshape(adapter_count, 4, rank_dim, model_dim)
    grad_in_down = jnp.swapaxes(sums[2], 2, 3)
    grad_in_up = sums[3].reshape(exp_in_up.shape)
    grad_out_down = jnp.swapaxes(sums[4], 2, 3)
    grad_out_up = sums[5]
    return (
        hidden_out[None],
        grad_in[None],
        grad_prev.transpose(1, 2, 0),
        grad_attn_down,
        grad_attn_up,
        grad_in_down,
        grad_in_up,
        grad_out_down,
        grad_out_up,
    )


def solution(mesh):
    return jax.shard_map(
        local,
        mesh=mesh,
        in_specs=(
            P(("dp", "expert"), "context", None),
            P(("dp", "expert"), "context", None),
            P(("dp", "expert"), "context"),
            P(("dp", "expert"), "context", None),
            P(),
            P(),
            P(),
            P(),
            P(),
            P(),
            P(),
            P(),
            P(),
            P(),
            P(),
            P("expert", None, None),
            P("expert", None, None),
            P(None, "expert", None, None),
            P(None, "expert", None, None, None),
            P(None, "expert", None, None),
            P(None, "expert", None, None),
            P(("dp", "expert"), "context", None),
        ),
        out_specs=(
            P(("dp", "expert"), "context", None),
            P(("dp", "expert"), "context", None),
            P(("dp", "expert"), "context", None),
            P(),
            P(),
            P(None, "expert", None, None),
            P(None, "expert", None, None, None),
            P(None, "expert", None, None),
            P(None, "expert", None, None),
        ),
        check_vma=False,
    )
```
